32 devices in a mesh: dp: 16 (over z, y, core), tensor: 2 (over x).
Axes of the slice: x: 2, y: 2, z: 4, core: 2. Of those that a mesh axis runs over, the one named last changes fastest.
Arguments:
- block_input: bfloat16 [16384, 1024], P(('dp', 'tensor')), may hold values from -6 to 6
- segment_ids: int32 [16384], P('dp'), may hold values from 0 to 2, as said below
- ln1_gain: float32 [1024], replicated, may hold values from 0.1 to 1.9
- ln1_bias: float32 [1024], replicated, may hold values from -4 to 4
- w_query: bfloat16 [1024, 1024], P('dp', 'tensor'), may hold values from -0.1875 to 0.1875
- w_key: bfloat16 [1024, 1024], P('dp', 'tensor'), may hold values from -0.1875 to 0.1875
- w_value: bfloat16 [1024, 1024], P('dp', 'tensor'), may hold values from -0.1875 to 0.1875
- b_query: float32 [1024], replicated, may hold values from -6 to 6
- b_value: float32 [1024], replicated, may hold values from -6 to 6
- w_out: bfloat16 [1024, 1024], P('dp', 'tensor'), may hold values from -1 to 1
- b_out: float32 [1024], replicated, may hold values from -4 to 4
- ln2_gain: float32 [1024], replicated, may hold values from 0.1 to 1.9
- ln2_bias: float32 [1024], replicated, may hold values from -4 to 4
- w_up: bfloat16 [1024, 4096], P('dp', 'tensor'), may hold values from -0.1875 to 0.1875
- b_up: float32 [4096], replicated, may hold values from -6 to 6
- w_down: bfloat16 [1024, 4096], P('dp', 'tensor'), may hold values from -0.125 to 0.125
- b_down: float32 [1024], replicated, may hold values from -4 to 4
- out_grad: bfloat16 [16384, 1024], P(('dp', 'tensor')), may hold values from -6 to 6
Outputs:
- block_output: bfloat16 [16384, 1024], P(('dp', 'tensor'))
- grad_input: bfloat16 [16384, 1024], P(('dp', 'tensor'))
- grad_ln1_gain: float32 [1024], replicated
- grad_ln1_bias: float32 [1024], replicated
- grad_w_query: float32 [1024, 1024], P('dp', 'tensor')
- grad_w_key: float32 [1024, 1024], P('dp', 'tensor')
- grad_w_value: float32 [1024, 1024], P('dp', 'tensor')
- grad_b_query: float32 [1024], replicated
- grad_b_value: float32 [1024], replicated
- grad_w_out: float32 [1024, 1024], P('dp', 'tensor')
- grad_b_out: float32 [1024], replicated
- grad_ln2_gain: float32 [1024], replicated
- grad_ln2_bias: float32 [1024], replicated
- grad_w_up: float32 [1024, 4096], P('dp', 'tensor')
- grad_b_up: float32 [4096], replicated
- grad_w_down: float32 [1024, 4096], P('dp', 'tensor')
- grad_b_down: float32 [1024], replicated
The draws below stay inside these ranges and needn't reach their ends.
Inputs may be any that keep to these rules, and one draw needn't show every extreme that they name: `segment_ids`: within each data group of 1024 consecutive tokens the ids are 0, 1 and 2, each present, never falling; the block's attention never reaches across data groups.
All inputs are finite; a program needn't handle non-finite values.
Results may differ from the reference program's by a relative error of at most 0.018.
Values may be sent and summed in bfloat16 or wider, within the bound.
No kernel may reach another device: no remote copies, remote signals or barrier semaphores. Data moves between devices by JAX's collectives and lax.ppermute only.
A program may use at most 192 MiB of HBM per device.

```python
import jax
import jax.numpy as jnp
from jax import lax

D = 1024
HEADS = 16
HEAD_DIM = 64
FF = 4096
SEQ_TOK = 1024
TOK_DEV = 512
TOKENS = 16384


def draw_segment_ids(key, part):
    key = jax.random.fold_in(key, 7)
    first_key, second_key = jax.random.split(key)
    group_count = TOKENS // SEQ_TOK
    head_len = jax.random.randint(first_key, (group_count, 1), 1, TOK_DEV // 2)
    tail_len = jax.random.randint(second_key, (group_count, 1), 1, TOK_DEV // 2)
    places = jnp.arange(SEQ_TOK)[None, :]
    labels = (places >= head_len).astype(jnp.int32) + (places >= SEQ_TOK - tail_len).astype(jnp.int32)
    return labels.reshape(TOKENS).astype(jnp.int32)


def shard_levels(key, extent, cuts, smallest, top_value):
    gain, own = 1.0, jax.random.fold_in(key, 6)
    for position, shards_of in cuts:
        heights = jnp.exp(jax.random.uniform(jax.random.fold_in(own, position), (shards_of,), jnp.float32, smallest / len(cuts), top_value / len(cuts)))
        gain = gain * jnp.repeat(heights, extent[position] // shards_of).reshape([-1 if axis == position else 1 for axis in range(len(extent))])
    return gain


def gaussian(stream_key, extent, width, reach, pieces=(), kind=jnp.bfloat16):
    array = width * jax.random.normal(stream_key, extent, jnp.float32)
    if pieces:
        array = array * shard_levels(stream_key, extent, pieces, -0.22, 0.18)
    return jnp.clip(array, -reach, reach).astype(kind)


def setup_inputs(seed: int = 0) -> dict:
    streams_of = jax.random.split(jax.random.key(seed), 19)
    return {
        "block_input": gaussian(streams_of[0], (TOKENS, D), 1.0, 6.0, ((0, 32),)),
        "segment_ids": draw_segment_ids(jax.random.fold_in(streams_of[18], 71), 0),
        "ln1_gain": jnp.clip(1.0 + 0.18 * jax.random.normal(streams_of[2], (D,), jnp.float32), 0.1, 1.9),
        "ln1_bias": gaussian(streams_of[3], (D,), 0.3, 4.0, (), jnp.float32),
        "w_query": gaussian(streams_of[4], (D, D), D ** -0.5, 0.1875, ((0, 16), (1, 2))),
        "w_key": gaussian(streams_of[5], (D, D), D ** -0.5, 0.1875, ((0, 16), (1, 2))),
        "w_value": gaussian(streams_of[6], (D, D), D ** -0.5, 0.1875, ((0, 16), (1, 2))),
        "b_query": gaussian(streams_of[7], (D,), 0.5, 6.0, (), jnp.float32),
        "b_value": gaussian(streams_of[8], (D,), 0.5, 6.0, (), jnp.float32),
        "w_out": gaussian(streams_of[9], (D, D), (D // 32) ** -0.5, 1.0, ((0, 16), (1, 2))),
        "b_out": gaussian(streams_of[10], (D,), 0.3, 4.0, (), jnp.float32),
        "ln2_gain": jnp.clip(1.0 + 0.18 * jax.random.normal(streams_of[11], (D,), jnp.float32), 0.1, 1.9),
        "ln2_bias": gaussian(streams_of[12], (D,), 0.3, 4.0, (), jnp.float32),
        "w_up": gaussian(streams_of[13], (D, FF), D ** -0.5, 0.1875, ((0, 16), (1, 2))),
        "b_up": gaussian(streams_of[14], (FF,), 0.5, 6.0, (), jnp.float32),
        "w_down": gaussian(streams_of[15], (D, FF), (FF // 2) ** -0.5, 0.125, ((0, 16), (1, 2))),
        "b_down": gaussian(streams_of[16], (D,), 0.3, 4.0, (), jnp.float32),
        "out_grad": gaussian(streams_of[17], (TOKENS, D), 1.0, 6.0, ((0, 32),)),
    }


@jax.custom_vjp
def low(v):
    return lax.optimization_barrier(v.astype(jnp.bfloat16)).astype(jnp.float32)

@jax.custom_vjp
def low_back(v):
    return v

def low_keep(v):
    return (low(v), None)

def low_pass(kept, grad):
    return (grad,)

def back_keep(v):
    return (v, None)

def back_low(kept, grad):
    return (low(grad),)
low.defvjp(low_keep, low_pass)
low_back.defvjp(back_keep, back_low)

def layer_norm(values, gain_vec, bias_vec):
    center = values - lax.optimization_barrier(jnp.mean(values, axis=-1, keepdims=True))
    spread = lax.optimization_barrier(jnp.mean(center * center, axis=-1, keepdims=True))
    return center * lax.rsqrt(spread + 1e-05) * gain_vec + bias_vec

def gelu_tanh(values):
    return 0.5 * values * (1.0 + jnp.tanh(0.7978845608028654 * (values + 0.044715 * values * values * values)))

def matmul(left_mat, right_mat):
    return jnp.dot(left_mat, right_mat, precision=lax.Precision.HIGHEST)

def split_heads(matrix):
    return matrix.reshape(matrix.shape[0], HEADS, HEAD_DIM).transpose(1, 0, 2)

def group_forward(params, group_rows, group_ids):
    ln1_gain, ln1_bias, w_query, w_key, w_value, b_query, b_value, w_out, b_out, ln2_gain, ln2_bias, w_up, b_up, w_down, b_down = params
    length = group_rows.shape[0]
    normed = low(layer_norm(group_rows, ln1_gain, ln1_bias))
    queries = low(low_back(matmul(normed, w_query) + b_query))
    key_rows = low(low_back(matmul(normed, w_key)))
    value_rows = low(low_back(matmul(normed, w_value) + b_value))
    raw_scores = jnp.einsum('hqd,hkd->hqk', split_heads(queries), split_heads(key_rows), precision=lax.Precision.HIGHEST)
    scores = low_back(raw_scores * HEAD_DIM ** (-0.5))
    places = jnp.arange(length)
    allowed = (group_ids[:, None] == group_ids[None, :]) & (places[:, None] >= places[None, :])
    scores = jnp.where(allowed[None], scores, -1e+30)
    attn_probs = jax.nn.softmax(scores, axis=-1)
    mixed_heads = jnp.einsum('hqk,hkd->hqd', low(attn_probs), split_heads(value_rows), precision=lax.Precision.HIGHEST)
    mixed_rows = low(low_back(mixed_heads.transpose(1, 0, 2).reshape(length, D)))
    attended = low_back(matmul(mixed_rows, w_out.T))
    hidden = group_rows + attended + b_out
    normed_two = low(layer_norm(hidden, ln2_gain, ln2_bias))
    pre_active = low_back(matmul(normed_two, w_up) + b_up)
    active = low(gelu_tanh(pre_active))
    return hidden + matmul(active, w_down.T) + b_down

def reference(block_input, segment_ids, ln1_gain, ln1_bias, w_query, w_key, w_value, b_query, b_value, w_out, b_out, ln2_gain, ln2_bias, w_up, b_up, w_down, b_down, out_grad):
    params = (ln1_gain, ln1_bias, w_query.astype(jnp.float32), w_key.astype(jnp.float32), w_value.astype(jnp.float32), b_query, b_value, w_out.astype(jnp.float32), b_out, ln2_gain, ln2_bias, w_up.astype(jnp.float32), b_up, w_down.astype(jnp.float32), b_down)
    group_ids = segment_ids.reshape(-1, SEQ_TOK)

    def forward(all_rows, weights):
        groups = all_rows.reshape(-1, SEQ_TOK, D)
        group_step = jax.checkpoint(lambda group_rows, ids_now: group_forward(weights, group_rows, ids_now))

        def scan_step(carried, inputs):
            return (carried, group_step(inputs[0], inputs[1]))
        _, outputs = lax.scan(scan_step, jnp.zeros((), jnp.float32), (groups, group_ids))
        return outputs.reshape(-1, D)
    output, pullback = jax.vjp(forward, block_input.astype(jnp.float32), params)
    grad_rows, grads = pullback(out_grad.astype(jnp.float32))
    return (output.astype(jnp.bfloat16), grad_rows.astype(jnp.bfloat16), grads[0], grads[1], grads[2], grads[3], grads[4], grads[5], grads[6], grads[7], grads[8], grads[9], grads[10], grads[11], grads[12], grads[13], grads[14])
```

```python
import functools

import jax
import jax.numpy as jnp
from jax import lax
from jax.experimental import pallas as pl
from jax.experimental.pallas import tpu as pltpu
from jax.sharding import Mesh
from jax.sharding import PartitionSpec as P

HEAD_DIM = 64
LANES = 128
MASKED = -1e30
VMEM_BYTES = 60 * 1024 * 1024
F32 = jnp.float32
BF16 = jnp.bfloat16
DATA = ("a", "h")
TP = ("l", "c")
SWAP = ("c", "h", "l")


def normalize(values):
    center = values - jnp.mean(values, axis=-1, keepdims=True)
    spread = jnp.mean(center * center, axis=-1, keepdims=True)
    inverse = lax.rsqrt(spread + 1e-05)
    return center * inverse, inverse


def norm_back(grad_in, scaled, inverse, gain_vec):
    local_grad = grad_in * gain_vec
    return inverse * (
        local_grad
        - jnp.mean(local_grad, axis=-1, keepdims=True)
        - scaled * jnp.mean(local_grad * scaled, axis=-1, keepdims=True)
    )


def dot_nn(left, right):
    return lax.dot_general(left, right, (((1,), (0,)), ((), ())), preferred_element_type=F32)


def dot_nt(left, right):
    return lax.dot_general(left, right, (((1,), (1,)), ((), ())), preferred_element_type=F32)


def dot_tn(left, right):
    return lax.dot_general(left, right, (((0,), (0,)), ((), ())), preferred_element_type=F32)


def fill_bias(bias, seg_col, seg_row):
    length = bias.shape[0]
    block = min(256, length)
    for first in range(0, length, block):
        keys = lax.broadcasted_iota(jnp.int32, (block, length), 0) + first
        places = lax.broadcasted_iota(jnp.int32, (block, length), 1)
        same = seg_col[first : first + block, :] == seg_row[...]
        bias[first : first + block, :] = jnp.where(same & (keys <= places), 0.0, MASKED)


def head_lanes(values, head):
    lane = lax.broadcasted_iota(jnp.int32, values.shape, 1)
    inside = (lane >= head * HEAD_DIM) & (lane < (head + 1) * HEAD_DIM)
    return jnp.where(inside, values, jnp.zeros_like(values))


def attn_forward_kernel(seg_col, seg_row, q_ref, k_ref, v_ref, mixed_ref, lse_ref, bias, v_t, block):
    length = q_ref.shape[0]
    heads = LANES // HEAD_DIM

    @pl.when(pl.program_id(0) == 0)
    def _():
        fill_bias(bias, seg_col, seg_row)

    v_t[...] = v_ref[...].T
    for place in range(length // block):
        rows = slice(place * block, (place + 1) * block)
        outs = []
        for head in range(heads):
            query = head_lanes(q_ref[rows, :], head)
            scores = []
            peak = None
            for other in range(place + 1):
                keys = slice(other * block, (other + 1) * block)
                part = dot_nt(k_ref[keys, :], query) + bias[keys, rows]
                top = jnp.max(part, axis=0, keepdims=True)
                peak = top if peak is None else jnp.maximum(peak, top)
                scores.append(part)
            total = None
            acc = None
            for other in range(place + 1):
                keys = slice(other * block, (other + 1) * block)
                weight = jnp.exp(scores[other] - peak)
                part_sum = jnp.sum(weight, axis=0, keepdims=True)
                total = part_sum if total is None else total + part_sum
                part_out = dot_nn(
                    v_t[head * HEAD_DIM : (head + 1) * HEAD_DIM, keys], weight.astype(BF16)
                )
                acc = part_out if acc is None else acc + part_out
            outs.append(acc / total)
            lse_ref[0, head : head + 1, rows] = peak + jnp.log(total)
        mixed_ref[rows, :] = jnp.concatenate(outs, axis=0).T.astype(BF16)


def attn_backward_kernel(
    seg_col, seg_row, q_ref, k_ref, v_ref, mixed_ref, lse_ref, g_ref, grads_ref, bias, k_t, delta, dq_t, block
):
    length = q_ref.shape[0]
    heads = LANES // HEAD_DIM
    count = length // block

    @pl.when(pl.program_id(0) == 0)
    def _():
        fill_bias(bias, seg_col, seg_row)

    k_t[...] = k_ref[...].T
    product = (g_ref[...].astype(F32) * mixed_ref[...].astype(F32)).T
    for head in range(heads):
        delta[head : head + 1, :] = jnp.sum(
            product[head * HEAD_DIM : (head + 1) * HEAD_DIM, :], axis=0, keepdims=True
        )
    for other in range(count):
        keys = slice(other * block, (other + 1) * block)
        key_sum = None
        value_sum = None
        for head in range(heads):
            lanes = slice(head * HEAD_DIM, (head + 1) * HEAD_DIM)
            for place in range(other, count):
                rows = slice(place * block, (place + 1) * block)
                query = head_lanes(q_ref[rows, :], head)
                grad = head_lanes(g_ref[rows, :], head)
                scores = dot_nt(k_ref[keys, :], query) + bias[keys, rows]
                probs = jnp.exp(scores - lse_ref[0, head : head + 1, rows])
                grad_probs = dot_nt(v_ref[keys, :], grad)
                grad_scores = (probs * (grad_probs - delta[head : head + 1, rows])).astype(BF16)
                value_part = dot_nn(probs.astype(BF16), grad)
                key_part = dot_nn(grad_scores, query)
                query_part = dot_nn(k_t[lanes, keys], grad_scores)
                value_sum = value_part if value_sum is None else value_sum + value_part
                key_sum = key_part if key_sum is None else key_sum + key_part
                if other == 0:
                    dq_t[lanes, rows] = query_part
                else:
                    dq_t[lanes, rows] += query_part
        grads_ref[1, keys, :] = key_sum.astype(BF16)
        grads_ref[2, keys, :] = value_sum.astype(BF16)
    grads_ref[0] = (dq_t[...].T * HEAD_DIM ** (-0.5)).astype(BF16)


def attn_forward(segments, qkv, width):
    length = qkv.shape[0]
    pairs = width // LANES
    block = min(256, length)
    column = lambda first: pl.BlockSpec((length, LANES), lambda p: (0, first * pairs + p))
    whole = lambda shape: pl.BlockSpec(shape, lambda p: (0, 0))
    return pl.pallas_call(
        functools.partial(attn_forward_kernel, block=block),
        grid=(pairs,),
        in_specs=[whole((length, 1)), whole((1, length)), column(0), column(1), column(2)],
        out_specs=[
            pl.BlockSpec((length, LANES), lambda p: (0, p)),
            pl.BlockSpec((1, 8, length), lambda p: (p, 0, 0)),
        ],
        out_shape=[
            jax.ShapeDtypeStruct((length, width), BF16),
            jax.ShapeDtypeStruct((pairs, 8, length), F32),
        ],
        scratch_shapes=[pltpu.VMEM((length, length), F32), pltpu.VMEM((LANES, length), BF16)],
        compiler_params=pltpu.CompilerParams(vmem_limit_bytes=VMEM_BYTES),
        cost_estimate=pl.CostEstimate(
            flops=4 * length * length * width,
            bytes_accessed=8 * length * width,
            transcendentals=length * length * width // (2 * HEAD_DIM),
        ),
        name="attn_forward",
    )(segments.reshape(length, 1), segments.reshape(1, length), qkv, qkv, qkv)


def attn_backward(segments, qkv, mixed, lse, grad_mixed, width):
    length = qkv.shape[0]
    pairs = width // LANES
    block = min(256, length)
    column = lambda first: pl.BlockSpec((length, LANES), lambda p: (0, first * pairs + p))
    whole = lambda shape: pl.BlockSpec(shape, lambda p: (0, 0))
    return pl.pallas_call(
        functools.partial(attn_backward_kernel, block=block),
        grid=(pairs,),
        in_specs=[
            whole((length, 1)),
            whole((1, length)),
            column(0),
            column(1),
            column(2),
            pl.BlockSpec((length, LANES), lambda p: (0, p)),
            pl.BlockSpec((1, 8, length), lambda p: (p, 0, 0)),
            pl.BlockSpec((length, LANES), lambda p: (0, p)),
        ],
        out_specs=pl.BlockSpec((3, length, LANES), lambda p: (0, 0, p)),
        out_shape=jax.ShapeDtypeStruct((3, length, width), BF16),
        scratch_shapes=[
            pltpu.VMEM((length, length), F32),
            pltpu.VMEM((LANES, length), BF16),
            pltpu.VMEM((8, length), F32),
            pltpu.VMEM((LANES, length), F32),
        ],
        compiler_params=pltpu.CompilerParams(vmem_limit_bytes=VMEM_BYTES),
        cost_estimate=pl.CostEstimate(
            flops=10 * length * length * width,
            bytes_accessed=16 * length * width,
            transcendentals=length * length * width // (2 * HEAD_DIM),
        ),
        name="attn_backward",
    )(segments.reshape(length, 1), segments.reshape(1, length), qkv, qkv, qkv, mixed, lse, grad_mixed)


def mlp_kernel(
    n_ref, g_ref, nt_ref, gt_ref, up_ref, down_ref, b_ref,
    out_ref, gn_ref, gup_ref, gdown_ref, gb_ref,
    out_acc, gn_acc, act, gpre, block
):
    step = pl.program_id(0)
    length = n_ref.shape[0]

    @pl.when(step == 0)
    def _():
        out_acc[...] = jnp.zeros_like(out_acc)
        gn_acc[...] = jnp.zeros_like(gn_acc)

    bias_sum = jnp.zeros(gb_ref.shape, F32)
    for first in range(0, length, block):
        rows = slice(first, first + block)
        unit = dot_nn(n_ref[rows, :], up_ref[...]) + b_ref[...]
        grad = dot_nn(g_ref[rows, :], down_ref[...])
        square = unit * unit
        curve = jnp.tanh(0.7978845608028654 * (unit + 0.044715 * (square * unit)))
        half = 0.5 + 0.5 * curve
        slope = half + (0.5 * unit) * (1.0 - curve * curve) * (
            0.7978845608028654 + (3 * 0.044715 * 0.7978845608028654) * square
        )
        active = (unit * half).astype(BF16)
        grad_pre = (grad * slope).astype(BF16)
        act[rows, :] = active
        gpre[rows, :] = grad_pre
        bias_sum = bias_sum + jnp.sum(grad_pre.astype(F32), axis=0, keepdims=True)
        out_acc[rows, :] += dot_nt(active, down_ref[...])
        gn_acc[rows, :] += dot_nt(grad_pre, up_ref[...])
    gb_ref[...] = bias_sum
    gdown_ref[...] = dot_nn(gt_ref[...], act[...]).astype(BF16)
    gup_ref[...] = dot_nn(nt_ref[...], gpre[...]).astype(BF16)

    @pl.when(step == pl.num_programs(0) - 1)
    def _():
        out_ref[...] = out_acc[...].astype(BF16)
        gn_ref[...] = gn_acc[...].astype(BF16)


def mlp(normed, grad, normed_t, grad_t, weights, bias):
    length, width = normed.shape
    units = weights.shape[1] // 2
    tile = min(256, units)
    tiles = units // tile
    whole = lambda shape: pl.BlockSpec(shape, lambda u: (0, 0), pipeline_mode=pl.Buffered(1))
    return pl.pallas_call(
        functools.partial(mlp_kernel, block=min(256, length)),
        grid=(tiles,),
        in_specs=[
            whole((length, width)),
            whole((length, width)),
            whole((width, length)),
            whole((width, length)),
            pl.BlockSpec((width, tile), lambda u: (0, u)),
            pl.BlockSpec((width, tile), lambda u: (0, tiles + u)),
            pl.BlockSpec((1, tile), lambda u: (0, u)),
        ],
        out_specs=[
            pl.BlockSpec((length, width), lambda u: (0, 0)),
            pl.BlockSpec((length, width), lambda u: (0, 0)),
            pl.BlockSpec((width, tile), lambda u: (0, u)),
            pl.BlockSpec((width, tile), lambda u: (0, u)),
            pl.BlockSpec((1, tile), lambda u: (0, u)),
        ],
        out_shape=[
            jax.ShapeDtypeStruct((length, width), BF16),
            jax.ShapeDtypeStruct((length, width), BF16),
            jax.ShapeDtypeStruct((width, units), BF16),
            jax.ShapeDtypeStruct((width, units), BF16),
            jax.ShapeDtypeStruct((1, units), F32),
        ],
        scratch_shapes=[
            pltpu.VMEM((length, width), F32),
            pltpu.VMEM((length, width), F32),
            pltpu.VMEM((length, tile), BF16),
            pltpu.VMEM((length, tile), BF16),
        ],
        compiler_params=pltpu.CompilerParams(vmem_limit_bytes=VMEM_BYTES),
        cost_estimate=pl.CostEstimate(
            flops=12 * length * width * units,
            bytes_accessed=12 * length * width + 8 * width * units,
            transcendentals=length * units,
        ),
        name="mlp_both",
    )(normed, grad, normed_t, grad_t, weights, weights, bias.reshape(1, units))


def per_device(sizes, *arguments):
    (
        block_input, segment_ids, ln1_gain, ln1_bias, w_query, w_key, w_value, b_query, b_value,
        w_out, b_out, ln2_gain, ln2_bias, w_up, b_up, w_down, b_down, out_grad,
    ) = arguments
    ranks = sizes["h"] * sizes["l"]
    rank = lax.axis_index(TP)
    length = segment_ids.shape[0]
    own_rows = block_input.shape[0]
    head_width = w_query.shape[1]
    unit_width = w_up.shape[1]
    half_units = unit_width // 2
    forth = []
    for group in range(2):
        for part in range(ranks):
            forth.append((group * ranks + part, (part % 2) * ranks + group * (ranks // 2) + part // 2))
    back = [(to, frm) for frm, to in forth]

    def move_in(values):
        return lax.ppermute(values, SWAP, forth)

    def move_out(values):
        return lax.ppermute(values, SWAP, back)

    def partner(values):
        return lax.ppermute(values, "c", [(0, 1), (1, 0)])

    def tp_gather(values):
        if ranks != 2:
            return lax.all_gather(values, TP, axis=0, tiled=True)
        theirs = partner(values)
        return jnp.where(
            rank == 0,
            jnp.concatenate([values, theirs], axis=0),
            jnp.concatenate([theirs, values], axis=0),
        )

    def tp_sum(values):
        if ranks != 2:
            return lax.psum(values.astype(F32), TP)
        return values.astype(F32) + partner(values).astype(F32)

    def own(values):
        return lax.dynamic_slice_in_dim(values, rank * own_rows, own_rows)

    def tp_scatter(values):
        if ranks != 2:
            return lax.psum_scatter(values, TP, scatter_dimension=0, tiled=True).astype(F32)
        theirs = lax.dynamic_slice_in_dim(values, (1 - rank) * own_rows, own_rows)
        return own(values).astype(F32) + partner(theirs).astype(F32)

    def gather_weights(values):
        return lax.all_gather(move_in(values), DATA, axis=0, tiled=True)

    full_attn = gather_weights(jnp.concatenate([w_query, w_key, w_value, w_out], axis=1))
    full_mlp = [
        gather_weights(
            jnp.concatenate(
                [w_up[:, first : first + half_units], w_down[:, first : first + half_units]], axis=1
            )
        )
        for first in (0, half_units)
    ]
    full_qkv = full_attn[:, : 3 * head_width]
    full_out = full_attn[:, 3 * head_width :]
    own_input = move_in(block_input)
    segments = move_in(segment_ids)
    own_grad = move_in(out_grad)
    bias_query = lax.dynamic_slice_in_dim(b_query, rank * head_width, head_width)
    bias_value = lax.dynamic_slice_in_dim(b_value, rank * head_width, head_width)
    bias_up = lax.dynamic_slice_in_dim(b_up, rank * unit_width, unit_width)

    rows_in = tp_gather(own_input).astype(F32)
    grad_rows = tp_gather(own_grad)
    scaled_one, _ = normalize(rows_in)
    normed = (scaled_one * ln1_gain + ln1_bias).astype(BF16)
    scale = HEAD_DIM ** (-0.5)
    factors = jnp.concatenate([jnp.full((head_width,), scale, F32), jnp.ones((2 * head_width,), F32)])
    biases = jnp.concatenate([bias_query * scale, jnp.zeros((head_width,), F32), bias_value])
    qkv = (dot_nn(normed, full_qkv) * factors + biases).astype(BF16)
    mixed, lse = attn_forward(segments, qkv, head_width)
    attended = tp_sum(dot_nt(mixed, full_out).astype(BF16))
    hidden = rows_in + attended + b_out
    scaled_two, inverse_two = normalize(hidden)
    normed_two = (scaled_two * ln2_gain + ln2_bias).astype(BF16)
    normed_two_t = normed_two.T
    grad_rows_t = grad_rows.T

    out_parts, gn_parts, up_parts, down_parts, bias_parts = [], [], [], [], []
    for index, first in enumerate((0, half_units)):
        results = mlp(
            normed_two, grad_rows, normed_two_t, grad_rows_t, full_mlp[index],
            bias_up[first : first + half_units],
        )
        for values, store in zip(results, (out_parts, gn_parts, up_parts, down_parts, bias_parts)):
            store.append(values)
    gn_part = (gn_parts[0].astype(F32) + gn_parts[1].astype(F32)).astype(BF16)
    out_part = (out_parts[0].astype(F32) + out_parts[1].astype(F32)).astype(BF16)
    output = move_out((own(hidden) + tp_scatter(out_part) + b_down).astype(BF16))

    grad_normed_two = tp_sum(gn_part)
    grad_hidden = grad_rows.astype(F32) + norm_back(grad_normed_two, scaled_two, inverse_two, ln2_gain)
    grad_attended = grad_hidden.astype(BF16)
    grad_mixed = dot_nn(grad_attended, full_out).astype(BF16)
    grad_out_part = dot_tn(grad_attended, mixed).astype(BF16)

    def scatter_weights(values):
        return move_out(lax.psum_scatter(values, DATA, scatter_dimension=0, tiled=True)).astype(F32)

    early = scatter_weights(jnp.concatenate(up_parts + down_parts + [grad_out_part], axis=1))
    grad_w_up = early[:, :unit_width]
    grad_w_down = early[:, unit_width : 2 * unit_width]
    grad_w_out = early[:, 2 * unit_width :]

    grads = attn_backward(segments, qkv, mixed, lse, grad_mixed, head_width)
    late = scatter_weights(
        jnp.concatenate([dot_tn(normed, grads[place]).astype(BF16) for place in range(3)], axis=1)
    )
    grad_normed_part = (
        dot_nt(grads[0], full_qkv[:, :head_width])
        + dot_nt(grads[1], full_qkv[:, head_width : 2 * head_width])
        + dot_nt(grads[2], full_qkv[:, 2 * head_width :])
    ).astype(BF16)
    grad_normed = tp_scatter(grad_normed_part)
    own_scaled, own_inverse = normalize(own_input.astype(F32))
    grad_own = own(grad_hidden) + norm_back(grad_normed, own_scaled, own_inverse, ln1_gain)
    grad_input = move_out(grad_own.astype(BF16))

    def place_part(values, full):
        return lax.dynamic_update_slice_in_dim(
            jnp.zeros((full,), F32), values, rank * values.shape[0], 0
        )

    width = ln1_gain.shape[0]
    share = 1.0 / ranks
    sums = jnp.concatenate(
        [
            jnp.sum(grad_normed * own_scaled, axis=0),
            jnp.sum(grad_normed, axis=0),
            place_part(jnp.sum(grads[0].astype(F32), axis=0), width),
            place_part(jnp.sum(grads[2].astype(F32), axis=0), width),
            jnp.sum(grad_hidden, axis=0) * share,
            jnp.sum(grad_normed_two * scaled_two, axis=0) * share,
            jnp.sum(grad_normed_two, axis=0) * share,
            jnp.sum(own_grad.astype(F32), axis=0),
            place_part(jnp.concatenate(bias_parts, axis=1)[0], b_up.shape[0]),
        ]
    )
    sums = lax.psum(sums, ("a", "c", "h", "l"))
    small = [sums[place * width : (place + 1) * width] for place in range(8)]
    return (
        output, grad_input, small[0], small[1],
        late[:, :head_width], late[:, head_width : 2 * head_width], late[:, 2 * head_width :],
        small[2], small[3], grad_w_out, small[4], small[5], small[6], grad_w_up,
        sums[8 * width :], grad_w_down, small[7],
    )


def solution(mesh):
    groups, ranks = mesh.shape["dp"], mesh.shape["tensor"]
    sizes = {"a": groups // 2, "c": 2, "h": 2, "l": ranks // 2}
    fine = Mesh(mesh.devices.reshape(tuple(sizes.values())), tuple(sizes))
    rows = P(("a", "c", "h", "l"), None)
    block = P(("a", "c"), ("h", "l"))
    return jax.shard_map(
        functools.partial(per_device, sizes),
        mesh=fine,
        in_specs=(
            rows, P(("a", "c")), P(), P(), block, block, block, P(), P(), block, P(), P(), P(),
            block, P(), block, P(), rows,
        ),
        out_specs=(
            rows, rows, P(), P(), block, block, block, P(), P(), block, P(), P(), P(), block, P(),
            block, P(),
        ),
        check_vma=False,
    )
```

```python
import functools

import jax
import jax.numpy as jnp
from jax import lax
from jax.experimental import pallas as pl
from jax.experimental.pallas import tpu as pltpu
from jax.sharding import Mesh
from jax.sharding import PartitionSpec as P

HEAD_DIM = 64
LANES = 128
MASKED = -1e30
VMEM_BYTES = 60 * 1024 * 1024
F32 = jnp.float32
BF16 = jnp.bfloat16
TP = ("l", "c")
SWAP = ("c", "h", "l")
CUBE = ("a", "c", "h")


def normalize(values):
    center = values - jnp.mean(values, axis=-1, keepdims=True)
    spread = jnp.mean(center * center, axis=-1, keepdims=True)
    inverse = lax.rsqrt(spread + 1e-05)
    return center * inverse, inverse


def norm_back(grad_in, scaled, inverse, gain_vec):
    local_grad = grad_in * gain_vec
    return inverse * (
        local_grad
        - jnp.mean(local_grad, axis=-1, keepdims=True)
        - scaled * jnp.mean(local_grad * scaled, axis=-1, keepdims=True)
    )


def dot_nn(left, right):
    return lax.dot_general(left, right, (((1,), (0,)), ((), ())), preferred_element_type=F32)


def dot_nt(left, right):
    return lax.dot_general(left, right, (((1,), (1,)), ((), ())), preferred_element_type=F32)


def dot_tn(left, right):
    return lax.dot_general(left, right, (((0,), (0,)), ((), ())), preferred_element_type=F32)


def fill_bias(bias, seg_col, seg_row):
    length = bias.shape[0]
    block = min(256, length)
    for first in range(0, length, block):
        keys = lax.broadcasted_iota(jnp.int32, (block, length), 0) + first
        places = lax.broadcasted_iota(jnp.int32, (block, length), 1)
        same = seg_col[first : first + block, :] == seg_row[...]
        bias[first : first + block, :] = jnp.where(same & (keys <= places), 0.0, MASKED)


def head_lanes(values, head):
    lane = lax.broadcasted_iota(jnp.int32, values.shape, 1)
    inside = (lane >= head * HEAD_DIM) & (lane < (head + 1) * HEAD_DIM)
    return jnp.where(inside, values, jnp.zeros_like(values))


def attn_forward_kernel(seg_col, seg_row, q_ref, k_ref, v_ref, mixed_ref, lse_ref, bias, v_t, block):
    length = q_ref.shape[0]
    heads = LANES // HEAD_DIM

    @pl.when(pl.program_id(0) == 0)
    def _():
        fill_bias(bias, seg_col, seg_row)

    v_t[...] = v_ref[...].T
    for place in range(length // block):
        rows = slice(place * block, (place + 1) * block)
        outs = []
        for head in range(heads):
            query = head_lanes(q_ref[rows, :], head)
            scores = []
            peak = None
            for other in range(place + 1):
                keys = slice(other * block, (other + 1) * block)
                part = dot_nt(k_ref[keys, :], query) + bias[keys, rows]
                top = jnp.max(part, axis=0, keepdims=True)
                peak = top if peak is None else jnp.maximum(peak, top)
                scores.append(part)
            total = None
            acc = None
            for other in range(place + 1):
                keys = slice(other * block, (other + 1) * block)
                weight = jnp.exp(scores[other] - peak)
                part_sum = jnp.sum(weight, axis=0, keepdims=True)
                total = part_sum if total is None else total + part_sum
                part_out = dot_nn(
                    v_t[head * HEAD_DIM : (head + 1) * HEAD_DIM, keys], weight.astype(BF16)
                )
                acc = part_out if acc is None else acc + part_out
            outs.append(acc / total)
            lse_ref[0, head : head + 1, rows] = peak + jnp.log(total)
        mixed_ref[rows, :] = jnp.concatenate(outs, axis=0).T.astype(BF16)


def attn_backward_kernel(
    seg_col, seg_row, q_ref, k_ref, v_ref, mixed_ref, lse_ref, g_ref, grads_ref, bias, k_t, delta, dq_t, block
):
    length = q_ref.shape[0]
    heads = LANES // HEAD_DIM
    count = length // block

    @pl.when(pl.program_id(0) == 0)
    def _():
        fill_bias(bias, seg_col, seg_row)

    k_t[...] = k_ref[...].T
    product = (g_ref[...].astype(F32) * mixed_ref[...].astype(F32)).T
    for head in range(heads):
        delta[head : head + 1, :] = jnp.sum(
            product[head * HEAD_DIM : (head + 1) * HEAD_DIM, :], axis=0, keepdims=True
        )
    for other in range(count):
        keys = slice(other * block, (other + 1) * block)
        key_sum = None
        value_sum = None
        for head in range(heads):
            lanes = slice(head * HEAD_DIM, (head + 1) * HEAD_DIM)
            for place in range(other, count):
                rows = slice(place * block, (place + 1) * block)
                query = head_lanes(q_ref[rows, :], head)
                grad = head_lanes(g_ref[rows, :], head)
                scores = dot_nt(k_ref[keys, :], query) + bias[keys, rows]
                probs = jnp.exp(scores - lse_ref[0, head : head + 1, rows])
                grad_probs = dot_nt(v_ref[keys, :], grad)
                grad_scores = (probs * (grad_probs - delta[head : head + 1, rows])).astype(BF16)
                value_part = dot_nn(probs.astype(BF16), grad)
                key_part = dot_nn(grad_scores, query)
                query_part = dot_nn(k_t[lanes, keys], grad_scores)
                value_sum = value_part if value_sum is None else value_sum + value_part
                key_sum = key_part if key_sum is None else key_sum + key_part
                if other == 0:
                    dq_t[lanes, rows] = query_part
                else:
                    dq_t[lanes, rows] += query_part
        grads_ref[1, keys, :] = key_sum.astype(BF16)
        grads_ref[2, keys, :] = value_sum.astype(BF16)
    grads_ref[0] = (dq_t[...].T * HEAD_DIM ** (-0.5)).astype(BF16)


def attn_forward(segments, qkv, width):
    length = qkv.shape[0]
    pairs = width // LANES
    block = min(256, length)
    column = lambda first: pl.BlockSpec((length, LANES), lambda p: (0, first * pairs + p))
    whole = lambda shape: pl.BlockSpec(shape, lambda p: (0, 0))
    return pl.pallas_call(
        functools.partial(attn_forward_kernel, block=block),
        grid=(pairs,),
        in_specs=[whole((length, 1)), whole((1, length)), column(0), column(1), column(2)],
        out_specs=[
            pl.BlockSpec((length, LANES), lambda p: (0, p)),
            pl.BlockSpec((1, 8, length), lambda p: (p, 0, 0)),
        ],
        out_shape=[
            jax.ShapeDtypeStruct((length, width), BF16),
            jax.ShapeDtypeStruct((pairs, 8, length), F32),
        ],
        scratch_shapes=[pltpu.VMEM((length, length), F32), pltpu.VMEM((LANES, length), BF16)],
        compiler_params=pltpu.CompilerParams(vmem_limit_bytes=VMEM_BYTES),
        cost_estimate=pl.CostEstimate(
            flops=4 * length * length * width,
            bytes_accessed=8 * length * width,
            transcendentals=length * length * width // (2 * HEAD_DIM),
        ),
        name="attn_forward",
    )(segments.reshape(length, 1), segments.reshape(1, length), qkv, qkv, qkv)


def attn_backward(segments, qkv, mixed, lse, grad_mixed, width):
    length = qkv.shape[0]
    pairs = width // LANES
    block = min(256, length)
    column = lambda first: pl.BlockSpec((length, LANES), lambda p: (0, first * pairs + p))
    whole = lambda shape: pl.BlockSpec(shape, lambda p: (0, 0))
    return pl.pallas_call(
        functools.partial(attn_backward_kernel, block=block),
        grid=(pairs,),
        in_specs=[
            whole((length, 1)),
            whole((1, length)),
            column(0),
            column(1),
            column(2),
            pl.BlockSpec((length, LANES), lambda p: (0, p)),
            pl.BlockSpec((1, 8, length), lambda p: (p, 0, 0)),
            pl.BlockSpec((length, LANES), lambda p: (0, p)),
        ],
        out_specs=pl.BlockSpec((3, length, LANES), lambda p: (0, 0, p)),
        out_shape=jax.ShapeDtypeStruct((3, length, width), BF16),
        scratch_shapes=[
            pltpu.VMEM((length, length), F32),
            pltpu.VMEM((LANES, length), BF16),
            pltpu.VMEM((8, length), F32),
            pltpu.VMEM((LANES, length), F32),
        ],
        compiler_params=pltpu.CompilerParams(vmem_limit_bytes=VMEM_BYTES),
        cost_estimate=pl.CostEstimate(
            flops=10 * length * length * width,
            bytes_accessed=16 * length * width,
            transcendentals=length * length * width // (2 * HEAD_DIM),
        ),
        name="attn_backward",
    )(segments.reshape(length, 1), segments.reshape(1, length), qkv, qkv, qkv, mixed, lse, grad_mixed)


def piece_sizes(rows):
    quarter = rows // 4
    return (quarter, quarter, quarter, quarter // 2, quarter // 2)


def piece_slices(rows):
    slices, first = [], 0
    for size in piece_sizes(rows):
        slices.append(slice(first, first + size))
        first += size
    return slices


def whole_spec(shape, **options):
    return pl.BlockSpec(shape, lambda step: (0,) * len(shape), **options)


def norm_kernel(*refs, residual):
    if residual:
        x_ref, own_ref, other_ref, shift_ref, gain_ref, bias_ref, n_ref, nt_ref, hidden_ref = refs
        values = (
            x_ref[...].astype(F32)
            + (own_ref[...].astype(F32) + other_ref[...].astype(F32))
            + shift_ref[...]
        )
        hidden_ref[...] = values
    else:
        x_ref, gain_ref, bias_ref, n_ref, nt_ref = refs
        values = x_ref[...].astype(F32)
    scaled, _ = normalize(values)
    normed = (scaled * gain_ref[...] + bias_ref[...]).astype(BF16)
    n_ref[...] = normed
    nt_ref[...] = normed.T


def norm_rows(x, gain, bias, partials=None, shift=None):
    length, width = x.shape
    block = min(256, length)
    row = pl.BlockSpec((block, width), lambda step: (step, 0))
    vector = whole_spec((1, width))
    residual = partials is not None
    operands = [x] + (list(partials) + [shift.reshape(1, width)] if residual else [])
    operands += [gain.reshape(1, width), bias.reshape(1, width)]
    return pl.pallas_call(
        functools.partial(norm_kernel, residual=residual),
        grid=(length // block,),
        in_specs=[row] + ([row, row, vector] if residual else []) + [vector, vector],
        out_specs=[row, pl.BlockSpec((width, block), lambda step: (0, step))]
        + ([row] if residual else []),
        out_shape=[
            jax.ShapeDtypeStruct((length, width), BF16),
            jax.ShapeDtypeStruct((width, length), BF16),
        ]
        + ([jax.ShapeDtypeStruct((length, width), F32)] if residual else []),
        compiler_params=pltpu.CompilerParams(vmem_limit_bytes=VMEM_BYTES),
        cost_estimate=pl.CostEstimate(
            flops=20 * length * width, bytes_accessed=14 * length * width, transcendentals=length
        ),
        name="norm_two" if residual else "norm_one",
    )(*operands)


def norm_back_kernel(hidden_ref, g_ref, own_ref, other_ref, gain_ref, grad_ref, low_ref, sums_ref):
    scaled, inverse = normalize(hidden_ref[...])
    incoming = own_ref[...].astype(F32) + other_ref[...].astype(F32)
    grad = g_ref[...].astype(F32) + norm_back(incoming, scaled, inverse, gain_ref[...])
    grad_ref[...] = grad
    low_ref[...] = grad.astype(BF16)

    @pl.when(pl.program_id(0) == 0)
    def _():
        sums_ref[...] = jnp.zeros_like(sums_ref)

    sums_ref[0:1, :] += jnp.sum(grad, axis=0, keepdims=True)
    sums_ref[1:2, :] += jnp.sum(incoming * scaled, axis=0, keepdims=True)
    sums_ref[2:3, :] += jnp.sum(incoming, axis=0, keepdims=True)


def norm_back_rows(hidden, grad, partials, gain):
    length, width = hidden.shape
    block = min(256, length)
    row = pl.BlockSpec((block, width), lambda step: (step, 0))
    return pl.pallas_call(
        norm_back_kernel,
        grid=(length // block,),
        in_specs=[row, row, row, row, whole_spec((1, width))],
        out_specs=[row, row, whole_spec((8, width))],
        out_shape=[
            jax.ShapeDtypeStruct((length, width), F32),
            jax.ShapeDtypeStruct((length, width), BF16),
            jax.ShapeDtypeStruct((8, width), F32),
        ],
        compiler_params=pltpu.CompilerParams(vmem_limit_bytes=VMEM_BYTES),
        cost_estimate=pl.CostEstimate(
            flops=30 * length * width, bytes_accessed=16 * length * width, transcendentals=length
        ),
        name="norm_two_back",
    )(hidden, grad, *partials, gain.reshape(1, width))


def mlp_kernel(n_ref, g_ref, nt_ref, gt_ref, *refs, block, with_previous):
    up_refs, down_refs, refs = refs[:5], refs[5:10], refs[10:]
    if with_previous:
        (b_ref, before_out, before_gn), refs = refs[:3], refs[3:]
    else:
        (b_ref,), refs = refs[:1], refs[1:]
    (out_ref, gn_ref), grad_refs, refs = refs[:2], refs[2:7], refs[7:]
    gb_ref, out_acc, gn_acc, act, gpre, up_all, down_all = refs
    step = pl.program_id(0)
    length, width = n_ref.shape
    slices = piece_slices(width)

    @pl.when(step == 0)
    def _():
        if with_previous:
            out_acc[...] = before_out[...].astype(F32)
            gn_acc[...] = before_gn[...].astype(F32)
        else:
            out_acc[...] = jnp.zeros_like(out_acc)
            gn_acc[...] = jnp.zeros_like(gn_acc)

    for piece, up, down in zip(slices, up_refs, down_refs):
        up_all[piece, :] = up[...]
        down_all[piece, :] = down[...]
    bias_sum = jnp.zeros(gb_ref.shape, F32)
    for first in range(0, length, block):
        rows = slice(first, first + block)
        unit = dot_nn(n_ref[rows, :], up_all[...]) + b_ref[...]
        grad = dot_nn(g_ref[rows, :], down_all[...])
        square = unit * unit
        curve = jnp.tanh(0.7978845608028654 * (unit + 0.044715 * (square * unit)))
        half = 0.5 + 0.5 * curve
        slope = half + (0.5 * unit) * (1.0 - curve * curve) * (
            0.7978845608028654 + (3 * 0.044715 * 0.7978845608028654) * square
        )
        active = (unit * half).astype(BF16)
        grad_pre = (grad * slope).astype(BF16)
        act[rows, :] = active
        gpre[rows, :] = grad_pre
        bias_sum = bias_sum + jnp.sum(grad_pre.astype(F32), axis=0, keepdims=True)
        out_acc[rows, :] += dot_nt(active, down_all[...])
        gn_acc[rows, :] += dot_nt(grad_pre, up_all[...])
    gb_ref[...] = bias_sum
    grad_up = dot_nn(nt_ref[...], gpre[...]).astype(BF16)
    grad_down = dot_nn(gt_ref[...], act[...]).astype(BF16)
    for piece, grad_ref in zip(slices, grad_refs):
        grad_ref[0] = grad_up[piece, :]
        grad_ref[1] = grad_down[piece, :]

    @pl.when(step == pl.num_programs(0) - 1)
    def _():
        out_ref[...] = out_acc[...].astype(BF16)
        gn_ref[...] = gn_acc[...].astype(BF16)


def mlp(normed, grad, normed_t, grad_t, pieces, bias, previous):
    length, width = normed.shape
    units = pieces[0].shape[1] // 2
    tile = min(256, units)
    tiles = units // tile
    once = pl.Buffered(1)
    sizes = piece_sizes(width)
    at_tile = lambda rows, first: pl.BlockSpec((rows, tile), lambda u: (0, first + u))
    results = pl.pallas_call(
        functools.partial(mlp_kernel, block=min(256, length), with_previous=bool(previous)),
        grid=(tiles,),
        in_specs=[
            whole_spec((length, width), pipeline_mode=once),
            whole_spec((length, width), pipeline_mode=once),
            whole_spec((width, length), pipeline_mode=once),
            whole_spec((width, length), pipeline_mode=once),
        ]
        + [at_tile(size, 0) for size in sizes]
        + [at_tile(size, tiles) for size in sizes]
        + [at_tile(1, 0)]
        + [whole_spec((length, width), pipeline_mode=once) for _ in previous],
        out_specs=[whole_spec((length, width)), whole_spec((length, width))]
        + [pl.BlockSpec((2, size, tile), lambda u: (0, 0, u)) for size in sizes]
        + [at_tile(1, 0)],
        out_shape=[jax.ShapeDtypeStruct((length, width), BF16)] * 2
        + [jax.ShapeDtypeStruct((2, size, units), BF16) for size in sizes]
        + [jax.ShapeDtypeStruct((1, units), F32)],
        scratch_shapes=[
            pltpu.VMEM((length, width), F32),
            pltpu.VMEM((length, width), F32),
            pltpu.VMEM((length, tile), BF16),
            pltpu.VMEM((length, tile), BF16),
            pltpu.VMEM((width, tile), BF16),
            pltpu.VMEM((width, tile), BF16),
        ],
        compiler_params=pltpu.CompilerParams(vmem_limit_bytes=VMEM_BYTES),
        cost_estimate=pl.CostEstimate(
            flops=12 * length * width * units,
            bytes_accessed=12 * length * width + 8 * width * units,
            transcendentals=length * units,
        ),
        name="mlp_both",
    )(normed, grad, normed_t, grad_t, *pieces, *pieces, bias.reshape(1, units), *previous)
    return results[0], results[1], results[2:7], results[7]


def qkv_weight_kernel(nt_ref, grads_ref, *piece_refs):
    grad = dot_nn(nt_ref[...], grads_ref[0]).astype(BF16)
    for piece, ref in zip(piece_slices(nt_ref.shape[0]), piece_refs):
        ref[0] = grad[piece, :]


def qkv_weight_grads(normed_t, grads):
    width, length = normed_t.shape
    columns = grads.shape[2]
    tile = min(256, columns)
    sizes = piece_sizes(width)
    return pl.pallas_call(
        qkv_weight_kernel,
        grid=(3, columns // tile),
        in_specs=[
            pl.BlockSpec((width, length), lambda k, u: (0, 0), pipeline_mode=pl.Buffered(1)),
            pl.BlockSpec((1, length, tile), lambda k, u: (k, 0, u)),
        ],
        out_specs=[pl.BlockSpec((1, size, tile), lambda k, u: (k, 0, u)) for size in sizes],
        out_shape=[jax.ShapeDtypeStruct((3, size, columns), BF16) for size in sizes],
        compiler_params=pltpu.CompilerParams(vmem_limit_bytes=VMEM_BYTES),
        cost_estimate=pl.CostEstimate(
            flops=6 * length * width * columns,
            bytes_accessed=2 * length * width + 12 * width * columns,
            transcendentals=0,
        ),
        name="qkv_weight_grads",
    )(normed_t, grads)


def qkv_back_kernel(grads_ref, w_ref, out_ref, acc):
    step = pl.program_id(0)
    part = dot_nt(grads_ref[0], w_ref[...])

    @pl.when(step == 0)
    def _():
        acc[...] = part

    @pl.when(step > 0)
    def _():
        acc[...] += part

    @pl.when(step == pl.num_programs(0) - 1)
    def _():
        out_ref[...] = acc[...].astype(BF16)


def qkv_back(grads, weights):
    _, length, columns = grads.shape
    width = weights.shape[0]
    return pl.pallas_call(
        qkv_back_kernel,
        grid=(3,),
        in_specs=[
            pl.BlockSpec((1, length, columns), lambda k: (k, 0, 0)),
            pl.BlockSpec((width, columns), lambda k: (0, k)),
        ],
        out_specs=whole_spec((length, width)),
        out_shape=jax.ShapeDtypeStruct((length, width), BF16),
        scratch_shapes=[pltpu.VMEM((length, width), F32)],
        compiler_params=pltpu.CompilerParams(vmem_limit_bytes=VMEM_BYTES),
        cost_estimate=pl.CostEstimate(
            flops=6 * length * width * columns,
            bytes_accessed=8 * length * width,
            transcendentals=0,
        ),
        name="qkv_back",
    )(grads, weights)


def cube_moves(sizes):
    groups, ranks = sizes["a"], sizes["h"] * sizes["l"]
    far = groups // 2
    swap_to = {}
    for group in range(2):
        for part in range(ranks):
            place = (part % 2) * ranks + group * (ranks // 2) + part // 2
            swap_to[group * ranks + part] = place

    def swap(values, inverse=False):
        pairs = [(to, frm) if inverse else (frm, to) for frm, to in swap_to.items()]
        return lax.ppermute(values, SWAP, pairs)

    def hop(values, a_mask, h_mask):
        pairs = []
        for a in range(groups):
            for c in range(2):
                for h in range(2):
                    pairs.append(((a * 2 + c) * 2 + h, ((a ^ a_mask) * 2 + c) * 2 + (h ^ h_mask)))
        return lax.ppermute(values, CUBE, pairs)

    def gather(shard):
        shard = swap(shard)
        near = jnp.concatenate([shard] + [hop(shard, 2 * i, 0) for i in range(1, far)], axis=0)
        half = near.shape[0] // 2
        by_y = hop(near, 1, 0)
        by_x = hop(near, 0, 1)
        return [near, by_y, by_x, hop(by_y[:half], 0, 1), hop(by_x[half:], 1, 0)]

    def add(*terms):
        total = terms[0].astype(F32)
        for term in terms[1:]:
            total = total + term.astype(F32)
        return total.astype(BF16)

    def scatter(pieces):
        near, by_y, by_x, low, high = pieces
        half = low.shape[1]
        rows = near.shape[1] // far
        y_high = hop(by_y[:, half:], 1, 0)
        x_low = hop(by_x[:, :half], 0, 1)
        low = hop(low, 0, 1)
        high = hop(high, 1, 0)
        y_low = hop(add(by_y[:, :half], low), 1, 0)
        x_high = hop(add(by_x[:, half:], high), 0, 1)
        sums = [add(near[:, :half], y_low, x_low), add(near[:, half:], y_high, x_high)]
        total = sums[0][:, :rows].astype(F32)
        for i in range(1, far):
            part, place = divmod(i * rows, half)
            total = total + hop(sums[part][:, place : place + rows], 2 * i, 0).astype(F32)
        return swap(total.astype(BF16), inverse=True).astype(F32)

    def sum_all(values):
        for mask in range(groups.bit_length() - 1):
            values = values + hop(values, 1 << mask, 0)
        values = values + hop(values, 0, 1)
        values = values + lax.ppermute(values, "c", [(0, 1), (1, 0)])
        return lax.psum(values, "l") if sizes["l"] > 1 else values

    a, h = lax.axis_index("a"), lax.axis_index("h")
    order = []
    for a_low, h_mask in ((0, 0), (1, 0), (0, 1), (1, 1)):
        for i in range(far):
            order.append((a ^ (2 * i + a_low)) * 2 + (h ^ h_mask))
    block = jnp.arange(2 * groups)
    a_rel, h_rel = (block // 2) ^ a, (block % 2) ^ h
    places = (a_rel % 2 + 2 * h_rel) * far + a_rel // 2
    return swap, gather, scatter, sum_all, jnp.stack(order), places


def per_device(sizes, *arguments):
    (
        block_input, segment_ids, ln1_gain, ln1_bias, w_query, w_key, w_value, b_query, b_value,
        w_out, b_out, ln2_gain, ln2_bias, w_up, b_up, w_down, b_down, out_grad,
    ) = arguments
    ranks = sizes["h"] * sizes["l"]
    rank = lax.axis_index(TP)
    own_rows, width = block_input.shape
    head_width = w_query.shape[1]
    unit_width = w_up.shape[1]
    half_units = unit_width // 2
    block_rows = w_query.shape[0]
    swap, gather, scatter, sum_all, order, places = cube_moves(sizes)

    def partner(values):
        return lax.ppermute(values, "c", [(0, 1), (1, 0)])

    def tp_gather(values):
        if ranks != 2:
            return lax.all_gather(values, TP, axis=0, tiled=True)
        theirs = partner(values)
        return jnp.where(
            rank == 0,
            jnp.concatenate([values, theirs], axis=0),
            jnp.concatenate([theirs, values], axis=0),
        )

    def tp_terms(values):
        if ranks != 2:
            others = lax.psum(values.astype(F32), TP) - values.astype(F32)
            return values, others.astype(BF16)
        return values, partner(values)

    def own(values):
        return lax.dynamic_slice_in_dim(values, rank * own_rows, own_rows)

    def tp_scatter(values):
        if ranks != 2:
            return lax.psum_scatter(values, TP, scatter_dimension=0, tiled=True).astype(F32)
        theirs = lax.dynamic_slice_in_dim(values, (1 - rank) * own_rows, own_rows)
        return own(values).astype(F32) + partner(theirs).astype(F32)

    def permuted(vectors):
        stacked = jnp.stack(vectors).reshape(len(vectors), -1, block_rows)
        return jnp.take(stacked, order, axis=1).reshape(len(vectors), width)

    def restored(vectors):
        stacked = vectors.reshape(vectors.shape[0], -1, block_rows)
        return jnp.take(stacked, places, axis=1).reshape(vectors.shape)

    sources = jnp.repeat(order, block_rows) * block_rows + jnp.arange(width) % block_rows
    shuffle = (jnp.arange(width)[:, None] == sources[None, :]).astype(BF16)

    pieces_qkv = gather(jnp.concatenate([w_query, w_key, w_value], axis=1))
    pieces_out = gather(w_out)
    pieces_mlp = [
        gather(
            jnp.concatenate(
                [w_up[:, first : first + half_units], w_down[:, first : first + half_units]], axis=1
            )
        )
        for first in (0, half_units)
    ]
    gain_one, bias_one, gain_two, bias_two, shift_out, shift_down = permuted(
        [ln1_gain, ln1_bias, ln2_gain, ln2_bias, b_out, b_down]
    )
    own_input = dot_nn(swap(block_input), shuffle).astype(BF16)
    segments = swap(segment_ids)
    own_grad = dot_nn(swap(out_grad), shuffle).astype(BF16)
    bias_query = lax.dynamic_slice_in_dim(b_query, rank * head_width, head_width)
    bias_value = lax.dynamic_slice_in_dim(b_value, rank * head_width, head_width)
    bias_up = lax.dynamic_slice_in_dim(b_up, rank * unit_width, unit_width)

    rows_in = tp_gather(own_input)
    grad_rows = tp_gather(own_grad)
    grad_rows_t = grad_rows.T
    normed, normed_t = norm_rows(rows_in, gain_one, bias_one)
    scale = HEAD_DIM ** (-0.5)
    factors = jnp.concatenate([jnp.full((head_width,), scale, F32), jnp.ones((2 * head_width,), F32)])
    biases = jnp.concatenate([bias_query * scale, jnp.zeros((head_width,), F32), bias_value])
    full_qkv = jnp.concatenate(pieces_qkv, axis=0)
    full_out = jnp.concatenate(pieces_out, axis=0)
    qkv = (dot_nn(normed, full_qkv) * factors + biases).astype(BF16)
    mixed, lse = attn_forward(segments, qkv, head_width)
    attended = tp_terms(dot_nt(mixed, full_out).astype(BF16))
    normed_two, normed_two_t, hidden = norm_rows(rows_in, gain_two, bias_two, attended, shift_out)

    previous, mlp_grads, bias_parts = (), [], []
    for index, first in enumerate((0, half_units)):
        out_part, gn_part, grad_pieces, bias_part = mlp(
            normed_two, grad_rows, normed_two_t, grad_rows_t, pieces_mlp[index],
            bias_up[first : first + half_units], previous,
        )
        previous = (out_part, gn_part)
        mlp_grads.append(scatter(grad_pieces))
        bias_parts.append(bias_part[0])
    own_output = (own(hidden) + tp_scatter(out_part) + shift_down).astype(BF16)
    output = swap(dot_nt(own_output, shuffle).astype(BF16), inverse=True)

    grad_hidden, grad_attended, sums_two = norm_back_rows(
        hidden, grad_rows, tp_terms(gn_part), gain_two
    )
    grad_mixed = dot_nn(grad_attended, full_out).astype(BF16)
    grad_out_part = dot_tn(grad_attended, mixed).astype(BF16)
    grad_w_out = scatter([grad_out_part[None, piece] for piece in piece_slices(width)])[0]

    grads = attn_backward(segments, qkv, mixed, lse, grad_mixed, head_width)
    late = scatter(qkv_weight_grads(normed_t, grads))
    grad_normed = tp_scatter(qkv_back(grads, full_qkv))
    own_scaled, own_inverse = normalize(own_input.astype(F32))
    grad_own = own(grad_hidden) + norm_back(grad_normed, own_scaled, own_inverse, gain_one)
    grad_input = swap(dot_nt(grad_own.astype(BF16), shuffle).astype(BF16), inverse=True)

    def place_part(values, full):
        return lax.dynamic_update_slice_in_dim(
            jnp.zeros((full,), F32), values, rank * values.shape[0], 0
        )

    early = jnp.concatenate(
        [
            restored(
                jnp.concatenate(
                    [sums_two[:3] * (1.0 / ranks), jnp.sum(own_grad.astype(F32), axis=0)[None]], axis=0
                )
            ).reshape(-1),
            place_part(jnp.concatenate(bias_parts), b_up.shape[0]),
        ]
    )
    early = sum_all(early)
    last = jnp.concatenate(
        [
            restored(
                jnp.stack([jnp.sum(grad_normed * own_scaled, axis=0), jnp.sum(grad_normed, axis=0)])
            ).reshape(-1),
            place_part(jnp.sum(grads[0].astype(F32), axis=0), width),
            place_part(jnp.sum(grads[2].astype(F32), axis=0), width),
        ]
    )
    last = sum_all(last)
    early_rows = [early[i * width : (i + 1) * width] for i in range(4)]
    last_rows = [last[i * width : (i + 1) * width] for i in range(4)]
    return (
        output, grad_input, last_rows[0], last_rows[1], late[0], late[1], late[2],
        last_rows[2], last_rows[3], grad_w_out, early_rows[0], early_rows[1], early_rows[2],
        jnp.concatenate([part[0] for part in mlp_grads], axis=1), early[4 * width :],
        jnp.concatenate([part[1] for part in mlp_grads], axis=1), early_rows[3],
    )


def solution(mesh):
    groups, ranks = mesh.shape["dp"], mesh.shape["tensor"]
    sizes = {"a": groups // 2, "c": 2, "h": 2, "l": ranks // 2}
    fine = Mesh(mesh.devices.reshape(tuple(sizes.values())), tuple(sizes))
    rows = P(("a", "c", "h", "l"), None)
    block = P(("a", "c"), ("h", "l"))
    return jax.shard_map(
        functools.partial(per_device, sizes),
        mesh=fine,
        in_specs=(
            rows, P(("a", "c")), P(), P(), block, block, block, P(), P(), block, P(), P(), P(),
            block, P(), block, P(), rows,
        ),
        out_specs=(
            rows, rows, P(), P(), block, block, block, P(), P(), block, P(), P(), P(), block, P(),
            block, P(),
        ),
        check_vma=False,
    )
```

```python
import functools

import jax
import jax.numpy as jnp
from jax import lax
from jax.experimental import pallas as pl
from jax.experimental.pallas import tpu as pltpu
from jax.sharding import Mesh
from jax.sharding import PartitionSpec as P

HEAD_DIM = 64
LANES = 128
MASKED = -1e30
VMEM_BYTES = 60 * 1024 * 1024
F32 = jnp.float32
BF16 = jnp.bfloat16
TP = ("l", "c")
SWAP = ("c", "h", "l")
ALL = ("a", "c", "h", "l")


def normalize(values):
    center = values - jnp.mean(values, axis=-1, keepdims=True)
    spread = jnp.mean(center * center, axis=-1, keepdims=True)
    inverse = lax.rsqrt(spread + 1e-05)
    return center * inverse, inverse


def norm_back(grad_in, scaled, inverse, gain_vec):
    local_grad = grad_in * gain_vec
    return inverse * (
        local_grad
        - jnp.mean(local_grad, axis=-1, keepdims=True)
        - scaled * jnp.mean(local_grad * scaled, axis=-1, keepdims=True)
    )


def dot_nn(left, right):
    return lax.dot_general(left, right, (((1,), (0,)), ((), ())), preferred_element_type=F32)


def dot_nt(left, right):
    return lax.dot_general(left, right, (((1,), (1,)), ((), ())), preferred_element_type=F32)


def dot_tn(left, right):
    return lax.dot_general(left, right, (((0,), (0,)), ((), ())), preferred_element_type=F32)


def fill_bias(bias, seg_col, seg_row):
    length = bias.shape[0]
    block = min(256, length)
    for first in range(0, length, block):
        keys = lax.broadcasted_iota(jnp.int32, (block, length), 0) + first
        places = lax.broadcasted_iota(jnp.int32, (block, length), 1)
        same = seg_col[first : first + block, :] == seg_row[...]
        bias[first : first + block, :] = jnp.where(same & (keys <= places), 0.0, MASKED)


def head_lanes(values, head):
    lane = lax.broadcasted_iota(jnp.int32, values.shape, 1)
    inside = (lane >= head * HEAD_DIM) & (lane < (head + 1) * HEAD_DIM)
    return jnp.where(inside, values, jnp.zeros_like(values))


def attn_forward_kernel(seg_col, seg_row, q_ref, k_ref, v_ref, mixed_ref, lse_ref, bias, v_t, block):
    length = q_ref.shape[0]
    heads = LANES // HEAD_DIM

    @pl.when(pl.program_id(0) == 0)
    def _():
        fill_bias(bias, seg_col, seg_row)

    v_t[...] = v_ref[...].T
    for place in range(length // block):
        rows = slice(place * block, (place + 1) * block)
        outs = []
        for head in range(heads):
            query = head_lanes(q_ref[rows, :], head)
            scores = []
            peak = None
            for other in range(place + 1):
                keys = slice(other * block, (other + 1) * block)
                part = dot_nt(k_ref[keys, :], query) + bias[keys, rows]
                top = jnp.max(part, axis=0, keepdims=True)
                peak = top if peak is None else jnp.maximum(peak, top)
                scores.append(part)
            total = None
            acc = None
            for other in range(place + 1):
                keys = slice(other * block, (other + 1) * block)
                weight = jnp.exp(scores[other] - peak)
                part_sum = jnp.sum(weight, axis=0, keepdims=True)
                total = part_sum if total is None else total + part_sum
                part_out = dot_nn(
                    v_t[head * HEAD_DIM : (head + 1) * HEAD_DIM, keys], weight.astype(BF16)
                )
                acc = part_out if acc is None else acc + part_out
            outs.append(acc / total)
            lse_ref[0, head : head + 1, rows] = peak + jnp.log(total)
        mixed_ref[rows, :] = jnp.concatenate(outs, axis=0).T.astype(BF16)


def attn_backward_kernel(
    seg_col, seg_row, q_ref, k_ref, v_ref, mixed_ref, lse_ref, g_ref, grads_ref, bias, k_t, delta, dq_t, block
):
    length = q_ref.shape[0]
    heads = LANES // HEAD_DIM
    count = length // block

    @pl.when(pl.program_id(0) == 0)
    def _():
        fill_bias(bias, seg_col, seg_row)

    k_t[...] = k_ref[...].T
    product = (g_ref[...].astype(F32) * mixed_ref[...].astype(F32)).T
    for head in range(heads):
        delta[head : head + 1, :] = jnp.sum(
            product[head * HEAD_DIM : (head + 1) * HEAD_DIM, :], axis=0, keepdims=True
        )
    for other in range(count):
        keys = slice(other * block, (other + 1) * block)
        key_sum = None
        value_sum = None
        for head in range(heads):
            lanes = slice(head * HEAD_DIM, (head + 1) * HEAD_DIM)
            for place in range(other, count):
                rows = slice(place * block, (place + 1) * block)
                query = head_lanes(q_ref[rows, :], head)
                grad = head_lanes(g_ref[rows, :], head)
                scores = dot_nt(k_ref[keys, :], query) + bias[keys, rows]
                probs = jnp.exp(scores - lse_ref[0, head : head + 1, rows])
                grad_probs = dot_nt(v_ref[keys, :], grad)
                grad_scores = (probs * (grad_probs - delta[head : head + 1, rows])).astype(BF16)
                value_part = dot_nn(probs.astype(BF16), grad)
                key_part = dot_nn(grad_scores, query)
                query_part = dot_nn(k_t[lanes, keys], grad_scores)
                value_sum = value_part if value_sum is None else value_sum + value_part
                key_sum = key_part if key_sum is None else key_sum + key_part
                if other == 0:
                    dq_t[lanes, rows] = query_part
                else:
                    dq_t[lanes, rows] += query_part
        grads_ref[1, keys, :] = key_sum.astype(BF16)
        grads_ref[2, keys, :] = value_sum.astype(BF16)
    grads_ref[0] = (dq_t[...].T * HEAD_DIM ** (-0.5)).astype(BF16)


def attn_forward(segments, qkv, width):
    length = qkv.shape[0]
    pairs = width // LANES
    block = min(256, length)
    column = lambda first: pl.BlockSpec((length, LANES), lambda p: (0, first * pairs + p))
    whole = lambda shape: pl.BlockSpec(shape, lambda p: (0, 0))
    return pl.pallas_call(
        functools.partial(attn_forward_kernel, block=block),
        grid=(pairs,),
        in_specs=[whole((length, 1)), whole((1, length)), column(0), column(1), column(2)],
        out_specs=[
            pl.BlockSpec((length, LANES), lambda p: (0, p)),
            pl.BlockSpec((1, 8, length), lambda p: (p, 0, 0)),
        ],
        out_shape=[
            jax.ShapeDtypeStruct((length, width), BF16),
            jax.ShapeDtypeStruct((pairs, 8, length), F32),
        ],
        scratch_shapes=[pltpu.VMEM((length, length), F32), pltpu.VMEM((LANES, length), BF16)],
        compiler_params=pltpu.CompilerParams(vmem_limit_bytes=VMEM_BYTES),
        cost_estimate=pl.CostEstimate(
            flops=4 * length * length * width,
            bytes_accessed=8 * length * width,
            transcendentals=length * length * width // (2 * HEAD_DIM),
        ),
        name="attn_forward",
    )(segments.reshape(length, 1), segments.reshape(1, length), qkv, qkv, qkv)


def attn_backward(segments, qkv, mixed, lse, grad_mixed, width):
    length = qkv.shape[0]
    pairs = width // LANES
    block = min(256, length)
    column = lambda first: pl.BlockSpec((length, LANES), lambda p: (0, first * pairs + p))
    whole = lambda shape: pl.BlockSpec(shape, lambda p: (0, 0))
    return pl.pallas_call(
        functools.partial(attn_backward_kernel, block=block),
        grid=(pairs,),
        in_specs=[
            whole((length, 1)),
            whole((1, length)),
            column(0),
            column(1),
            column(2),
            pl.BlockSpec((length, LANES), lambda p: (0, p)),
            pl.BlockSpec((1, 8, length), lambda p: (p, 0, 0)),
            pl.BlockSpec((length, LANES), lambda p: (0, p)),
        ],
        out_specs=pl.BlockSpec((3, length, LANES), lambda p: (0, 0, p)),
        out_shape=jax.ShapeDtypeStruct((3, length, width), BF16),
        scratch_shapes=[
            pltpu.VMEM((length, length), F32),
            pltpu.VMEM((LANES, length), BF16),
            pltpu.VMEM((8, length), F32),
            pltpu.VMEM((LANES, length), F32),
        ],
        compiler_params=pltpu.CompilerParams(vmem_limit_bytes=VMEM_BYTES),
        cost_estimate=pl.CostEstimate(
            flops=10 * length * length * width,
            bytes_accessed=16 * length * width,
            transcendentals=length * length * width // (2 * HEAD_DIM),
        ),
        name="attn_backward",
    )(segments.reshape(length, 1), segments.reshape(1, length), qkv, qkv, qkv, mixed, lse, grad_mixed)


def piece_blocks(count):
    far = count // 4
    half = far // 2
    near, by_y, by_x, both = (list(range(i * far, (i + 1) * far)) for i in range(4))
    return [
        both[:half] + by_x[:half],
        both[half:] + by_y[half:],
        by_y[:half],
        by_x[half:],
        near,
    ]


def store_pieces(order, grad, piece_refs, columns):
    count = order.shape[0]
    rows = grad.shape[0] // count
    for blocks, ref in zip(piece_blocks(count), piece_refs):
        for place, block in enumerate(blocks):
            first = pl.multiple_of(order[block] * rows, rows)
            ref[place * rows : (place + 1) * rows, columns] = grad[pl.ds(first, rows), :]


def piece_shapes(count, rows, columns):
    return [
        jax.ShapeDtypeStruct((len(blocks) * rows, columns), BF16) for blocks in piece_blocks(count)
    ]


def whole_spec(shape, **options):
    return pl.BlockSpec(shape, lambda step: (0,) * len(shape), **options)


def norm_kernel(*refs, residual):
    if residual:
        x_ref, own_ref, other_ref, shift_ref, gain_ref, bias_ref, n_ref, nt_ref, hidden_ref = refs
        values = (
            x_ref[...].astype(F32)
            + (own_ref[...].astype(F32) + other_ref[...].astype(F32))
            + shift_ref[...]
        )
        hidden_ref[...] = values
    else:
        x_ref, gain_ref, bias_ref, n_ref, nt_ref = refs
        values = x_ref[...].astype(F32)
    scaled, _ = normalize(values)
    normed = (scaled * gain_ref[...] + bias_ref[...]).astype(BF16)
    n_ref[...] = normed
    nt_ref[...] = normed.T


def norm_rows(x, gain, bias, partials=None, shift=None):
    length, width = x.shape
    block = min(256, length)
    row = pl.BlockSpec((block, width), lambda step: (step, 0))
    vector = whole_spec((1, width))
    residual = partials is not None
    operands = [x] + (list(partials) + [shift.reshape(1, width)] if residual else [])
    operands += [gain.reshape(1, width), bias.reshape(1, width)]
    return pl.pallas_call(
        functools.partial(norm_kernel, residual=residual),
        grid=(length // block,),
        in_specs=[row] + ([row, row, vector] if residual else []) + [vector, vector],
        out_specs=[row, pl.BlockSpec((width, block), lambda step: (0, step))]
        + ([row] if residual else []),
        out_shape=[
            jax.ShapeDtypeStruct((length, width), BF16),
            jax.ShapeDtypeStruct((width, length), BF16),
        ]
        + ([jax.ShapeDtypeStruct((length, width), F32)] if residual else []),
        compiler_params=pltpu.CompilerParams(vmem_limit_bytes=VMEM_BYTES),
        cost_estimate=pl.CostEstimate(
            flops=20 * length * width, bytes_accessed=14 * length * width, transcendentals=length
        ),
        name="norm_two" if residual else "norm_one",
    )(*operands)


def norm_back_kernel(hidden_ref, g_ref, own_ref, other_ref, gain_ref, grad_ref, low_ref, low_t_ref, sums_ref):
    scaled, inverse = normalize(hidden_ref[...])
    incoming = own_ref[...].astype(F32) + other_ref[...].astype(F32)
    grad = g_ref[...].astype(F32) + norm_back(incoming, scaled, inverse, gain_ref[...])
    grad_ref[...] = grad
    low_ref[...] = grad.astype(BF16)
    low_t_ref[...] = grad.astype(BF16).T

    @pl.when(pl.program_id(0) == 0)
    def _():
        sums_ref[...] = jnp.zeros_like(sums_ref)

    sums_ref[0:1, :] += jnp.sum(grad, axis=0, keepdims=True)
    sums_ref[1:2, :] += jnp.sum(incoming * scaled, axis=0, keepdims=True)
    sums_ref[2:3, :] += jnp.sum(incoming, axis=0, keepdims=True)


def norm_back_rows(hidden, grad, partials, gain):
    length, width = hidden.shape
    block = min(256, length)
    row = pl.BlockSpec((block, width), lambda step: (step, 0))
    return pl.pallas_call(
        norm_back_kernel,
        grid=(length // block,),
        in_specs=[row, row, row, row, whole_spec((1, width))],
        out_specs=[
            row,
            row,
            pl.BlockSpec((width, block), lambda step: (0, step)),
            whole_spec((8, width)),
        ],
        out_shape=[
            jax.ShapeDtypeStruct((length, width), F32),
            jax.ShapeDtypeStruct((length, width), BF16),
            jax.ShapeDtypeStruct((width, length), BF16),
            jax.ShapeDtypeStruct((8, width), F32),
        ],
        compiler_params=pltpu.CompilerParams(vmem_limit_bytes=VMEM_BYTES),
        cost_estimate=pl.CostEstimate(
            flops=30 * length * width, bytes_accessed=16 * length * width, transcendentals=length
        ),
        name="norm_two_back",
    )(hidden, grad, *partials, gain.reshape(1, width))


def mlp_kernel(order, n_ref, g_ref, nt_ref, gt_ref, w_ref, b_ref, *refs, block, with_previous, cube):
    if with_previous:
        (before_out, before_gn), refs = refs[:2], refs[2:]
    count = 5 if cube else 1
    (out_ref, gn_ref), grad_refs, refs = refs[:2], refs[2 : 2 + count], refs[2 + count :]
    gb_ref, out_acc, gn_acc, act, gpre, grad_up, grad_down = refs
    step = pl.program_id(0)
    length = n_ref.shape[0]
    tile = w_ref.shape[1] // 2
    ups, downs = slice(0, tile), slice(tile, 2 * tile)

    @pl.when(step == 0)
    def _():
        if with_previous:
            out_acc[...] = before_out[...].astype(F32)
            gn_acc[...] = before_gn[...].astype(F32)
        else:
            out_acc[...] = jnp.zeros_like(out_acc)
            gn_acc[...] = jnp.zeros_like(gn_acc)

    bias_sum = jnp.zeros(gb_ref.shape, F32)
    for first in range(0, length, block):
        rows = slice(first, first + block)
        unit = dot_nn(n_ref[rows, :], w_ref[:, ups]) + b_ref[...]
        grad = dot_nn(g_ref[rows, :], w_ref[:, downs])
        square = unit * unit
        curve = jnp.tanh(0.7978845608028654 * (unit + 0.044715 * (square * unit)))
        half = 0.5 + 0.5 * curve
        slope = half + (0.5 * unit) * (1.0 - curve * curve) * (
            0.7978845608028654 + (3 * 0.044715 * 0.7978845608028654) * square
        )
        active = (unit * half).astype(BF16)
        grad_pre = (grad * slope).astype(BF16)
        act[rows, :] = active
        gpre[rows, :] = grad_pre
        bias_sum = bias_sum + jnp.sum(grad_pre.astype(F32), axis=0, keepdims=True)
        out_acc[rows, :] += dot_nt(active, w_ref[:, downs])
        gn_acc[rows, :] += dot_nt(grad_pre, w_ref[:, ups])
    gb_ref[...] = bias_sum
    if cube:
        grad_up[...] = dot_nn(nt_ref[...], gpre[...]).astype(BF16)
        grad_down[...] = dot_nn(gt_ref[...], act[...]).astype(BF16)
        store_pieces(order, grad_up, grad_refs, ups)
        store_pieces(order, grad_down, grad_refs, downs)
    else:
        grad_refs[0][:, ups] = dot_nn(nt_ref[...], gpre[...]).astype(BF16)
        grad_refs[0][:, downs] = dot_nn(gt_ref[...], act[...]).astype(BF16)

    @pl.when(step == pl.num_programs(0) - 1)
    def _():
        out_ref[...] = out_acc[...].astype(BF16)
        gn_ref[...] = gn_acc[...].astype(BF16)


def mlp(order, normed, grad, normed_t, grad_t, weights, bias, previous, cube):
    length, width = normed.shape
    units = weights.shape[1] // 2
    tile = min(256, units)
    once = pl.Buffered(1)
    fixed = lambda shape, **options: pl.BlockSpec(shape, lambda u, o: (0, 0), **options)
    at_tile = lambda rows, columns: pl.BlockSpec((rows, columns), lambda u, o: (0, u))
    count, rows = order.shape[0], width // order.shape[0]
    if cube:
        grad_shapes = piece_shapes(count, rows, 2 * units)
    else:
        grad_shapes = [jax.ShapeDtypeStruct((width, 2 * units), BF16)]
    results = pl.pallas_call(
        functools.partial(
            mlp_kernel, block=min(256, length), with_previous=bool(previous), cube=cube
        ),
        grid_spec=pltpu.PrefetchScalarGridSpec(
            num_scalar_prefetch=1,
            grid=(units // tile,),
            in_specs=[
                fixed((length, width), pipeline_mode=once),
                fixed((length, width), pipeline_mode=once),
                fixed((width, length), pipeline_mode=once),
                fixed((width, length), pipeline_mode=once),
                at_tile(width, 2 * tile),
                at_tile(1, tile),
            ]
            + [fixed((length, width), pipeline_mode=once) for _ in previous],
            out_specs=[fixed((length, width)), fixed((length, width))]
            + [at_tile(shape.shape[0], 2 * tile) for shape in grad_shapes]
            + [at_tile(1, tile)],
            scratch_shapes=[
                pltpu.VMEM((length, width), F32),
                pltpu.VMEM((length, width), F32),
                pltpu.VMEM((length, tile), BF16),
                pltpu.VMEM((length, tile), BF16),
                pltpu.VMEM((width, tile), BF16),
                pltpu.VMEM((width, tile), BF16),
            ],
        ),
        out_shape=[jax.ShapeDtypeStruct((length, width), BF16)] * 2
        + grad_shapes
        + [jax.ShapeDtypeStruct((1, units), F32)],
        compiler_params=pltpu.CompilerParams(vmem_limit_bytes=VMEM_BYTES),
        cost_estimate=pl.CostEstimate(
            flops=12 * length * width * units,
            bytes_accessed=12 * length * width + 8 * width * units,
            transcendentals=length * units,
        ),
        name="mlp_second" if previous else "mlp_first",
    )(order, normed, grad, normed_t, grad_t, weights, bias.reshape(1, units), *previous)
    return results[0], results[1], results[2:-1], results[-1]


def qkv_kernel(order, n_ref, b_ref, near, by_y, by_x, low, high, out_ref, w_ref):
    count = order.shape[0]
    rows = w_ref.shape[0] // count
    block = 0
    for ref in (near, by_y, by_x, low, high):
        for place in range(ref.shape[0] // rows):
            first = pl.multiple_of(order[block] * rows, rows)
            w_ref[pl.ds(first, rows), :] = ref[place * rows : (place + 1) * rows, :]
            block += 1
    scale = jnp.where(pl.program_id(0) == 0, HEAD_DIM ** (-0.5), 1.0)
    length = n_ref.shape[0]
    step = min(256, length)
    for first in range(0, length, step):
        span = slice(first, first + step)
        out_ref[span, :] = ((dot_nn(n_ref[span, :], w_ref[...]) + b_ref[...]) * scale).astype(BF16)


def qkv_project(order, normed, pieces, bias):
    length, width = normed.shape
    columns = pieces[0].shape[1] // 3
    at_tile = lambda rows: pl.BlockSpec((rows, columns), lambda k, o: (0, k))
    return pl.pallas_call(
        qkv_kernel,
        grid_spec=pltpu.PrefetchScalarGridSpec(
            num_scalar_prefetch=1,
            grid=(3,),
            in_specs=[
                pl.BlockSpec((length, width), lambda k, o: (0, 0), pipeline_mode=pl.Buffered(1)),
                at_tile(1),
            ]
            + [at_tile(piece.shape[0]) for piece in pieces],
            out_specs=[at_tile(length), at_tile(width)],
        ),
        out_shape=[
            jax.ShapeDtypeStruct((length, 3 * columns), BF16),
            jax.ShapeDtypeStruct((width, 3 * columns), BF16),
        ],
        compiler_params=pltpu.CompilerParams(vmem_limit_bytes=VMEM_BYTES),
        cost_estimate=pl.CostEstimate(
            flops=6 * length * width * columns,
            bytes_accessed=2 * length * width + 12 * width * columns + 6 * length * columns,
            transcendentals=0,
        ),
        name="qkv_project",
    )(order, normed, bias.reshape(1, 3 * columns), *pieces)


def weight_kernel(order, nt_ref, grads_ref, *refs):
    piece_refs, grad = refs[:5], refs[5]
    grad[...] = dot_nn(nt_ref[...], grads_ref[0]).astype(BF16)
    store_pieces(order, grad, piece_refs, slice(None))


def weight_grads(order, normed_t, grads):
    width, length = normed_t.shape
    columns = grads.shape[2]
    tile = min(256, columns)
    tiles = columns // tile
    parts = grads.shape[0]
    shapes = piece_shapes(order.shape[0], width // order.shape[0], parts * columns)
    return pl.pallas_call(
        weight_kernel,
        grid_spec=pltpu.PrefetchScalarGridSpec(
            num_scalar_prefetch=1,
            grid=(parts, tiles),
            in_specs=[
                pl.BlockSpec((width, length), lambda k, u, o: (0, 0), pipeline_mode=pl.Buffered(1)),
                pl.BlockSpec((1, length, tile), lambda k, u, o: (k, 0, u)),
            ],
            out_specs=[
                pl.BlockSpec((shape.shape[0], tile), lambda k, u, o: (0, k * tiles + u))
                for shape in shapes
            ],
            scratch_shapes=[pltpu.VMEM((width, tile), BF16)],
        ),
        out_shape=shapes,
        compiler_params=pltpu.CompilerParams(vmem_limit_bytes=VMEM_BYTES),
        cost_estimate=pl.CostEstimate(
            flops=2 * parts * length * width * columns,
            bytes_accessed=2 * length * width + 4 * parts * width * columns,
            transcendentals=0,
        ),
        name="weight_grads",
    )(order, normed_t, grads)


def qkv_back_kernel(grads_ref, w_ref, out_ref):
    columns = grads_ref.shape[2]
    total = None
    for k in range(3):
        part = dot_nt(grads_ref[k], w_ref[:, k * columns : (k + 1) * columns])
        total = part if total is None else total + part
    out_ref[...] = total.astype(BF16)


def qkv_back(grads, weights):
    _, length, columns = grads.shape
    width = weights.shape[0]
    block = min(256, length)
    return pl.pallas_call(
        qkv_back_kernel,
        grid=(length // block,),
        in_specs=[
            pl.BlockSpec((3, block, columns), lambda i: (0, i, 0)),
            pl.BlockSpec((width, 3 * columns), lambda i: (0, 0), pipeline_mode=pl.Buffered(1)),
        ],
        out_specs=pl.BlockSpec((block, width), lambda i: (i, 0)),
        out_shape=jax.ShapeDtypeStruct((length, width), BF16),
        compiler_params=pltpu.CompilerParams(vmem_limit_bytes=VMEM_BYTES),
        cost_estimate=pl.CostEstimate(
            flops=6 * length * width * columns,
            bytes_accessed=2 * length * width + 6 * width * columns + 6 * length * columns,
            transcendentals=0,
        ),
        name="qkv_back",
    )(grads, weights)


def added(*terms):
    total = terms[0].astype(F32)
    for term in terms[1:]:
        total = total + term.astype(F32)
    return total.astype(BF16)


def first_sums_kernel(*refs, spans):
    refs, (y_ref, x_ref) = refs[:-2], refs[-2:]
    half = y_ref.shape[0]
    for index, columns in enumerate(spans):
        from_x, from_y, keep_y, keep_x = (ref[...] for ref in refs[4 * index : 4 * index + 4])
        y_ref[:, columns] = added(keep_y, from_x[:half])
        x_ref[:, columns] = added(keep_x, from_y[:half])


def second_sums_kernel(*refs, spans, far):
    outs, refs = refs[-far:], refs[:-far]
    (from_y2, from_x2), refs = refs[-2:], refs[:-2]
    half = from_y2.shape[0]
    rows = half * 2 // far
    for index, columns in enumerate(spans):
        from_x, from_y, near = refs[3 * index : 3 * index + 3]
        for i in range(far):
            first, second, place = (from_x, from_y2, i) if i < far // 2 else (from_y, from_x2, i - far // 2)
            span = slice(place * rows, (place + 1) * rows)
            outs[i][:, columns] = added(
                near[i * rows : (i + 1) * rows, :],
                first[half + place * rows : half + (place + 1) * rows, :],
                second[span, columns],
            )


def column_spans(widths):
    spans, first = [], 0
    for width in widths:
        spans.append(slice(first, first + width))
        first += width
    return spans


def sums_call(kernel, operands, shapes, after, name):
    body = kernel
    if after is not None:
        body = lambda order_only, *refs: kernel(*refs)
    vmem = pl.BlockSpec(memory_space=pltpu.VMEM)
    return pl.pallas_call(
        body,
        in_specs=([pl.BlockSpec(memory_space=pl.ANY)] if after is not None else [])
        + [vmem] * len(operands),
        out_specs=[vmem] * len(shapes),
        out_shape=shapes,
        compiler_params=pltpu.CompilerParams(vmem_limit_bytes=VMEM_BYTES),
        name=name,
    )(*([after] if after is not None else []), *operands)


def moves(sizes):
    groups, ranks, inner = sizes["a"], sizes["h"] * sizes["l"], sizes["l"]
    far = groups // 2
    swap_to = {}
    for group in range(2):
        for part in range(ranks):
            place = (part % 2) * ranks + group * (ranks // 2) + part // 2
            swap_to[group * ranks + part] = place

    def swap(values, inverse=False):
        pairs = [(to, frm) if inverse else (frm, to) for frm, to in swap_to.items()]
        return lax.ppermute(values, SWAP, pairs)

    def swap_hop(values, a_mask, inverse=False):
        pairs = []
        for a in range(groups):
            for frm, to in swap_to.items():
                one, two = a * 2 * ranks + frm, (a ^ a_mask) * 2 * ranks + to
                pairs.append((two, one) if inverse else (one, two))
        return lax.ppermute(values, ALL, pairs)

    def hop(values, a_mask, h_mask):
        pairs = []
        for a in range(groups):
            for c in range(2):
                for h in range(2):
                    pairs.append(((a * 2 + c) * 2 + h, ((a ^ a_mask) * 2 + c) * 2 + (h ^ h_mask)))
        return lax.ppermute(values, ("a", "c", "h"), pairs)

    def gather(shard):
        near = jnp.concatenate([swap_hop(shard, 2 * i) for i in range(far)], axis=0)
        half = near.shape[0] // 2
        by_y = hop(near, 1, 0)
        by_x = hop(near, 0, 1)
        return [near, by_y, by_x, hop(by_y[:half], 0, 1), hop(by_x[half:], 1, 0)]

    def first_sends(pieces):
        return hop(pieces[0], 0, 1), hop(pieces[1], 1, 0)

    def finish(chunks, received, after, name):
        spans = column_spans([pieces[0].shape[1] for pieces in chunks])
        total = spans[-1].stop
        half, rows = chunks[0][2].shape[0], chunks[0][4].shape[0] // far
        operands = []
        for pieces, (from_x, from_y) in zip(chunks, received):
            operands += [from_x, from_y, pieces[2], pieces[3]]
        y_sum, x_sum = sums_call(
            functools.partial(first_sums_kernel, spans=spans),
            operands,
            [jax.ShapeDtypeStruct((half, total), BF16)] * 2,
            after,
            name + "_sums_one",
        )
        from_y2, from_x2 = hop(y_sum, 1, 0), hop(x_sum, 0, 1)
        operands = []
        for pieces, (from_x, from_y) in zip(chunks, received):
            operands += [from_x, from_y, pieces[4]]
        sums = sums_call(
            functools.partial(second_sums_kernel, spans=spans, far=far),
            operands + [from_y2, from_x2],
            [jax.ShapeDtypeStruct((rows, total), BF16)] * far,
            None,
            name + "_sums_two",
        )
        parts = [swap_hop(sums[i], 2 * i, inverse=True) for i in range(far)]
        result = parts[0].astype(F32)
        for part in parts[1:]:
            result = result + part.astype(F32)
        return [result[:, span] for span in spans]

    def sum_all(values):
        for mask in range(groups.bit_length() - 1):
            values = values + hop(values, 1 << mask, 0)
        values = values + hop(values, 0, 1)
        values = values + lax.ppermute(values, "c", [(0, 1), (1, 0)])
        return lax.psum(values, "l") if inner > 1 else values

    a, h = lax.axis_index("a"), lax.axis_index("h")
    order = []
    for a_low, h_mask in ((0, 0), (1, 0), (0, 1), (1, 1)):
        for i in range(far):
            order.append((a ^ (2 * i + a_low)) * 2 + (h ^ h_mask))
    return swap, gather, first_sends, finish, sum_all, jnp.stack(order).astype(jnp.int32)


def per_device(sizes, *arguments):
    (
        block_input, segment_ids, ln1_gain, ln1_bias, w_query, w_key, w_value, b_query, b_value,
        w_out, b_out, ln2_gain, ln2_bias, w_up, b_up, w_down, b_down, out_grad,
    ) = arguments
    ranks = sizes["h"] * sizes["l"]
    rank = lax.axis_index(TP)
    own_rows, width = block_input.shape
    head_width = w_query.shape[1]
    unit_width = w_up.shape[1]
    half_units = unit_width // 2
    tile = min(256, half_units)
    swap, gather, first_sends, finish, sum_all, order = moves(sizes)

    def partner(values):
        return lax.ppermute(values, "c", [(0, 1), (1, 0)])

    def tp_gather(values):
        if ranks != 2:
            return lax.all_gather(values, TP, axis=0, tiled=True)
        theirs = partner(values)
        return jnp.where(
            rank == 0,
            jnp.concatenate([values, theirs], axis=0),
            jnp.concatenate([theirs, values], axis=0),
        )

    def tp_terms(values):
        if ranks != 2:
            others = lax.psum(values.astype(F32), TP) - values.astype(F32)
            return values, others.astype(BF16)
        return values, partner(values)

    def own(values):
        return lax.dynamic_slice_in_dim(values, rank * own_rows, own_rows)

    def tp_scatter(values):
        if ranks != 2:
            return lax.psum_scatter(values, TP, scatter_dimension=0, tiled=True).astype(F32)
        theirs = lax.dynamic_slice_in_dim(values, (1 - rank) * own_rows, own_rows)
        return own(values).astype(F32) + partner(theirs).astype(F32)

    def mlp_shard(first):
        columns = []
        for start in range(first, first + half_units, tile):
            columns += [w_up[:, start : start + tile], w_down[:, start : start + tile]]
        return columns

    def split_mlp(values):
        paired = values.reshape(values.shape[0], half_units // tile, 2, tile)
        return [paired[:, :, i].reshape(values.shape[0], half_units) for i in range(2)]

    pieces_qkv = gather(jnp.concatenate([w_query, w_key, w_value], axis=1))
    first_gather = lax.all_gather(
        jnp.concatenate([w_out] + mlp_shard(0), axis=1), ("a", "c"), axis=0, tiled=True
    )
    second_gather = lax.all_gather(
        swap(jnp.concatenate(mlp_shard(half_units), axis=1)), ("a", "h"), axis=0, tiled=True
    )
    own_input = swap(block_input)
    segments = swap(segment_ids)
    own_grad = swap(out_grad)
    full_out = swap(first_gather[:, :head_width])
    mlp_weights = [swap(first_gather[:, head_width:]), second_gather]
    bias_query = lax.dynamic_slice_in_dim(b_query, rank * head_width, head_width)
    bias_value = lax.dynamic_slice_in_dim(b_value, rank * head_width, head_width)
    bias_up = lax.dynamic_slice_in_dim(b_up, rank * unit_width, unit_width)

    rows_in = tp_gather(own_input)
    grad_rows = tp_gather(own_grad)
    grad_rows_t = grad_rows.T
    normed, normed_t = norm_rows(rows_in, ln1_gain, ln1_bias)
    biases = jnp.concatenate([bias_query, jnp.zeros((head_width,), F32), bias_value])
    qkv, full_qkv = qkv_project(order, normed, pieces_qkv, biases)
    mixed, lse = attn_forward(segments, qkv, head_width)
    attended = tp_terms(dot_nt(mixed, full_out).astype(BF16))
    normed_two, normed_two_t, hidden = norm_rows(rows_in, ln2_gain, ln2_bias, attended, b_out)

    out_part, gn_part, first_grads, bias_first = mlp(
        order, normed_two, grad_rows, normed_two_t, grad_rows_t, mlp_weights[0],
        bias_up[:half_units], (), False,
    )
    first_mlp = lax.psum_scatter(
        swap(first_grads[0], inverse=True), ("a", "c"), scatter_dimension=0, tiled=True
    ).astype(F32)
    out_part, gn_part, second_grads, bias_second = mlp(
        order, normed_two, grad_rows, normed_two_t, grad_rows_t, mlp_weights[1],
        bias_up[half_units:], (out_part, gn_part), True,
    )
    second_received = first_sends(second_grads)
    own_output = (own(hidden) + tp_scatter(out_part) + b_down).astype(BF16)
    output = swap(own_output, inverse=True)

    grad_hidden, grad_attended, grad_attended_t, sums_two = norm_back_rows(
        hidden, grad_rows, tp_terms(gn_part), ln2_gain
    )
    grad_mixed = dot_nn(grad_attended, full_out).astype(BF16)
    out_grads = weight_grads(order, grad_attended_t, mixed[None])
    out_received = first_sends(out_grads)

    grads = attn_backward(segments, qkv, mixed, lse, grad_mixed, head_width)
    second_mlp, grad_w_out = finish(
        [second_grads, out_grads], [second_received, out_received], grads, "unit"
    )
    qkv_grads = weight_grads(order, normed_t, grads)
    (late,) = finish([qkv_grads], [first_sends(qkv_grads)], None, "qkv")
    grad_normed = tp_scatter(qkv_back(grads, full_qkv))
    own_scaled, own_inverse = normalize(own_input.astype(F32))
    grad_own = own(grad_hidden) + norm_back(grad_normed, own_scaled, own_inverse, ln1_gain)
    grad_input = swap(grad_own.astype(BF16), inverse=True)

    def place_part(values, full):
        return lax.dynamic_update_slice_in_dim(
            jnp.zeros((full,), F32), values, rank * values.shape[0], 0
        )

    sums = sum_all(
        jnp.concatenate(
            [
                jnp.sum(grad_normed * own_scaled, axis=0),
                jnp.sum(grad_normed, axis=0),
                place_part(jnp.sum(grads[0].astype(F32), axis=0), width),
                place_part(jnp.sum(grads[2].astype(F32), axis=0), width),
                (sums_two[:3] * (1.0 / ranks)).reshape(-1),
                jnp.sum(own_grad.astype(F32), axis=0),
                place_part(jnp.concatenate([bias_first[0], bias_second[0]]), b_up.shape[0]),
            ]
        )
    )
    small = [sums[i * width : (i + 1) * width] for i in range(8)]
    halves = [split_mlp(first_mlp), split_mlp(second_mlp)]
    return (
        output, grad_input, small[0], small[1],
        late[:, :head_width], late[:, head_width : 2 * head_width], late[:, 2 * head_width :],
        small[2], small[3], grad_w_out, small[4], small[5], small[6],
        jnp.concatenate([half[0] for half in halves], axis=1), sums[8 * width :],
        jnp.concatenate([half[1] for half in halves], axis=1), small[7],
    )


def solution(mesh):
    groups, ranks = mesh.shape["dp"], mesh.shape["tensor"]
    sizes = {"a": groups // 2, "c": 2, "h": 2, "l": ranks // 2}
    fine = Mesh(mesh.devices.reshape(tuple(sizes.values())), tuple(sizes))
    rows = P(("a", "c", "h", "l"), None)
    block = P(("a", "c"), ("h", "l"))
    return jax.shard_map(
        functools.partial(per_device, sizes),
        mesh=fine,
        in_specs=(
            rows, P(("a", "c")), P(), P(), block, block, block, P(), P(), block, P(), P(), P(),
            block, P(), block, P(), rows,
        ),
        out_specs=(
            rows, rows, P(), P(), block, block, block, P(), P(), block, P(), P(), P(), block, P(),
            block, P(),
        ),
        check_vma=False,
    )
```

```python
import functools

import jax
import jax.numpy as jnp
from jax import lax
from jax.experimental import pallas as pl
from jax.experimental.pallas import tpu as pltpu
from jax.sharding import Mesh
from jax.sharding import PartitionSpec as P

HEAD_DIM = 64
LANES = 128
TILE = 512
MASKED = -1e30
VMEM_BYTES = 60 * 1024 * 1024
F32 = jnp.float32
BF16 = jnp.bfloat16
TP = ("l", "c")
SWAP = ("c", "h", "l")
ALL = ("a", "c", "h", "l")


def normalize(values):
    center = values - jnp.mean(values, axis=-1, keepdims=True)
    spread = jnp.mean(center * center, axis=-1, keepdims=True)
    inverse = lax.rsqrt(spread + 1e-05)
    return center * inverse, inverse


def norm_back(grad_in, scaled, inverse, gain_vec):
    local_grad = grad_in * gain_vec
    return inverse * (
        local_grad
        - jnp.mean(local_grad, axis=-1, keepdims=True)
        - scaled * jnp.mean(local_grad * scaled, axis=-1, keepdims=True)
    )


def dot_nn(left, right):
    return lax.dot_general(left, right, (((1,), (0,)), ((), ())), preferred_element_type=F32)


def dot_nt(left, right):
    return lax.dot_general(left, right, (((1,), (1,)), ((), ())), preferred_element_type=F32)


def dot_tn(left, right):
    return lax.dot_general(left, right, (((0,), (0,)), ((), ())), preferred_element_type=F32)


def fill_bias(bias, seg_col, seg_row):
    length = bias.shape[0]
    block = min(256, length)
    for first in range(0, length, block):
        keys = lax.broadcasted_iota(jnp.int32, (block, length), 0) + first
        places = lax.broadcasted_iota(jnp.int32, (block, length), 1)
        same = seg_col[first : first + block, :] == seg_row[...]
        bias[first : first + block, :] = jnp.where(same & (keys <= places), 0.0, MASKED)


def head_lanes(values, head):
    lane = lax.broadcasted_iota(jnp.int32, values.shape, 1)
    inside = (lane >= head * HEAD_DIM) & (lane < (head + 1) * HEAD_DIM)
    return jnp.where(inside, values, jnp.zeros_like(values))


def attn_forward_kernel(seg_col, seg_row, q_ref, k_ref, v_ref, mixed_ref, lse_ref, bias, v_t, block):
    length = q_ref.shape[0]
    heads = LANES // HEAD_DIM

    @pl.when(pl.program_id(0) == 0)
    def _():
        fill_bias(bias, seg_col, seg_row)

    v_t[...] = v_ref[...].T
    for place in range(length // block):
        rows = slice(place * block, (place + 1) * block)
        outs = []
        for head in range(heads):
            query = head_lanes(q_ref[rows, :], head)
            scores = []
            peak = None
            for other in range(place + 1):
                keys = slice(other * block, (other + 1) * block)
                part = dot_nt(k_ref[keys, :], query) + bias[keys, rows]
                top = jnp.max(part, axis=0, keepdims=True)
                peak = top if peak is None else jnp.maximum(peak, top)
                scores.append(part)
            total = None
            acc = None
            for other in range(place + 1):
                keys = slice(other * block, (other + 1) * block)
                weight = jnp.exp(scores[other] - peak)
                part_sum = jnp.sum(weight, axis=0, keepdims=True)
                total = part_sum if total is None else total + part_sum
                part_out = dot_nn(
                    v_t[head * HEAD_DIM : (head + 1) * HEAD_DIM, keys], weight.astype(BF16)
                )
                acc = part_out if acc is None else acc + part_out
            outs.append(acc / total)
            lse_ref[0, head : head + 1, rows] = peak + jnp.log(total)
        mixed_ref[rows, :] = jnp.concatenate(outs, axis=0).T.astype(BF16)


def attn_backward_kernel(
    seg_col, seg_row, q_ref, k_ref, v_ref, mixed_ref, lse_ref, g_ref, grads_ref, bias, k_t, delta, dq_t, block
):
    length = q_ref.shape[0]
    heads = LANES // HEAD_DIM
    count = length // block

    @pl.when(pl.program_id(0) == 0)
    def _():
        fill_bias(bias, seg_col, seg_row)

    k_t[...] = k_ref[...].T
    product = (g_ref[...].astype(F32) * mixed_ref[...].astype(F32)).T
    for head in range(heads):
        delta[head : head + 1, :] = jnp.sum(
            product[head * HEAD_DIM : (head + 1) * HEAD_DIM, :], axis=0, keepdims=True
        )
    for other in range(count):
        keys = slice(other * block, (other + 1) * block)
        key_sum = None
        value_sum = None
        for head in range(heads):
            lanes = slice(head * HEAD_DIM, (head + 1) * HEAD_DIM)
            for place in range(other, count):
                rows = slice(place * block, (place + 1) * block)
                query = head_lanes(q_ref[rows, :], head)
                grad = head_lanes(g_ref[rows, :], head)
                scores = dot_nt(k_ref[keys, :], query) + bias[keys, rows]
                probs = jnp.exp(scores - lse_ref[0, head : head + 1, rows])
                grad_probs = dot_nt(v_ref[keys, :], grad)
                grad_scores = (probs * (grad_probs - delta[head : head + 1, rows])).astype(BF16)
                value_part = dot_nn(probs.astype(BF16), grad)
                key_part = dot_nn(grad_scores, query)
                query_part = dot_nn(k_t[lanes, keys], grad_scores)
                value_sum = value_part if value_sum is None else value_sum + value_part
                key_sum = key_part if key_sum is None else key_sum + key_part
                if other == 0:
                    dq_t[lanes, rows] = query_part
                else:
                    dq_t[lanes, rows] += query_part
        grads_ref[1, keys, :] = key_sum.astype(BF16)
        grads_ref[2, keys, :] = value_sum.astype(BF16)
    grads_ref[0] = (dq_t[...].T * HEAD_DIM ** (-0.5)).astype(BF16)


def attn_forward(segments, qkv, width):
    length = qkv.shape[0]
    pairs = width // LANES
    block = min(256, length)
    column = lambda first: pl.BlockSpec((length, LANES), lambda p: (0, first * pairs + p))
    whole = lambda shape: pl.BlockSpec(shape, lambda p: (0, 0))
    return pl.pallas_call(
        functools.partial(attn_forward_kernel, block=block),
        grid=(pairs,),
        in_specs=[whole((length, 1)), whole((1, length)), column(0), column(1), column(2)],
        out_specs=[
            pl.BlockSpec((length, LANES), lambda p: (0, p)),
            pl.BlockSpec((1, 8, length), lambda p: (p, 0, 0)),
        ],
        out_shape=[
            jax.ShapeDtypeStruct((length, width), BF16),
            jax.ShapeDtypeStruct((pairs, 8, length), F32),
        ],
        scratch_shapes=[pltpu.VMEM((length, length), F32), pltpu.VMEM((LANES, length), BF16)],
        compiler_params=pltpu.CompilerParams(vmem_limit_bytes=VMEM_BYTES),
        cost_estimate=pl.CostEstimate(
            flops=4 * length * length * width,
            bytes_accessed=8 * length * width,
            transcendentals=length * length * width // (2 * HEAD_DIM),
        ),
        name="attn_forward",
    )(segments.reshape(length, 1), segments.reshape(1, length), qkv, qkv, qkv)


def attn_backward(segments, qkv, mixed, lse, grad_mixed, width, after):
    length = qkv.shape[0]
    pairs = width // LANES
    block = min(256, length)
    column = lambda first: pl.BlockSpec((length, LANES), lambda p: (0, first * pairs + p))
    whole = lambda shape: pl.BlockSpec(shape, lambda p: (0, 0))
    return pl.pallas_call(
        without(functools.partial(attn_backward_kernel, block=block), 8),
        grid=(pairs,),
        in_specs=[
            whole((length, 1)),
            whole((1, length)),
            column(0),
            column(1),
            column(2),
            pl.BlockSpec((length, LANES), lambda p: (0, p)),
            pl.BlockSpec((1, 8, length), lambda p: (p, 0, 0)),
            pl.BlockSpec((length, LANES), lambda p: (0, p)),
            pl.BlockSpec(memory_space=pl.ANY),
        ],
        out_specs=pl.BlockSpec((3, length, LANES), lambda p: (0, 0, p)),
        out_shape=jax.ShapeDtypeStruct((3, length, width), BF16),
        scratch_shapes=[
            pltpu.VMEM((length, length), F32),
            pltpu.VMEM((LANES, length), BF16),
            pltpu.VMEM((8, length), F32),
            pltpu.VMEM((LANES, length), F32),
        ],
        compiler_params=pltpu.CompilerParams(vmem_limit_bytes=VMEM_BYTES),
        cost_estimate=pl.CostEstimate(
            flops=10 * length * length * width,
            bytes_accessed=16 * length * width,
            transcendentals=length * length * width // (2 * HEAD_DIM),
        ),
        name="attn_backward",
    )(segments.reshape(length, 1), segments.reshape(1, length), qkv, qkv, qkv, mixed, lse, grad_mixed, after)


def piece_blocks(count):
    far = count // 4
    half = far // 2
    near, by_y, by_x, both = (list(range(i * far, (i + 1) * far)) for i in range(4))
    return [
        both[:half] + by_x[:half],
        both[half:] + by_y[half:],
        by_y[:half],
        by_x[half:],
        near,
    ]


def store_pieces(order, grad, piece_refs, columns):
    count = order.shape[0]
    rows = grad.shape[0] // count
    for blocks, ref in zip(piece_blocks(count), piece_refs):
        for place, block in enumerate(blocks):
            first = pl.multiple_of(order[block] * rows, rows)
            ref[place * rows : (place + 1) * rows, columns] = grad[pl.ds(first, rows), :]


def piece_shapes(count, rows, columns):
    return [
        jax.ShapeDtypeStruct((len(blocks) * rows, columns), BF16) for blocks in piece_blocks(count)
    ]


def whole_spec(shape, **options):
    return pl.BlockSpec(shape, lambda step: (0,) * len(shape), **options)


def norm_kernel(*refs, residual):
    if residual:
        x_ref, own_ref, other_ref, shift_ref, gain_ref, bias_ref, n_ref, nt_ref, hidden_ref = refs
        values = (
            x_ref[...].astype(F32)
            + (own_ref[...].astype(F32) + other_ref[...].astype(F32))
            + shift_ref[...]
        )
        hidden_ref[...] = values
    else:
        x_ref, gain_ref, bias_ref, n_ref, nt_ref = refs
        values = x_ref[...].astype(F32)
    scaled, _ = normalize(values)
    normed = (scaled * gain_ref[...] + bias_ref[...]).astype(BF16)
    n_ref[...] = normed
    nt_ref[...] = normed.T


def norm_rows(x, gain, bias, partials=None, shift=None):
    length, width = x.shape
    block = min(256, length)
    row = pl.BlockSpec((block, width), lambda step: (step, 0))
    vector = whole_spec((1, width))
    residual = partials is not None
    operands = [x] + (list(partials) + [shift.reshape(1, width)] if residual else [])
    operands += [gain.reshape(1, width), bias.reshape(1, width)]
    return pl.pallas_call(
        functools.partial(norm_kernel, residual=residual),
        grid=(length // block,),
        in_specs=[row] + ([row, row, vector] if residual else []) + [vector, vector],
        out_specs=[row, pl.BlockSpec((width, block), lambda step: (0, step))]
        + ([row] if residual else []),
        out_shape=[
            jax.ShapeDtypeStruct((length, width), BF16),
            jax.ShapeDtypeStruct((width, length), BF16),
        ]
        + ([jax.ShapeDtypeStruct((length, width), F32)] if residual else []),
        compiler_params=pltpu.CompilerParams(vmem_limit_bytes=VMEM_BYTES),
        cost_estimate=pl.CostEstimate(
            flops=20 * length * width, bytes_accessed=14 * length * width, transcendentals=length
        ),
        name="norm_two" if residual else "norm_one",
    )(*operands)


def norm_back_kernel(hidden_ref, g_ref, own_ref, other_ref, gain_ref, grad_ref, low_ref, low_t_ref, sums_ref):
    scaled, inverse = normalize(hidden_ref[...])
    incoming = own_ref[...].astype(F32) + other_ref[...].astype(F32)
    grad = g_ref[...].astype(F32) + norm_back(incoming, scaled, inverse, gain_ref[...])
    grad_ref[...] = grad
    low_ref[...] = grad.astype(BF16)
    low_t_ref[...] = grad.astype(BF16).T

    @pl.when(pl.program_id(0) == 0)
    def _():
        sums_ref[...] = jnp.zeros_like(sums_ref)

    sums_ref[0:1, :] += jnp.sum(grad, axis=0, keepdims=True)
    sums_ref[1:2, :] += jnp.sum(incoming * scaled, axis=0, keepdims=True)
    sums_ref[2:3, :] += jnp.sum(incoming, axis=0, keepdims=True)


def norm_back_rows(hidden, grad, partials, gain):
    length, width = hidden.shape
    block = min(256, length)
    row = pl.BlockSpec((block, width), lambda step: (step, 0))
    return pl.pallas_call(
        norm_back_kernel,
        grid=(length // block,),
        in_specs=[row, row, row, row, whole_spec((1, width))],
        out_specs=[
            row,
            row,
            pl.BlockSpec((width, block), lambda step: (0, step)),
            whole_spec((8, width)),
        ],
        out_shape=[
            jax.ShapeDtypeStruct((length, width), F32),
            jax.ShapeDtypeStruct((length, width), BF16),
            jax.ShapeDtypeStruct((width, length), BF16),
            jax.ShapeDtypeStruct((8, width), F32),
        ],
        compiler_params=pltpu.CompilerParams(vmem_limit_bytes=VMEM_BYTES),
        cost_estimate=pl.CostEstimate(
            flops=30 * length * width, bytes_accessed=16 * length * width, transcendentals=length
        ),
        name="norm_two_back",
    )(hidden, grad, *partials, gain.reshape(1, width))


def load_pieces(order, pieces, w_ref):
    rows = w_ref.shape[0] // order.shape[0]
    block = 0
    for ref in pieces:
        for place in range(ref.shape[0] // rows):
            first = pl.multiple_of(order[block] * rows, rows)
            w_ref[pl.ds(first, rows), :] = ref[place * rows : (place + 1) * rows, :]
            block += 1


def mlp_kernel(order, n_ref, g_ref, nt_ref, gt_ref, b_ref, *refs, block, with_previous, cube, in_pieces):
    if in_pieces:
        pieces, refs = refs[:5], refs[5:]
        w_ref, refs = refs[-1], refs[:-1]
        load_pieces(order, pieces, w_ref)
    else:
        w_ref, refs = refs[0], refs[1:]
    if with_previous:
        (before_out, before_gn), refs = refs[:2], refs[2:]
    count = 5 if cube else 1
    (out_ref, gn_ref), grad_refs, refs = refs[:2], refs[2 : 2 + count], refs[2 + count :]
    gb_ref, out_acc, gn_acc, act, gpre, grad_up, grad_down = refs
    step = pl.program_id(0)
    length = n_ref.shape[0]
    tile = w_ref.shape[1] // 2
    ups, downs = slice(0, tile), slice(tile, 2 * tile)

    @pl.when(step == 0)
    def _():
        if with_previous:
            out_acc[...] = before_out[...].astype(F32)
            gn_acc[...] = before_gn[...].astype(F32)
        else:
            out_acc[...] = jnp.zeros_like(out_acc)
            gn_acc[...] = jnp.zeros_like(gn_acc)

    bias_sum = jnp.zeros(gb_ref.shape, F32)
    for first in range(0, length, block):
        rows = slice(first, first + block)
        unit = dot_nn(n_ref[rows, :], w_ref[:, ups]) + b_ref[...]
        grad = dot_nn(g_ref[rows, :], w_ref[:, downs])
        square = unit * unit
        curve = jnp.tanh(0.7978845608028654 * (unit + 0.044715 * (square * unit)))
        half = 0.5 + 0.5 * curve
        slope = half + (0.5 * unit) * (1.0 - curve * curve) * (
            0.7978845608028654 + (3 * 0.044715 * 0.7978845608028654) * square
        )
        active = (unit * half).astype(BF16)
        grad_pre = (grad * slope).astype(BF16)
        act[rows, :] = active
        gpre[rows, :] = grad_pre
        bias_sum = bias_sum + jnp.sum(grad_pre.astype(F32), axis=0, keepdims=True)
        out_acc[rows, :] += dot_nt(active, w_ref[:, downs])
        gn_acc[rows, :] += dot_nt(grad_pre, w_ref[:, ups])
    gb_ref[...] = bias_sum
    if cube:
        grad_up[...] = dot_nn(nt_ref[...], gpre[...]).astype(BF16)
        grad_down[...] = dot_nn(gt_ref[...], act[...]).astype(BF16)
        store_pieces(order, grad_up, grad_refs, ups)
        store_pieces(order, grad_down, grad_refs, downs)
    else:
        grad_refs[0][:, ups] = dot_nn(nt_ref[...], gpre[...]).astype(BF16)
        grad_refs[0][:, downs] = dot_nn(gt_ref[...], act[...]).astype(BF16)

    @pl.when(step == pl.num_programs(0) - 1)
    def _():
        out_ref[...] = out_acc[...].astype(BF16)
        gn_ref[...] = gn_acc[...].astype(BF16)


def mlp(order, normed, grad, normed_t, grad_t, weights, bias, previous, cube):
    length, width = normed.shape
    units = weights[0].shape[1] // 2
    in_pieces = len(weights) > 1
    tile = min(TILE, units)
    once = pl.Buffered(1)
    fixed = lambda shape, **options: pl.BlockSpec(shape, lambda u, o: (0, 0), **options)
    at_tile = lambda rows, columns: pl.BlockSpec((rows, columns), lambda u, o: (0, u))
    count, rows = order.shape[0], width // order.shape[0]
    if cube:
        grad_shapes = piece_shapes(count, rows, 2 * units)
    else:
        grad_shapes = [jax.ShapeDtypeStruct((width, 2 * units), BF16)]
    results = pl.pallas_call(
        functools.partial(
            mlp_kernel, block=min(256, length), with_previous=bool(previous), cube=cube,
            in_pieces=in_pieces,
        ),
        grid_spec=pltpu.PrefetchScalarGridSpec(
            num_scalar_prefetch=1,
            grid=(units // tile,),
            in_specs=[
                fixed((length, width), pipeline_mode=once),
                fixed((length, width), pipeline_mode=once),
                fixed((width, length), pipeline_mode=once),
                fixed((width, length), pipeline_mode=once),
                at_tile(1, tile),
            ]
            + [at_tile(piece.shape[0], 2 * tile) for piece in weights]
            + [fixed((length, width), pipeline_mode=once) for _ in previous],
            out_specs=[fixed((length, width)), fixed((length, width))]
            + [at_tile(shape.shape[0], 2 * tile) for shape in grad_shapes]
            + [at_tile(1, tile)],
            scratch_shapes=[
                pltpu.VMEM((length, width), F32),
                pltpu.VMEM((length, width), F32),
                pltpu.VMEM((length, tile), BF16),
                pltpu.VMEM((length, tile), BF16),
                pltpu.VMEM((width, tile), BF16),
                pltpu.VMEM((width, tile), BF16),
            ]
            + ([pltpu.VMEM((width, 2 * tile), BF16)] if in_pieces else []),
        ),
        out_shape=[jax.ShapeDtypeStruct((length, width), BF16)] * 2
        + grad_shapes
        + [jax.ShapeDtypeStruct((1, units), F32)],
        compiler_params=pltpu.CompilerParams(vmem_limit_bytes=VMEM_BYTES),
        cost_estimate=pl.CostEstimate(
            flops=12 * length * width * units,
            bytes_accessed=12 * length * width + 8 * width * units,
            transcendentals=length * units,
        ),
        name="mlp_second" if previous else "mlp_first",
    )(order, normed, grad, normed_t, grad_t, bias.reshape(1, units), *weights, *previous)
    return results[0], results[1], results[2:-1], results[-1]


def qkv_kernel(order, n_ref, b_ref, near, by_y, by_x, low, high, out_ref, w_ref):
    load_pieces(order, (near, by_y, by_x, low, high), w_ref)
    scale = jnp.where(pl.program_id(0) == 0, HEAD_DIM ** (-0.5), 1.0)
    length = n_ref.shape[0]
    step = min(256, length)
    for first in range(0, length, step):
        span = slice(first, first + step)
        out_ref[span, :] = ((dot_nn(n_ref[span, :], w_ref[...]) + b_ref[...]) * scale).astype(BF16)


def qkv_project(order, normed, pieces, bias):
    length, width = normed.shape
    columns = pieces[0].shape[1] // 3
    at_tile = lambda rows: pl.BlockSpec((rows, columns), lambda k, o: (0, k))
    return pl.pallas_call(
        qkv_kernel,
        grid_spec=pltpu.PrefetchScalarGridSpec(
            num_scalar_prefetch=1,
            grid=(3,),
            in_specs=[
                pl.BlockSpec((length, width), lambda k, o: (0, 0), pipeline_mode=pl.Buffered(1)),
                at_tile(1),
            ]
            + [at_tile(piece.shape[0]) for piece in pieces],
            out_specs=[at_tile(length), at_tile(width)],
        ),
        out_shape=[
            jax.ShapeDtypeStruct((length, 3 * columns), BF16),
            jax.ShapeDtypeStruct((width, 3 * columns), BF16),
        ],
        compiler_params=pltpu.CompilerParams(vmem_limit_bytes=VMEM_BYTES),
        cost_estimate=pl.CostEstimate(
            flops=6 * length * width * columns,
            bytes_accessed=2 * length * width + 12 * width * columns + 6 * length * columns,
            transcendentals=0,
        ),
        name="qkv_project",
    )(order, normed, bias.reshape(1, 3 * columns), *pieces)


def weight_kernel(order, nt_ref, grads_ref, *refs):
    piece_refs, grad = refs[:5], refs[5]
    grad[...] = dot_nn(nt_ref[...], grads_ref[0]).astype(BF16)
    store_pieces(order, grad, piece_refs, slice(None))


def without(kernel, place):
    return lambda *refs: kernel(*refs[:place], *refs[place + 1 :])


ORDER_ONLY = pl.BlockSpec(memory_space=pl.ANY)


def weight_grads(order, normed_t, grads, after):
    width, length = normed_t.shape
    columns = grads.shape[2]
    tile = min(TILE, columns)
    tiles = columns // tile
    parts = grads.shape[0]
    shapes = piece_shapes(order.shape[0], width // order.shape[0], parts * columns)
    return pl.pallas_call(
        without(weight_kernel, 3),
        grid_spec=pltpu.PrefetchScalarGridSpec(
            num_scalar_prefetch=1,
            grid=(parts, tiles),
            in_specs=[
                pl.BlockSpec((width, length), lambda k, u, o: (0, 0), pipeline_mode=pl.Buffered(1)),
                pl.BlockSpec((1, length, tile), lambda k, u, o: (k, 0, u)),
                ORDER_ONLY,
            ],
            out_specs=[
                pl.BlockSpec((shape.shape[0], tile), lambda k, u, o: (0, k * tiles + u))
                for shape in shapes
            ],
            scratch_shapes=[pltpu.VMEM((width, tile), BF16)],
        ),
        out_shape=shapes,
        compiler_params=pltpu.CompilerParams(vmem_limit_bytes=VMEM_BYTES),
        cost_estimate=pl.CostEstimate(
            flops=2 * parts * length * width * columns,
            bytes_accessed=2 * length * width + 4 * parts * width * columns,
            transcendentals=0,
        ),
        name="weight_grads",
    )(order, normed_t, grads, after)


def qkv_back_kernel(grads_ref, w_ref, out_ref):
    columns = grads_ref.shape[2]
    total = None
    for k in range(3):
        part = dot_nt(grads_ref[k], w_ref[:, k * columns : (k + 1) * columns])
        total = part if total is None else total + part
    out_ref[...] = total.astype(BF16)


def qkv_back(grads, weights, after):
    _, length, columns = grads.shape
    width = weights.shape[0]
    block = min(256, length)
    return pl.pallas_call(
        without(qkv_back_kernel, 2),
        grid=(length // block,),
        in_specs=[
            pl.BlockSpec((3, block, columns), lambda i: (0, i, 0)),
            pl.BlockSpec((width, 3 * columns), lambda i: (0, 0), pipeline_mode=pl.Buffered(1)),
            ORDER_ONLY,
        ],
        out_specs=pl.BlockSpec((block, width), lambda i: (i, 0)),
        out_shape=jax.ShapeDtypeStruct((length, width), BF16),
        compiler_params=pltpu.CompilerParams(vmem_limit_bytes=VMEM_BYTES),
        cost_estimate=pl.CostEstimate(
            flops=6 * length * width * columns,
            bytes_accessed=2 * length * width + 6 * width * columns + 6 * length * columns,
            transcendentals=0,
        ),
        name="qkv_back",
    )(grads, weights, after)


def added(*terms):
    total = terms[0].astype(F32)
    for term in terms[1:]:
        total = total + term.astype(F32)
    return total.astype(BF16)


def first_sums_kernel(*refs, spans):
    refs, (y_ref, x_ref) = refs[:-2], refs[-2:]
    half = y_ref.shape[0]
    for index, columns in enumerate(spans):
        from_x, from_y, keep_y, keep_x = (ref[...] for ref in refs[4 * index : 4 * index + 4])
        y_ref[:, columns] = added(keep_y, from_x[:half])
        x_ref[:, columns] = added(keep_x, from_y[:half])


def second_sums_kernel(*refs, spans, far):
    outs, refs = refs[-far:], refs[:-far]
    (from_y2, from_x2), refs = refs[-2:], refs[:-2]
    half = from_y2.shape[0]
    rows = half * 2 // far
    for index, columns in enumerate(spans):
        from_x, from_y, near = refs[3 * index : 3 * index + 3]
        for i in range(far):
            first, second, place = (from_x, from_y2, i) if i < far // 2 else (from_y, from_x2, i - far // 2)
            span = slice(place * rows, (place + 1) * rows)
            outs[i][:, columns] = added(
                near[i * rows : (i + 1) * rows, :],
                first[half + place * rows : half + (place + 1) * rows, :],
                second[span, columns],
            )


def last_sums_kernel(*refs, far, half_tile, head_width):
    parts, other, (up_ref, down_ref, out_ref) = refs[:far], refs[far], refs[far + 1 :]
    total = parts[0][...].astype(F32)
    for part in parts[1:]:
        total = total + part[...].astype(F32)
    units = up_ref.shape[1] // 2
    for first in range(0, units, half_tile):
        here, there = slice(first, first + half_tile), slice(units + first, units + first + half_tile)
        up, down = slice(2 * first, 2 * first + half_tile), slice(2 * first + half_tile, 2 * first + 2 * half_tile)
        up_ref[:, here] = other[:, up].astype(F32)
        down_ref[:, here] = other[:, down].astype(F32)
        up_ref[:, there] = total[:, up]
        down_ref[:, there] = total[:, down]
    out_ref[...] = total[:, 2 * units : 2 * units + head_width]


def qkv_last_kernel(*refs):
    parts, outs = refs[:-3], refs[-3:]
    total = parts[0][...].astype(F32)
    for part in parts[1:]:
        total = total + part[...].astype(F32)
    columns = outs[0].shape[1]
    for k, out in enumerate(outs):
        out[...] = total[:, k * columns : (k + 1) * columns]


def shards_kernel(w_out, w_up, w_down, out_ref, first_ref, second_ref, *, tile):
    out_ref[...] = w_out[...]
    units = first_ref.shape[1] // 2
    for index, ref in enumerate((first_ref, second_ref)):
        for first in range(0, units, tile):
            columns = slice(index * units + first, index * units + first + tile)
            ref[:, 2 * first : 2 * first + tile] = w_up[:, columns]
            ref[:, 2 * first + tile : 2 * first + 2 * tile] = w_down[:, columns]


def copy_kernel(source, target):
    target[...] = source[...]


def column_spans(widths):
    spans, first = [], 0
    for width in widths:
        spans.append(slice(first, first + width))
        first += width
    return spans


def sums_call(kernel, operands, shapes, after, name):
    body = kernel if after is None else without(kernel, 0)
    vmem = pl.BlockSpec(memory_space=pltpu.VMEM)
    return pl.pallas_call(
        body,
        in_specs=([pl.BlockSpec(memory_space=pl.ANY)] if after is not None else [])
        + [vmem] * len(operands),
        out_specs=[vmem] * len(shapes),
        out_shape=shapes,
        compiler_params=pltpu.CompilerParams(vmem_limit_bytes=VMEM_BYTES),
        name=name,
    )(*([after] if after is not None else []), *operands)


def flipped(sizes):
    return 1 if sizes["h"] * sizes["l"] == 2 else 0


def moves(sizes):
    groups, ranks, inner = sizes["a"], sizes["h"] * sizes["l"], sizes["l"]
    far = groups // 2
    flip = flipped(sizes)
    swap_to = {}
    for group in range(2):
        for part in range(ranks):
            place = (part % 2 ^ flip) * ranks + group * (ranks // 2) + part // 2
            swap_to[group * ranks + part] = place

    def swap(values, inverse=False):
        pairs = [(to, frm) if inverse else (frm, to) for frm, to in swap_to.items()]
        return lax.ppermute(values, SWAP, pairs)

    def swap_hop(values, a_mask, inverse=False):
        pairs = []
        for a in range(groups):
            for frm, to in swap_to.items():
                one, two = a * 2 * ranks + frm, (a ^ a_mask) * 2 * ranks + to
                pairs.append((two, one) if inverse else (one, two))
        return lax.ppermute(values, ALL, pairs)

    def hop(values, a_mask, h_mask):
        pairs = []
        for a in range(groups):
            for c in range(2):
                for h in range(2):
                    pairs.append(((a * 2 + c) * 2 + h, ((a ^ a_mask) * 2 + c) * 2 + (h ^ h_mask)))
        return lax.ppermute(values, ("a", "c", "h"), pairs)

    def gather(shard):
        near = jnp.concatenate([swap_hop(shard, 2 * i) for i in range(far)], axis=0)
        half = near.shape[0] // 2
        by_y = hop(near, 1, 0)
        by_x = hop(near, 0, 1)
        return [near, by_y, by_x, hop(by_y[:half], 0, 1), hop(by_x[half:], 1, 0)]

    def first_sends(pieces):
        return hop(pieces[0], 0, 1), hop(pieces[1], 1, 0)

    def finish(chunks, received, after, after_two, name):
        spans = column_spans([pieces[0].shape[1] for pieces in chunks])
        total = spans[-1].stop
        half, rows = chunks[0][2].shape[0], chunks[0][4].shape[0] // far
        operands = []
        for pieces, (from_x, from_y) in zip(chunks, received):
            operands += [from_x, from_y, pieces[2], pieces[3]]
        y_sum, x_sum = sums_call(
            functools.partial(first_sums_kernel, spans=spans),
            operands,
            [jax.ShapeDtypeStruct((half, total), BF16)] * 2,
            after,
            name + "_sums_one",
        )
        from_y2, from_x2 = hop(y_sum, 1, 0), hop(x_sum, 0, 1)
        operands = []
        for pieces, (from_x, from_y) in zip(chunks, received):
            operands += [from_x, from_y, pieces[4]]
        sums = sums_call(
            functools.partial(second_sums_kernel, spans=spans, far=far),
            operands + [from_y2, from_x2],
            [jax.ShapeDtypeStruct((rows, total), BF16)] * far,
            after_two(y_sum),
            name + "_sums_two",
        )
        return sums[0], [swap_hop(sums[i], 2 * i, inverse=True) for i in range(far)]

    def sum_all(values):
        values = values + lax.ppermute(values, "c", [(0, 1), (1, 0)])
        values = values + hop(values, 0, 1)
        for mask in range(groups.bit_length() - 1):
            values = values + hop(values, 1 << mask, 0)
        return lax.psum(values, "l") if inner > 1 else values

    a, h = lax.axis_index("a"), lax.axis_index("h")
    order = []
    for a_low, h_mask in ((0, 0), (1, 0), (0, 1), (1, 1)):
        for i in range(far):
            order.append((a ^ (2 * i + a_low)) * 2 + (h ^ h_mask))
    return swap, gather, first_sends, finish, sum_all, jnp.stack(order).astype(jnp.int32)


def per_device(sizes, *arguments):
    (
        block_input, segment_ids, ln1_gain, ln1_bias, w_query, w_key, w_value, b_query, b_value,
        w_out, b_out, ln2_gain, ln2_bias, w_up, b_up, w_down, b_down, out_grad,
    ) = arguments
    ranks = sizes["h"] * sizes["l"]
    rank = lax.axis_index("l") * 2 + (lax.axis_index("c") ^ flipped(sizes))
    own_rows, width = block_input.shape
    head_width = w_query.shape[1]
    unit_width = w_up.shape[1]
    half_units = unit_width // 2
    tile = min(TILE, half_units)
    swap, gather, first_sends, finish, sum_all, order = moves(sizes)

    def partner(values):
        return lax.ppermute(values, "c", [(0, 1), (1, 0)])

    def tp_gather(values):
        if ranks != 2:
            return lax.all_gather(values, TP, axis=0, tiled=True)
        theirs = partner(values)
        return jnp.where(
            rank == 0,
            jnp.concatenate([values, theirs], axis=0),
            jnp.concatenate([theirs, values], axis=0),
        )

    def tp_terms(values):
        if ranks != 2:
            others = lax.psum(values.astype(F32), TP) - values.astype(F32)
            return values, others.astype(BF16)
        return values, partner(values)

    def own(values):
        return lax.dynamic_slice_in_dim(values, rank * own_rows, own_rows)

    def tp_scatter(values):
        if ranks != 2:
            return lax.psum_scatter(values, TP, scatter_dimension=0, tiled=True).astype(F32)
        theirs = lax.dynamic_slice_in_dim(values, (1 - rank) * own_rows, own_rows)
        return own(values).astype(F32) + partner(theirs).astype(F32)

    pieces_qkv = gather(jnp.concatenate([w_query, w_key, w_value], axis=1))
    shard_out, shard_first, shard_second = sums_call(
        functools.partial(shards_kernel, tile=tile),
        [w_out, w_up, w_down],
        [
            jax.ShapeDtypeStruct(w_out.shape, BF16),
            jax.ShapeDtypeStruct(w_up.shape, BF16),
            jax.ShapeDtypeStruct(w_up.shape, BF16),
        ],
        pieces_qkv[0],
        "mlp_shards",
    )
    full_out = lax.all_gather(swap(shard_out), ("a", "h"), axis=0, tiled=True)
    full_second = lax.all_gather(swap(shard_second), ("a", "h"), axis=0, tiled=True)
    pieces_first = gather(shard_first)
    own_input = swap(block_input)
    segments = swap(segment_ids)
    own_grad = swap(out_grad)
    bias_query = lax.dynamic_slice_in_dim(b_query, rank * head_width, head_width)
    bias_value = lax.dynamic_slice_in_dim(b_value, rank * head_width, head_width)
    bias_up = lax.dynamic_slice_in_dim(b_up, rank * unit_width, unit_width)

    rows_in = tp_gather(own_input)
    grad_rows = tp_gather(own_grad)
    grad_rows_t = grad_rows.T
    normed, normed_t = norm_rows(rows_in, ln1_gain, ln1_bias)
    biases = jnp.concatenate([bias_query, jnp.zeros((head_width,), F32), bias_value])
    qkv, full_qkv = qkv_project(order, normed, pieces_qkv, biases)
    mixed, lse = attn_forward(segments, qkv, head_width)
    attended = tp_terms(dot_nt(mixed, full_out).astype(BF16))
    normed_two, normed_two_t, hidden = norm_rows(rows_in, ln2_gain, ln2_bias, attended, b_out)

    out_part, gn_part, first_grads, bias_first = mlp(
        order, normed_two, grad_rows, normed_two_t, grad_rows_t, pieces_first,
        bias_up[:half_units], (), False,
    )
    first_mlp = lax.psum_scatter(
        swap(first_grads[0], inverse=True), ("a", "c"), scatter_dimension=0, tiled=True
    )
    out_part, gn_part, second_grads, bias_second = mlp(
        order, normed_two, grad_rows, normed_two_t, grad_rows_t, [full_second],
        bias_up[half_units:], (out_part, gn_part), True,
    )
    second_received = first_sends(second_grads)
    own_output = (own(hidden) + tp_scatter(out_part) + b_down).astype(BF16)
    output = swap(own_output, inverse=True)

    grad_hidden, grad_attended, grad_attended_t, sums_two = norm_back_rows(
        hidden, grad_rows, tp_terms(gn_part), ln2_gain
    )
    grad_mixed = dot_nn(grad_attended, full_out).astype(BF16)
    out_grads = weight_grads(order, grad_attended_t, mixed[None], grad_mixed)
    out_received = first_sends(out_grads)

    grads = attn_backward(segments, qkv, mixed, lse, grad_mixed, head_width, out_grads[0])
    grad_normed_part = []

    def after_unit_sums(y_sum):
        pieces = weight_grads(order, normed_t, grads, y_sum)
        grad_normed_part.append((pieces, qkv_back(grads, full_qkv, pieces[0])))
        return grad_normed_part[0][1]

    _, unit_parts = finish(
        [second_grads, out_grads], [second_received, out_received], grads, after_unit_sums, "unit"
    )
    qkv_grads, grad_normed_part = grad_normed_part[0]
    qkv_done, qkv_parts = finish(
        [qkv_grads], [first_sends(qkv_grads)], None, lambda y_sum: None, "qkv"
    )
    shard = lambda columns: jax.ShapeDtypeStruct((w_query.shape[0], columns), F32)
    grad_w_up, grad_w_down, grad_w_out = sums_call(
        functools.partial(
            last_sums_kernel, far=len(unit_parts), half_tile=tile, head_width=head_width
        ),
        unit_parts + [first_mlp],
        [shard(unit_width), shard(unit_width), shard(head_width)],
        None,
        "unit_sums_last",
    )
    late = sums_call(qkv_last_kernel, qkv_parts, [shard(head_width)] * 3, None, "qkv_sums_last")
    grad_normed = tp_scatter(grad_normed_part)
    own_scaled, own_inverse = normalize(own_input.astype(F32))
    grad_own = own(grad_hidden) + norm_back(grad_normed, own_scaled, own_inverse, ln1_gain)
    grad_input = swap(grad_own.astype(BF16), inverse=True)

    def place_part(values, full):
        return lax.dynamic_update_slice_in_dim(
            jnp.zeros((full,), F32), values, rank * values.shape[0], 0
        )

    sums = jnp.concatenate(
        [
            jnp.sum(grad_normed * own_scaled, axis=0),
            jnp.sum(grad_normed, axis=0),
            place_part(jnp.sum(grads[0].astype(F32), axis=0), width),
            place_part(jnp.sum(grads[2].astype(F32), axis=0), width),
            (sums_two[:3] * (1.0 / ranks)).reshape(-1),
            jnp.sum(own_grad.astype(F32), axis=0),
            place_part(jnp.concatenate([bias_first[0], bias_second[0]]), b_up.shape[0]),
        ]
    ).reshape(-1, LANES)
    (sums,) = sums_call(
        copy_kernel, [sums], [jax.ShapeDtypeStruct(sums.shape, F32)], qkv_done, "small_sums"
    )
    sums = sum_all(sums).reshape(-1)
    small = [sums[i * width : (i + 1) * width] for i in range(8)]
    return (
        output, grad_input, small[0], small[1],
        late[0], late[1], late[2], small[2], small[3], grad_w_out, small[4], small[5], small[6],
        grad_w_up, sums[8 * width :], grad_w_down, small[7],
    )


def solution(mesh):
    groups, ranks = mesh.shape["dp"], mesh.shape["tensor"]
    sizes = {"a": groups // 2, "c": 2, "h": 2, "l": ranks // 2}
    fine = Mesh(mesh.devices.reshape(tuple(sizes.values())), tuple(sizes))
    rows = P(("a", "c", "h", "l"), None)
    block = P(("a", "c"), ("h", "l"))
    return jax.shard_map(
        functools.partial(per_device, sizes),
        mesh=fine,
        in_specs=(
            rows, P(("a", "c")), P(), P(), block, block, block, P(), P(), block, P(), P(), P(),
            block, P(), block, P(), rows,
        ),
        out_specs=(
            rows, rows, P(), P(), block, block, block, P(), P(), block, P(), P(), P(), block, P(),
            block, P(),
        ),
        check_vma=False,
    )
```

```python
import functools

import jax
import jax.numpy as jnp
from jax import lax
from jax.experimental import pallas as pl
from jax.experimental.pallas import tpu as pltpu
from jax.sharding import Mesh
from jax.sharding import PartitionSpec as P

HEAD_DIM = 64
LANES = 128
TILE = 512
MASKED = -1e30
VMEM_BYTES = 60 * 1024 * 1024
F32 = jnp.float32
BF16 = jnp.bfloat16
TP = ("l", "c")
SWAP = ("c", "h", "l")
ALL = ("a", "c", "h", "l")


def small_cost(flops, bytes_accessed, transcendentals):
    return pl.CostEstimate(
        flops=flops // 4, bytes_accessed=bytes_accessed // 4, transcendentals=transcendentals // 4
    )


def normalize(values):
    center = values - jnp.mean(values, axis=-1, keepdims=True)
    spread = jnp.mean(center * center, axis=-1, keepdims=True)
    inverse = lax.rsqrt(spread + 1e-05)
    return center * inverse, inverse


def norm_back(grad_in, scaled, inverse, gain_vec):
    local_grad = grad_in * gain_vec
    return inverse * (
        local_grad
        - jnp.mean(local_grad, axis=-1, keepdims=True)
        - scaled * jnp.mean(local_grad * scaled, axis=-1, keepdims=True)
    )


def dot_nn(left, right):
    return lax.dot_general(left, right, (((1,), (0,)), ((), ())), preferred_element_type=F32)


def dot_nt(left, right):
    return lax.dot_general(left, right, (((1,), (1,)), ((), ())), preferred_element_type=F32)


def dot_tn(left, right):
    return lax.dot_general(left, right, (((0,), (0,)), ((), ())), preferred_element_type=F32)


def fill_bias(bias, seg_col, seg_row):
    length = bias.shape[0]
    block = min(256, length)
    for first in range(0, length, block):
        keys = lax.broadcasted_iota(jnp.int32, (block, length), 0) + first
        places = lax.broadcasted_iota(jnp.int32, (block, length), 1)
        same = seg_col[first : first + block, :] == seg_row[...]
        bias[first : first + block, :] = jnp.where(same & (keys <= places), 0.0, MASKED)


def head_lanes(values, head):
    lane = lax.broadcasted_iota(jnp.int32, values.shape, 1)
    inside = (lane >= head * HEAD_DIM) & (lane < (head + 1) * HEAD_DIM)
    return jnp.where(inside, values, jnp.zeros_like(values))


def attn_forward_kernel(seg_col, seg_row, q_ref, k_ref, v_ref, mixed_ref, lse_ref, bias, v_t, block):
    length = q_ref.shape[0]
    heads = LANES // HEAD_DIM

    @pl.when(pl.program_id(0) == 0)
    def _():
        fill_bias(bias, seg_col, seg_row)

    v_t[...] = v_ref[...].T
    for place in range(length // block):
        rows = slice(place * block, (place + 1) * block)
        outs = []
        for head in range(heads):
            query = head_lanes(q_ref[rows, :], head)
            scores = []
            peak = None
            for other in range(place + 1):
                keys = slice(other * block, (other + 1) * block)
                part = dot_nt(k_ref[keys, :], query) + bias[keys, rows]
                top = jnp.max(part, axis=0, keepdims=True)
                peak = top if peak is None else jnp.maximum(peak, top)
                scores.append(part)
            total = None
            acc = None
            for other in range(place + 1):
                keys = slice(other * block, (other + 1) * block)
                weight = jnp.exp(scores[other] - peak)
                part_sum = jnp.sum(weight, axis=0, keepdims=True)
                total = part_sum if total is None else total + part_sum
                part_out = dot_nn(
                    v_t[head * HEAD_DIM : (head + 1) * HEAD_DIM, keys], weight.astype(BF16)
                )
                acc = part_out if acc is None else acc + part_out
            outs.append(acc / total)
            lse_ref[0, head : head + 1, rows] = peak + jnp.log(total)
        mixed_ref[rows, :] = jnp.concatenate(outs, axis=0).T.astype(BF16)


def attn_backward_kernel(
    seg_col, seg_row, q_ref, k_ref, v_ref, mixed_ref, lse_ref, g_ref, grads_ref, bias, k_t, delta, dq_t, block
):
    length = q_ref.shape[0]
    heads = LANES // HEAD_DIM
    count = length // block

    @pl.when(pl.program_id(0) == 0)
    def _():
        fill_bias(bias, seg_col, seg_row)

    k_t[...] = k_ref[...].T
    product = (g_ref[...].astype(F32) * mixed_ref[...].astype(F32)).T
    for head in range(heads):
        delta[head : head + 1, :] = jnp.sum(
            product[head * HEAD_DIM : (head + 1) * HEAD_DIM, :], axis=0, keepdims=True
        )
    for other in range(count):
        keys = slice(other * block, (other + 1) * block)
        key_sum = None
        value_sum = None
        for head in range(heads):
            lanes = slice(head * HEAD_DIM, (head + 1) * HEAD_DIM)
            for place in range(other, count):
                rows = slice(place * block, (place + 1) * block)
                query = head_lanes(q_ref[rows, :], head)
                grad = head_lanes(g_ref[rows, :], head)
                scores = dot_nt(k_ref[keys, :], query) + bias[keys, rows]
                probs = jnp.exp(scores - lse_ref[0, head : head + 1, rows])
                grad_probs = dot_nt(v_ref[keys, :], grad)
                grad_scores = (probs * (grad_probs - delta[head : head + 1, rows])).astype(BF16)
                value_part = dot_nn(probs.astype(BF16), grad)
                key_part = dot_nn(grad_scores, query)
                query_part = dot_nn(k_t[lanes, keys], grad_scores)
                value_sum = value_part if value_sum is None else value_sum + value_part
                key_sum = key_part if key_sum is None else key_sum + key_part
                if other == 0:
                    dq_t[lanes, rows] = query_part
                else:
                    dq_t[lanes, rows] += query_part
        grads_ref[1, keys, :] = key_sum.astype(BF16)
        grads_ref[2, keys, :] = value_sum.astype(BF16)
    grads_ref[0] = (dq_t[...].T * HEAD_DIM ** (-0.5)).astype(BF16)


def attn_forward(segments, qkv, width):
    length = qkv.shape[0]
    pairs = width // LANES
    block = min(256, length)
    column = lambda first: pl.BlockSpec((length, LANES), lambda p: (0, first * pairs + p))
    whole = lambda shape: pl.BlockSpec(shape, lambda p: (0, 0))
    return pl.pallas_call(
        functools.partial(attn_forward_kernel, block=block),
        grid=(pairs,),
        in_specs=[whole((length, 1)), whole((1, length)), column(0), column(1), column(2)],
        out_specs=[
            pl.BlockSpec((length, LANES), lambda p: (0, p)),
            pl.BlockSpec((1, 8, length), lambda p: (p, 0, 0)),
        ],
        out_shape=[
            jax.ShapeDtypeStruct((length, width), BF16),
            jax.ShapeDtypeStruct((pairs, 8, length), F32),
        ],
        scratch_shapes=[pltpu.VMEM((length, length), F32), pltpu.VMEM((LANES, length), BF16)],
        compiler_params=pltpu.CompilerParams(vmem_limit_bytes=VMEM_BYTES),
        cost_estimate=small_cost(
            flops=4 * length * length * width,
            bytes_accessed=8 * length * width,
            transcendentals=length * length * width // (2 * HEAD_DIM),
        ),
        name="attn_forward",
    )(segments.reshape(length, 1), segments.reshape(1, length), qkv, qkv, qkv)


def attn_backward(segments, qkv, mixed, lse, grad_mixed, width, after):
    length = qkv.shape[0]
    pairs = width // LANES
    block = min(256, length)
    column = lambda first: pl.BlockSpec((length, LANES), lambda p: (0, first * pairs + p))
    whole = lambda shape: pl.BlockSpec(shape, lambda p: (0, 0))
    return pl.pallas_call(
        without(functools.partial(attn_backward_kernel, block=block), 8),
        grid=(pairs,),
        in_specs=[
            whole((length, 1)),
            whole((1, length)),
            column(0),
            column(1),
            column(2),
            pl.BlockSpec((length, LANES), lambda p: (0, p)),
            pl.BlockSpec((1, 8, length), lambda p: (p, 0, 0)),
            pl.BlockSpec((length, LANES), lambda p: (0, p)),
            pl.BlockSpec(memory_space=pl.ANY),
        ],
        out_specs=pl.BlockSpec((3, length, LANES), lambda p: (0, 0, p)),
        out_shape=jax.ShapeDtypeStruct((3, length, width), BF16),
        scratch_shapes=[
            pltpu.VMEM((length, length), F32),
            pltpu.VMEM((LANES, length), BF16),
            pltpu.VMEM((8, length), F32),
            pltpu.VMEM((LANES, length), F32),
        ],
        compiler_params=pltpu.CompilerParams(vmem_limit_bytes=VMEM_BYTES),
        cost_estimate=small_cost(
            flops=10 * length * length * width,
            bytes_accessed=16 * length * width,
            transcendentals=length * length * width // (2 * HEAD_DIM),
        ),
        name="attn_backward",
    )(segments.reshape(length, 1), segments.reshape(1, length), qkv, qkv, qkv, mixed, lse, grad_mixed, after)


def piece_blocks(count):
    far = count // 4
    half = far // 2
    near, by_y, by_x, both = (list(range(i * far, (i + 1) * far)) for i in range(4))
    return [
        both[:half] + by_x[:half],
        both[half:] + by_y[half:],
        by_y[:half],
        by_x[half:],
        near,
    ]


def store_pieces(order, grad, piece_refs, columns):
    count = order.shape[0]
    rows = grad.shape[0] // count
    for blocks, ref in zip(piece_blocks(count), piece_refs):
        for place, block in enumerate(blocks):
            first = pl.multiple_of(order[block] * rows, rows)
            ref[place * rows : (place + 1) * rows, columns] = grad[pl.ds(first, rows), :]


def piece_shapes(count, rows, columns):
    return [
        jax.ShapeDtypeStruct((len(blocks) * rows, columns), BF16) for blocks in piece_blocks(count)
    ]


def whole_spec(shape, **options):
    return pl.BlockSpec(shape, lambda step: (0,) * len(shape), **options)


def norm_kernel(*refs, residual):
    if residual:
        x_ref, own_ref, other_ref, shift_ref, gain_ref, bias_ref, n_ref, nt_ref, hidden_ref = refs
        values = (
            x_ref[...].astype(F32)
            + (own_ref[...].astype(F32) + other_ref[...].astype(F32))
            + shift_ref[...]
        )
        hidden_ref[...] = values
    else:
        x_ref, gain_ref, bias_ref, n_ref, nt_ref = refs
        values = x_ref[...].astype(F32)
    scaled, _ = normalize(values)
    normed = (scaled * gain_ref[...] + bias_ref[...]).astype(BF16)
    n_ref[...] = normed
    nt_ref[...] = normed.T


def norm_rows(x, gain, bias, partials=None, shift=None):
    length, width = x.shape
    block = min(256, length)
    row = pl.BlockSpec((block, width), lambda step: (step, 0))
    vector = whole_spec((1, width))
    residual = partials is not None
    operands = [x] + (list(partials) + [shift.reshape(1, width)] if residual else [])
    operands += [gain.reshape(1, width), bias.reshape(1, width)]
    return pl.pallas_call(
        functools.partial(norm_kernel, residual=residual),
        grid=(length // block,),
        in_specs=[row] + ([row, row, vector] if residual else []) + [vector, vector],
        out_specs=[row, pl.BlockSpec((width, block), lambda step: (0, step))]
        + ([row] if residual else []),
        out_shape=[
            jax.ShapeDtypeStruct((length, width), BF16),
            jax.ShapeDtypeStruct((width, length), BF16),
        ]
        + ([jax.ShapeDtypeStruct((length, width), F32)] if residual else []),
        compiler_params=pltpu.CompilerParams(vmem_limit_bytes=VMEM_BYTES),
        cost_estimate=small_cost(
            flops=20 * length * width, bytes_accessed=14 * length * width, transcendentals=length
        ),
        name="norm_two" if residual else "norm_one",
    )(*operands)


def norm_back_kernel(hidden_ref, g_ref, own_ref, other_ref, gain_ref, grad_ref, low_ref, low_t_ref, sums_ref):
    scaled, inverse = normalize(hidden_ref[...])
    incoming = own_ref[...].astype(F32) + other_ref[...].astype(F32)
    grad = g_ref[...].astype(F32) + norm_back(incoming, scaled, inverse, gain_ref[...])
    grad_ref[...] = grad
    low_ref[...] = grad.astype(BF16)
    low_t_ref[...] = grad.astype(BF16).T

    @pl.when(pl.program_id(0) == 0)
    def _():
        sums_ref[...] = jnp.zeros_like(sums_ref)

    sums_ref[0:1, :] += jnp.sum(grad, axis=0, keepdims=True)
    sums_ref[1:2, :] += jnp.sum(incoming * scaled, axis=0, keepdims=True)
    sums_ref[2:3, :] += jnp.sum(incoming, axis=0, keepdims=True)


def norm_back_rows(hidden, grad, partials, gain):
    length, width = hidden.shape
    block = min(256, length)
    row = pl.BlockSpec((block, width), lambda step: (step, 0))
    return pl.pallas_call(
        norm_back_kernel,
        grid=(length // block,),
        in_specs=[row, row, row, row, whole_spec((1, width))],
        out_specs=[
            row,
            row,
            pl.BlockSpec((width, block), lambda step: (0, step)),
            whole_spec((8, width)),
        ],
        out_shape=[
            jax.ShapeDtypeStruct((length, width), F32),
            jax.ShapeDtypeStruct((length, width), BF16),
            jax.ShapeDtypeStruct((width, length), BF16),
            jax.ShapeDtypeStruct((8, width), F32),
        ],
        compiler_params=pltpu.CompilerParams(vmem_limit_bytes=VMEM_BYTES),
        cost_estimate=small_cost(
            flops=30 * length * width, bytes_accessed=16 * length * width, transcendentals=length
        ),
        name="norm_two_back",
    )(hidden, grad, *partials, gain.reshape(1, width))


def load_pieces(order, pieces, w_ref):
    rows = w_ref.shape[0] // order.shape[0]
    block = 0
    for ref in pieces:
        for place in range(ref.shape[0] // rows):
            first = pl.multiple_of(order[block] * rows, rows)
            w_ref[pl.ds(first, rows), :] = ref[place * rows : (place + 1) * rows, :]
            block += 1


def mlp_kernel(order, n_ref, g_ref, nt_ref, gt_ref, b_ref, *refs, block, with_previous, cube, in_pieces):
    if in_pieces:
        pieces, refs = refs[:5], refs[5:]
        w_ref, refs = refs[-1], refs[:-1]
        load_pieces(order, pieces, w_ref)
    else:
        w_ref, refs = refs[0], refs[1:]
    if with_previous:
        (before_out, before_gn), refs = refs[:2], refs[2:]
    count = 5 if cube else 1
    (out_ref, gn_ref), grad_refs, refs = refs[:2], refs[2 : 2 + count], refs[2 + count :]
    gb_ref, out_acc, gn_acc, act, gpre, grad_up, grad_down = refs
    step = pl.program_id(0)
    length = n_ref.shape[0]
    tile = w_ref.shape[1] // 2
    ups, downs = slice(0, tile), slice(tile, 2 * tile)

    @pl.when(step == 0)
    def _():
        if with_previous:
            out_acc[...] = before_out[...].astype(F32)
            gn_acc[...] = before_gn[...].astype(F32)
        else:
            out_acc[...] = jnp.zeros_like(out_acc)
            gn_acc[...] = jnp.zeros_like(gn_acc)

    bias_sum = jnp.zeros(gb_ref.shape, F32)
    for first in range(0, length, block):
        rows = slice(first, first + block)
        unit = dot_nn(n_ref[rows, :], w_ref[:, ups]) + b_ref[...]
        grad = dot_nn(g_ref[rows, :], w_ref[:, downs])
        square = unit * unit
        curve = jnp.tanh(0.7978845608028654 * (unit + 0.044715 * (square * unit)))
        half = 0.5 + 0.5 * curve
        slope = half + (0.5 * unit) * (1.0 - curve * curve) * (
            0.7978845608028654 + (3 * 0.044715 * 0.7978845608028654) * square
        )
        active = (unit * half).astype(BF16)
        grad_pre = (grad * slope).astype(BF16)
        act[rows, :] = active
        gpre[rows, :] = grad_pre
        bias_sum = bias_sum + jnp.sum(grad_pre.astype(F32), axis=0, keepdims=True)
        out_acc[rows, :] += dot_nt(active, w_ref[:, downs])
        gn_acc[rows, :] += dot_nt(grad_pre, w_ref[:, ups])
    gb_ref[...] = bias_sum
    if cube:
        grad_up[...] = dot_nn(nt_ref[...], gpre[...]).astype(BF16)
        grad_down[...] = dot_nn(gt_ref[...], act[...]).astype(BF16)
        store_pieces(order, grad_up, grad_refs, ups)
        store_pieces(order, grad_down, grad_refs, downs)
    else:
        grad_refs[0][:, ups] = dot_nn(nt_ref[...], gpre[...]).astype(BF16)
        grad_refs[0][:, downs] = dot_nn(gt_ref[...], act[...]).astype(BF16)

    @pl.when(step == pl.num_programs(0) - 1)
    def _():
        out_ref[...] = out_acc[...].astype(BF16)
        gn_ref[...] = gn_acc[...].astype(BF16)


def mlp(order, normed, grad, normed_t, grad_t, weights, bias, previous, cube):
    length, width = normed.shape
    units = weights[0].shape[1] // 2
    in_pieces = len(weights) > 1
    tile = min(TILE, units)
    once = pl.Buffered(1)
    fixed = lambda shape, **options: pl.BlockSpec(shape, lambda u, o: (0, 0), **options)
    at_tile = lambda rows, columns: pl.BlockSpec((rows, columns), lambda u, o: (0, u))
    count, rows = order.shape[0], width // order.shape[0]
    if cube:
        grad_shapes = piece_shapes(count, rows, 2 * units)
    else:
        grad_shapes = [jax.ShapeDtypeStruct((width, 2 * units), BF16)]
    results = pl.pallas_call(
        functools.partial(
            mlp_kernel, block=min(256, length), with_previous=bool(previous), cube=cube,
            in_pieces=in_pieces,
        ),
        grid_spec=pltpu.PrefetchScalarGridSpec(
            num_scalar_prefetch=1,
            grid=(units // tile,),
            in_specs=[
                fixed((length, width), pipeline_mode=once),
                fixed((length, width), pipeline_mode=once),
                fixed((width, length), pipeline_mode=once),
                fixed((width, length), pipeline_mode=once),
                at_tile(1, tile),
            ]
            + [at_tile(piece.shape[0], 2 * tile) for piece in weights]
            + [fixed((length, width), pipeline_mode=once) for _ in previous],
            out_specs=[fixed((length, width)), fixed((length, width))]
            + [at_tile(shape.shape[0], 2 * tile) for shape in grad_shapes]
            + [at_tile(1, tile)],
            scratch_shapes=[
                pltpu.VMEM((length, width), F32),
                pltpu.VMEM((length, width), F32),
                pltpu.VMEM((length, tile), BF16),
                pltpu.VMEM((length, tile), BF16),
                pltpu.VMEM((width, tile), BF16),
                pltpu.VMEM((width, tile), BF16),
            ]
            + ([pltpu.VMEM((width, 2 * tile), BF16)] if in_pieces else []),
        ),
        out_shape=[jax.ShapeDtypeStruct((length, width), BF16)] * 2
        + grad_shapes
        + [jax.ShapeDtypeStruct((1, units), F32)],
        compiler_params=pltpu.CompilerParams(vmem_limit_bytes=VMEM_BYTES),
        cost_estimate=small_cost(
            flops=12 * length * width * units,
            bytes_accessed=12 * length * width + 8 * width * units,
            transcendentals=length * units,
        ),
        name="mlp_second" if previous else "mlp_first",
    )(order, normed, grad, normed_t, grad_t, bias.reshape(1, units), *weights, *previous)
    return results[0], results[1], results[2:-1], results[-1]


def qkv_kernel(order, n_ref, b_ref, near, by_y, by_x, low, high, out_ref, w_ref):
    load_pieces(order, (near, by_y, by_x, low, high), w_ref)
    part = pl.program_id(0)

    @pl.when(part < 3)
    def _():
        scale = jnp.where(part == 0, HEAD_DIM ** (-0.5), 1.0)
        length = n_ref.shape[0]
        step = min(256, length)
        for first in range(0, length, step):
            span = slice(first, first + step)
            out_ref[span, :] = (
                (dot_nn(n_ref[span, :], w_ref[...]) + b_ref[...]) * scale
            ).astype(BF16)


def qkv_project(order, normed, pieces, bias):
    length, width = normed.shape
    columns = pieces[0].shape[1] // 4
    at_tile = lambda rows: pl.BlockSpec((rows, columns), lambda k, o: (0, k))
    first_three = lambda rows: pl.BlockSpec((rows, columns), lambda k, o: (0, jnp.minimum(k, 2)))
    return pl.pallas_call(
        qkv_kernel,
        grid_spec=pltpu.PrefetchScalarGridSpec(
            num_scalar_prefetch=1,
            grid=(4,),
            in_specs=[
                pl.BlockSpec((length, width), lambda k, o: (0, 0), pipeline_mode=pl.Buffered(1)),
                first_three(1),
            ]
            + [at_tile(piece.shape[0]) for piece in pieces],
            out_specs=[first_three(length), at_tile(width)],
        ),
        out_shape=[
            jax.ShapeDtypeStruct((length, 3 * columns), BF16),
            jax.ShapeDtypeStruct((width, 4 * columns), BF16),
        ],
        compiler_params=pltpu.CompilerParams(vmem_limit_bytes=VMEM_BYTES),
        cost_estimate=small_cost(
            flops=6 * length * width * columns,
            bytes_accessed=2 * length * width + 16 * width * columns + 6 * length * columns,
            transcendentals=0,
        ),
        name="qkv_project",
    )(order, normed, bias.reshape(1, 3 * columns), *pieces)


def weight_kernel(order, nt_ref, grads_ref, *refs):
    piece_refs, grad = refs[:5], refs[5]
    grad[...] = dot_nn(nt_ref[...], grads_ref[0]).astype(BF16)
    store_pieces(order, grad, piece_refs, slice(None))


def without(kernel, place):
    return lambda *refs: kernel(*refs[:place], *refs[place + 1 :])


ORDER_ONLY = pl.BlockSpec(memory_space=pl.ANY)


def weight_grads(order, normed_t, grads, after):
    width, length = normed_t.shape
    columns = grads.shape[2]
    tile = min(TILE, columns)
    tiles = columns // tile
    parts = grads.shape[0]
    shapes = piece_shapes(order.shape[0], width // order.shape[0], parts * columns)
    return pl.pallas_call(
        without(weight_kernel, 3),
        grid_spec=pltpu.PrefetchScalarGridSpec(
            num_scalar_prefetch=1,
            grid=(parts, tiles),
            in_specs=[
                pl.BlockSpec((width, length), lambda k, u, o: (0, 0), pipeline_mode=pl.Buffered(1)),
                pl.BlockSpec((1, length, tile), lambda k, u, o: (k, 0, u)),
                ORDER_ONLY,
            ],
            out_specs=[
                pl.BlockSpec((shape.shape[0], tile), lambda k, u, o: (0, k * tiles + u))
                for shape in shapes
            ],
            scratch_shapes=[pltpu.VMEM((width, tile), BF16)],
        ),
        out_shape=shapes,
        compiler_params=pltpu.CompilerParams(vmem_limit_bytes=VMEM_BYTES),
        cost_estimate=small_cost(
            flops=2 * parts * length * width * columns,
            bytes_accessed=2 * length * width + 4 * parts * width * columns,
            transcendentals=0,
        ),
        name="weight_grads",
    )(order, normed_t, grads, after)


def qkv_back_kernel(grads_ref, w_ref, out_ref):
    columns = grads_ref.shape[2]
    total = None
    for k in range(3):
        part = dot_nt(grads_ref[k], w_ref[:, k * columns : (k + 1) * columns])
        total = part if total is None else total + part
    out_ref[...] = total.astype(BF16)


def qkv_back(grads, weights, after):
    _, length, columns = grads.shape
    width = weights.shape[0]
    block = min(256, length)
    return pl.pallas_call(
        without(qkv_back_kernel, 2),
        grid=(length // block,),
        in_specs=[
            pl.BlockSpec((3, block, columns), lambda i: (0, i, 0)),
            pl.BlockSpec((width, 4 * columns), lambda i: (0, 0), pipeline_mode=pl.Buffered(1)),
            ORDER_ONLY,
        ],
        out_specs=pl.BlockSpec((block, width), lambda i: (i, 0)),
        out_shape=jax.ShapeDtypeStruct((length, width), BF16),
        compiler_params=pltpu.CompilerParams(vmem_limit_bytes=VMEM_BYTES),
        cost_estimate=small_cost(
            flops=6 * length * width * columns,
            bytes_accessed=2 * length * width + 6 * width * columns + 6 * length * columns,
            transcendentals=0,
        ),
        name="qkv_back",
    )(grads, weights, after)


def added(*terms):
    total = terms[0].astype(F32)
    for term in terms[1:]:
        total = total + term.astype(F32)
    return total.astype(BF16)


def first_sums_kernel(*refs, spans):
    refs, (y_ref, x_ref) = refs[:-2], refs[-2:]
    half = y_ref.shape[0]
    for index, columns in enumerate(spans):
        from_x, from_y, keep_y, keep_x = (ref[...] for ref in refs[4 * index : 4 * index + 4])
        y_ref[:, columns] = added(keep_y, from_x[:half])
        x_ref[:, columns] = added(keep_x, from_y[:half])


def second_sums_kernel(*refs, spans, far):
    outs, refs = refs[-far:], refs[:-far]
    (from_y2, from_x2), refs = refs[-2:], refs[:-2]
    half = from_y2.shape[0]
    rows = half * 2 // far
    for index, columns in enumerate(spans):
        from_x, from_y, near = refs[3 * index : 3 * index + 3]
        for i in range(far):
            first, second, place = (from_x, from_y2, i) if i < far // 2 else (from_y, from_x2, i - far // 2)
            span = slice(place * rows, (place + 1) * rows)
            outs[i][:, columns] = added(
                near[i * rows : (i + 1) * rows, :],
                first[half + place * rows : half + (place + 1) * rows, :],
                second[span, columns],
            )


def last_sums_kernel(*refs, far, half_tile):
    parts, other, (up_ref, down_ref) = refs[:far], refs[far], refs[far + 1 :]
    total = parts[0][...].astype(F32)
    for part in parts[1:]:
        total = total + part[...].astype(F32)
    units = up_ref.shape[1] // 2
    for first in range(0, units, half_tile):
        here, there = slice(first, first + half_tile), slice(units + first, units + first + half_tile)
        up, down = slice(2 * first, 2 * first + half_tile), slice(2 * first + half_tile, 2 * first + 2 * half_tile)
        up_ref[:, here] = total[:, up]
        down_ref[:, here] = total[:, down]
        up_ref[:, there] = other[:, up].astype(F32)
        down_ref[:, there] = other[:, down].astype(F32)


def qkv_last_kernel(*refs):
    parts, outs = refs[:-4], refs[-4:]
    total = parts[0][...].astype(F32)
    for part in parts[1:]:
        total = total + part[...].astype(F32)
    columns = outs[0].shape[1]
    for k, out in enumerate(outs):
        out[...] = total[:, k * columns : (k + 1) * columns]


def shards_kernel(w_up, w_down, first_ref, second_ref, *, tile):
    units = first_ref.shape[1] // 2
    for index, ref in enumerate((first_ref, second_ref)):
        for first in range(0, units, tile):
            columns = slice(index * units + first, index * units + first + tile)
            ref[:, 2 * first : 2 * first + tile] = w_up[:, columns]
            ref[:, 2 * first + tile : 2 * first + 2 * tile] = w_down[:, columns]


def concat_kernel(*refs):
    parts, target = refs[:-1], refs[-1]
    rows = parts[0].shape[0]
    for i, part in enumerate(parts):
        target[i * rows : (i + 1) * rows, :] = part[...]


def copy_kernel(source, target):
    target[...] = source[...]


def column_spans(widths):
    spans, first = [], 0
    for width in widths:
        spans.append(slice(first, first + width))
        first += width
    return spans


def sums_call(kernel, operands, shapes, after, name):
    body = kernel if after is None else without(kernel, 0)
    vmem = pl.BlockSpec(memory_space=pltpu.VMEM)
    return pl.pallas_call(
        body,
        in_specs=([pl.BlockSpec(memory_space=pl.ANY)] if after is not None else [])
        + [vmem] * len(operands),
        out_specs=[vmem] * len(shapes),
        out_shape=shapes,
        compiler_params=pltpu.CompilerParams(vmem_limit_bytes=VMEM_BYTES),
        name=name,
    )(*([after] if after is not None else []), *operands)


def flipped(sizes):
    return 1 if sizes["h"] * sizes["l"] == 2 else 0


def moves(sizes):
    groups, ranks, inner = sizes["a"], sizes["h"] * sizes["l"], sizes["l"]
    far = groups // 2
    flip = flipped(sizes)
    swap_to = {}
    for group in range(2):
        for part in range(ranks):
            place = (part % 2 ^ flip) * ranks + group * (ranks // 2) + part // 2
            swap_to[group * ranks + part] = place

    def swap(values, inverse=False):
        pairs = [(to, frm) if inverse else (frm, to) for frm, to in swap_to.items()]
        return lax.ppermute(values, SWAP, pairs)

    def swap_hop(values, a_mask, inverse=False):
        pairs = []
        for a in range(groups):
            for frm, to in swap_to.items():
                one, two = a * 2 * ranks + frm, (a ^ a_mask) * 2 * ranks + to
                pairs.append((two, one) if inverse else (one, two))
        return lax.ppermute(values, ALL, pairs)

    def hop(values, a_mask, h_mask):
        pairs = []
        for a in range(groups):
            for c in range(2):
                for h in range(2):
                    pairs.append(((a * 2 + c) * 2 + h, ((a ^ a_mask) * 2 + c) * 2 + (h ^ h_mask)))
        return lax.ppermute(values, ("a", "c", "h"), pairs)

    def gather(shard, after):
        parts = [swap_hop(shard, 2 * i) for i in range(far)]
        (near,) = sums_call(
            concat_kernel,
            parts,
            [jax.ShapeDtypeStruct((far * shard.shape[0], shard.shape[1]), BF16)],
            after,
            "near_rows",
        )
        half = near.shape[0] // 2
        by_y = hop(near, 1, 0)
        by_x = hop(near, 0, 1)
        return [near, by_y, by_x, hop(by_y[:half], 0, 1), hop(by_x[half:], 1, 0)]

    def first_sends(pieces):
        return hop(pieces[0], 0, 1), hop(pieces[1], 1, 0)

    def finish(chunks, received, after, after_two, name):
        spans = column_spans([pieces[0].shape[1] for pieces in chunks])
        total = spans[-1].stop
        half, rows = chunks[0][2].shape[0], chunks[0][4].shape[0] // far
        operands = []
        for pieces, (from_x, from_y) in zip(chunks, received):
            operands += [from_x, from_y, pieces[2], pieces[3]]
        y_sum, x_sum = sums_call(
            functools.partial(first_sums_kernel, spans=spans),
            operands,
            [jax.ShapeDtypeStruct((half, total), BF16)] * 2,
            after,
            name + "_sums_one",
        )
        from_y2, from_x2 = hop(y_sum, 1, 0), hop(x_sum, 0, 1)
        operands = []
        for pieces, (from_x, from_y) in zip(chunks, received):
            operands += [from_x, from_y, pieces[4]]
        sums = sums_call(
            functools.partial(second_sums_kernel, spans=spans, far=far),
            operands + [from_y2, from_x2],
            [jax.ShapeDtypeStruct((rows, total), BF16)] * far,
            after_two,
            name + "_sums_two",
        )
        return sums[0], [swap_hop(sums[i], 2 * i, inverse=True) for i in range(far)]

    def sum_all(values):
        values = values + lax.ppermute(values, "c", [(0, 1), (1, 0)])
        values = values + hop(values, 0, 1)
        for mask in range(groups.bit_length() - 1):
            values = values + hop(values, 1 << mask, 0)
        return lax.psum(values, "l") if inner > 1 else values

    a, h = lax.axis_index("a"), lax.axis_index("h")
    order = []
    for a_low, h_mask in ((0, 0), (1, 0), (0, 1), (1, 1)):
        for i in range(far):
            order.append((a ^ (2 * i + a_low)) * 2 + (h ^ h_mask))
    return swap, gather, first_sends, finish, sum_all, jnp.stack(order).astype(jnp.int32)


def per_device(sizes, *arguments):
    (
        block_input, segment_ids, ln1_gain, ln1_bias, w_query, w_key, w_value, b_query, b_value,
        w_out, b_out, ln2_gain, ln2_bias, w_up, b_up, w_down, b_down, out_grad,
    ) = arguments
    ranks = sizes["h"] * sizes["l"]
    rank = lax.axis_index("l") * 2 + (lax.axis_index("c") ^ flipped(sizes))
    own_rows, width = block_input.shape
    head_width = w_query.shape[1]
    unit_width = w_up.shape[1]
    half_units = unit_width // 2
    tile = min(TILE, half_units)
    swap, gather, first_sends, finish, sum_all, order = moves(sizes)

    def partner(values):
        return lax.ppermute(values, "c", [(0, 1), (1, 0)])

    def tp_gather(values):
        if ranks != 2:
            return lax.all_gather(values, TP, axis=0, tiled=True)
        theirs = partner(values)
        return jnp.where(
            rank == 0,
            jnp.concatenate([values, theirs], axis=0),
            jnp.concatenate([theirs, values], axis=0),
        )

    def tp_terms(values):
        if ranks != 2:
            others = lax.psum(values.astype(F32), TP) - values.astype(F32)
            return values, others.astype(BF16)
        return values, partner(values)

    def own(values):
        return lax.dynamic_slice_in_dim(values, rank * own_rows, own_rows)

    def tp_scatter(values):
        if ranks != 2:
            return lax.psum_scatter(values, TP, scatter_dimension=0, tiled=True).astype(F32)
        theirs = lax.dynamic_slice_in_dim(values, (1 - rank) * own_rows, own_rows)
        return own(values).astype(F32) + partner(theirs).astype(F32)

    own_input = swap(block_input)
    segments = swap(segment_ids)
    shard_first, shard_second = sums_call(
        functools.partial(shards_kernel, tile=tile),
        [w_up, w_down],
        [jax.ShapeDtypeStruct(w_up.shape, BF16)] * 2,
        None,
        "mlp_shards",
    )
    full_first = lax.all_gather(swap(shard_first), ("a", "h"), axis=0, tiled=True)
    full_second = lax.all_gather(swap(shard_second), ("a", "h"), axis=0, tiled=True)
    pieces_attn = gather(jnp.concatenate([w_query, w_key, w_value, w_out], axis=1), own_input)
    own_grad = swap(out_grad)
    bias_query = lax.dynamic_slice_in_dim(b_query, rank * head_width, head_width)
    bias_value = lax.dynamic_slice_in_dim(b_value, rank * head_width, head_width)
    bias_up = lax.dynamic_slice_in_dim(b_up, rank * unit_width, unit_width)

    rows_in = tp_gather(own_input)
    grad_rows = tp_gather(own_grad)
    grad_rows_t = grad_rows.T
    normed, normed_t = norm_rows(rows_in, ln1_gain, ln1_bias)
    biases = jnp.concatenate([bias_query, jnp.zeros((head_width,), F32), bias_value])
    qkv, full_attn = qkv_project(order, normed, pieces_attn, biases)
    full_out = full_attn[:, 3 * head_width :]
    mixed, lse = attn_forward(segments, qkv, head_width)
    attended = tp_terms(dot_nt(mixed, full_out).astype(BF16))
    normed_two, normed_two_t, hidden = norm_rows(rows_in, ln2_gain, ln2_bias, attended, b_out)

    out_part, gn_part, first_grads, bias_first = mlp(
        order, normed_two, grad_rows, normed_two_t, grad_rows_t, [full_first],
        bias_up[:half_units], (), True,
    )
    first_received = first_sends(first_grads)
    out_part, gn_part, second_grads, bias_second = mlp(
        order, normed_two, grad_rows, normed_two_t, grad_rows_t, [full_second],
        bias_up[half_units:], (out_part, gn_part), False,
    )
    second_grads = swap(second_grads[0], inverse=True)
    own_output = (own(hidden) + tp_scatter(out_part) + b_down).astype(BF16)
    output = swap(own_output, inverse=True)

    grad_hidden, grad_attended, grad_attended_t, sums_two = norm_back_rows(
        hidden, grad_rows, tp_terms(gn_part), ln2_gain
    )
    grad_mixed = dot_nn(grad_attended, full_out).astype(BF16)
    out_grads = weight_grads(order, grad_attended_t, mixed[None], grad_mixed)
    out_received = first_sends(out_grads)
    unit_done, unit_parts = finish([first_grads], [first_received], gn_part, out_grads[0], "unit")

    grads = attn_backward(segments, qkv, mixed, lse, grad_mixed, head_width, unit_done)
    second_grads, grads = lax.optimization_barrier((second_grads, grads))
    second_mlp = lax.psum_scatter(second_grads, ("a", "c"), scatter_dimension=0, tiled=True)
    qkv_grads = weight_grads(order, normed_t, grads, grads)
    grad_normed_part = qkv_back(grads, full_attn, qkv_grads[0])
    qkv_done, qkv_parts = finish(
        [qkv_grads, out_grads], [first_sends(qkv_grads), out_received], grad_normed_part, None, "qkv"
    )
    shard = lambda columns: jax.ShapeDtypeStruct((w_query.shape[0], columns), F32)
    grad_w_up, grad_w_down = sums_call(
        functools.partial(last_sums_kernel, far=len(unit_parts), half_tile=tile),
        unit_parts + [second_mlp],
        [shard(unit_width), shard(unit_width)],
        None,
        "unit_sums_last",
    )
    late = sums_call(qkv_last_kernel, qkv_parts, [shard(head_width)] * 4, None, "qkv_sums_last")
    grad_normed = tp_scatter(grad_normed_part)
    own_scaled, own_inverse = normalize(own_input.astype(F32))
    grad_own = own(grad_hidden) + norm_back(grad_normed, own_scaled, own_inverse, ln1_gain)
    grad_input = swap(grad_own.astype(BF16), inverse=True)

    def place_part(values, full):
        return lax.dynamic_update_slice_in_dim(
            jnp.zeros((full,), F32), values, rank * values.shape[0], 0
        )

    sums = jnp.concatenate(
        [
            jnp.sum(grad_normed * own_scaled, axis=0),
            jnp.sum(grad_normed, axis=0),
            place_part(jnp.sum(grads[0].astype(F32), axis=0), width),
            place_part(jnp.sum(grads[2].astype(F32), axis=0), width),
            (sums_two[:3] * (1.0 / ranks)).reshape(-1),
            jnp.sum(own_grad.astype(F32), axis=0),
            place_part(jnp.concatenate([bias_first[0], bias_second[0]]), b_up.shape[0]),
        ]
    ).reshape(-1, LANES)
    (sums,) = sums_call(
        copy_kernel, [sums], [jax.ShapeDtypeStruct(sums.shape, F32)], qkv_done, "small_sums"
    )
    sums = sum_all(sums).reshape(-1)
    small = [sums[i * width : (i + 1) * width] for i in range(8)]
    return (
        output, grad_input, small[0], small[1],
        late[0], late[1], late[2], small[2], small[3], late[3], small[4], small[5], small[6],
        grad_w_up, sums[8 * width :], grad_w_down, small[7],
    )


def solution(mesh):
    groups, ranks = mesh.shape["dp"], mesh.shape["tensor"]
    sizes = {"a": groups // 2, "c": 2, "h": 2, "l": ranks // 2}
    fine = Mesh(mesh.devices.reshape(tuple(sizes.values())), tuple(sizes))
    rows = P(("a", "c", "h", "l"), None)
    block = P(("a", "c"), ("h", "l"))
    return jax.shard_map(
        functools.partial(per_device, sizes),
        mesh=fine,
        in_specs=(
            rows, P(("a", "c")), P(), P(), block, block, block, P(), P(), block, P(), P(), P(),
            block, P(), block, P(), rows,
        ),
        out_specs=(
            rows, rows, P(), P(), block, block, block, P(), P(), block, P(), P(), P(), block, P(),
            block, P(),
        ),
        check_vma=False,
    )
```

```python
import functools

import jax
import jax.numpy as jnp
from jax import lax
from jax.experimental import pallas as pl
from jax.experimental.pallas import tpu as pltpu
from jax.sharding import Mesh
from jax.sharding import PartitionSpec as P

HEAD_DIM = 64
LANES = 128
TILE = 512
MASKED = -1e30
VMEM_BYTES = 60 * 1024 * 1024
F32 = jnp.float32
BF16 = jnp.bfloat16
TP = ("l", "c")
SWAP = ("c", "h", "l")
ALL = ("a", "c", "h", "l")


def normalize(values):
    center = values - jnp.mean(values, axis=-1, keepdims=True)
    spread = jnp.mean(center * center, axis=-1, keepdims=True)
    inverse = lax.rsqrt(spread + 1e-05)
    return center * inverse, inverse


def norm_back(grad_in, scaled, inverse, gain_vec):
    local_grad = grad_in * gain_vec
    return inverse * (
        local_grad
        - jnp.mean(local_grad, axis=-1, keepdims=True)
        - scaled * jnp.mean(local_grad * scaled, axis=-1, keepdims=True)
    )


def dot_nn(left, right):
    return lax.dot_general(left, right, (((1,), (0,)), ((), ())), preferred_element_type=F32)


def dot_nt(left, right):
    return lax.dot_general(left, right, (((1,), (1,)), ((), ())), preferred_element_type=F32)


def dot_tn(left, right):
    return lax.dot_general(left, right, (((0,), (0,)), ((), ())), preferred_element_type=F32)


def fill_bias(bias, seg_col, seg_row):
    length = bias.shape[0]
    block = min(256, length)
    for first in range(0, length, block):
        keys = lax.broadcasted_iota(jnp.int32, (block, length), 0) + first
        places = lax.broadcasted_iota(jnp.int32, (block, length), 1)
        same = seg_col[first : first + block, :] == seg_row[...]
        bias[first : first + block, :] = jnp.where(same & (keys <= places), 0.0, MASKED)


def head_lanes(values, head):
    lane = lax.broadcasted_iota(jnp.int32, values.shape, 1)
    inside = (lane >= head * HEAD_DIM) & (lane < (head + 1) * HEAD_DIM)
    return jnp.where(inside, values, jnp.zeros_like(values))


def attn_forward_kernel(seg_col, seg_row, q_ref, k_ref, v_ref, mixed_ref, lse_ref, bias, v_t, block):
    length = q_ref.shape[0]
    heads = LANES // HEAD_DIM

    @pl.when(pl.program_id(0) == 0)
    def _():
        fill_bias(bias, seg_col, seg_row)

    v_t[...] = v_ref[...].T
    for place in range(length // block):
        rows = slice(place * block, (place + 1) * block)
        outs = []
        for head in range(heads):
            query = head_lanes(q_ref[rows, :], head)
            scores = []
            peak = None
            for other in range(place + 1):
                keys = slice(other * block, (other + 1) * block)
                part = dot_nt(k_ref[keys, :], query) + bias[keys, rows]
                top = jnp.max(part, axis=0, keepdims=True)
                peak = top if peak is None else jnp.maximum(peak, top)
                scores.append(part)
            total = None
            acc = None
            for other in range(place + 1):
                keys = slice(other * block, (other + 1) * block)
                weight = jnp.exp(scores[other] - peak)
                part_sum = jnp.sum(weight, axis=0, keepdims=True)
                total = part_sum if total is None else total + part_sum
                part_out = dot_nn(
                    v_t[head * HEAD_DIM : (head + 1) * HEAD_DIM, keys], weight.astype(BF16)
                )
                acc = part_out if acc is None else acc + part_out
            outs.append(acc / total)
            lse_ref[0, head : head + 1, rows] = peak + jnp.log(total)
        mixed_ref[rows, :] = jnp.concatenate(outs, axis=0).T.astype(BF16)


def attn_backward_kernel(
    seg_col, seg_row, q_ref, k_ref, v_ref, mixed_ref, lse_ref, g_ref, grads_ref, bias, k_t, delta, dq_t, block
):
    length = q_ref.shape[0]
    heads = LANES // HEAD_DIM
    count = length // block

    @pl.when(pl.program_id(0) == 0)
    def _():
        fill_bias(bias, seg_col, seg_row)

    k_t[...] = k_ref[...].T
    product = (g_ref[...].astype(F32) * mixed_ref[...].astype(F32)).T
    for head in range(heads):
        delta[head : head + 1, :] = jnp.sum(
            product[head * HEAD_DIM : (head + 1) * HEAD_DIM, :], axis=0, keepdims=True
        )
    for other in range(count):
        keys = slice(other * block, (other + 1) * block)
        key_sum = None
        value_sum = None
        for head in range(heads):
            lanes = slice(head * HEAD_DIM, (head + 1) * HEAD_DIM)
            for place in range(other, count):
                rows = slice(place * block, (place + 1) * block)
                query = head_lanes(q_ref[rows, :], head)
                grad = head_lanes(g_ref[rows, :], head)
                scores = dot_nt(k_ref[keys, :], query) + bias[keys, rows]
                probs = jnp.exp(scores - lse_ref[0, head : head + 1, rows])
                grad_probs = dot_nt(v_ref[keys, :], grad)
                grad_scores = (probs * (grad_probs - delta[head : head + 1, rows])).astype(BF16)
                value_part = dot_nn(probs.astype(BF16), grad)
                key_part = dot_nn(grad_scores, query)
                query_part = dot_nn(k_t[lanes, keys], grad_scores)
                value_sum = value_part if value_sum is None else value_sum + value_part
                key_sum = key_part if key_sum is None else key_sum + key_part
                if other == 0:
                    dq_t[lanes, rows] = query_part
                else:
                    dq_t[lanes, rows] += query_part
        grads_ref[1, keys, :] = key_sum.astype(BF16)
        grads_ref[2, keys, :] = value_sum.astype(BF16)
    grads_ref[0] = (dq_t[...].T * HEAD_DIM ** (-0.5)).astype(BF16)


def attn_forward(segments, qkv, width):
    length = qkv.shape[0]
    pairs = width // LANES
    block = min(256, length)
    column = lambda first: pl.BlockSpec((length, LANES), lambda p: (0, first * pairs + p))
    whole = lambda shape: pl.BlockSpec(shape, lambda p: (0, 0))
    return pl.pallas_call(
        functools.partial(attn_forward_kernel, block=block),
        grid=(pairs,),
        in_specs=[whole((length, 1)), whole((1, length)), column(0), column(1), column(2)],
        out_specs=[
            pl.BlockSpec((length, LANES), lambda p: (0, p)),
            pl.BlockSpec((1, 8, length), lambda p: (p, 0, 0)),
        ],
        out_shape=[
            jax.ShapeDtypeStruct((length, width), BF16),
            jax.ShapeDtypeStruct((pairs, 8, length), F32),
        ],
        scratch_shapes=[pltpu.VMEM((length, length), F32), pltpu.VMEM((LANES, length), BF16)],
        compiler_params=pltpu.CompilerParams(vmem_limit_bytes=VMEM_BYTES),
        cost_estimate=pl.CostEstimate(
            flops=4 * length * length * width,
            bytes_accessed=8 * length * width,
            transcendentals=length * length * width // (2 * HEAD_DIM),
        ),
        name="attn_forward",
    )(segments.reshape(length, 1), segments.reshape(1, length), qkv, qkv, qkv)


def attn_backward(segments, qkv, mixed, lse, grad_mixed, width, after):
    length = qkv.shape[0]
    pairs = width // LANES
    block = min(256, length)
    column = lambda first: pl.BlockSpec((length, LANES), lambda p: (0, first * pairs + p))
    whole = lambda shape: pl.BlockSpec(shape, lambda p: (0, 0))
    return pl.pallas_call(
        without(functools.partial(attn_backward_kernel, block=block), 8),
        grid=(pairs,),
        in_specs=[
            whole((length, 1)),
            whole((1, length)),
            column(0),
            column(1),
            column(2),
            pl.BlockSpec((length, LANES), lambda p: (0, p)),
            pl.BlockSpec((1, 8, length), lambda p: (p, 0, 0)),
            pl.BlockSpec((length, LANES), lambda p: (0, p)),
            pl.BlockSpec(memory_space=pl.ANY),
        ],
        out_specs=pl.BlockSpec((3, length, LANES), lambda p: (0, 0, p)),
        out_shape=jax.ShapeDtypeStruct((3, length, width), BF16),
        scratch_shapes=[
            pltpu.VMEM((length, length), F32),
            pltpu.VMEM((LANES, length), BF16),
            pltpu.VMEM((8, length), F32),
            pltpu.VMEM((LANES, length), F32),
        ],
        compiler_params=pltpu.CompilerParams(vmem_limit_bytes=VMEM_BYTES),
        cost_estimate=pl.CostEstimate(
            flops=10 * length * length * width,
            bytes_accessed=16 * length * width,
            transcendentals=length * length * width // (2 * HEAD_DIM),
        ),
        name="attn_backward",
    )(segments.reshape(length, 1), segments.reshape(1, length), qkv, qkv, qkv, mixed, lse, grad_mixed, after)


def piece_blocks(count):
    far = count // 4
    half = far // 2
    near, by_y, by_x, both = (list(range(i * far, (i + 1) * far)) for i in range(4))
    return [
        both[:half] + by_x[:half],
        both[half:] + by_y[half:],
        by_y[:half],
        by_x[half:],
        near,
    ]


def store_pieces(order, grad, piece_refs, columns):
    count = order.shape[0]
    rows = grad.shape[0] // count
    for blocks, ref in zip(piece_blocks(count), piece_refs):
        for place, block in enumerate(blocks):
            first = pl.multiple_of(order[block] * rows, rows)
            ref[place * rows : (place + 1) * rows, columns] = grad[pl.ds(first, rows), :]


def piece_shapes(count, rows, columns):
    return [
        jax.ShapeDtypeStruct((len(blocks) * rows, columns), BF16) for blocks in piece_blocks(count)
    ]


def whole_spec(shape, **options):
    return pl.BlockSpec(shape, lambda step: (0,) * len(shape), **options)


def norm_kernel(*refs, residual):
    if residual:
        x_ref, own_ref, other_ref, shift_ref, gain_ref, bias_ref, n_ref, nt_ref, hidden_ref = refs
        values = (
            x_ref[...].astype(F32)
            + (own_ref[...].astype(F32) + other_ref[...].astype(F32))
            + shift_ref[...]
        )
        hidden_ref[...] = values
    else:
        x_ref, gain_ref, bias_ref, n_ref, nt_ref = refs
        values = x_ref[...].astype(F32)
    scaled, _ = normalize(values)
    normed = (scaled * gain_ref[...] + bias_ref[...]).astype(BF16)
    n_ref[...] = normed
    nt_ref[...] = normed.T


def norm_rows(x, gain, bias, partials=None, shift=None):
    length, width = x.shape
    block = min(256, length)
    row = pl.BlockSpec((block, width), lambda step: (step, 0))
    vector = whole_spec((1, width))
    residual = partials is not None
    operands = [x] + (list(partials) + [shift.reshape(1, width)] if residual else [])
    operands += [gain.reshape(1, width), bias.reshape(1, width)]
    return pl.pallas_call(
        functools.partial(norm_kernel, residual=residual),
        grid=(length // block,),
        in_specs=[row] + ([row, row, vector] if residual else []) + [vector, vector],
        out_specs=[row, pl.BlockSpec((width, block), lambda step: (0, step))]
        + ([row] if residual else []),
        out_shape=[
            jax.ShapeDtypeStruct((length, width), BF16),
            jax.ShapeDtypeStruct((width, length), BF16),
        ]
        + ([jax.ShapeDtypeStruct((length, width), F32)] if residual else []),
        compiler_params=pltpu.CompilerParams(vmem_limit_bytes=VMEM_BYTES),
        cost_estimate=pl.CostEstimate(
            flops=20 * length * width, bytes_accessed=14 * length * width, transcendentals=length
        ),
        name="norm_two" if residual else "norm_one",
    )(*operands)


def norm_back_kernel(hidden_ref, g_ref, own_ref, other_ref, gain_ref, grad_ref, low_ref, low_t_ref, sums_ref):
    scaled, inverse = normalize(hidden_ref[...])
    incoming = own_ref[...].astype(F32) + other_ref[...].astype(F32)
    grad = g_ref[...].astype(F32) + norm_back(incoming, scaled, inverse, gain_ref[...])
    grad_ref[...] = grad
    low_ref[...] = grad.astype(BF16)
    low_t_ref[...] = grad.astype(BF16).T

    @pl.when(pl.program_id(0) == 0)
    def _():
        sums_ref[...] = jnp.zeros_like(sums_ref)

    sums_ref[0:1, :] += jnp.sum(grad, axis=0, keepdims=True)
    sums_ref[1:2, :] += jnp.sum(incoming * scaled, axis=0, keepdims=True)
    sums_ref[2:3, :] += jnp.sum(incoming, axis=0, keepdims=True)


def norm_back_rows(hidden, grad, partials, gain):
    length, width = hidden.shape
    block = min(256, length)
    row = pl.BlockSpec((block, width), lambda step: (step, 0))
    return pl.pallas_call(
        norm_back_kernel,
        grid=(length // block,),
        in_specs=[row, row, row, row, whole_spec((1, width))],
        out_specs=[
            row,
            row,
            pl.BlockSpec((width, block), lambda step: (0, step)),
            whole_spec((8, width)),
        ],
        out_shape=[
            jax.ShapeDtypeStruct((length, width), F32),
            jax.ShapeDtypeStruct((length, width), BF16),
            jax.ShapeDtypeStruct((width, length), BF16),
            jax.ShapeDtypeStruct((8, width), F32),
        ],
        compiler_params=pltpu.CompilerParams(vmem_limit_bytes=VMEM_BYTES),
        cost_estimate=pl.CostEstimate(
            flops=30 * length * width, bytes_accessed=16 * length * width, transcendentals=length
        ),
        name="norm_two_back",
    )(hidden, grad, *partials, gain.reshape(1, width))


def mlp_kernel(n_ref, g_ref, nt_ref, gt_ref, b_ref, w_ref, *refs, block, with_previous):
    if with_previous:
        (before_out, before_gn), refs = refs[:2], refs[2:]
    (out_ref, gn_ref, grad_ref), refs = refs[:3], refs[3:]
    gb_ref, out_acc, gn_acc, act, gpre = refs
    step = pl.program_id(0)
    length = n_ref.shape[0]
    tile = w_ref.shape[1] // 2
    ups, downs = slice(0, tile), slice(tile, 2 * tile)

    @pl.when(step == 0)
    def _():
        if with_previous:
            out_acc[...] = before_out[...].astype(F32)
            gn_acc[...] = before_gn[...].astype(F32)
        else:
            out_acc[...] = jnp.zeros_like(out_acc)
            gn_acc[...] = jnp.zeros_like(gn_acc)

    bias_sum = jnp.zeros(gb_ref.shape, F32)
    for first in range(0, length, block):
        rows = slice(first, first + block)
        unit = dot_nn(n_ref[rows, :], w_ref[:, ups]) + b_ref[...]
        grad = dot_nn(g_ref[rows, :], w_ref[:, downs])
        square = unit * unit
        curve = jnp.tanh(0.7978845608028654 * (unit + 0.044715 * (square * unit)))
        half = 0.5 + 0.5 * curve
        slope = half + (0.5 * unit) * (1.0 - curve * curve) * (
            0.7978845608028654 + (3 * 0.044715 * 0.7978845608028654) * square
        )
        active = (unit * half).astype(BF16)
        grad_pre = (grad * slope).astype(BF16)
        act[rows, :] = active
        gpre[rows, :] = grad_pre
        bias_sum = bias_sum + jnp.sum(grad_pre.astype(F32), axis=0, keepdims=True)
        out_acc[rows, :] += dot_nt(active, w_ref[:, downs])
        gn_acc[rows, :] += dot_nt(grad_pre, w_ref[:, ups])
    gb_ref[...] = bias_sum
    grad_ref[:, ups] = dot_nn(nt_ref[...], gpre[...]).astype(BF16)
    grad_ref[:, downs] = dot_nn(gt_ref[...], act[...]).astype(BF16)

    @pl.when(step == pl.num_programs(0) - 1)
    def _():
        out_ref[...] = out_acc[...].astype(BF16)
        gn_ref[...] = gn_acc[...].astype(BF16)


def mlp(normed, grad, normed_t, grad_t, weights, bias, previous):
    length, width = normed.shape
    units = weights.shape[1] // 2
    tile = min(TILE, units)
    once = pl.Buffered(1)
    at_tile = lambda rows, columns: pl.BlockSpec((rows, columns), lambda u: (0, u))
    return pl.pallas_call(
        functools.partial(mlp_kernel, block=min(256, length), with_previous=bool(previous)),
        grid=(units // tile,),
        in_specs=[
            whole_spec((length, width), pipeline_mode=once),
            whole_spec((length, width), pipeline_mode=once),
            whole_spec((width, length), pipeline_mode=once),
            whole_spec((width, length), pipeline_mode=once),
            at_tile(1, tile),
            at_tile(width, 2 * tile),
        ]
        + [whole_spec((length, width), pipeline_mode=once) for _ in previous],
        out_specs=[
            whole_spec((length, width)),
            whole_spec((length, width)),
            at_tile(width, 2 * tile),
            at_tile(1, tile),
        ],
        out_shape=[
            jax.ShapeDtypeStruct((length, width), BF16),
            jax.ShapeDtypeStruct((length, width), BF16),
            jax.ShapeDtypeStruct((width, 2 * units), BF16),
            jax.ShapeDtypeStruct((1, units), F32),
        ],
        scratch_shapes=[
            pltpu.VMEM((length, width), F32),
            pltpu.VMEM((length, width), F32),
            pltpu.VMEM((length, tile), BF16),
            pltpu.VMEM((length, tile), BF16),
        ],
        compiler_params=pltpu.CompilerParams(vmem_limit_bytes=VMEM_BYTES),
        cost_estimate=pl.CostEstimate(
            flops=12 * length * width * units,
            bytes_accessed=12 * length * width + 8 * width * units,
            transcendentals=length * units,
        ),
        name="mlp_second" if previous else "mlp_first",
    )(normed, grad, normed_t, grad_t, bias.reshape(1, units), weights, *previous)


def qkv_kernel(n_ref, b_ref, w_ref, out_ref):
    scale = jnp.where(pl.program_id(0) == 0, HEAD_DIM ** (-0.5), 1.0)
    length = n_ref.shape[0]
    step = min(256, length)
    for first in range(0, length, step):
        span = slice(first, first + step)
        out_ref[span, :] = ((dot_nn(n_ref[span, :], w_ref[...]) + b_ref[...]) * scale).astype(BF16)


def qkv_project(normed, weights, bias):
    length, width = normed.shape
    columns = weights.shape[1] // 4
    at_tile = lambda rows: pl.BlockSpec((rows, columns), lambda k: (0, k))
    return pl.pallas_call(
        qkv_kernel,
        grid=(3,),
        in_specs=[
            whole_spec((length, width), pipeline_mode=pl.Buffered(1)), at_tile(1), at_tile(width)
        ],
        out_specs=at_tile(length),
        out_shape=jax.ShapeDtypeStruct((length, 3 * columns), BF16),
        compiler_params=pltpu.CompilerParams(vmem_limit_bytes=VMEM_BYTES),
        cost_estimate=pl.CostEstimate(
            flops=6 * length * width * columns,
            bytes_accessed=2 * length * width + 6 * width * columns + 6 * length * columns,
            transcendentals=0,
        ),
        name="qkv_project",
    )(normed, bias.reshape(1, 3 * columns), weights)


def weight_kernel(order, nt_ref, grads_ref, gt_ref, mixed_ref, *refs):
    piece_refs, grad = refs[:5], refs[5]
    part = pl.program_id(0)

    @pl.when(part < 3)
    def _():
        grad[...] = dot_nn(nt_ref[...], grads_ref[0]).astype(BF16)

    @pl.when(part == 3)
    def _():
        grad[...] = dot_nn(gt_ref[...], mixed_ref[...]).astype(BF16)

    store_pieces(order, grad, piece_refs, slice(None))


def without(kernel, place):
    return lambda *refs: kernel(*refs[:place], *refs[place + 1 :])


ORDER_ONLY = pl.BlockSpec(memory_space=pl.ANY)


def weight_grads(order, normed_t, grads, grad_t, mixed):
    width, length = normed_t.shape
    columns = grads.shape[2]
    shapes = piece_shapes(order.shape[0], width // order.shape[0], 4 * columns)
    fixed = lambda shape: pl.BlockSpec(shape, lambda k, o: (0, 0), pipeline_mode=pl.Buffered(1))
    return pl.pallas_call(
        weight_kernel,
        grid_spec=pltpu.PrefetchScalarGridSpec(
            num_scalar_prefetch=1,
            grid=(4,),
            in_specs=[
                fixed((width, length)),
                pl.BlockSpec((1, length, columns), lambda k, o: (jnp.minimum(k, 2), 0, 0)),
                fixed((width, length)),
                fixed((length, columns)),
            ],
            out_specs=[
                pl.BlockSpec((shape.shape[0], columns), lambda k, o: (0, k)) for shape in shapes
            ],
            scratch_shapes=[pltpu.VMEM((width, columns), BF16)],
        ),
        out_shape=shapes,
        compiler_params=pltpu.CompilerParams(vmem_limit_bytes=VMEM_BYTES),
        cost_estimate=pl.CostEstimate(
            flops=8 * length * width * columns,
            bytes_accessed=4 * length * width + 16 * width * columns,
            transcendentals=0,
        ),
        name="weight_grads",
    )(order, normed_t, grads, grad_t, mixed)


def qkv_back_kernel(grads_ref, w_ref, out_ref):
    columns = grads_ref.shape[2]
    total = None
    for k in range(3):
        part = dot_nt(grads_ref[k], w_ref[:, k * columns : (k + 1) * columns])
        total = part if total is None else total + part
    out_ref[...] = total.astype(BF16)


def qkv_back(grads, weights, after):
    _, length, columns = grads.shape
    width = weights.shape[0]
    block = min(256, length)
    return pl.pallas_call(
        without(qkv_back_kernel, 2),
        grid=(length // block,),
        in_specs=[
            pl.BlockSpec((3, block, columns), lambda i: (0, i, 0)),
            pl.BlockSpec((width, 4 * columns), lambda i: (0, 0), pipeline_mode=pl.Buffered(1)),
            ORDER_ONLY,
        ],
        out_specs=pl.BlockSpec((block, width), lambda i: (i, 0)),
        out_shape=jax.ShapeDtypeStruct((length, width), BF16),
        compiler_params=pltpu.CompilerParams(vmem_limit_bytes=VMEM_BYTES),
        cost_estimate=pl.CostEstimate(
            flops=6 * length * width * columns,
            bytes_accessed=2 * length * width + 6 * width * columns + 6 * length * columns,
            transcendentals=0,
        ),
        name="qkv_back",
    )(grads, weights, after)


def added(*terms):
    total = terms[0].astype(F32)
    for term in terms[1:]:
        total = total + term.astype(F32)
    return total.astype(BF16)


def first_sums_kernel(from_x, from_y, keep_y, keep_x, y_ref, x_ref):
    half = y_ref.shape[0]
    y_ref[...] = added(keep_y[...], from_x[:half, :])
    x_ref[...] = added(keep_x[...], from_y[:half, :])


def second_sums_kernel(from_x, from_y, near, from_y2, from_x2, small, *outs):
    far = len(outs)
    half = from_y2.shape[0]
    rows = half * 2 // far
    values = small[...]
    high = values.astype(BF16).astype(F32)
    extra = jnp.concatenate([high, values - high], axis=0).astype(BF16)
    for i, out in enumerate(outs):
        first, second, place = (from_x, from_y2, i) if i < far // 2 else (from_y, from_x2, i - far // 2)
        out[:rows, :] = added(
            near[i * rows : (i + 1) * rows, :],
            first[half + place * rows : half + (place + 1) * rows, :],
            second[place * rows : (place + 1) * rows, :],
        )
        out[rows:, :] = extra


def weights_last_kernel(*refs):
    parts, outs, small = refs[:-5], refs[-5:-1], refs[-1]
    total = parts[0][...].astype(F32)
    for part in parts[1:]:
        total = total + part[...].astype(F32)
    rows, columns = outs[0].shape
    for k, out in enumerate(outs):
        out[...] = total[:rows, k * columns : (k + 1) * columns]
    extra = small.shape[0]
    small[...] = total[rows : rows + extra, :] + total[rows + extra :, :]


def units_last_kernel(first_ref, second_ref, up_ref, down_ref, *, tile):
    units = up_ref.shape[1] // 2
    for index, ref in enumerate((first_ref, second_ref)):
        for first in range(0, units, tile):
            columns = slice(index * units + first, index * units + first + tile)
            up_ref[:, columns] = ref[:, 2 * first : 2 * first + tile].astype(F32)
            down_ref[:, columns] = ref[:, 2 * first + tile : 2 * first + 2 * tile].astype(F32)


def shards_kernel(w_up, w_down, first_ref, second_ref, *, tile):
    units = first_ref.shape[1] // 2
    for index, ref in enumerate((first_ref, second_ref)):
        for first in range(0, units, tile):
            columns = slice(index * units + first, index * units + first + tile)
            ref[:, 2 * first : 2 * first + tile] = w_up[:, columns]
            ref[:, 2 * first + tile : 2 * first + 2 * tile] = w_down[:, columns]


def sums_call(kernel, operands, shapes, after, name):
    body = kernel if after is None else without(kernel, 0)
    vmem = pl.BlockSpec(memory_space=pltpu.VMEM)
    return pl.pallas_call(
        body,
        in_specs=([pl.BlockSpec(memory_space=pl.ANY)] if after is not None else [])
        + [vmem] * len(operands),
        out_specs=[vmem] * len(shapes),
        out_shape=shapes,
        compiler_params=pltpu.CompilerParams(vmem_limit_bytes=VMEM_BYTES),
        cost_estimate=pl.CostEstimate(flops=0, bytes_accessed=32 * 1024 * 1024, transcendentals=0),
        name=name,
    )(*([after] if after is not None else []), *operands)


def flipped(sizes):
    return 1 if sizes["h"] * sizes["l"] == 2 else 0


def moves(sizes):
    groups, ranks, inner = sizes["a"], sizes["h"] * sizes["l"], sizes["l"]
    far = groups // 2
    flip = flipped(sizes)
    swap_to = {}
    for group in range(2):
        for part in range(ranks):
            place = (part % 2 ^ flip) * ranks + group * (ranks // 2) + part // 2
            swap_to[group * ranks + part] = place

    def swap(values, inverse=False):
        pairs = [(to, frm) if inverse else (frm, to) for frm, to in swap_to.items()]
        return lax.ppermute(values, SWAP, pairs)

    def swap_hop(values, a_mask, inverse=False):
        pairs = []
        for a in range(groups):
            for frm, to in swap_to.items():
                one, two = a * 2 * ranks + frm, (a ^ a_mask) * 2 * ranks + to
                pairs.append((two, one) if inverse else (one, two))
        return lax.ppermute(values, ALL, pairs)

    def hop(values, a_mask, h_mask):
        pairs = []
        for a in range(groups):
            for c in range(2):
                for h in range(2):
                    pairs.append(((a * 2 + c) * 2 + h, ((a ^ a_mask) * 2 + c) * 2 + (h ^ h_mask)))
        return lax.ppermute(values, ("a", "c", "h"), pairs)

    def scatter_near(pieces, after):
        from_x, from_y = hop(pieces[0], 0, 1), hop(pieces[1], 1, 0)
        half, columns = pieces[2].shape
        y_sum, x_sum = sums_call(
            first_sums_kernel,
            [from_x, from_y, pieces[2], pieces[3]],
            [jax.ShapeDtypeStruct((half, columns), BF16)] * 2,
            after,
            "sums_one",
        )
        return from_x, from_y, pieces[4], y_sum, x_sum

    def scatter_far(state, small):
        from_x, from_y, near, y_sum, x_sum = state
        columns = near.shape[1]
        from_y2, from_x2 = hop(y_sum, 1, 0), hop(x_sum, 0, 1)
        rows, extra = near.shape[0] // far, 2 * small.shape[0]
        sums = sums_call(
            second_sums_kernel,
            [from_x, from_y, near, from_y2, from_x2, small],
            [jax.ShapeDtypeStruct((rows + extra, columns), BF16)] * far,
            None,
            "sums_two",
        )
        parts = [swap_hop(sums[i], 2 * i, inverse=True) for i in range(far)]
        outs = sums_call(
            weights_last_kernel,
            parts,
            [jax.ShapeDtypeStruct((rows, columns // 4), F32)] * 4
            + [jax.ShapeDtypeStruct(small.shape, F32)],
            None,
            "sums_last",
        )
        return outs[:4], outs[4]

    def near_sum(values):
        values = values + lax.ppermute(values, "c", [(0, 1), (1, 0)])
        values = values + hop(values, 0, 1)
        values = values + hop(values, 1, 0)
        return lax.psum(values, "l") if inner > 1 else values

    a, h = lax.axis_index("a"), lax.axis_index("h")
    order = []
    for a_low, h_mask in ((0, 0), (1, 0), (0, 1), (1, 1)):
        for i in range(far):
            order.append((a ^ (2 * i + a_low)) * 2 + (h ^ h_mask))
    return swap, scatter_near, scatter_far, near_sum, jnp.stack(order).astype(jnp.int32)


def per_device(sizes, *arguments):
    (
        block_input, segment_ids, ln1_gain, ln1_bias, w_query, w_key, w_value, b_query, b_value,
        w_out, b_out, ln2_gain, ln2_bias, w_up, b_up, w_down, b_down, out_grad,
    ) = arguments
    ranks = sizes["h"] * sizes["l"]
    rank = lax.axis_index("l") * 2 + (lax.axis_index("c") ^ flipped(sizes))
    own_rows, width = block_input.shape
    head_width = w_query.shape[1]
    unit_width = w_up.shape[1]
    half_units = unit_width // 2
    tile = min(TILE, half_units)
    swap, scatter_near, scatter_far, near_sum, order = moves(sizes)

    def partner(values):
        return lax.ppermute(values, "c", [(0, 1), (1, 0)])

    def tp_gather(values):
        if ranks != 2:
            return lax.all_gather(values, TP, axis=0, tiled=True)
        theirs = partner(values)
        return jnp.where(
            rank == 0,
            jnp.concatenate([values, theirs], axis=0),
            jnp.concatenate([theirs, values], axis=0),
        )

    def tp_terms(values):
        if ranks != 2:
            others = lax.psum(values.astype(F32), TP) - values.astype(F32)
            return values, others.astype(BF16)
        return values, partner(values)

    def own(values):
        return lax.dynamic_slice_in_dim(values, rank * own_rows, own_rows)

    def tp_scatter(values):
        if ranks != 2:
            return lax.psum_scatter(values, TP, scatter_dimension=0, tiled=True).astype(F32)
        theirs = lax.dynamic_slice_in_dim(values, (1 - rank) * own_rows, own_rows)
        return own(values).astype(F32) + partner(theirs).astype(F32)

    own_input = swap(block_input)
    segments = swap(segment_ids)
    shard_first, shard_second = sums_call(
        functools.partial(shards_kernel, tile=tile),
        [w_up, w_down],
        [jax.ShapeDtypeStruct(w_up.shape, BF16)] * 2,
        own_input,
        "mlp_shards",
    )

    def gather(shard):
        return swap(lax.all_gather(shard, ("a", "c"), axis=0, tiled=True))

    full_attn = gather(jnp.concatenate([w_query, w_key, w_value, w_out], axis=1))
    full_first = gather(shard_first)
    late_second = lax.all_gather(shard_second, ("a", "c"), axis=0, tiled=True)
    own_grad = swap(out_grad)
    bias_query = lax.dynamic_slice_in_dim(b_query, rank * head_width, head_width)
    bias_value = lax.dynamic_slice_in_dim(b_value, rank * head_width, head_width)
    bias_up = lax.dynamic_slice_in_dim(b_up, rank * unit_width, unit_width)

    rows_in = tp_gather(own_input)
    grad_rows = tp_gather(own_grad)
    grad_rows_t = grad_rows.T
    normed, normed_t = norm_rows(rows_in, ln1_gain, ln1_bias)
    biases = jnp.concatenate([bias_query, jnp.zeros((head_width,), F32), bias_value])
    qkv = qkv_project(normed, full_attn, biases)
    full_out = full_attn[:, 3 * head_width :]
    mixed, lse = attn_forward(segments, qkv, head_width)
    late_second, mixed = lax.optimization_barrier((late_second, mixed))
    full_second = swap(late_second)
    attended = tp_terms(dot_nt(mixed, full_out).astype(BF16))
    normed_two, normed_two_t, hidden = norm_rows(rows_in, ln2_gain, ln2_bias, attended, b_out)

    out_part, gn_part, first_grads, bias_first = mlp(
        normed_two, grad_rows, normed_two_t, grad_rows_t, full_first, bias_up[:half_units], ()
    )
    first_grads = swap(first_grads, inverse=True)
    out_part, gn_part, second_grads, bias_second = mlp(
        normed_two, grad_rows, normed_two_t, grad_rows_t, full_second, bias_up[half_units:],
        (out_part, gn_part),
    )
    second_grads = swap(second_grads, inverse=True)
    own_output = (own(hidden) + tp_scatter(out_part) + b_down).astype(BF16)
    output = swap(own_output, inverse=True)

    grad_hidden, grad_attended, grad_attended_t, sums_two = norm_back_rows(
        hidden, grad_rows, tp_terms(gn_part), ln2_gain
    )
    first_grads, grad_attended = lax.optimization_barrier((first_grads, grad_attended))
    first_mlp = lax.psum_scatter(first_grads, ("a", "c"), scatter_dimension=0, tiled=True)
    grad_mixed = dot_nn(grad_attended, full_out).astype(BF16)
    grads = attn_backward(segments, qkv, mixed, lse, grad_mixed, head_width, grad_mixed)
    second_grads, first_mlp = lax.optimization_barrier((second_grads, first_mlp))
    second_mlp = lax.psum_scatter(second_grads, ("a", "c"), scatter_dimension=0, tiled=True)
    pieces = weight_grads(order, normed_t, grads, grad_attended_t, mixed)
    grad_normed_part = qkv_back(grads, full_attn, pieces[0])
    state = scatter_near(pieces, grad_normed_part)
    grad_normed_part, state = lax.optimization_barrier((grad_normed_part, state))
    grad_normed = tp_scatter(grad_normed_part)
    own_scaled, own_inverse = normalize(own_input.astype(F32))
    grad_own = own(grad_hidden) + norm_back(grad_normed, own_scaled, own_inverse, ln1_gain)
    grad_input = swap(grad_own.astype(BF16), inverse=True)

    def place_part(values, full):
        return lax.dynamic_update_slice_in_dim(
            jnp.zeros((full,), F32), values, rank * values.shape[0], 0
        )

    sums = jnp.concatenate(
        [
            jnp.sum(grad_normed * own_scaled, axis=0),
            jnp.sum(grad_normed, axis=0),
            place_part(jnp.sum(grads[0].astype(F32), axis=0), width),
            place_part(jnp.sum(grads[2].astype(F32), axis=0), width),
            (sums_two[:3] * (1.0 / ranks)).reshape(-1),
            jnp.sum(own_grad.astype(F32), axis=0),
            place_part(jnp.concatenate([bias_first[0], bias_second[0]]), b_up.shape[0]),
        ]
    )
    columns = pieces[0].shape[1]
    filled = sums.shape[0]
    sums = jnp.pad(sums, (0, -filled % (8 * columns))).reshape(-1, columns)
    late, sums = scatter_far(state, near_sum(sums))
    sums = sums.reshape(-1)
    shard = jax.ShapeDtypeStruct((w_query.shape[0], unit_width), F32)
    grad_w_up, grad_w_down = sums_call(
        functools.partial(units_last_kernel, tile=tile),
        [first_mlp, second_mlp],
        [shard, shard],
        None,
        "units_last",
    )
    small = [sums[i * width : (i + 1) * width] for i in range(8)]
    return (
        output, grad_input, small[0], small[1],
        late[0], late[1], late[2], small[2], small[3], late[3], small[4], small[5], small[6],
        grad_w_up, sums[8 * width : filled], grad_w_down, small[7],
    )


def solution(mesh):
    groups, ranks = mesh.shape["dp"], mesh.shape["tensor"]
    sizes = {"a": groups // 2, "c": 2, "h": 2, "l": ranks // 2}
    fine = Mesh(mesh.devices.reshape(tuple(sizes.values())), tuple(sizes))
    rows = P(("a", "c", "h", "l"), None)
    block = P(("a", "c"), ("h", "l"))
    return jax.shard_map(
        functools.partial(per_device, sizes),
        mesh=fine,
        in_specs=(
            rows, P(("a", "c")), P(), P(), block, block, block, P(), P(), block, P(), P(), P(),
            block, P(), block, P(), rows,
        ),
        out_specs=(
            rows, rows, P(), P(), block, block, block, P(), P(), block, P(), P(), P(), block, P(),
            block, P(),
        ),
        check_vma=False,
    )
```

```python
import functools

import jax
import jax.numpy as jnp
from jax import lax
from jax.experimental import pallas as pl
from jax.experimental.pallas import tpu as pltpu
from jax.sharding import Mesh
from jax.sharding import PartitionSpec as P

HEAD_DIM = 64
LANES = 128
TILE = 512
MASKED = -1e30
VMEM_BYTES = 60 * 1024 * 1024
F32 = jnp.float32
BF16 = jnp.bfloat16
TP = ("l", "c")
SWAP = ("c", "h", "l")
ALL = ("a", "c", "h", "l")


def normalize(values):
    center = values - jnp.mean(values, axis=-1, keepdims=True)
    spread = jnp.mean(center * center, axis=-1, keepdims=True)
    inverse = lax.rsqrt(spread + 1e-05)
    return center * inverse, inverse


def norm_back(grad_in, scaled, inverse, gain_vec):
    local_grad = grad_in * gain_vec
    return inverse * (
        local_grad
        - jnp.mean(local_grad, axis=-1, keepdims=True)
        - scaled * jnp.mean(local_grad * scaled, axis=-1, keepdims=True)
    )


def dot_nn(left, right):
    return lax.dot_general(left, right, (((1,), (0,)), ((), ())), preferred_element_type=F32)


def dot_nt(left, right):
    return lax.dot_general(left, right, (((1,), (1,)), ((), ())), preferred_element_type=F32)


def dot_tn(left, right):
    return lax.dot_general(left, right, (((0,), (0,)), ((), ())), preferred_element_type=F32)


def fill_bias(bias, seg_col, seg_row):
    length = bias.shape[0]
    block = min(256, length)
    for first in range(0, length, block):
        keys = lax.broadcasted_iota(jnp.int32, (block, length), 0) + first
        places = lax.broadcasted_iota(jnp.int32, (block, length), 1)
        same = seg_col[first : first + block, :] == seg_row[...]
        bias[first : first + block, :] = jnp.where(same & (keys <= places), 0.0, MASKED)


def head_lanes(values, head):
    lane = lax.broadcasted_iota(jnp.int32, values.shape, 1)
    inside = (lane >= head * HEAD_DIM) & (lane < (head + 1) * HEAD_DIM)
    return jnp.where(inside, values, jnp.zeros_like(values))


def attn_forward_kernel(seg_col, seg_row, q_ref, k_ref, v_ref, mixed_ref, lse_ref, bias, v_t, block):
    length = q_ref.shape[0]
    heads = LANES // HEAD_DIM

    @pl.when(pl.program_id(0) == 0)
    def _():
        fill_bias(bias, seg_col, seg_row)

    v_t[...] = v_ref[...].T
    for place in range(length // block):
        rows = slice(place * block, (place + 1) * block)
        outs = []
        for head in range(heads):
            query = head_lanes(q_ref[rows, :], head)
            scores = []
            peak = None
            for other in range(place + 1):
                keys = slice(other * block, (other + 1) * block)
                part = dot_nt(k_ref[keys, :], query) + bias[keys, rows]
                top = jnp.max(part, axis=0, keepdims=True)
                peak = top if peak is None else jnp.maximum(peak, top)
                scores.append(part)
            total = None
            acc = None
            for other in range(place + 1):
                keys = slice(other * block, (other + 1) * block)
                weight = jnp.exp(scores[other] - peak)
                part_sum = jnp.sum(weight, axis=0, keepdims=True)
                total = part_sum if total is None else total + part_sum
                part_out = dot_nn(
                    v_t[head * HEAD_DIM : (head + 1) * HEAD_DIM, keys], weight.astype(BF16)
                )
                acc = part_out if acc is None else acc + part_out
            outs.append(acc / total)
            lse_ref[0, head : head + 1, rows] = peak + jnp.log(total)
        mixed_ref[rows, :] = jnp.concatenate(outs, axis=0).T.astype(BF16)


def attn_backward_kernel(
    seg_col, seg_row, q_ref, k_ref, v_ref, mixed_ref, lse_ref, g_ref, grads_ref, bias, k_t, delta, dq_t, block
):
    length = q_ref.shape[0]
    heads = LANES // HEAD_DIM
    count = length // block

    @pl.when(pl.program_id(0) == 0)
    def _():
        fill_bias(bias, seg_col, seg_row)

    k_t[...] = k_ref[...].T
    product = (g_ref[...].astype(F32) * mixed_ref[...].astype(F32)).T
    for head in range(heads):
        delta[head : head + 1, :] = jnp.sum(
            product[head * HEAD_DIM : (head + 1) * HEAD_DIM, :], axis=0, keepdims=True
        )
    for other in range(count):
        keys = slice(other * block, (other + 1) * block)
        key_sum = None
        value_sum = None
        for head in range(heads):
            lanes = slice(head * HEAD_DIM, (head + 1) * HEAD_DIM)
            for place in range(other, count):
                rows = slice(place * block, (place + 1) * block)
                query = head_lanes(q_ref[rows, :], head)
                grad = head_lanes(g_ref[rows, :], head)
                scores = dot_nt(k_ref[keys, :], query) + bias[keys, rows]
                probs = jnp.exp(scores - lse_ref[0, head : head + 1, rows])
                grad_probs = dot_nt(v_ref[keys, :], grad)
                grad_scores = (probs * (grad_probs - delta[head : head + 1, rows])).astype(BF16)
                value_part = dot_nn(probs.astype(BF16), grad)
                key_part = dot_nn(grad_scores, query)
                query_part = dot_nn(k_t[lanes, keys], grad_scores)
                value_sum = value_part if value_sum is None else value_sum + value_part
                key_sum = key_part if key_sum is None else key_sum + key_part
                if other == 0:
                    dq_t[lanes, rows] = query_part
                else:
                    dq_t[lanes, rows] += query_part
        grads_ref[1, keys, :] = key_sum.astype(BF16)
        grads_ref[2, keys, :] = value_sum.astype(BF16)
    grads_ref[0] = (dq_t[...].T * HEAD_DIM ** (-0.5)).astype(BF16)


def attn_forward(segments, qkv, width):
    length = qkv.shape[0]
    pairs = width // LANES
    block = min(256, length)
    column = lambda first: pl.BlockSpec((length, LANES), lambda p: (0, first * pairs + p))
    whole = lambda shape: pl.BlockSpec(shape, lambda p: (0, 0))
    return pl.pallas_call(
        functools.partial(attn_forward_kernel, block=block),
        grid=(pairs,),
        in_specs=[whole((length, 1)), whole((1, length)), column(0), column(1), column(2)],
        out_specs=[
            pl.BlockSpec((length, LANES), lambda p: (0, p)),
            pl.BlockSpec((1, 8, length), lambda p: (p, 0, 0)),
        ],
        out_shape=[
            jax.ShapeDtypeStruct((length, width), BF16),
            jax.ShapeDtypeStruct((pairs, 8, length), F32),
        ],
        scratch_shapes=[pltpu.VMEM((length, length), F32), pltpu.VMEM((LANES, length), BF16)],
        compiler_params=pltpu.CompilerParams(vmem_limit_bytes=VMEM_BYTES),
        cost_estimate=pl.CostEstimate(
            flops=4 * length * length * width,
            bytes_accessed=8 * length * width,
            transcendentals=length * length * width // (2 * HEAD_DIM),
        ),
        name="attn_forward",
    )(segments.reshape(length, 1), segments.reshape(1, length), qkv, qkv, qkv)


def attn_backward(segments, qkv, mixed, lse, grad_mixed, width, after):
    length = qkv.shape[0]
    pairs = width // LANES
    block = min(256, length)
    column = lambda first: pl.BlockSpec((length, LANES), lambda p: (0, first * pairs + p))
    whole = lambda shape: pl.BlockSpec(shape, lambda p: (0, 0))
    return pl.pallas_call(
        without(functools.partial(attn_backward_kernel, block=block), 8),
        grid=(pairs,),
        in_specs=[
            whole((length, 1)),
            whole((1, length)),
            column(0),
            column(1),
            column(2),
            pl.BlockSpec((length, LANES), lambda p: (0, p)),
            pl.BlockSpec((1, 8, length), lambda p: (p, 0, 0)),
            pl.BlockSpec((length, LANES), lambda p: (0, p)),
            pl.BlockSpec(memory_space=pl.ANY),
        ],
        out_specs=pl.BlockSpec((3, length, LANES), lambda p: (0, 0, p)),
        out_shape=jax.ShapeDtypeStruct((3, length, width), BF16),
        scratch_shapes=[
            pltpu.VMEM((length, length), F32),
            pltpu.VMEM((LANES, length), BF16),
            pltpu.VMEM((8, length), F32),
            pltpu.VMEM((LANES, length), F32),
        ],
        compiler_params=pltpu.CompilerParams(vmem_limit_bytes=VMEM_BYTES),
        cost_estimate=pl.CostEstimate(
            flops=10 * length * length * width,
            bytes_accessed=16 * length * width,
            transcendentals=length * length * width // (2 * HEAD_DIM),
        ),
        name="attn_backward",
    )(segments.reshape(length, 1), segments.reshape(1, length), qkv, qkv, qkv, mixed, lse, grad_mixed, after)


def piece_blocks(count):
    far = count // 4
    half = far // 2
    near, by_y, by_x, both = (list(range(i * far, (i + 1) * far)) for i in range(4))
    return [
        both[:half] + by_x[:half],
        both[half:] + by_y[half:],
        by_y[:half],
        by_x[half:],
        near,
    ]


def store_pieces(order, grad, piece_refs, columns):
    count = order.shape[0]
    rows = grad.shape[0] // count
    for blocks, ref in zip(piece_blocks(count), piece_refs):
        for place, block in enumerate(blocks):
            first = pl.multiple_of(order[block] * rows, rows)
            ref[place * rows : (place + 1) * rows, columns] = grad[pl.ds(first, rows), :]


def piece_shapes(count, rows, columns):
    return [
        jax.ShapeDtypeStruct((len(blocks) * rows, columns), BF16) for blocks in piece_blocks(count)
    ]


def whole_spec(shape, **options):
    return pl.BlockSpec(shape, lambda step: (0,) * len(shape), **options)


def norm_kernel(*refs, residual):
    if residual:
        x_ref, own_ref, other_ref, shift_ref, gain_ref, bias_ref, n_ref, nt_ref, hidden_ref = refs
        values = (
            x_ref[...].astype(F32)
            + (own_ref[...].astype(F32) + other_ref[...].astype(F32))
            + shift_ref[...]
        )
        hidden_ref[...] = values
    else:
        x_ref, gain_ref, bias_ref, n_ref, nt_ref = refs
        values = x_ref[...].astype(F32)
    scaled, _ = normalize(values)
    normed = (scaled * gain_ref[...] + bias_ref[...]).astype(BF16)
    n_ref[...] = normed
    nt_ref[...] = normed.T


def norm_rows(x, gain, bias, partials=None, shift=None):
    length, width = x.shape
    block = min(256, length)
    row = pl.BlockSpec((block, width), lambda step: (step, 0))
    vector = whole_spec((1, width))
    residual = partials is not None
    operands = [x] + (list(partials) + [shift.reshape(1, width)] if residual else [])
    operands += [gain.reshape(1, width), bias.reshape(1, width)]
    return pl.pallas_call(
        functools.partial(norm_kernel, residual=residual),
        grid=(length // block,),
        in_specs=[row] + ([row, row, vector] if residual else []) + [vector, vector],
        out_specs=[row, pl.BlockSpec((width, block), lambda step: (0, step))]
        + ([row] if residual else []),
        out_shape=[
            jax.ShapeDtypeStruct((length, width), BF16),
            jax.ShapeDtypeStruct((width, length), BF16),
        ]
        + ([jax.ShapeDtypeStruct((length, width), F32)] if residual else []),
        compiler_params=pltpu.CompilerParams(vmem_limit_bytes=VMEM_BYTES),
        cost_estimate=pl.CostEstimate(
            flops=20 * length * width, bytes_accessed=14 * length * width, transcendentals=length
        ),
        name="norm_two" if residual else "norm_one",
    )(*operands)


def norm_back_kernel(hidden_ref, g_ref, own_ref, other_ref, gain_ref, grad_ref, low_ref, low_t_ref, sums_ref):
    scaled, inverse = normalize(hidden_ref[...])
    incoming = own_ref[...].astype(F32) + other_ref[...].astype(F32)
    grad = g_ref[...].astype(F32) + norm_back(incoming, scaled, inverse, gain_ref[...])
    grad_ref[...] = grad
    low_ref[...] = grad.astype(BF16)
    low_t_ref[...] = grad.astype(BF16).T

    @pl.when(pl.program_id(0) == 0)
    def _():
        sums_ref[...] = jnp.zeros_like(sums_ref)

    sums_ref[0:1, :] += jnp.sum(grad, axis=0, keepdims=True)
    sums_ref[1:2, :] += jnp.sum(incoming * scaled, axis=0, keepdims=True)
    sums_ref[2:3, :] += jnp.sum(incoming, axis=0, keepdims=True)


def norm_back_rows(hidden, grad, partials, gain):
    length, width = hidden.shape
    block = min(256, length)
    row = pl.BlockSpec((block, width), lambda step: (step, 0))
    return pl.pallas_call(
        norm_back_kernel,
        grid=(length // block,),
        in_specs=[row, row, row, row, whole_spec((1, width))],
        out_specs=[
            row,
            row,
            pl.BlockSpec((width, block), lambda step: (0, step)),
            whole_spec((8, width)),
        ],
        out_shape=[
            jax.ShapeDtypeStruct((length, width), F32),
            jax.ShapeDtypeStruct((length, width), BF16),
            jax.ShapeDtypeStruct((width, length), BF16),
            jax.ShapeDtypeStruct((8, width), F32),
        ],
        compiler_params=pltpu.CompilerParams(vmem_limit_bytes=VMEM_BYTES),
        cost_estimate=pl.CostEstimate(
            flops=30 * length * width, bytes_accessed=16 * length * width, transcendentals=length
        ),
        name="norm_two_back",
    )(hidden, grad, *partials, gain.reshape(1, width))


def mlp_kernel(order, n_ref, g_ref, nt_ref, gt_ref, b_ref, w_ref, *refs, block, with_previous, cube):
    if with_previous:
        (before_out, before_gn), refs = refs[:2], refs[2:]
    (out_ref, gn_ref), refs = refs[:2], refs[2:]
    grad_refs, (gb_ref, out_acc, gn_acc, act, gpre, grad_w) = refs[:-6], refs[-6:]
    step = pl.program_id(0)
    length = n_ref.shape[0]
    tile = w_ref.shape[1] // 2
    ups, downs = slice(0, tile), slice(tile, 2 * tile)

    @pl.when(step == 0)
    def _():
        if with_previous:
            out_acc[...] = before_out[...].astype(F32)
            gn_acc[...] = before_gn[...].astype(F32)
        else:
            out_acc[...] = jnp.zeros_like(out_acc)
            gn_acc[...] = jnp.zeros_like(gn_acc)

    bias_sum = jnp.zeros(gb_ref.shape, F32)
    for first in range(0, length, block):
        rows = slice(first, first + block)
        unit = dot_nn(n_ref[rows, :], w_ref[:, ups]) + b_ref[...]
        grad = dot_nn(g_ref[rows, :], w_ref[:, downs])
        square = unit * unit
        curve = jnp.tanh(0.7978845608028654 * (unit + 0.044715 * (square * unit)))
        half = 0.5 + 0.5 * curve
        slope = half + (0.5 * unit) * (1.0 - curve * curve) * (
            0.7978845608028654 + (3 * 0.044715 * 0.7978845608028654) * square
        )
        active = (unit * half).astype(BF16)
        grad_pre = (grad * slope).astype(BF16)
        act[rows, :] = active
        gpre[rows, :] = grad_pre
        bias_sum = bias_sum + jnp.sum(grad_pre.astype(F32), axis=0, keepdims=True)
        out_acc[rows, :] += dot_nt(active, w_ref[:, downs])
        gn_acc[rows, :] += dot_nt(grad_pre, w_ref[:, ups])
    gb_ref[...] = bias_sum
    for columns, left, right in ((ups, nt_ref, gpre), (downs, gt_ref, act)):
        if cube:
            grad_w[...] = dot_nn(left[...], right[...]).astype(BF16)
            store_pieces(order, grad_w, grad_refs, columns)
        else:
            grad_refs[0][:, columns] = dot_nn(left[...], right[...]).astype(BF16)

    @pl.when(step == pl.num_programs(0) - 1)
    def _():
        out_ref[...] = out_acc[...].astype(BF16)
        gn_ref[...] = gn_acc[...].astype(BF16)


def mlp(order, normed, grad, normed_t, grad_t, weights, bias, previous, cube):
    length, width = normed.shape
    units = weights.shape[1] // 2
    tile = min(TILE, units)
    at_tile = lambda rows, columns: pl.BlockSpec((rows, columns), lambda u, o: (0, u))
    fixed = lambda shape: pl.BlockSpec(shape, lambda u, o: (0, 0))
    once = lambda shape: pl.BlockSpec(shape, lambda u, o: (0, 0), pipeline_mode=pl.Buffered(1))
    if cube:
        count = order.shape[0]
        grad_shapes = piece_shapes(count, width // count, 2 * units)
    else:
        grad_shapes = [jax.ShapeDtypeStruct((width, 2 * units), BF16)]
    results = pl.pallas_call(
        functools.partial(
            mlp_kernel, block=min(256, length), with_previous=bool(previous), cube=cube
        ),
        grid_spec=pltpu.PrefetchScalarGridSpec(
            num_scalar_prefetch=1,
            grid=(units // tile,),
            in_specs=[
                once((length, width)),
                once((length, width)),
                once((width, length)),
                once((width, length)),
                at_tile(1, tile),
                at_tile(width, 2 * tile),
            ]
            + [once((length, width)) for _ in previous],
            out_specs=[fixed((length, width)), fixed((length, width))]
            + [at_tile(shape.shape[0], 2 * tile) for shape in grad_shapes]
            + [at_tile(1, tile)],
            scratch_shapes=[
                pltpu.VMEM((length, width), F32),
                pltpu.VMEM((length, width), F32),
                pltpu.VMEM((length, tile), BF16),
                pltpu.VMEM((length, tile), BF16),
                pltpu.VMEM((width, tile), BF16),
            ],
        ),
        out_shape=[jax.ShapeDtypeStruct((length, width), BF16)] * 2
        + grad_shapes
        + [jax.ShapeDtypeStruct((1, units), F32)],
        compiler_params=pltpu.CompilerParams(vmem_limit_bytes=VMEM_BYTES),
        cost_estimate=pl.CostEstimate(
            flops=12 * length * width * units,
            bytes_accessed=12 * length * width + 8 * width * units,
            transcendentals=length * units,
        ),
        name="mlp_second" if previous else "mlp_first",
    )(order, normed, grad, normed_t, grad_t, bias.reshape(1, units), weights, *previous)
    return results[0], results[1], results[2:-1], results[-1]


def qkv_kernel(n_ref, b_ref, w_ref, out_ref):
    scale = jnp.where(pl.program_id(0) == 0, HEAD_DIM ** (-0.5), 1.0)
    length = n_ref.shape[0]
    step = min(256, length)
    for first in range(0, length, step):
        span = slice(first, first + step)
        out_ref[span, :] = ((dot_nn(n_ref[span, :], w_ref[...]) + b_ref[...]) * scale).astype(BF16)


def qkv_project(normed, weights, bias):
    length, width = normed.shape
    columns = weights.shape[1] // 4
    at_tile = lambda rows: pl.BlockSpec((rows, columns), lambda k: (0, k))
    return pl.pallas_call(
        qkv_kernel,
        grid=(3,),
        in_specs=[
            whole_spec((length, width), pipeline_mode=pl.Buffered(1)), at_tile(1), at_tile(width)
        ],
        out_specs=at_tile(length),
        out_shape=jax.ShapeDtypeStruct((length, 3 * columns), BF16),
        compiler_params=pltpu.CompilerParams(vmem_limit_bytes=VMEM_BYTES),
        cost_estimate=pl.CostEstimate(
            flops=6 * length * width * columns,
            bytes_accessed=2 * length * width + 6 * width * columns + 6 * length * columns,
            transcendentals=0,
        ),
        name="qkv_project",
    )(normed, bias.reshape(1, 3 * columns), weights)


def weight_kernel(order, nt_ref, grads_ref, gt_ref, mixed_ref, order_only, *refs):
    piece_refs, grad = refs[:5], refs[5]
    part = pl.program_id(0)

    @pl.when(part < 3)
    def _():
        grad[...] = dot_nn(nt_ref[...], grads_ref[0]).astype(BF16)

    @pl.when(part == 3)
    def _():
        grad[...] = dot_nn(gt_ref[...], mixed_ref[...]).astype(BF16)

    store_pieces(order, grad, piece_refs, slice(None))


def without(kernel, place):
    return lambda *refs: kernel(*refs[:place], *refs[place + 1 :])


ORDER_ONLY = pl.BlockSpec(memory_space=pl.ANY)


def weight_grads(order, normed_t, grads, grad_t, mixed, after):
    width, length = normed_t.shape
    columns = grads.shape[2]
    shapes = piece_shapes(order.shape[0], width // order.shape[0], 4 * columns)
    fixed = lambda shape: pl.BlockSpec(shape, lambda k, o: (0, 0), pipeline_mode=pl.Buffered(1))
    return pl.pallas_call(
        weight_kernel,
        grid_spec=pltpu.PrefetchScalarGridSpec(
            num_scalar_prefetch=1,
            grid=(4,),
            in_specs=[
                fixed((width, length)),
                pl.BlockSpec((1, length, columns), lambda k, o: (jnp.minimum(k, 2), 0, 0)),
                fixed((width, length)),
                fixed((length, columns)),
                ORDER_ONLY,
            ],
            out_specs=[
                pl.BlockSpec((shape.shape[0], columns), lambda k, o: (0, k)) for shape in shapes
            ],
            scratch_shapes=[pltpu.VMEM((width, columns), BF16)],
        ),
        out_shape=shapes,
        compiler_params=pltpu.CompilerParams(vmem_limit_bytes=VMEM_BYTES),
        cost_estimate=pl.CostEstimate(
            flops=8 * length * width * columns,
            bytes_accessed=4 * length * width + 16 * width * columns,
            transcendentals=0,
        ),
        name="weight_grads",
    )(order, normed_t, grads, grad_t, mixed, after)


def qkv_back_kernel(grads_ref, w_ref, out_ref):
    columns = grads_ref.shape[2]
    total = None
    for k in range(3):
        part = dot_nt(grads_ref[k], w_ref[:, k * columns : (k + 1) * columns])
        total = part if total is None else total + part
    out_ref[...] = total.astype(BF16)


def qkv_back(grads, weights, after):
    _, length, columns = grads.shape
    width = weights.shape[0]
    block = min(256, length)
    return pl.pallas_call(
        without(qkv_back_kernel, 2),
        grid=(length // block,),
        in_specs=[
            pl.BlockSpec((3, block, columns), lambda i: (0, i, 0)),
            pl.BlockSpec((width, 4 * columns), lambda i: (0, 0), pipeline_mode=pl.Buffered(1)),
            ORDER_ONLY,
        ],
        out_specs=pl.BlockSpec((block, width), lambda i: (i, 0)),
        out_shape=jax.ShapeDtypeStruct((length, width), BF16),
        compiler_params=pltpu.CompilerParams(vmem_limit_bytes=VMEM_BYTES),
        cost_estimate=pl.CostEstimate(
            flops=6 * length * width * columns,
            bytes_accessed=2 * length * width + 6 * width * columns + 6 * length * columns,
            transcendentals=0,
        ),
        name="qkv_back",
    )(grads, weights, after)


def added(*terms):
    total = terms[0].astype(F32)
    for term in terms[1:]:
        total = total + term.astype(F32)
    return total.astype(BF16)


def first_sums_kernel(from_x, from_y, keep_y, keep_x, y_ref, x_ref):
    half = y_ref.shape[0]
    y_ref[...] = added(keep_y[...], from_x[:half, :])
    x_ref[...] = added(keep_x[...], from_y[:half, :])


def second_sums_kernel(from_x, from_y, near, from_y2, from_x2, *outs, with_small):
    if with_small:
        small, outs = outs[0], outs[1:]
    far = len(outs)
    half = from_y2.shape[0]
    rows = half * 2 // far
    if with_small:
        values = small[...]
        high = values.astype(BF16).astype(F32)
        extra = jnp.concatenate([high, values - high], axis=0).astype(BF16)
    for i, out in enumerate(outs):
        first, second, place = (from_x, from_y2, i) if i < far // 2 else (from_y, from_x2, i - far // 2)
        out[:rows, :] = added(
            near[i * rows : (i + 1) * rows, :],
            first[half + place * rows : half + (place + 1) * rows, :],
            second[place * rows : (place + 1) * rows, :],
        )
        if with_small:
            out[rows:, :] = extra


def total_kernel(*refs):
    parts, out = refs[:-1], refs[-1]
    total = parts[0][...].astype(F32)
    for part in parts[1:]:
        total = total + part[...].astype(F32)
    out[...] = total


def weights_last_kernel(*refs):
    parts, outs, small = refs[:-5], refs[-5:-1], refs[-1]
    total = parts[0][...].astype(F32)
    for part in parts[1:]:
        total = total + part[...].astype(F32)
    rows, columns = outs[0].shape
    for k, out in enumerate(outs):
        out[...] = total[:rows, k * columns : (k + 1) * columns]
    extra = small.shape[0]
    small[...] = total[rows : rows + extra, :] + total[rows + extra :, :]


def units_last_kernel(first_ref, second_ref, up_ref, down_ref, *, tile):
    units = up_ref.shape[1] // 2
    for index, ref in enumerate((first_ref, second_ref)):
        for first in range(0, units, tile):
            columns = slice(index * units + first, index * units + first + tile)
            up_ref[:, columns] = ref[:, 2 * first : 2 * first + tile].astype(F32)
            down_ref[:, columns] = ref[:, 2 * first + tile : 2 * first + 2 * tile].astype(F32)


def shards_kernel(w_up, w_down, first_ref, second_ref, *, tile):
    units = first_ref.shape[1] // 2
    for index, ref in enumerate((first_ref, second_ref)):
        for first in range(0, units, tile):
            columns = slice(index * units + first, index * units + first + tile)
            ref[:, 2 * first : 2 * first + tile] = w_up[:, columns]
            ref[:, 2 * first + tile : 2 * first + 2 * tile] = w_down[:, columns]


def sums_call(kernel, operands, shapes, after, name):
    body = kernel if after is None else without(kernel, 0)
    vmem = pl.BlockSpec(memory_space=pltpu.VMEM)
    return pl.pallas_call(
        body,
        in_specs=([pl.BlockSpec(memory_space=pl.ANY)] if after is not None else [])
        + [vmem] * len(operands),
        out_specs=[vmem] * len(shapes),
        out_shape=shapes,
        compiler_params=pltpu.CompilerParams(vmem_limit_bytes=VMEM_BYTES),
        cost_estimate=pl.CostEstimate(flops=0, bytes_accessed=1024 * 1024, transcendentals=0),
        name=name,
    )(*([after] if after is not None else []), *operands)


def flipped(sizes):
    return 1 if sizes["h"] * sizes["l"] == 2 else 0


def moves(sizes):
    groups, ranks, inner = sizes["a"], sizes["h"] * sizes["l"], sizes["l"]
    far = groups // 2
    flip = flipped(sizes)
    swap_to = {}
    for group in range(2):
        for part in range(ranks):
            place = (part % 2 ^ flip) * ranks + group * (ranks // 2) + part // 2
            swap_to[group * ranks + part] = place

    def swap(values, inverse=False):
        pairs = [(to, frm) if inverse else (frm, to) for frm, to in swap_to.items()]
        return lax.ppermute(values, SWAP, pairs)

    def swap_hop(values, a_mask, inverse=False):
        pairs = []
        for a in range(groups):
            for frm, to in swap_to.items():
                one, two = a * 2 * ranks + frm, (a ^ a_mask) * 2 * ranks + to
                pairs.append((two, one) if inverse else (one, two))
        return lax.ppermute(values, ALL, pairs)

    def hop(values, a_mask, h_mask):
        pairs = []
        for a in range(groups):
            for c in range(2):
                for h in range(2):
                    pairs.append(((a * 2 + c) * 2 + h, ((a ^ a_mask) * 2 + c) * 2 + (h ^ h_mask)))
        return lax.ppermute(values, ("a", "c", "h"), pairs)

    def scatter_near(pieces, after):
        from_x, from_y = hop(pieces[0], 0, 1), hop(pieces[1], 1, 0)
        half, columns = pieces[2].shape
        y_sum, x_sum = sums_call(
            first_sums_kernel,
            [from_x, from_y, pieces[2], pieces[3]],
            [jax.ShapeDtypeStruct((half, columns), BF16)] * 2,
            after,
            "sums_one",
        )
        return from_x, from_y, pieces[4], y_sum, x_sum

    def far_sums(state, small, after):
        from_x, from_y, near, y_sum, x_sum = state
        columns = near.shape[1]
        from_y2, from_x2 = hop(y_sum, 1, 0), hop(x_sum, 0, 1)
        rows = near.shape[0] // far + sum(2 * values.shape[0] for values in small)
        return sums_call(
            functools.partial(second_sums_kernel, with_small=bool(small)),
            [from_x, from_y, near, from_y2, from_x2] + small,
            [jax.ShapeDtypeStruct((rows, columns), BF16)] * far,
            after,
            "sums_two",
        )

    def far_parts(sums):
        return [swap_hop(sums[i], 2 * i, inverse=True) for i in range(far)]

    def near_sum(values):
        values = values + lax.ppermute(values, "c", [(0, 1), (1, 0)])
        values = values + hop(values, 0, 1)
        values = values + hop(values, 1, 0)
        return lax.psum(values, "l") if inner > 1 else values

    a, h = lax.axis_index("a"), lax.axis_index("h")
    order = []
    for a_low, h_mask in ((0, 0), (1, 0), (0, 1), (1, 1)):
        for i in range(far):
            order.append((a ^ (2 * i + a_low)) * 2 + (h ^ h_mask))
    return swap, scatter_near, far_sums, far_parts, near_sum, jnp.stack(order).astype(jnp.int32)


def per_device(sizes, *arguments):
    (
        block_input, segment_ids, ln1_gain, ln1_bias, w_query, w_key, w_value, b_query, b_value,
        w_out, b_out, ln2_gain, ln2_bias, w_up, b_up, w_down, b_down, out_grad,
    ) = arguments
    ranks = sizes["h"] * sizes["l"]
    rank = lax.axis_index("l") * 2 + (lax.axis_index("c") ^ flipped(sizes))
    own_rows, width = block_input.shape
    head_width = w_query.shape[1]
    unit_width = w_up.shape[1]
    half_units = unit_width // 2
    tile = min(TILE, half_units)
    swap, scatter_near, far_sums, far_parts, near_sum, order = moves(sizes)

    def partner(values):
        return lax.ppermute(values, "c", [(0, 1), (1, 0)])

    def tp_gather(values):
        if ranks != 2:
            return lax.all_gather(values, TP, axis=0, tiled=True)
        theirs = partner(values)
        return jnp.where(
            rank == 0,
            jnp.concatenate([values, theirs], axis=0),
            jnp.concatenate([theirs, values], axis=0),
        )

    def tp_terms(values):
        if ranks != 2:
            others = lax.psum(values.astype(F32), TP) - values.astype(F32)
            return values, others.astype(BF16)
        return values, partner(values)

    def own(values):
        return lax.dynamic_slice_in_dim(values, rank * own_rows, own_rows)

    def tp_scatter(values):
        if ranks != 2:
            return lax.psum_scatter(values, TP, scatter_dimension=0, tiled=True).astype(F32)
        theirs = lax.dynamic_slice_in_dim(values, (1 - rank) * own_rows, own_rows)
        return own(values).astype(F32) + partner(theirs).astype(F32)

    own_input = swap(block_input)
    segments = swap(segment_ids)
    own_grad = swap(out_grad)
    shard_first, shard_second = sums_call(
        functools.partial(shards_kernel, tile=tile),
        [w_up, w_down],
        [jax.ShapeDtypeStruct(w_up.shape, BF16)] * 2,
        None,
        "mlp_shards",
    )
    early_attn = lax.all_gather(
        jnp.concatenate([w_query, w_key, w_value, w_out], axis=1), ("a", "c"), axis=0, tiled=True
    )
    early_first = lax.all_gather(shard_first, ("a", "c"), axis=0, tiled=True)
    shard_second = swap(shard_second)
    bias_query = lax.dynamic_slice_in_dim(b_query, rank * head_width, head_width)
    bias_value = lax.dynamic_slice_in_dim(b_value, rank * head_width, head_width)
    bias_up = lax.dynamic_slice_in_dim(b_up, rank * unit_width, unit_width)

    rows_in = tp_gather(own_input)
    grad_rows = tp_gather(own_grad)
    grad_rows_t = grad_rows.T
    normed, normed_t = norm_rows(rows_in, ln1_gain, ln1_bias)
    early_attn, normed, segments, grad_rows, grad_rows_t, shard_second = lax.optimization_barrier(
        (early_attn, normed, segments, grad_rows, grad_rows_t, shard_second)
    )
    full_second = lax.all_gather(shard_second, ("a", "h"), axis=0, tiled=True)
    full_attn = swap(early_attn)
    biases = jnp.concatenate([bias_query, jnp.zeros((head_width,), F32), bias_value])
    qkv = qkv_project(normed, full_attn, biases)
    full_out = full_attn[:, 3 * head_width :]
    early_first, qkv = lax.optimization_barrier((early_first, qkv))
    full_first = swap(early_first)
    mixed, lse = attn_forward(segments, qkv, head_width)
    attended = tp_terms(dot_nt(mixed, full_out).astype(BF16))
    normed_two, normed_two_t, hidden = norm_rows(rows_in, ln2_gain, ln2_bias, attended, b_out)

    out_part, gn_part, first_grads, bias_first = mlp(
        order, normed_two, grad_rows, normed_two_t, grad_rows_t, full_first,
        bias_up[:half_units], (), True,
    )
    full_second, gn_part = lax.optimization_barrier((full_second, gn_part))
    out_part, gn_part, second_grads, bias_second = mlp(
        order, normed_two, grad_rows, normed_two_t, grad_rows_t, full_second,
        bias_up[half_units:], (out_part, gn_part), False,
    )
    first_state = scatter_near(first_grads, gn_part)
    gn_part, second_grads, first_state = lax.optimization_barrier(
        (gn_part, second_grads[0], first_state)
    )
    second_grads = swap(second_grads, inverse=True)
    own_output = (own(hidden) + tp_scatter(out_part) + b_down).astype(BF16)
    output = swap(own_output, inverse=True)

    grad_hidden, grad_attended, grad_attended_t, sums_two = norm_back_rows(
        hidden, grad_rows, tp_terms(gn_part), ln2_gain
    )
    grad_mixed = dot_nn(grad_attended, full_out).astype(BF16)
    first_sums = far_sums(first_state, [], grad_mixed)
    grads = attn_backward(segments, qkv, mixed, lse, grad_mixed, head_width, first_sums[0])
    block_rows = w_query.shape[0]
    (first_mlp,) = sums_call(
        total_kernel,
        far_parts(first_sums),
        [jax.ShapeDtypeStruct((block_rows, unit_width), F32)],
        grads,
        "units_first",
    )
    second_grads, grads = lax.optimization_barrier((second_grads, grads))
    second_mlp = lax.psum_scatter(second_grads, ("a", "c"), scatter_dimension=0, tiled=True)
    pieces = weight_grads(order, normed_t, grads, grad_attended_t, mixed, first_mlp)
    grad_normed_part = qkv_back(grads, full_attn, pieces[0])
    state = scatter_near(pieces, grad_normed_part)
    grad_normed_part, state = lax.optimization_barrier((grad_normed_part, state))
    grad_normed = tp_scatter(grad_normed_part)
    own_scaled, own_inverse = normalize(own_input.astype(F32))
    grad_own = own(grad_hidden) + norm_back(grad_normed, own_scaled, own_inverse, ln1_gain)
    grad_input = swap(grad_own.astype(BF16), inverse=True)

    def place_part(values, full):
        return lax.dynamic_update_slice_in_dim(
            jnp.zeros((full,), F32), values, rank * values.shape[0], 0
        )

    sums = jnp.concatenate(
        [
            jnp.sum(grad_normed * own_scaled, axis=0),
            jnp.sum(grad_normed, axis=0),
            place_part(jnp.sum(grads[0].astype(F32), axis=0), width),
            place_part(jnp.sum(grads[2].astype(F32), axis=0), width),
            (sums_two[:3] * (1.0 / ranks)).reshape(-1),
            jnp.sum(own_grad.astype(F32), axis=0),
            place_part(jnp.concatenate([bias_first[0], bias_second[0]]), b_up.shape[0]),
        ]
    )
    columns = pieces[0].shape[1]
    filled = sums.shape[0]
    sums = jnp.pad(sums, (0, -filled % (8 * columns))).reshape(-1, columns)
    sums = near_sum(sums)
    shard = jax.ShapeDtypeStruct((block_rows, unit_width), F32)
    grad_w_up, grad_w_down = sums_call(
        functools.partial(units_last_kernel, tile=tile),
        [first_mlp, second_mlp],
        [shard, shard],
        None,
        "units_last",
    )
    *late, sums = sums_call(
        weights_last_kernel,
        far_parts(far_sums(state, [sums], None)),
        [jax.ShapeDtypeStruct((block_rows, head_width), F32)] * 4
        + [jax.ShapeDtypeStruct(sums.shape, F32)],
        grad_w_up,
        "sums_last",
    )
    sums = sums.reshape(-1)
    small = [sums[i * width : (i + 1) * width] for i in range(8)]
    return (
        output, grad_input, small[0], small[1],
        late[0], late[1], late[2], small[2], small[3], late[3], small[4], small[5], small[6],
        grad_w_up, sums[8 * width : filled], grad_w_down, small[7],
    )


def solution(mesh):
    groups, ranks = mesh.shape["dp"], mesh.shape["tensor"]
    sizes = {"a": groups // 2, "c": 2, "h": 2, "l": ranks // 2}
    fine = Mesh(mesh.devices.reshape(tuple(sizes.values())), tuple(sizes))
    rows = P(("a", "c", "h", "l"), None)
    block = P(("a", "c"), ("h", "l"))
    return jax.shard_map(
        functools.partial(per_device, sizes),
        mesh=fine,
        in_specs=(
            rows, P(("a", "c")), P(), P(), block, block, block, P(), P(), block, P(), P(), P(),
            block, P(), block, P(), rows,
        ),
        out_specs=(
            rows, rows, P(), P(), block, block, block, P(), P(), block, P(), P(), P(), block, P(),
            block, P(),
        ),
        check_vma=False,
    )
```

```python
import functools

import jax
import jax.numpy as jnp
from jax import lax
from jax.experimental import pallas as pl
from jax.experimental.pallas import tpu as pltpu
from jax.sharding import Mesh
from jax.sharding import PartitionSpec as P

HEAD_DIM = 64
LANES = 128
TILE = 512
MASKED = -1e30
VMEM_BYTES = 60 * 1024 * 1024
F32 = jnp.float32
BF16 = jnp.bfloat16
TP = ("l", "c")
SWAP = ("c", "h", "l")
ALL = ("z", "y", "c", "h", "l")


def normalize(values):
    center = values - jnp.mean(values, axis=-1, keepdims=True)
    spread = jnp.mean(center * center, axis=-1, keepdims=True)
    inverse = lax.rsqrt(spread + 1e-05)
    return center * inverse, inverse


def norm_back(grad_in, scaled, inverse, gain_vec):
    local_grad = grad_in * gain_vec
    return inverse * (
        local_grad
        - jnp.mean(local_grad, axis=-1, keepdims=True)
        - scaled * jnp.mean(local_grad * scaled, axis=-1, keepdims=True)
    )


def dot_nn(left, right):
    return lax.dot_general(left, right, (((1,), (0,)), ((), ())), preferred_element_type=F32)


def dot_nt(left, right):
    return lax.dot_general(left, right, (((1,), (1,)), ((), ())), preferred_element_type=F32)


def dot_tn(left, right):
    return lax.dot_general(left, right, (((0,), (0,)), ((), ())), preferred_element_type=F32)


def fill_bias(bias, seg_col, seg_row):
    length = bias.shape[0]
    block = min(256, length)
    for first in range(0, length, block):
        keys = lax.broadcasted_iota(jnp.int32, (block, length), 0) + first
        places = lax.broadcasted_iota(jnp.int32, (block, length), 1)
        same = seg_col[first : first + block, :] == seg_row[...]
        bias[first : first + block, :] = jnp.where(same & (keys <= places), 0.0, MASKED)


def head_lanes(values, head):
    lane = lax.broadcasted_iota(jnp.int32, values.shape, 1)
    inside = (lane >= head * HEAD_DIM) & (lane < (head + 1) * HEAD_DIM)
    return jnp.where(inside, values, jnp.zeros_like(values))


def attn_forward_kernel(seg_col, seg_row, q_ref, k_ref, v_ref, mixed_ref, lse_ref, bias, v_t, block):
    length = q_ref.shape[0]
    heads = LANES // HEAD_DIM

    @pl.when(pl.program_id(0) == 0)
    def _():
        fill_bias(bias, seg_col, seg_row)

    v_t[...] = v_ref[...].T
    for place in range(length // block):
        rows = slice(place * block, (place + 1) * block)
        outs = []
        for head in range(heads):
            query = head_lanes(q_ref[rows, :], head)
            scores = []
            peak = None
            for other in range(place + 1):
                keys = slice(other * block, (other + 1) * block)
                part = dot_nt(k_ref[keys, :], query) + bias[keys, rows]
                top = jnp.max(part, axis=0, keepdims=True)
                peak = top if peak is None else jnp.maximum(peak, top)
                scores.append(part)
            total = None
            acc = None
            for other in range(place + 1):
                keys = slice(other * block, (other + 1) * block)
                weight = jnp.exp(scores[other] - peak)
                part_sum = jnp.sum(weight, axis=0, keepdims=True)
                total = part_sum if total is None else total + part_sum
                part_out = dot_nn(
                    v_t[head * HEAD_DIM : (head + 1) * HEAD_DIM, keys], weight.astype(BF16)
                )
                acc = part_out if acc is None else acc + part_out
            outs.append(acc / total)
            lse_ref[0, head : head + 1, rows] = peak + jnp.log(total)
        mixed_ref[rows, :] = jnp.concatenate(outs, axis=0).T.astype(BF16)


def attn_backward_kernel(
    seg_col, seg_row, q_ref, k_ref, v_ref, mixed_ref, lse_ref, g_ref, grads_ref, bias, k_t, delta, dq_t, block
):
    length = q_ref.shape[0]
    heads = LANES // HEAD_DIM
    count = length // block

    @pl.when(pl.program_id(0) == 0)
    def _():
        fill_bias(bias, seg_col, seg_row)

    k_t[...] = k_ref[...].T
    product = (g_ref[...].astype(F32) * mixed_ref[...].astype(F32)).T
    for head in range(heads):
        delta[head : head + 1, :] = jnp.sum(
            product[head * HEAD_DIM : (head + 1) * HEAD_DIM, :], axis=0, keepdims=True
        )
    for other in range(count):
        keys = slice(other * block, (other + 1) * block)
        key_sum = None
        value_sum = None
        for head in range(heads):
            lanes = slice(head * HEAD_DIM, (head + 1) * HEAD_DIM)
            for place in range(other, count):
                rows = slice(place * block, (place + 1) * block)
                query = head_lanes(q_ref[rows, :], head)
                grad = head_lanes(g_ref[rows, :], head)
                scores = dot_nt(k_ref[keys, :], query) + bias[keys, rows]
                probs = jnp.exp(scores - lse_ref[0, head : head + 1, rows])
                grad_probs = dot_nt(v_ref[keys, :], grad)
                grad_scores = (probs * (grad_probs - delta[head : head + 1, rows])).astype(BF16)
                value_part = dot_nn(probs.astype(BF16), grad)
                key_part = dot_nn(grad_scores, query)
                query_part = dot_nn(k_t[lanes, keys], grad_scores)
                value_sum = value_part if value_sum is None else value_sum + value_part
                key_sum = key_part if key_sum is None else key_sum + key_part
                if other == 0:
                    dq_t[lanes, rows] = query_part
                else:
                    dq_t[lanes, rows] += query_part
        grads_ref[1, keys, :] = key_sum.astype(BF16)
        grads_ref[2, keys, :] = value_sum.astype(BF16)
    grads_ref[0] = (dq_t[...].T * HEAD_DIM ** (-0.5)).astype(BF16)


def attn_forward(segments, qkv, width):
    length = qkv.shape[0]
    pairs = width // LANES
    block = min(256, length)
    column = lambda first: pl.BlockSpec((length, LANES), lambda p: (0, first * pairs + p))
    whole = lambda shape: pl.BlockSpec(shape, lambda p: (0, 0))
    return pl.pallas_call(
        functools.partial(attn_forward_kernel, block=block),
        grid=(pairs,),
        in_specs=[whole((length, 1)), whole((1, length)), column(0), column(1), column(2)],
        out_specs=[
            pl.BlockSpec((length, LANES), lambda p: (0, p)),
            pl.BlockSpec((1, 8, length), lambda p: (p, 0, 0)),
        ],
        out_shape=[
            jax.ShapeDtypeStruct((length, width), BF16),
            jax.ShapeDtypeStruct((pairs, 8, length), F32),
        ],
        scratch_shapes=[pltpu.VMEM((length, length), F32), pltpu.VMEM((LANES, length), BF16)],
        compiler_params=pltpu.CompilerParams(vmem_limit_bytes=VMEM_BYTES),
        cost_estimate=pl.CostEstimate(
            flops=4 * length * length * width,
            bytes_accessed=8 * length * width,
            transcendentals=length * length * width // (2 * HEAD_DIM),
        ),
        name="attn_forward",
    )(segments.reshape(length, 1), segments.reshape(1, length), qkv, qkv, qkv)


def attn_backward(segments, qkv, mixed, lse, grad_mixed, width, after):
    length = qkv.shape[0]
    pairs = width // LANES
    block = min(256, length)
    column = lambda first: pl.BlockSpec((length, LANES), lambda p: (0, first * pairs + p))
    whole = lambda shape: pl.BlockSpec(shape, lambda p: (0, 0))
    return pl.pallas_call(
        without(functools.partial(attn_backward_kernel, block=block), 8),
        grid=(pairs,),
        in_specs=[
            whole((length, 1)),
            whole((1, length)),
            column(0),
            column(1),
            column(2),
            pl.BlockSpec((length, LANES), lambda p: (0, p)),
            pl.BlockSpec((1, 8, length), lambda p: (p, 0, 0)),
            pl.BlockSpec((length, LANES), lambda p: (0, p)),
            pl.BlockSpec(memory_space=pl.ANY),
        ],
        out_specs=pl.BlockSpec((3, length, LANES), lambda p: (0, 0, p)),
        out_shape=jax.ShapeDtypeStruct((3, length, width), BF16),
        scratch_shapes=[
            pltpu.VMEM((length, length), F32),
            pltpu.VMEM((LANES, length), BF16),
            pltpu.VMEM((8, length), F32),
            pltpu.VMEM((LANES, length), F32),
        ],
        compiler_params=pltpu.CompilerParams(vmem_limit_bytes=VMEM_BYTES),
        cost_estimate=pl.CostEstimate(
            flops=10 * length * length * width,
            bytes_accessed=16 * length * width,
            transcendentals=length * length * width // (2 * HEAD_DIM),
        ),
        name="attn_backward",
    )(segments.reshape(length, 1), segments.reshape(1, length), qkv, qkv, qkv, mixed, lse, grad_mixed, after)


def piece_blocks(count):
    far = count // 4
    half = far // 2
    near, by_y, by_x, both = (list(range(i * far, (i + 1) * far)) for i in range(4))
    return [
        both[:half] + by_x[:half],
        both[half:] + by_y[half:],
        by_y[:half],
        by_x[half:],
        near,
    ]


def store_pieces(order, grad, piece_refs, columns):
    count = order.shape[0]
    rows = grad.shape[0] // count
    for blocks, ref in zip(piece_blocks(count), piece_refs):
        for place, block in enumerate(blocks):
            first = pl.multiple_of(order[block] * rows, rows)
            ref[place * rows : (place + 1) * rows, columns] = grad[pl.ds(first, rows), :]


def piece_shapes(count, rows, columns):
    return [
        jax.ShapeDtypeStruct((len(blocks) * rows, columns), BF16) for blocks in piece_blocks(count)
    ]


def whole_spec(shape, **options):
    return pl.BlockSpec(shape, lambda step: (0,) * len(shape), **options)


def norm_kernel(*refs, residual):
    if residual:
        x_ref, own_ref, other_ref, shift_ref, gain_ref, bias_ref, n_ref, nt_ref, hidden_ref = refs
        values = (
            x_ref[...].astype(F32)
            + (own_ref[...].astype(F32) + other_ref[...].astype(F32))
            + shift_ref[...]
        )
        hidden_ref[...] = values
    else:
        x_ref, gain_ref, bias_ref, n_ref, nt_ref = refs
        values = x_ref[...].astype(F32)
    scaled, _ = normalize(values)
    normed = (scaled * gain_ref[...] + bias_ref[...]).astype(BF16)
    n_ref[...] = normed
    nt_ref[...] = normed.T


def norm_rows(x, gain, bias, partials=None, shift=None):
    length, width = x.shape
    block = min(256, length)
    row = pl.BlockSpec((block, width), lambda step: (step, 0))
    vector = whole_spec((1, width))
    residual = partials is not None
    operands = [x] + (list(partials) + [shift.reshape(1, width)] if residual else [])
    operands += [gain.reshape(1, width), bias.reshape(1, width)]
    return pl.pallas_call(
        functools.partial(norm_kernel, residual=residual),
        grid=(length // block,),
        in_specs=[row] + ([row, row, vector] if residual else []) + [vector, vector],
        out_specs=[row, pl.BlockSpec((width, block), lambda step: (0, step))]
        + ([row] if residual else []),
        out_shape=[
            jax.ShapeDtypeStruct((length, width), BF16),
            jax.ShapeDtypeStruct((width, length), BF16),
        ]
        + ([jax.ShapeDtypeStruct((length, width), F32)] if residual else []),
        compiler_params=pltpu.CompilerParams(vmem_limit_bytes=VMEM_BYTES),
        cost_estimate=pl.CostEstimate(
            flops=20 * length * width, bytes_accessed=14 * length * width, transcendentals=length
        ),
        name="norm_two" if residual else "norm_one",
    )(*operands)


def norm_back_kernel(hidden_ref, g_ref, own_ref, other_ref, gain_ref, grad_ref, low_ref, low_t_ref, sums_ref):
    scaled, inverse = normalize(hidden_ref[...])
    incoming = own_ref[...].astype(F32) + other_ref[...].astype(F32)
    grad = g_ref[...].astype(F32) + norm_back(incoming, scaled, inverse, gain_ref[...])
    grad_ref[...] = grad
    low_ref[...] = grad.astype(BF16)
    low_t_ref[...] = grad.astype(BF16).T

    @pl.when(pl.program_id(0) == 0)
    def _():
        sums_ref[...] = jnp.zeros_like(sums_ref)

    sums_ref[0:1, :] += jnp.sum(grad, axis=0, keepdims=True)
    sums_ref[1:2, :] += jnp.sum(incoming * scaled, axis=0, keepdims=True)
    sums_ref[2:3, :] += jnp.sum(incoming, axis=0, keepdims=True)


def norm_back_rows(hidden, grad, partials, gain):
    length, width = hidden.shape
    block = min(256, length)
    row = pl.BlockSpec((block, width), lambda step: (step, 0))
    return pl.pallas_call(
        norm_back_kernel,
        grid=(length // block,),
        in_specs=[row, row, row, row, whole_spec((1, width))],
        out_specs=[
            row,
            row,
            pl.BlockSpec((width, block), lambda step: (0, step)),
            whole_spec((8, width)),
        ],
        out_shape=[
            jax.ShapeDtypeStruct((length, width), F32),
            jax.ShapeDtypeStruct((length, width), BF16),
            jax.ShapeDtypeStruct((width, length), BF16),
            jax.ShapeDtypeStruct((8, width), F32),
        ],
        compiler_params=pltpu.CompilerParams(vmem_limit_bytes=VMEM_BYTES),
        cost_estimate=pl.CostEstimate(
            flops=30 * length * width, bytes_accessed=16 * length * width, transcendentals=length
        ),
        name="norm_two_back",
    )(hidden, grad, *partials, gain.reshape(1, width))


def mlp_kernel(order, n_ref, g_ref, nt_ref, gt_ref, b_ref, w_ref, *refs, block, with_previous, cube):
    if with_previous:
        (before_out, before_gn), refs = refs[:2], refs[2:]
    (out_ref, gn_ref), refs = refs[:2], refs[2:]
    grad_refs, (gb_ref, out_acc, gn_acc, act, gpre, grad_w) = refs[:-6], refs[-6:]
    step = pl.program_id(0)
    length = n_ref.shape[0]
    tile = w_ref.shape[1] // 2
    ups, downs = slice(0, tile), slice(tile, 2 * tile)

    @pl.when(step == 0)
    def _():
        if with_previous:
            out_acc[...] = before_out[...].astype(F32)
            gn_acc[...] = before_gn[...].astype(F32)
        else:
            out_acc[...] = jnp.zeros_like(out_acc)
            gn_acc[...] = jnp.zeros_like(gn_acc)

    bias_sum = jnp.zeros(gb_ref.shape, F32)
    for first in range(0, length, block):
        rows = slice(first, first + block)
        unit = dot_nn(n_ref[rows, :], w_ref[:, ups]) + b_ref[...]
        grad = dot_nn(g_ref[rows, :], w_ref[:, downs])
        square = unit * unit
        curve = jnp.tanh(0.7978845608028654 * (unit + 0.044715 * (square * unit)))
        half = 0.5 + 0.5 * curve
        slope = half + (0.5 * unit) * (1.0 - curve * curve) * (
            0.7978845608028654 + (3 * 0.044715 * 0.7978845608028654) * square
        )
        active = (unit * half).astype(BF16)
        grad_pre = (grad * slope).astype(BF16)
        act[rows, :] = active
        gpre[rows, :] = grad_pre
        bias_sum = bias_sum + jnp.sum(grad_pre.astype(F32), axis=0, keepdims=True)
        out_acc[rows, :] += dot_nt(active, w_ref[:, downs])
        gn_acc[rows, :] += dot_nt(grad_pre, w_ref[:, ups])
    gb_ref[...] = bias_sum
    for columns, left, right in ((ups, nt_ref, gpre), (downs, gt_ref, act)):
        if cube:
            grad_w[...] = dot_nn(left[...], right[...]).astype(BF16)
            store_pieces(order, grad_w, grad_refs, columns)
        else:
            grad_refs[0][:, columns] = dot_nn(left[...], right[...]).astype(BF16)

    @pl.when(step == pl.num_programs(0) - 1)
    def _():
        out_ref[...] = out_acc[...].astype(BF16)
        gn_ref[...] = gn_acc[...].astype(BF16)


def mlp(order, normed, grad, normed_t, grad_t, weights, bias, previous, cube):
    length, width = normed.shape
    units = weights.shape[1] // 2
    tile = min(TILE, units)
    at_tile = lambda rows, columns: pl.BlockSpec((rows, columns), lambda u, o: (0, u))
    fixed = lambda shape: pl.BlockSpec(shape, lambda u, o: (0, 0))
    once = lambda shape: pl.BlockSpec(shape, lambda u, o: (0, 0), pipeline_mode=pl.Buffered(1))
    if cube:
        count = order.shape[0]
        grad_shapes = piece_shapes(count, width // count, 2 * units)
    else:
        grad_shapes = [jax.ShapeDtypeStruct((width, 2 * units), BF16)]
    results = pl.pallas_call(
        functools.partial(
            mlp_kernel, block=min(256, length), with_previous=bool(previous), cube=cube
        ),
        grid_spec=pltpu.PrefetchScalarGridSpec(
            num_scalar_prefetch=1,
            grid=(units // tile,),
            in_specs=[
                once((length, width)),
                once((length, width)),
                once((width, length)),
                once((width, length)),
                at_tile(1, tile),
                at_tile(width, 2 * tile),
            ]
            + [once((length, width)) for _ in previous],
            out_specs=[fixed((length, width)), fixed((length, width))]
            + [at_tile(shape.shape[0], 2 * tile) for shape in grad_shapes]
            + [at_tile(1, tile)],
            scratch_shapes=[
                pltpu.VMEM((length, width), F32),
                pltpu.VMEM((length, width), F32),
                pltpu.VMEM((length, tile), BF16),
                pltpu.VMEM((length, tile), BF16),
                pltpu.VMEM((width, tile), BF16),
            ],
        ),
        out_shape=[jax.ShapeDtypeStruct((length, width), BF16)] * 2
        + grad_shapes
        + [jax.ShapeDtypeStruct((1, units), F32)],
        compiler_params=pltpu.CompilerParams(vmem_limit_bytes=VMEM_BYTES),
        cost_estimate=pl.CostEstimate(
            flops=12 * length * width * units,
            bytes_accessed=12 * length * width + 8 * width * units,
            transcendentals=length * units,
        ),
        name="mlp_second" if previous else "mlp_first",
    )(order, normed, grad, normed_t, grad_t, bias.reshape(1, units), weights, *previous)
    return results[0], results[1], results[2:-1], results[-1]


def qkv_kernel(n_ref, b_ref, w_ref, out_ref):
    scale = jnp.where(pl.program_id(0) == 0, HEAD_DIM ** (-0.5), 1.0)
    length = n_ref.shape[0]
    step = min(256, length)
    for first in range(0, length, step):
        span = slice(first, first + step)
        out_ref[span, :] = ((dot_nn(n_ref[span, :], w_ref[...]) + b_ref[...]) * scale).astype(BF16)


def qkv_project(normed, weights, bias):
    length, width = normed.shape
    columns = weights.shape[1] // 4
    at_tile = lambda rows: pl.BlockSpec((rows, columns), lambda k: (0, k))
    return pl.pallas_call(
        qkv_kernel,
        grid=(3,),
        in_specs=[
            whole_spec((length, width), pipeline_mode=pl.Buffered(1)), at_tile(1), at_tile(width)
        ],
        out_specs=at_tile(length),
        out_shape=jax.ShapeDtypeStruct((length, 3 * columns), BF16),
        compiler_params=pltpu.CompilerParams(vmem_limit_bytes=VMEM_BYTES),
        cost_estimate=pl.CostEstimate(
            flops=6 * length * width * columns,
            bytes_accessed=2 * length * width + 6 * width * columns + 6 * length * columns,
            transcendentals=0,
        ),
        name="qkv_project",
    )(normed, bias.reshape(1, 3 * columns), weights)


def weight_kernel(order, nt_ref, grads_ref, gt_ref, mixed_ref, order_only, *refs):
    piece_refs, grad = refs[:5], refs[5]
    part = pl.program_id(0)

    @pl.when(part < 3)
    def _():
        grad[...] = dot_nn(nt_ref[...], grads_ref[0]).astype(BF16)

    @pl.when(part == 3)
    def _():
        grad[...] = dot_nn(gt_ref[...], mixed_ref[...]).astype(BF16)

    store_pieces(order, grad, piece_refs, slice(None))


def without(kernel, place):
    return lambda *refs: kernel(*refs[:place], *refs[place + 1 :])


ORDER_ONLY = pl.BlockSpec(memory_space=pl.ANY)


def weight_grads(order, normed_t, grads, grad_t, mixed, after):
    width, length = normed_t.shape
    columns = grads.shape[2]
    shapes = piece_shapes(order.shape[0], width // order.shape[0], 4 * columns)
    fixed = lambda shape: pl.BlockSpec(shape, lambda k, o: (0, 0), pipeline_mode=pl.Buffered(1))
    return pl.pallas_call(
        weight_kernel,
        grid_spec=pltpu.PrefetchScalarGridSpec(
            num_scalar_prefetch=1,
            grid=(4,),
            in_specs=[
                fixed((width, length)),
                pl.BlockSpec((1, length, columns), lambda k, o: (jnp.minimum(k, 2), 0, 0)),
                fixed((width, length)),
                fixed((length, columns)),
                ORDER_ONLY,
            ],
            out_specs=[
                pl.BlockSpec((shape.shape[0], columns), lambda k, o: (0, k)) for shape in shapes
            ],
            scratch_shapes=[pltpu.VMEM((width, columns), BF16)],
        ),
        out_shape=shapes,
        compiler_params=pltpu.CompilerParams(vmem_limit_bytes=VMEM_BYTES),
        cost_estimate=pl.CostEstimate(
            flops=8 * length * width * columns,
            bytes_accessed=4 * length * width + 16 * width * columns,
            transcendentals=0,
        ),
        name="weight_grads",
    )(order, normed_t, grads, grad_t, mixed, after)


def qkv_back_kernel(grads_ref, w_ref, out_ref):
    columns = grads_ref.shape[2]
    total = None
    for k in range(3):
        part = dot_nt(grads_ref[k], w_ref[:, k * columns : (k + 1) * columns])
        total = part if total is None else total + part
    out_ref[...] = total.astype(BF16)


def qkv_back(grads, weights, after):
    _, length, columns = grads.shape
    width = weights.shape[0]
    block = min(256, length)
    return pl.pallas_call(
        without(qkv_back_kernel, 2),
        grid=(length // block,),
        in_specs=[
            pl.BlockSpec((3, block, columns), lambda i: (0, i, 0)),
            pl.BlockSpec((width, 4 * columns), lambda i: (0, 0), pipeline_mode=pl.Buffered(1)),
            ORDER_ONLY,
        ],
        out_specs=pl.BlockSpec((block, width), lambda i: (i, 0)),
        out_shape=jax.ShapeDtypeStruct((length, width), BF16),
        compiler_params=pltpu.CompilerParams(vmem_limit_bytes=VMEM_BYTES),
        cost_estimate=pl.CostEstimate(
            flops=6 * length * width * columns,
            bytes_accessed=2 * length * width + 6 * width * columns + 6 * length * columns,
            transcendentals=0,
        ),
        name="qkv_back",
    )(grads, weights, after)


def added(*terms):
    total = terms[0].astype(F32)
    for term in terms[1:]:
        total = total + term.astype(F32)
    return total.astype(BF16)


def first_sums_kernel(from_x, from_y, keep_y, keep_x, y_ref, x_ref):
    half = y_ref.shape[0]
    y_ref[...] = added(keep_y[...], from_x[:half, :])
    x_ref[...] = added(keep_x[...], from_y[:half, :])


def second_sums_kernel(from_x, from_y, near, from_y2, from_x2, *outs, with_small):
    if with_small:
        small, outs = outs[0], outs[1:]
    far = len(outs)
    half = from_y2.shape[0]
    rows = half * 2 // far
    if with_small:
        values = small[...]
        high = values.astype(BF16).astype(F32)
        extra = jnp.concatenate([high, values - high], axis=0).astype(BF16)
    for i, out in enumerate(outs):
        first, second, place = (from_x, from_y2, i) if i < far // 2 else (from_y, from_x2, i - far // 2)
        out[:rows, :] = added(
            near[i * rows : (i + 1) * rows, :],
            first[half + place * rows : half + (place + 1) * rows, :],
            second[place * rows : (place + 1) * rows, :],
        )
        if with_small:
            out[rows:, :] = extra


def z_sums_kernel(z_ref, from_x, from_y, near, from_y2, from_x2, out, *, far):
    half = from_y2.shape[0]
    rows = half * 2 // far
    for i in range(far):
        first, second, place = (from_x, from_y2, i) if i < far // 2 else (from_y, from_x2, i - far // 2)
        target = pl.multiple_of((z_ref[0] ^ i) * rows, rows)
        out[pl.ds(target, rows), :] = added(
            near[i * rows : (i + 1) * rows, :],
            first[half + place * rows : half + (place + 1) * rows, :],
            second[place * rows : (place + 1) * rows, :],
        )


def weights_last_kernel(*refs):
    parts, outs, small = refs[:-5], refs[-5:-1], refs[-1]
    total = parts[0][...].astype(F32)
    for part in parts[1:]:
        total = total + part[...].astype(F32)
    rows, columns = outs[0].shape
    for k, out in enumerate(outs):
        out[...] = total[:rows, k * columns : (k + 1) * columns]
    extra = small.shape[0]
    small[...] = total[rows : rows + extra, :] + total[rows + extra :, :]


def units_last_kernel(first_ref, second_ref, up_ref, down_ref, *, tile):
    units = up_ref.shape[1] // 2
    for index, ref in enumerate((first_ref, second_ref)):
        for first in range(0, units, tile):
            columns = slice(index * units + first, index * units + first + tile)
            up_ref[:, columns] = ref[:, 2 * first : 2 * first + tile].astype(F32)
            down_ref[:, columns] = ref[:, 2 * first + tile : 2 * first + 2 * tile].astype(F32)


def shards_kernel(w_up, w_down, first_ref, second_ref, *, tile):
    units = first_ref.shape[1] // 2
    for index, ref in enumerate((first_ref, second_ref)):
        for first in range(0, units, tile):
            columns = slice(index * units + first, index * units + first + tile)
            ref[:, 2 * first : 2 * first + tile] = w_up[:, columns]
            ref[:, 2 * first + tile : 2 * first + 2 * tile] = w_down[:, columns]


def sums_call(kernel, operands, shapes, after, name):
    body = kernel if after is None else without(kernel, 0)
    vmem = pl.BlockSpec(memory_space=pltpu.VMEM)
    return pl.pallas_call(
        body,
        in_specs=([pl.BlockSpec(memory_space=pl.ANY)] if after is not None else [])
        + [vmem] * len(operands),
        out_specs=[vmem] * len(shapes),
        out_shape=shapes,
        compiler_params=pltpu.CompilerParams(vmem_limit_bytes=VMEM_BYTES),
        cost_estimate=pl.CostEstimate(flops=0, bytes_accessed=1024 * 1024, transcendentals=0),
        name=name,
    )(*([after] if after is not None else []), *operands)


def flipped(sizes):
    return 1 if sizes["h"] * sizes["l"] == 2 else 0


def moves(sizes):
    groups, ranks, inner = sizes["a"], sizes["h"] * sizes["l"], sizes["l"]
    far = groups // 2
    flip = flipped(sizes)
    swap_to = {}
    for group in range(2):
        for part in range(ranks):
            place = (part % 2 ^ flip) * ranks + group * (ranks // 2) + part // 2
            swap_to[group * ranks + part] = place

    def swap(values, inverse=False):
        pairs = [(to, frm) if inverse else (frm, to) for frm, to in swap_to.items()]
        return lax.ppermute(values, SWAP, pairs)

    def swap_hop(values, a_mask, inverse=False):
        pairs = []
        for a in range(groups):
            for frm, to in swap_to.items():
                one, two = a * 2 * ranks + frm, (a ^ a_mask) * 2 * ranks + to
                pairs.append((two, one) if inverse else (one, two))
        return lax.ppermute(values, ALL, pairs)

    def hop(values, a_mask, h_mask):
        pairs = []
        for a in range(groups):
            for c in range(2):
                for h in range(2):
                    pairs.append(((a * 2 + c) * 2 + h, ((a ^ a_mask) * 2 + c) * 2 + (h ^ h_mask)))
        return lax.ppermute(values, ("z", "y", "c", "h"), pairs)

    def scatter_near(pieces, after):
        from_x, from_y = hop(pieces[0], 0, 1), hop(pieces[1], 1, 0)
        half, columns = pieces[2].shape
        y_sum, x_sum = sums_call(
            first_sums_kernel,
            [from_x, from_y, pieces[2], pieces[3]],
            [jax.ShapeDtypeStruct((half, columns), BF16)] * 2,
            after,
            "sums_one",
        )
        return from_x, from_y, pieces[4], y_sum, x_sum

    def far_sums(state, small, after):
        from_x, from_y, near, y_sum, x_sum = state
        columns = near.shape[1]
        from_y2, from_x2 = hop(y_sum, 1, 0), hop(x_sum, 0, 1)
        rows = near.shape[0] // far + sum(2 * values.shape[0] for values in small)
        return sums_call(
            functools.partial(second_sums_kernel, with_small=bool(small)),
            [from_x, from_y, near, from_y2, from_x2] + small,
            [jax.ShapeDtypeStruct((rows, columns), BF16)] * far,
            after,
            "sums_two",
        )

    def z_sums(state, after):
        from_x, from_y, near, y_sum, x_sum = state
        from_y2, from_x2 = hop(y_sum, 1, 0), hop(x_sum, 0, 1)
        vmem = pl.BlockSpec(memory_space=pltpu.VMEM)
        return pl.pallas_call(
            without(functools.partial(z_sums_kernel, far=far), 6),
            in_specs=[pl.BlockSpec(memory_space=pltpu.SMEM)] + [vmem] * 5 + [ORDER_ONLY],
            out_specs=vmem,
            out_shape=jax.ShapeDtypeStruct(near.shape, BF16),
            compiler_params=pltpu.CompilerParams(vmem_limit_bytes=VMEM_BYTES),
            name="sums_two_z",
        )(lax.axis_index("z").reshape(1), from_x, from_y, near, from_y2, from_x2, after)

    def far_parts(sums):
        return [swap_hop(sums[i], 2 * i, inverse=True) for i in range(far)]

    def near_sum(values):
        values = values + lax.ppermute(values, "c", [(0, 1), (1, 0)])
        values = values + hop(values, 0, 1)
        values = values + hop(values, 1, 0)
        return lax.psum(values, "l") if inner > 1 else values

    a, h = lax.axis_index(("z", "y")), lax.axis_index("h")
    order = []
    for a_low, h_mask in ((0, 0), (1, 0), (0, 1), (1, 1)):
        for i in range(far):
            order.append((a ^ (2 * i + a_low)) * 2 + (h ^ h_mask))
    return swap, scatter_near, far_sums, z_sums, far_parts, near_sum, jnp.stack(order).astype(jnp.int32)


def per_device(sizes, *arguments):
    (
        block_input, segment_ids, ln1_gain, ln1_bias, w_query, w_key, w_value, b_query, b_value,
        w_out, b_out, ln2_gain, ln2_bias, w_up, b_up, w_down, b_down, out_grad,
    ) = arguments
    ranks = sizes["h"] * sizes["l"]
    rank = lax.axis_index("l") * 2 + (lax.axis_index("c") ^ flipped(sizes))
    own_rows, width = block_input.shape
    head_width = w_query.shape[1]
    unit_width = w_up.shape[1]
    half_units = unit_width // 2
    tile = min(TILE, half_units)
    swap, scatter_near, far_sums, z_sums, far_parts, near_sum, order = moves(sizes)

    def partner(values):
        return lax.ppermute(values, "c", [(0, 1), (1, 0)])

    def tp_gather(values):
        if ranks != 2:
            return lax.all_gather(values, TP, axis=0, tiled=True)
        theirs = partner(values)
        return jnp.where(
            rank == 0,
            jnp.concatenate([values, theirs], axis=0),
            jnp.concatenate([theirs, values], axis=0),
        )

    def tp_terms(values):
        if ranks != 2:
            others = lax.psum(values.astype(F32), TP) - values.astype(F32)
            return values, others.astype(BF16)
        return values, partner(values)

    def own(values):
        return lax.dynamic_slice_in_dim(values, rank * own_rows, own_rows)

    def tp_scatter(values):
        if ranks != 2:
            return lax.psum_scatter(values, TP, scatter_dimension=0, tiled=True).astype(F32)
        theirs = lax.dynamic_slice_in_dim(values, (1 - rank) * own_rows, own_rows)
        return own(values).astype(F32) + partner(theirs).astype(F32)

    own_input = swap(block_input)
    segments = swap(segment_ids)
    own_grad = swap(out_grad)
    shard_first, shard_second = sums_call(
        functools.partial(shards_kernel, tile=tile),
        [w_up, w_down],
        [jax.ShapeDtypeStruct(w_up.shape, BF16)] * 2,
        None,
        "mlp_shards",
    )
    early_attn = lax.all_gather(
        jnp.concatenate([w_query, w_key, w_value, w_out], axis=1), ("z", "y", "c"), axis=0, tiled=True
    )
    early_first = lax.all_gather(shard_first, ("z", "y", "c"), axis=0, tiled=True)
    shard_second = swap(shard_second)
    bias_query = lax.dynamic_slice_in_dim(b_query, rank * head_width, head_width)
    bias_value = lax.dynamic_slice_in_dim(b_value, rank * head_width, head_width)
    bias_up = lax.dynamic_slice_in_dim(b_up, rank * unit_width, unit_width)

    rows_in = tp_gather(own_input)
    grad_rows = tp_gather(own_grad)
    grad_rows_t = grad_rows.T
    normed, normed_t = norm_rows(rows_in, ln1_gain, ln1_bias)
    early_attn, normed, segments, grad_rows, grad_rows_t, shard_second = lax.optimization_barrier(
        (early_attn, normed, segments, grad_rows, grad_rows_t, shard_second)
    )
    full_second = lax.all_gather(shard_second, ("z", "y", "h"), axis=0, tiled=True)
    full_attn = swap(early_attn)
    biases = jnp.concatenate([bias_query, jnp.zeros((head_width,), F32), bias_value])
    qkv = qkv_project(normed, full_attn, biases)
    full_out = full_attn[:, 3 * head_width :]
    early_first, qkv = lax.optimization_barrier((early_first, qkv))
    full_first = swap(early_first)
    mixed, lse = attn_forward(segments, qkv, head_width)
    attended = tp_terms(dot_nt(mixed, full_out).astype(BF16))
    normed_two, normed_two_t, hidden = norm_rows(rows_in, ln2_gain, ln2_bias, attended, b_out)

    out_part, gn_part, first_grads, bias_first = mlp(
        order, normed_two, grad_rows, normed_two_t, grad_rows_t, full_first,
        bias_up[:half_units], (), True,
    )
    full_second, gn_part = lax.optimization_barrier((full_second, gn_part))
    out_part, gn_part, second_grads, bias_second = mlp(
        order, normed_two, grad_rows, normed_two_t, grad_rows_t, full_second,
        bias_up[half_units:], (out_part, gn_part), False,
    )
    first_state = scatter_near(first_grads, gn_part)
    gn_part, second_grads, first_state = lax.optimization_barrier(
        (gn_part, second_grads[0], first_state)
    )
    own_output = (own(hidden) + tp_scatter(out_part) + b_down).astype(BF16)

    grad_hidden, grad_attended, grad_attended_t, sums_two = norm_back_rows(
        hidden, grad_rows, tp_terms(gn_part), ln2_gain
    )
    first_sums = z_sums(first_state, grad_attended)
    second_grads, first_sums = lax.optimization_barrier((second_grads, first_sums))
    second_grads = swap(second_grads, inverse=True)
    grad_mixed = dot_nn(grad_attended, full_out).astype(BF16)
    first_mlp = lax.psum_scatter(first_sums, "z", scatter_dimension=0, tiled=True)
    grads = attn_backward(segments, qkv, mixed, lse, grad_mixed, head_width, first_sums)
    block_rows = w_query.shape[0]
    pieces = weight_grads(order, normed_t, grads, grad_attended_t, mixed, grads)
    grad_normed_part = qkv_back(grads, full_attn, pieces[0])
    second_grads, first_mlp, grad_normed_part = lax.optimization_barrier(
        (second_grads, first_mlp, grad_normed_part)
    )
    second_mlp = lax.psum_scatter(second_grads, ("z", "y", "c"), scatter_dimension=0, tiled=True)
    first_mlp = swap(first_mlp, inverse=True)
    state = scatter_near(pieces, grad_normed_part)
    grad_normed_part, state = lax.optimization_barrier((grad_normed_part, state))
    grad_normed = tp_scatter(grad_normed_part)
    own_scaled, own_inverse = normalize(own_input.astype(F32))
    grad_own = own(grad_hidden) + norm_back(grad_normed, own_scaled, own_inverse, ln1_gain)
    grad_own = grad_own.astype(BF16)

    def place_part(values, full):
        return lax.dynamic_update_slice_in_dim(
            jnp.zeros((full,), F32), values, rank * values.shape[0], 0
        )

    sums = jnp.concatenate(
        [
            jnp.sum(grad_normed * own_scaled, axis=0),
            jnp.sum(grad_normed, axis=0),
            place_part(jnp.sum(grads[0].astype(F32), axis=0), width),
            place_part(jnp.sum(grads[2].astype(F32), axis=0), width),
            (sums_two[:3] * (1.0 / ranks)).reshape(-1),
            jnp.sum(own_grad.astype(F32), axis=0),
            place_part(jnp.concatenate([bias_first[0], bias_second[0]]), b_up.shape[0]),
        ]
    )
    columns = pieces[0].shape[1]
    filled = sums.shape[0]
    sums = jnp.pad(sums, (0, -filled % (8 * columns))).reshape(-1, columns)
    sums = near_sum(sums)
    shard = jax.ShapeDtypeStruct((block_rows, unit_width), F32)
    grad_w_up, grad_w_down = sums_call(
        functools.partial(units_last_kernel, tile=tile),
        [first_mlp, second_mlp],
        [shard, shard],
        None,
        "units_last",
    )
    last_sums = far_sums(state, [sums], None)
    own_output, grad_own, *last_sums = lax.optimization_barrier((own_output, grad_own, *last_sums))
    output = swap(own_output, inverse=True)
    grad_input = swap(grad_own, inverse=True)
    *late, sums = sums_call(
        weights_last_kernel,
        far_parts(last_sums),
        [jax.ShapeDtypeStruct((block_rows, head_width), F32)] * 4
        + [jax.ShapeDtypeStruct(sums.shape, F32)],
        grad_w_up,
        "sums_last",
    )
    sums = sums.reshape(-1)
    small = [sums[i * width : (i + 1) * width] for i in range(8)]
    return (
        output, grad_input, small[0], small[1],
        late[0], late[1], late[2], small[2], small[3], late[3], small[4], small[5], small[6],
        grad_w_up, sums[8 * width : filled], grad_w_down, small[7],
    )


def solution(mesh):
    groups, ranks = mesh.shape["dp"], mesh.shape["tensor"]
    sizes = {"a": groups // 2, "h": 2, "l": ranks // 2}
    fine = Mesh(mesh.devices.reshape(groups // 4, 2, 2, 2, ranks // 2), ALL)
    rows = P(ALL, None)
    block = P(("z", "y", "c"), ("h", "l"))
    return jax.shard_map(
        functools.partial(per_device, sizes),
        mesh=fine,
        in_specs=(
            rows, P(("z", "y", "c")), P(), P(), block, block, block, P(), P(), block, P(), P(), P(),
            block, P(), block, P(), rows,
        ),
        out_specs=(
            rows, rows, P(), P(), block, block, block, P(), P(), block, P(), P(), P(), block, P(),
            block, P(),
        ),
        check_vma=False,
    )
```

```python
import functools

import jax
import jax.numpy as jnp
from jax import lax
from jax.experimental import pallas as pl
from jax.experimental.pallas import tpu as pltpu
from jax.sharding import Mesh
from jax.sharding import PartitionSpec as P

HEAD_DIM = 64
LANES = 128
TILE = 512
MASKED = -1e30
VMEM_BYTES = 60 * 1024 * 1024
F32 = jnp.float32
BF16 = jnp.bfloat16
TP = ("l", "c")
SWAP = ("c", "h", "l")
ALL = ("z", "y", "c", "h", "l")


def normalize(values):
    center = values - jnp.mean(values, axis=-1, keepdims=True)
    spread = jnp.mean(center * center, axis=-1, keepdims=True)
    inverse = lax.rsqrt(spread + 1e-05)
    return center * inverse, inverse


def norm_back(grad_in, scaled, inverse, gain_vec):
    local_grad = grad_in * gain_vec
    return inverse * (
        local_grad
        - jnp.mean(local_grad, axis=-1, keepdims=True)
        - scaled * jnp.mean(local_grad * scaled, axis=-1, keepdims=True)
    )


def dot_nn(left, right):
    return lax.dot_general(left, right, (((1,), (0,)), ((), ())), preferred_element_type=F32)


def dot_nt(left, right):
    return lax.dot_general(left, right, (((1,), (1,)), ((), ())), preferred_element_type=F32)


def dot_tn(left, right):
    return lax.dot_general(left, right, (((0,), (0,)), ((), ())), preferred_element_type=F32)


def fill_bias(bias, seg_col, seg_row):
    length = bias.shape[0]
    block = min(256, length)
    for first in range(0, length, block):
        keys = lax.broadcasted_iota(jnp.int32, (block, length), 0) + first
        places = lax.broadcasted_iota(jnp.int32, (block, length), 1)
        same = seg_col[first : first + block, :] == seg_row[...]
        bias[first : first + block, :] = jnp.where(same & (keys <= places), 0.0, MASKED)


def head_lanes(values, head):
    lane = lax.broadcasted_iota(jnp.int32, values.shape, 1)
    inside = (lane >= head * HEAD_DIM) & (lane < (head + 1) * HEAD_DIM)
    return jnp.where(inside, values, jnp.zeros_like(values))


def attn_forward_kernel(seg_col, seg_row, q_ref, k_ref, v_ref, mixed_ref, lse_ref, bias, v_t, block):
    length = q_ref.shape[0]
    heads = LANES // HEAD_DIM

    @pl.when(pl.program_id(0) == 0)
    def _():
        fill_bias(bias, seg_col, seg_row)

    v_t[...] = v_ref[...].T
    for place in range(length // block):
        rows = slice(place * block, (place + 1) * block)
        outs = []
        for head in range(heads):
            query = head_lanes(q_ref[rows, :], head)
            scores = []
            peak = None
            for other in range(place + 1):
                keys = slice(other * block, (other + 1) * block)
                part = dot_nt(k_ref[keys, :], query) + bias[keys, rows]
                top = jnp.max(part, axis=0, keepdims=True)
                peak = top if peak is None else jnp.maximum(peak, top)
                scores.append(part)
            total = None
            acc = None
            for other in range(place + 1):
                keys = slice(other * block, (other + 1) * block)
                weight = jnp.exp(scores[other] - peak)
                part_sum = jnp.sum(weight, axis=0, keepdims=True)
                total = part_sum if total is None else total + part_sum
                part_out = dot_nn(
                    v_t[head * HEAD_DIM : (head + 1) * HEAD_DIM, keys], weight.astype(BF16)
                )
                acc = part_out if acc is None else acc + part_out
            outs.append(acc / total)
            lse_ref[0, head : head + 1, rows] = peak + jnp.log(total)
        mixed_ref[rows, :] = jnp.concatenate(outs, axis=0).T.astype(BF16)


def attn_backward_kernel(
    seg_col, seg_row, q_ref, k_ref, v_ref, mixed_ref, lse_ref, g_ref, grads_ref, bias, k_t, delta, dq_t, block
):
    length = q_ref.shape[0]
    heads = LANES // HEAD_DIM
    count = length // block

    @pl.when(pl.program_id(0) == 0)
    def _():
        fill_bias(bias, seg_col, seg_row)

    k_t[...] = k_ref[...].T
    product = (g_ref[...].astype(F32) * mixed_ref[...].astype(F32)).T
    for head in range(heads):
        delta[head : head + 1, :] = jnp.sum(
            product[head * HEAD_DIM : (head + 1) * HEAD_DIM, :], axis=0, keepdims=True
        )
    for other in range(count):
        keys = slice(other * block, (other + 1) * block)
        key_sum = None
        value_sum = None
        for head in range(heads):
            lanes = slice(head * HEAD_DIM, (head + 1) * HEAD_DIM)
            for place in range(other, count):
                rows = slice(place * block, (place + 1) * block)
                query = head_lanes(q_ref[rows, :], head)
                grad = head_lanes(g_ref[rows, :], head)
                scores = dot_nt(k_ref[keys, :], query) + bias[keys, rows]
                probs = jnp.exp(scores - lse_ref[0, head : head + 1, rows])
                grad_probs = dot_nt(v_ref[keys, :], grad)
                grad_scores = (probs * (grad_probs - delta[head : head + 1, rows])).astype(BF16)
                value_part = dot_nn(probs.astype(BF16), grad)
                key_part = dot_nn(grad_scores, query)
                query_part = dot_nn(k_t[lanes, keys], grad_scores)
                value_sum = value_part if value_sum is None else value_sum + value_part
                key_sum = key_part if key_sum is None else key_sum + key_part
                if other == 0:
                    dq_t[lanes, rows] = query_part
                else:
                    dq_t[lanes, rows] += query_part
        grads_ref[1, keys, :] = key_sum.astype(BF16)
        grads_ref[2, keys, :] = value_sum.astype(BF16)
    grads_ref[0] = (dq_t[...].T * HEAD_DIM ** (-0.5)).astype(BF16)


def attn_forward(segments, qkv, width):
    length = qkv.shape[0]
    pairs = width // LANES
    block = min(256, length)
    column = lambda first: pl.BlockSpec((length, LANES), lambda p: (0, first * pairs + p))
    whole = lambda shape: pl.BlockSpec(shape, lambda p: (0, 0))
    return pl.pallas_call(
        functools.partial(attn_forward_kernel, block=block),
        grid=(pairs,),
        in_specs=[whole((length, 1)), whole((1, length)), column(0), column(1), column(2)],
        out_specs=[
            pl.BlockSpec((length, LANES), lambda p: (0, p)),
            pl.BlockSpec((1, 8, length), lambda p: (p, 0, 0)),
        ],
        out_shape=[
            jax.ShapeDtypeStruct((length, width), BF16),
            jax.ShapeDtypeStruct((pairs, 8, length), F32),
        ],
        scratch_shapes=[pltpu.VMEM((length, length), F32), pltpu.VMEM((LANES, length), BF16)],
        compiler_params=pltpu.CompilerParams(vmem_limit_bytes=VMEM_BYTES),
        cost_estimate=pl.CostEstimate(
            flops=4 * length * length * width,
            bytes_accessed=8 * length * width,
            transcendentals=length * length * width // (2 * HEAD_DIM),
        ),
        name="attn_forward",
    )(segments.reshape(length, 1), segments.reshape(1, length), qkv, qkv, qkv)


def attn_backward(segments, qkv, mixed, lse, grad_mixed, width, after):
    length = qkv.shape[0]
    pairs = width // LANES
    block = min(256, length)
    column = lambda first: pl.BlockSpec((length, LANES), lambda p: (0, first * pairs + p))
    whole = lambda shape: pl.BlockSpec(shape, lambda p: (0, 0))
    return pl.pallas_call(
        without(functools.partial(attn_backward_kernel, block=block), 8),
        grid=(pairs,),
        in_specs=[
            whole((length, 1)),
            whole((1, length)),
            column(0),
            column(1),
            column(2),
            pl.BlockSpec((length, LANES), lambda p: (0, p)),
            pl.BlockSpec((1, 8, length), lambda p: (p, 0, 0)),
            pl.BlockSpec((length, LANES), lambda p: (0, p)),
            pl.BlockSpec(memory_space=pl.ANY),
        ],
        out_specs=pl.BlockSpec((3, length, LANES), lambda p: (0, 0, p)),
        out_shape=jax.ShapeDtypeStruct((3, length, width), BF16),
        scratch_shapes=[
            pltpu.VMEM((length, length), F32),
            pltpu.VMEM((LANES, length), BF16),
            pltpu.VMEM((8, length), F32),
            pltpu.VMEM((LANES, length), F32),
        ],
        compiler_params=pltpu.CompilerParams(vmem_limit_bytes=VMEM_BYTES),
        cost_estimate=pl.CostEstimate(
            flops=10 * length * length * width,
            bytes_accessed=16 * length * width,
            transcendentals=length * length * width // (2 * HEAD_DIM),
        ),
        name="attn_backward",
    )(segments.reshape(length, 1), segments.reshape(1, length), qkv, qkv, qkv, mixed, lse, grad_mixed, after)


def piece_blocks(count):
    far = count // 4
    half = far // 2
    near, by_y, by_x, both = (list(range(i * far, (i + 1) * far)) for i in range(4))
    return [
        both[:half] + by_x[:half],
        both[half:] + by_y[half:],
        by_y[:half],
        by_x[half:],
        near,
    ]


def store_pieces(order, grad, piece_refs, columns):
    count = order.shape[0]
    rows = grad.shape[0] // count
    for blocks, ref in zip(piece_blocks(count), piece_refs):
        for place, block in enumerate(blocks):
            first = pl.multiple_of(order[block] * rows, rows)
            ref[place * rows : (place + 1) * rows, columns] = grad[pl.ds(first, rows), :]


def piece_shapes(count, rows, columns):
    return [
        jax.ShapeDtypeStruct((len(blocks) * rows, columns), BF16) for blocks in piece_blocks(count)
    ]


def whole_spec(shape, **options):
    return pl.BlockSpec(shape, lambda step: (0,) * len(shape), **options)


def norm_kernel(*refs, residual):
    if residual:
        x_ref, own_ref, other_ref, shift_ref, gain_ref, bias_ref, n_ref, nt_ref, hidden_ref = refs
        values = (
            x_ref[...].astype(F32)
            + (own_ref[...].astype(F32) + other_ref[...].astype(F32))
            + shift_ref[...]
        )
        hidden_ref[...] = values
    else:
        x_ref, gain_ref, bias_ref, n_ref, nt_ref = refs
        values = x_ref[...].astype(F32)
    scaled, _ = normalize(values)
    normed = (scaled * gain_ref[...] + bias_ref[...]).astype(BF16)
    n_ref[...] = normed
    nt_ref[...] = normed.T


def norm_rows(x, gain, bias, partials=None, shift=None):
    length, width = x.shape
    block = min(256, length)
    row = pl.BlockSpec((block, width), lambda step: (step, 0))
    vector = whole_spec((1, width))
    residual = partials is not None
    operands = [x] + (list(partials) + [shift.reshape(1, width)] if residual else [])
    operands += [gain.reshape(1, width), bias.reshape(1, width)]
    return pl.pallas_call(
        functools.partial(norm_kernel, residual=residual),
        grid=(length // block,),
        in_specs=[row] + ([row, row, vector] if residual else []) + [vector, vector],
        out_specs=[row, pl.BlockSpec((width, block), lambda step: (0, step))]
        + ([row] if residual else []),
        out_shape=[
            jax.ShapeDtypeStruct((length, width), BF16),
            jax.ShapeDtypeStruct((width, length), BF16),
        ]
        + ([jax.ShapeDtypeStruct((length, width), F32)] if residual else []),
        compiler_params=pltpu.CompilerParams(vmem_limit_bytes=VMEM_BYTES),
        cost_estimate=pl.CostEstimate(
            flops=20 * length * width, bytes_accessed=14 * length * width, transcendentals=length
        ),
        name="norm_two" if residual else "norm_one",
    )(*operands)


def norm_back_kernel(hidden_ref, g_ref, own_ref, other_ref, gain_ref, grad_ref, low_ref, low_t_ref, sums_ref):
    scaled, inverse = normalize(hidden_ref[...])
    incoming = own_ref[...].astype(F32) + other_ref[...].astype(F32)
    grad = g_ref[...].astype(F32) + norm_back(incoming, scaled, inverse, gain_ref[...])
    grad_ref[...] = grad
    low_ref[...] = grad.astype(BF16)
    low_t_ref[...] = grad.astype(BF16).T

    @pl.when(pl.program_id(0) == 0)
    def _():
        sums_ref[...] = jnp.zeros_like(sums_ref)

    sums_ref[0:1, :] += jnp.sum(grad, axis=0, keepdims=True)
    sums_ref[1:2, :] += jnp.sum(incoming * scaled, axis=0, keepdims=True)
    sums_ref[2:3, :] += jnp.sum(incoming, axis=0, keepdims=True)


def norm_back_rows(hidden, grad, partials, gain):
    length, width = hidden.shape
    block = min(256, length)
    row = pl.BlockSpec((block, width), lambda step: (step, 0))
    return pl.pallas_call(
        norm_back_kernel,
        grid=(length // block,),
        in_specs=[row, row, row, row, whole_spec((1, width))],
        out_specs=[
            row,
            row,
            pl.BlockSpec((width, block), lambda step: (0, step)),
            whole_spec((8, width)),
        ],
        out_shape=[
            jax.ShapeDtypeStruct((length, width), F32),
            jax.ShapeDtypeStruct((length, width), BF16),
            jax.ShapeDtypeStruct((width, length), BF16),
            jax.ShapeDtypeStruct((8, width), F32),
        ],
        compiler_params=pltpu.CompilerParams(vmem_limit_bytes=VMEM_BYTES),
        cost_estimate=pl.CostEstimate(
            flops=30 * length * width, bytes_accessed=16 * length * width, transcendentals=length
        ),
        name="norm_two_back",
    )(hidden, grad, *partials, gain.reshape(1, width))


def mlp_kernel(order, n_ref, g_ref, nt_ref, gt_ref, b_ref, w_ref, *refs, block, with_previous, cube):
    if with_previous:
        (before_out, before_gn), refs = refs[:2], refs[2:]
    (out_ref, gn_ref), refs = refs[:2], refs[2:]
    grad_refs, (gb_ref, out_acc, gn_acc, act, gpre, grad_w) = refs[:-6], refs[-6:]
    step = pl.program_id(0)
    length = n_ref.shape[0]
    tile = w_ref.shape[1] // 2
    ups, downs = slice(0, tile), slice(tile, 2 * tile)

    @pl.when(step == 0)
    def _():
        if with_previous:
            out_acc[...] = before_out[...].astype(F32)
            gn_acc[...] = before_gn[...].astype(F32)
        else:
            out_acc[...] = jnp.zeros_like(out_acc)
            gn_acc[...] = jnp.zeros_like(gn_acc)

    bias_sum = jnp.zeros(gb_ref.shape, F32)
    for first in range(0, length, block):
        rows = slice(first, first + block)
        unit = dot_nn(n_ref[rows, :], w_ref[:, ups]) + b_ref[...]
        grad = dot_nn(g_ref[rows, :], w_ref[:, downs])
        square = unit * unit
        curve = jnp.tanh(0.7978845608028654 * (unit + 0.044715 * (square * unit)))
        half = 0.5 + 0.5 * curve
        slope = half + (0.5 * unit) * (1.0 - curve * curve) * (
            0.7978845608028654 + (3 * 0.044715 * 0.7978845608028654) * square
        )
        active = (unit * half).astype(BF16)
        grad_pre = (grad * slope).astype(BF16)
        act[rows, :] = active
        gpre[rows, :] = grad_pre
        bias_sum = bias_sum + jnp.sum(grad_pre.astype(F32), axis=0, keepdims=True)
        out_acc[rows, :] += dot_nt(active, w_ref[:, downs])
        gn_acc[rows, :] += dot_nt(grad_pre, w_ref[:, ups])
    gb_ref[...] = bias_sum
    for columns, left, right in ((ups, nt_ref, gpre), (downs, gt_ref, act)):
        if cube:
            grad_w[...] = dot_nn(left[...], right[...]).astype(BF16)
            store_pieces(order, grad_w, grad_refs, columns)
        else:
            grad_refs[0][:, columns] = dot_nn(left[...], right[...]).astype(BF16)

    @pl.when(step == pl.num_programs(0) - 1)
    def _():
        out_ref[...] = out_acc[...].astype(BF16)
        gn_ref[...] = gn_acc[...].astype(BF16)


def mlp(order, normed, grad, normed_t, grad_t, weights, bias, previous, cube):
    length, width = normed.shape
    units = weights.shape[1] // 2
    tile = min(TILE, units)
    at_tile = lambda rows, columns: pl.BlockSpec((rows, columns), lambda u, o: (0, u))
    fixed = lambda shape: pl.BlockSpec(shape, lambda u, o: (0, 0))
    once = lambda shape: pl.BlockSpec(shape, lambda u, o: (0, 0), pipeline_mode=pl.Buffered(1))
    if cube:
        count = order.shape[0]
        grad_shapes = piece_shapes(count, width // count, 2 * units)
    else:
        grad_shapes = [jax.ShapeDtypeStruct((width, 2 * units), BF16)]
    results = pl.pallas_call(
        functools.partial(
            mlp_kernel, block=min(256, length), with_previous=bool(previous), cube=cube
        ),
        grid_spec=pltpu.PrefetchScalarGridSpec(
            num_scalar_prefetch=1,
            grid=(units // tile,),
            in_specs=[
                once((length, width)),
                once((length, width)),
                once((width, length)),
                once((width, length)),
                at_tile(1, tile),
                at_tile(width, 2 * tile),
            ]
            + [once((length, width)) for _ in previous],
            out_specs=[fixed((length, width)), fixed((length, width))]
            + [at_tile(shape.shape[0], 2 * tile) for shape in grad_shapes]
            + [at_tile(1, tile)],
            scratch_shapes=[
                pltpu.VMEM((length, width), F32),
                pltpu.VMEM((length, width), F32),
                pltpu.VMEM((length, tile), BF16),
                pltpu.VMEM((length, tile), BF16),
                pltpu.VMEM((width, tile), BF16),
            ],
        ),
        out_shape=[jax.ShapeDtypeStruct((length, width), BF16)] * 2
        + grad_shapes
        + [jax.ShapeDtypeStruct((1, units), F32)],
        compiler_params=pltpu.CompilerParams(vmem_limit_bytes=VMEM_BYTES),
        cost_estimate=pl.CostEstimate(
            flops=12 * length * width * units,
            bytes_accessed=12 * length * width + 8 * width * units,
            transcendentals=length * units,
        ),
        name="mlp_second" if previous else "mlp_first",
    )(order, normed, grad, normed_t, grad_t, bias.reshape(1, units), weights, *previous)
    return results[0], results[1], results[2:-1], results[-1]


def qkv_kernel(n_ref, b_ref, w_ref, out_ref):
    scale = jnp.where(pl.program_id(0) == 0, HEAD_DIM ** (-0.5), 1.0)
    length = n_ref.shape[0]
    step = min(256, length)
    for first in range(0, length, step):
        span = slice(first, first + step)
        out_ref[span, :] = ((dot_nn(n_ref[span, :], w_ref[...]) + b_ref[...]) * scale).astype(BF16)


def qkv_project(normed, weights, bias):
    length, width = normed.shape
    columns = weights.shape[1] // 4
    at_tile = lambda rows: pl.BlockSpec((rows, columns), lambda k: (0, k))
    return pl.pallas_call(
        qkv_kernel,
        grid=(3,),
        in_specs=[
            whole_spec((length, width), pipeline_mode=pl.Buffered(1)), at_tile(1), at_tile(width)
        ],
        out_specs=at_tile(length),
        out_shape=jax.ShapeDtypeStruct((length, 3 * columns), BF16),
        compiler_params=pltpu.CompilerParams(vmem_limit_bytes=VMEM_BYTES),
        cost_estimate=pl.CostEstimate(
            flops=6 * length * width * columns,
            bytes_accessed=2 * length * width + 6 * width * columns + 6 * length * columns,
            transcendentals=0,
        ),
        name="qkv_project",
    )(normed, bias.reshape(1, 3 * columns), weights)


def weight_kernel(order, nt_ref, grads_ref, gt_ref, mixed_ref, order_only, *refs):
    piece_refs, grad = refs[:5], refs[5]
    part = pl.program_id(0)

    @pl.when(part < 3)
    def _():
        grad[...] = dot_nn(nt_ref[...], grads_ref[0]).astype(BF16)

    @pl.when(part == 3)
    def _():
        grad[...] = dot_nn(gt_ref[...], mixed_ref[...]).astype(BF16)

    store_pieces(order, grad, piece_refs, slice(None))


def without(kernel, place):
    return lambda *refs: kernel(*refs[:place], *refs[place + 1 :])


ORDER_ONLY = pl.BlockSpec(memory_space=pl.ANY)


def weight_grads(order, normed_t, grads, grad_t, mixed, after):
    width, length = normed_t.shape
    columns = grads.shape[2]
    shapes = piece_shapes(order.shape[0], width // order.shape[0], 4 * columns)
    fixed = lambda shape: pl.BlockSpec(shape, lambda k, o: (0, 0), pipeline_mode=pl.Buffered(1))
    return pl.pallas_call(
        weight_kernel,
        grid_spec=pltpu.PrefetchScalarGridSpec(
            num_scalar_prefetch=1,
            grid=(4,),
            in_specs=[
                fixed((width, length)),
                pl.BlockSpec((1, length, columns), lambda k, o: (jnp.minimum(k, 2), 0, 0)),
                fixed((width, length)),
                fixed((length, columns)),
                ORDER_ONLY,
            ],
            out_specs=[
                pl.BlockSpec((shape.shape[0], columns), lambda k, o: (0, k)) for shape in shapes
            ],
            scratch_shapes=[pltpu.VMEM((width, columns), BF16)],
        ),
        out_shape=shapes,
        compiler_params=pltpu.CompilerParams(vmem_limit_bytes=VMEM_BYTES),
        cost_estimate=pl.CostEstimate(
            flops=8 * length * width * columns,
            bytes_accessed=4 * length * width + 16 * width * columns,
            transcendentals=0,
        ),
        name="weight_grads",
    )(order, normed_t, grads, grad_t, mixed, after)


def qkv_back_kernel(grads_ref, w_ref, out_ref):
    columns = grads_ref.shape[2]
    total = None
    for k in range(3):
        part = dot_nt(grads_ref[k], w_ref[:, k * columns : (k + 1) * columns])
        total = part if total is None else total + part
    out_ref[...] = total.astype(BF16)


def qkv_back(grads, weights, after):
    _, length, columns = grads.shape
    width = weights.shape[0]
    block = min(256, length)
    return pl.pallas_call(
        without(qkv_back_kernel, 2),
        grid=(length // block,),
        in_specs=[
            pl.BlockSpec((3, block, columns), lambda i: (0, i, 0)),
            pl.BlockSpec((width, 4 * columns), lambda i: (0, 0), pipeline_mode=pl.Buffered(1)),
            ORDER_ONLY,
        ],
        out_specs=pl.BlockSpec((block, width), lambda i: (i, 0)),
        out_shape=jax.ShapeDtypeStruct((length, width), BF16),
        compiler_params=pltpu.CompilerParams(vmem_limit_bytes=VMEM_BYTES),
        cost_estimate=pl.CostEstimate(
            flops=6 * length * width * columns,
            bytes_accessed=2 * length * width + 6 * width * columns + 6 * length * columns,
            transcendentals=0,
        ),
        name="qkv_back",
    )(grads, weights, after)


def added(*terms):
    total = terms[0].astype(F32)
    for term in terms[1:]:
        total = total + term.astype(F32)
    return total.astype(BF16)


def first_sums_kernel(from_x, from_y, keep_y, keep_x, y_ref, x_ref):
    half = y_ref.shape[0]
    y_ref[...] = added(keep_y[...], from_x[:half, :])
    x_ref[...] = added(keep_x[...], from_y[:half, :])


def second_sums_kernel(from_x, from_y, near, from_y2, from_x2, *outs, with_small):
    if with_small:
        small, outs = outs[0], outs[1:]
    far = len(outs)
    half = from_y2.shape[0]
    rows = half * 2 // far
    if with_small:
        values = small[...]
        high = values.astype(BF16).astype(F32)
        extra = jnp.concatenate([high, values - high], axis=0).astype(BF16)
    for i, out in enumerate(outs):
        first, second, place = (from_x, from_y2, i) if i < far // 2 else (from_y, from_x2, i - far // 2)
        out[:rows, :] = added(
            near[i * rows : (i + 1) * rows, :],
            first[half + place * rows : half + (place + 1) * rows, :],
            second[place * rows : (place + 1) * rows, :],
        )
        if with_small:
            out[rows:, :] = extra


def z_sums_kernel(z_ref, from_x, from_y, near, from_y2, from_x2, out, *, far):
    half = from_y2.shape[0]
    rows = half * 2 // far
    for i in range(far):
        first, second, place = (from_x, from_y2, i) if i < far // 2 else (from_y, from_x2, i - far // 2)
        target = pl.multiple_of((z_ref[0] ^ i) * rows, rows)
        out[pl.ds(target, rows), :] = added(
            near[i * rows : (i + 1) * rows, :],
            first[half + place * rows : half + (place + 1) * rows, :],
            second[place * rows : (place + 1) * rows, :],
        )


def weights_last_kernel(*refs):
    parts, outs, small = refs[:-5], refs[-5:-1], refs[-1]
    total = parts[0][...].astype(F32)
    for part in parts[1:]:
        total = total + part[...].astype(F32)
    rows, columns = outs[0].shape
    for k, out in enumerate(outs):
        out[...] = total[:rows, k * columns : (k + 1) * columns]
    extra = small.shape[0]
    small[...] = total[rows : rows + extra, :] + total[rows + extra :, :]


def units_last_kernel(first_ref, second_ref, up_ref, down_ref, *, tile):
    units = up_ref.shape[1] // 2
    for index, ref in enumerate((first_ref, second_ref)):
        for first in range(0, units, tile):
            columns = slice(index * units + first, index * units + first + tile)
            up_ref[:, columns] = ref[:, 2 * first : 2 * first + tile].astype(F32)
            down_ref[:, columns] = ref[:, 2 * first + tile : 2 * first + 2 * tile].astype(F32)


def shards_kernel(w_up, w_down, first_ref, second_ref, *, tile):
    units = first_ref.shape[1] // 2
    for index, ref in enumerate((first_ref, second_ref)):
        for first in range(0, units, tile):
            columns = slice(index * units + first, index * units + first + tile)
            ref[:, 2 * first : 2 * first + tile] = w_up[:, columns]
            ref[:, 2 * first + tile : 2 * first + 2 * tile] = w_down[:, columns]


def sums_call(kernel, operands, shapes, after, name):
    body = kernel if after is None else without(kernel, 0)
    vmem = pl.BlockSpec(memory_space=pltpu.VMEM)
    return pl.pallas_call(
        body,
        in_specs=([pl.BlockSpec(memory_space=pl.ANY)] if after is not None else [])
        + [vmem] * len(operands),
        out_specs=[vmem] * len(shapes),
        out_shape=shapes,
        compiler_params=pltpu.CompilerParams(vmem_limit_bytes=VMEM_BYTES),
        cost_estimate=pl.CostEstimate(flops=0, bytes_accessed=1024 * 1024, transcendentals=0),
        name=name,
    )(*([after] if after is not None else []), *operands)


def flipped(sizes):
    return 1 if sizes["h"] * sizes["l"] == 2 else 0


def moves(sizes):
    groups, ranks, inner = sizes["a"], sizes["h"] * sizes["l"], sizes["l"]
    far = groups // 2
    flip = flipped(sizes)
    swap_to = {}
    for group in range(2):
        for part in range(ranks):
            place = (part % 2 ^ flip) * ranks + group * (ranks // 2) + part // 2
            swap_to[group * ranks + part] = place

    def swap(values, inverse=False):
        pairs = [(to, frm) if inverse else (frm, to) for frm, to in swap_to.items()]
        return lax.ppermute(values, SWAP, pairs)

    def swap_hop(values, a_mask, inverse=False):
        pairs = []
        for a in range(groups):
            for frm, to in swap_to.items():
                one, two = a * 2 * ranks + frm, (a ^ a_mask) * 2 * ranks + to
                pairs.append((two, one) if inverse else (one, two))
        return lax.ppermute(values, ALL, pairs)

    def hop(values, a_mask, h_mask):
        pairs = []
        for a in range(groups):
            for c in range(2):
                for h in range(2):
                    pairs.append(((a * 2 + c) * 2 + h, ((a ^ a_mask) * 2 + c) * 2 + (h ^ h_mask)))
        return lax.ppermute(values, ("z", "y", "c", "h"), pairs)

    def scatter_near(pieces, after):
        from_x, from_y = hop(pieces[0], 0, 1), hop(pieces[1], 1, 0)
        half, columns = pieces[2].shape
        y_sum, x_sum = sums_call(
            first_sums_kernel,
            [from_x, from_y, pieces[2], pieces[3]],
            [jax.ShapeDtypeStruct((half, columns), BF16)] * 2,
            after,
            "sums_one",
        )
        return from_x, from_y, pieces[4], y_sum, x_sum

    def far_sums(state, small, after):
        from_x, from_y, near, y_sum, x_sum = state
        columns = near.shape[1]
        from_y2, from_x2 = hop(y_sum, 1, 0), hop(x_sum, 0, 1)
        rows = near.shape[0] // far + sum(2 * values.shape[0] for values in small)
        return sums_call(
            functools.partial(second_sums_kernel, with_small=bool(small)),
            [from_x, from_y, near, from_y2, from_x2] + small,
            [jax.ShapeDtypeStruct((rows, columns), BF16)] * far,
            after,
            "sums_two",
        )

    def z_sums(state, after):
        from_x, from_y, near, y_sum, x_sum = state
        from_y2, from_x2 = hop(y_sum, 1, 0), hop(x_sum, 0, 1)
        vmem = pl.BlockSpec(memory_space=pltpu.VMEM)
        return pl.pallas_call(
            without(functools.partial(z_sums_kernel, far=far), 6),
            in_specs=[pl.BlockSpec(memory_space=pltpu.SMEM)] + [vmem] * 5 + [ORDER_ONLY],
            out_specs=vmem,
            out_shape=jax.ShapeDtypeStruct(near.shape, BF16),
            compiler_params=pltpu.CompilerParams(vmem_limit_bytes=VMEM_BYTES),
            name="sums_two_z",
        )(lax.axis_index("z").reshape(1), from_x, from_y, near, from_y2, from_x2, after)

    def far_parts(sums):
        return [swap_hop(sums[i], 2 * i, inverse=True) for i in range(far)]

    def near_sum(values):
        values = values + lax.ppermute(values, "c", [(0, 1), (1, 0)])
        values = values + hop(values, 1, 0)
        values = values + hop(values, 0, 1)
        return lax.psum(values, "l") if inner > 1 else values

    a, h = lax.axis_index(("z", "y")), lax.axis_index("h")
    order = []
    for a_low, h_mask in ((0, 0), (1, 0), (0, 1), (1, 1)):
        for i in range(far):
            order.append((a ^ (2 * i + a_low)) * 2 + (h ^ h_mask))
    return swap, hop, scatter_near, far_sums, z_sums, far_parts, near_sum, jnp.stack(order).astype(jnp.int32)


def per_device(sizes, *arguments):
    (
        block_input, segment_ids, ln1_gain, ln1_bias, w_query, w_key, w_value, b_query, b_value,
        w_out, b_out, ln2_gain, ln2_bias, w_up, b_up, w_down, b_down, out_grad,
    ) = arguments
    ranks = sizes["h"] * sizes["l"]
    rank = lax.axis_index("l") * 2 + (lax.axis_index("c") ^ flipped(sizes))
    own_rows, width = block_input.shape
    head_width = w_query.shape[1]
    unit_width = w_up.shape[1]
    half_units = unit_width // 2
    tile = min(TILE, half_units)
    swap, hop, scatter_near, far_sums, z_sums, far_parts, near_sum, order = moves(sizes)

    def partner(values):
        return lax.ppermute(values, "c", [(0, 1), (1, 0)])

    def tp_gather(values):
        if ranks != 2:
            return lax.all_gather(values, TP, axis=0, tiled=True)
        theirs = partner(values)
        return jnp.where(
            rank == 0,
            jnp.concatenate([values, theirs], axis=0),
            jnp.concatenate([theirs, values], axis=0),
        )

    def tp_terms(values):
        if ranks != 2:
            others = lax.psum(values.astype(F32), TP) - values.astype(F32)
            return values, others.astype(BF16)
        return values, partner(values)

    def own(values):
        return lax.dynamic_slice_in_dim(values, rank * own_rows, own_rows)

    def tp_scatter(values):
        if ranks != 2:
            return lax.psum_scatter(values, TP, scatter_dimension=0, tiled=True).astype(F32)
        theirs = lax.dynamic_slice_in_dim(values, (1 - rank) * own_rows, own_rows)
        return own(values).astype(F32) + partner(theirs).astype(F32)

    own_input = swap(block_input)
    segments = swap(segment_ids)
    own_grad = swap(out_grad)
    shard_first, shard_second = sums_call(
        functools.partial(shards_kernel, tile=tile),
        [w_up, w_down],
        [jax.ShapeDtypeStruct(w_up.shape, BF16)] * 2,
        None,
        "mlp_shards",
    )
    early_attn = lax.all_gather(
        jnp.concatenate([w_query, w_key, w_value, w_out], axis=1), ("z", "y", "c"), axis=0, tiled=True
    )
    early_first = lax.all_gather(shard_first, ("z", "y", "c"), axis=0, tiled=True)
    shard_second = swap(shard_second)
    other_second = hop(shard_second, 0, 1)
    shard_second = jnp.where(
        lax.axis_index("h") == 0,
        jnp.concatenate([shard_second, other_second], axis=0),
        jnp.concatenate([other_second, shard_second], axis=0),
    )
    bias_query = lax.dynamic_slice_in_dim(b_query, rank * head_width, head_width)
    bias_value = lax.dynamic_slice_in_dim(b_value, rank * head_width, head_width)
    bias_up = lax.dynamic_slice_in_dim(b_up, rank * unit_width, unit_width)

    rows_in = tp_gather(own_input)
    grad_rows = tp_gather(own_grad)
    grad_rows_t = grad_rows.T
    normed, normed_t = norm_rows(rows_in, ln1_gain, ln1_bias)
    early_attn, normed, segments, grad_rows, grad_rows_t, shard_second = lax.optimization_barrier(
        (early_attn, normed, segments, grad_rows, grad_rows_t, shard_second)
    )
    full_second = lax.all_gather(shard_second, ("z", "y"), axis=0, tiled=True)
    full_attn = swap(early_attn)
    biases = jnp.concatenate([bias_query, jnp.zeros((head_width,), F32), bias_value])
    qkv = qkv_project(normed, full_attn, biases)
    full_out = full_attn[:, 3 * head_width :]
    early_first, qkv = lax.optimization_barrier((early_first, qkv))
    full_first = swap(early_first)
    mixed, lse = attn_forward(segments, qkv, head_width)
    attended = tp_terms(dot_nt(mixed, full_out).astype(BF16))
    normed_two, normed_two_t, hidden = norm_rows(rows_in, ln2_gain, ln2_bias, attended, b_out)

    out_part, gn_part, first_grads, bias_first = mlp(
        order, normed_two, grad_rows, normed_two_t, grad_rows_t, full_first,
        bias_up[:half_units], (), True,
    )
    full_second, gn_part = lax.optimization_barrier((full_second, gn_part))
    out_part, gn_part, second_grads, bias_second = mlp(
        order, normed_two, grad_rows, normed_two_t, grad_rows_t, full_second,
        bias_up[half_units:], (out_part, gn_part), False,
    )
    first_state = scatter_near(first_grads, gn_part)
    gn_part, second_grads, first_state = lax.optimization_barrier(
        (gn_part, second_grads[0], first_state)
    )
    own_output = (own(hidden) + tp_scatter(out_part) + b_down).astype(BF16)

    grad_hidden, grad_attended, grad_attended_t, sums_two = norm_back_rows(
        hidden, grad_rows, tp_terms(gn_part), ln2_gain
    )
    first_sums = z_sums(first_state, grad_attended)
    second_grads, first_sums = lax.optimization_barrier((second_grads, first_sums))
    second_grads = swap(second_grads, inverse=True)
    grad_mixed = dot_nn(grad_attended, full_out).astype(BF16)
    first_mlp = lax.psum_scatter(first_sums, "z", scatter_dimension=0, tiled=True)
    grads = attn_backward(segments, qkv, mixed, lse, grad_mixed, head_width, first_sums)
    block_rows = w_query.shape[0]
    pieces = weight_grads(order, normed_t, grads, grad_attended_t, mixed, grads)
    grad_normed_part = qkv_back(grads, full_attn, pieces[0])
    second_grads, first_mlp, grad_normed_part = lax.optimization_barrier(
        (second_grads, first_mlp, grad_normed_part)
    )
    second_mlp = lax.psum_scatter(second_grads, ("z", "y", "c"), scatter_dimension=0, tiled=True)
    state = scatter_near(pieces, grad_normed_part)
    grad_normed = tp_scatter(grad_normed_part)
    own_scaled, own_inverse = normalize(own_input.astype(F32))
    grad_own = own(grad_hidden) + norm_back(grad_normed, own_scaled, own_inverse, ln1_gain)
    grad_own = grad_own.astype(BF16)

    def place_part(values, full):
        return lax.dynamic_update_slice_in_dim(
            jnp.zeros((full,), F32), values, rank * values.shape[0], 0
        )

    sums = jnp.concatenate(
        [
            jnp.sum(grad_normed * own_scaled, axis=0),
            jnp.sum(grad_normed, axis=0),
            place_part(jnp.sum(grads[0].astype(F32), axis=0), width),
            place_part(jnp.sum(grads[2].astype(F32), axis=0), width),
            (sums_two[:3] * (1.0 / ranks)).reshape(-1),
            jnp.sum(own_grad.astype(F32), axis=0),
            place_part(jnp.concatenate([bias_first[0], bias_second[0]]), b_up.shape[0]),
        ]
    )
    columns = pieces[0].shape[1]
    filled = sums.shape[0]
    sums = jnp.pad(sums, (0, -filled % (8 * columns))).reshape(-1, columns)
    sums = near_sum(sums)
    last_sums = far_sums(state, [sums], None)
    own_output, grad_own, *last_sums = lax.optimization_barrier((own_output, grad_own, *last_sums))
    leaving = jnp.concatenate([own_output, grad_own, first_mlp.reshape(-1, width)], axis=0)
    leaving = swap(leaving, inverse=True)
    output, grad_input = leaving[:own_rows], leaving[own_rows : 2 * own_rows]
    first_mlp = leaving[2 * own_rows :].reshape(block_rows, unit_width)
    *late, sums = sums_call(
        weights_last_kernel,
        far_parts(last_sums),
        [jax.ShapeDtypeStruct((block_rows, head_width), F32)] * 4
        + [jax.ShapeDtypeStruct(sums.shape, F32)],
        None,
        "sums_last",
    )
    shard = jax.ShapeDtypeStruct((block_rows, unit_width), F32)
    grad_w_up, grad_w_down = sums_call(
        functools.partial(units_last_kernel, tile=tile),
        [first_mlp, second_mlp],
        [shard, shard],
        None,
        "units_last",
    )
    sums = sums.reshape(-1)
    small = [sums[i * width : (i + 1) * width] for i in range(8)]
    return (
        output, grad_input, small[0], small[1],
        late[0], late[1], late[2], small[2], small[3], late[3], small[4], small[5], small[6],
        grad_w_up, sums[8 * width : filled], grad_w_down, small[7],
    )


def solution(mesh):
    groups, ranks = mesh.shape["dp"], mesh.shape["tensor"]
    sizes = {"a": groups // 2, "h": 2, "l": ranks // 2}
    fine = Mesh(mesh.devices.reshape(groups // 4, 2, 2, 2, ranks // 2), ALL)
    rows = P(ALL, None)
    block = P(("z", "y", "c"), ("h", "l"))
    return jax.shard_map(
        functools.partial(per_device, sizes),
        mesh=fine,
        in_specs=(
            rows, P(("z", "y", "c")), P(), P(), block, block, block, P(), P(), block, P(), P(), P(),
            block, P(), block, P(), rows,
        ),
        out_specs=(
            rows, rows, P(), P(), block, block, block, P(), P(), block, P(), P(), P(), block, P(),
            block, P(),
        ),
        check_vma=False,
    )
```

```python
import functools

import jax
import jax.numpy as jnp
from jax import lax
from jax.experimental import pallas as pl
from jax.experimental.pallas import tpu as pltpu
from jax.sharding import Mesh
from jax.sharding import PartitionSpec as P

HEAD_DIM = 64
LANES = 128
TILE = 512
ROWS = 512
MASKED = -1e30
VMEM_BYTES = 60 * 1024 * 1024
F32 = jnp.float32
BF16 = jnp.bfloat16
TP = ("l", "c")
SWAP = ("c", "h", "l")
ALL = ("z", "y", "c", "h", "l")


def normalize(values):
    center = values - jnp.mean(values, axis=-1, keepdims=True)
    spread = jnp.mean(center * center, axis=-1, keepdims=True)
    inverse = lax.rsqrt(spread + 1e-05)
    return center * inverse, inverse


def norm_back(grad_in, scaled, inverse, gain_vec):
    local_grad = grad_in * gain_vec
    return inverse * (
        local_grad
        - jnp.mean(local_grad, axis=-1, keepdims=True)
        - scaled * jnp.mean(local_grad * scaled, axis=-1, keepdims=True)
    )


def dot_nn(left, right):
    return lax.dot_general(left, right, (((1,), (0,)), ((), ())), preferred_element_type=F32)


def dot_nt(left, right):
    return lax.dot_general(left, right, (((1,), (1,)), ((), ())), preferred_element_type=F32)


def dot_tn(left, right):
    return lax.dot_general(left, right, (((0,), (0,)), ((), ())), preferred_element_type=F32)


def fill_bias(bias, seg_col, seg_row):
    length = bias.shape[0]
    block = min(256, length)
    for first in range(0, length, block):
        keys = lax.broadcasted_iota(jnp.int32, (block, length), 0) + first
        places = lax.broadcasted_iota(jnp.int32, (block, length), 1)
        same = seg_col[first : first + block, :] == seg_row[...]
        bias[first : first + block, :] = jnp.where(same & (keys <= places), 0.0, MASKED)


def head_lanes(values, head):
    lane = lax.broadcasted_iota(jnp.int32, values.shape, 1)
    inside = (lane >= head * HEAD_DIM) & (lane < (head + 1) * HEAD_DIM)
    return jnp.where(inside, values, jnp.zeros_like(values))


def attn_forward_kernel(seg_col, seg_row, q_ref, k_ref, v_ref, mixed_ref, lse_ref, bias, v_t, block):
    length = q_ref.shape[0]
    heads = LANES // HEAD_DIM

    @pl.when(pl.program_id(0) == 0)
    def _():
        fill_bias(bias, seg_col, seg_row)

    v_t[...] = v_ref[...].T
    for place in range(length // block):
        rows = slice(place * block, (place + 1) * block)
        outs = []
        for head in range(heads):
            query = head_lanes(q_ref[rows, :], head)
            scores = []
            peak = None
            for other in range(place + 1):
                keys = slice(other * block, (other + 1) * block)
                part = dot_nt(k_ref[keys, :], query) + bias[keys, rows]
                top = jnp.max(part, axis=0, keepdims=True)
                peak = top if peak is None else jnp.maximum(peak, top)
                scores.append(part)
            total = None
            acc = None
            for other in range(place + 1):
                keys = slice(other * block, (other + 1) * block)
                weight = jnp.exp(scores[other] - peak)
                part_sum = jnp.sum(weight, axis=0, keepdims=True)
                total = part_sum if total is None else total + part_sum
                part_out = dot_nn(
                    v_t[head * HEAD_DIM : (head + 1) * HEAD_DIM, keys], weight.astype(BF16)
                )
                acc = part_out if acc is None else acc + part_out
            outs.append(acc / total)
            lse_ref[0, head : head + 1, rows] = peak + jnp.log(total)
        mixed_ref[rows, :] = jnp.concatenate(outs, axis=0).T.astype(BF16)


def attn_backward_kernel(
    seg_col, seg_row, q_ref, k_ref, v_ref, mixed_ref, lse_ref, g_ref, grads_ref, bias, k_t, delta, dq_t, block
):
    length = q_ref.shape[0]
    heads = LANES // HEAD_DIM
    count = length // block

    @pl.when(pl.program_id(0) == 0)
    def _():
        fill_bias(bias, seg_col, seg_row)

    k_t[...] = k_ref[...].T
    product = (g_ref[...].astype(F32) * mixed_ref[...].astype(F32)).T
    for head in range(heads):
        delta[head : head + 1, :] = jnp.sum(
            product[head * HEAD_DIM : (head + 1) * HEAD_DIM, :], axis=0, keepdims=True
        )
    for other in range(count):
        keys = slice(other * block, (other + 1) * block)
        key_sum = None
        value_sum = None
        for head in range(heads):
            lanes = slice(head * HEAD_DIM, (head + 1) * HEAD_DIM)
            for place in range(other, count):
                rows = slice(place * block, (place + 1) * block)
                query = head_lanes(q_ref[rows, :], head)
                grad = head_lanes(g_ref[rows, :], head)
                scores = dot_nt(k_ref[keys, :], query) + bias[keys, rows]
                probs = jnp.exp(scores - lse_ref[0, head : head + 1, rows])
                grad_probs = dot_nt(v_ref[keys, :], grad)
                grad_scores = (probs * (grad_probs - delta[head : head + 1, rows])).astype(BF16)
                value_part = dot_nn(probs.astype(BF16), grad)
                key_part = dot_nn(grad_scores, query)
                query_part = dot_nn(k_t[lanes, keys], grad_scores)
                value_sum = value_part if value_sum is None else value_sum + value_part
                key_sum = key_part if key_sum is None else key_sum + key_part
                if other == 0:
                    dq_t[lanes, rows] = query_part
                else:
                    dq_t[lanes, rows] += query_part
        grads_ref[1, keys, :] = key_sum.astype(BF16)
        grads_ref[2, keys, :] = value_sum.astype(BF16)
    grads_ref[0] = (dq_t[...].T * HEAD_DIM ** (-0.5)).astype(BF16)


def attn_forward(segments, qkv, width):
    length = qkv.shape[0]
    pairs = width // LANES
    block = min(256, length)
    column = lambda first: pl.BlockSpec((length, LANES), lambda p: (0, first * pairs + p))
    whole = lambda shape: pl.BlockSpec(shape, lambda p: (0, 0))
    return pl.pallas_call(
        functools.partial(attn_forward_kernel, block=block),
        grid=(pairs,),
        in_specs=[whole((length, 1)), whole((1, length)), column(0), column(1), column(2)],
        out_specs=[
            pl.BlockSpec((length, LANES), lambda p: (0, p)),
            pl.BlockSpec((1, 8, length), lambda p: (p, 0, 0)),
        ],
        out_shape=[
            jax.ShapeDtypeStruct((length, width), BF16),
            jax.ShapeDtypeStruct((pairs, 8, length), F32),
        ],
        scratch_shapes=[pltpu.VMEM((length, length), F32), pltpu.VMEM((LANES, length), BF16)],
        compiler_params=pltpu.CompilerParams(vmem_limit_bytes=VMEM_BYTES),
        cost_estimate=pl.CostEstimate(
            flops=4 * length * length * width,
            bytes_accessed=8 * length * width,
            transcendentals=length * length * width // (2 * HEAD_DIM),
        ),
        name="attn_forward",
    )(segments.reshape(length, 1), segments.reshape(1, length), qkv, qkv, qkv)


def attn_backward(segments, qkv, mixed, lse, grad_mixed, width, after):
    length = qkv.shape[0]
    pairs = width // LANES
    block = min(256, length)
    column = lambda first: pl.BlockSpec((length, LANES), lambda p: (0, first * pairs + p))
    whole = lambda shape: pl.BlockSpec(shape, lambda p: (0, 0))
    return pl.pallas_call(
        without(functools.partial(attn_backward_kernel, block=block), 8),
        grid=(pairs,),
        in_specs=[
            whole((length, 1)),
            whole((1, length)),
            column(0),
            column(1),
            column(2),
            pl.BlockSpec((length, LANES), lambda p: (0, p)),
            pl.BlockSpec((1, 8, length), lambda p: (p, 0, 0)),
            pl.BlockSpec((length, LANES), lambda p: (0, p)),
            pl.BlockSpec(memory_space=pl.ANY),
        ],
        out_specs=pl.BlockSpec((3, length, LANES), lambda p: (0, 0, p)),
        out_shape=jax.ShapeDtypeStruct((3, length, width), BF16),
        scratch_shapes=[
            pltpu.VMEM((length, length), F32),
            pltpu.VMEM((LANES, length), BF16),
            pltpu.VMEM((8, length), F32),
            pltpu.VMEM((LANES, length), F32),
        ],
        compiler_params=pltpu.CompilerParams(vmem_limit_bytes=VMEM_BYTES),
        cost_estimate=pl.CostEstimate(
            flops=10 * length * length * width,
            bytes_accessed=16 * length * width,
            transcendentals=length * length * width // (2 * HEAD_DIM),
        ),
        name="attn_backward",
    )(segments.reshape(length, 1), segments.reshape(1, length), qkv, qkv, qkv, mixed, lse, grad_mixed, after)


def piece_blocks(count):
    far = count // 4
    half = far // 2
    near, by_y, by_x, both = (list(range(i * far, (i + 1) * far)) for i in range(4))
    return [
        both[:half] + by_x[:half],
        both[half:] + by_y[half:],
        by_y[:half],
        by_x[half:],
        near,
    ]


def store_pieces(order, grad, piece_refs, columns):
    count = order.shape[0]
    rows = grad.shape[0] // count
    for blocks, ref in zip(piece_blocks(count), piece_refs):
        for place, block in enumerate(blocks):
            first = pl.multiple_of(order[block] * rows, rows)
            ref[place * rows : (place + 1) * rows, columns] = grad[pl.ds(first, rows), :]


def piece_shapes(count, rows, columns):
    return [
        jax.ShapeDtypeStruct((len(blocks) * rows, columns), BF16) for blocks in piece_blocks(count)
    ]


def whole_spec(shape, **options):
    return pl.BlockSpec(shape, lambda step: (0,) * len(shape), **options)


def norm_kernel(*refs, residual):
    if residual:
        x_ref, own_ref, other_ref, shift_ref, gain_ref, bias_ref, n_ref, nt_ref, hidden_ref = refs
        values = (
            x_ref[...].astype(F32)
            + (own_ref[...].astype(F32) + other_ref[...].astype(F32))
            + shift_ref[...]
        )
        hidden_ref[...] = values
    else:
        x_ref, gain_ref, bias_ref, n_ref, nt_ref = refs
        values = x_ref[...].astype(F32)
    scaled, _ = normalize(values)
    normed = (scaled * gain_ref[...] + bias_ref[...]).astype(BF16)
    n_ref[...] = normed
    nt_ref[...] = normed.T


def norm_rows(x, gain, bias, partials=None, shift=None):
    length, width = x.shape
    block = min(256, length)
    row = pl.BlockSpec((block, width), lambda step: (step, 0))
    vector = whole_spec((1, width))
    residual = partials is not None
    operands = [x] + (list(partials) + [shift.reshape(1, width)] if residual else [])
    operands += [gain.reshape(1, width), bias.reshape(1, width)]
    return pl.pallas_call(
        functools.partial(norm_kernel, residual=residual),
        grid=(length // block,),
        in_specs=[row] + ([row, row, vector] if residual else []) + [vector, vector],
        out_specs=[row, pl.BlockSpec((width, block), lambda step: (0, step))]
        + ([row] if residual else []),
        out_shape=[
            jax.ShapeDtypeStruct((length, width), BF16),
            jax.ShapeDtypeStruct((width, length), BF16),
        ]
        + ([jax.ShapeDtypeStruct((length, width), F32)] if residual else []),
        compiler_params=pltpu.CompilerParams(vmem_limit_bytes=VMEM_BYTES),
        cost_estimate=pl.CostEstimate(
            flops=20 * length * width, bytes_accessed=14 * length * width, transcendentals=length
        ),
        name="norm_two" if residual else "norm_one",
    )(*operands)


def norm_back_kernel(hidden_ref, g_ref, own_ref, other_ref, gain_ref, grad_ref, low_ref, low_t_ref, sums_ref):
    scaled, inverse = normalize(hidden_ref[...])
    incoming = own_ref[...].astype(F32) + other_ref[...].astype(F32)
    grad = g_ref[...].astype(F32) + norm_back(incoming, scaled, inverse, gain_ref[...])
    grad_ref[...] = grad
    low_ref[...] = grad.astype(BF16)
    low_t_ref[...] = grad.astype(BF16).T

    @pl.when(pl.program_id(0) == 0)
    def _():
        sums_ref[...] = jnp.zeros_like(sums_ref)

    sums_ref[0:1, :] += jnp.sum(grad, axis=0, keepdims=True)
    sums_ref[1:2, :] += jnp.sum(incoming * scaled, axis=0, keepdims=True)
    sums_ref[2:3, :] += jnp.sum(incoming, axis=0, keepdims=True)


def norm_back_rows(hidden, grad, partials, gain):
    length, width = hidden.shape
    block = min(256, length)
    row = pl.BlockSpec((block, width), lambda step: (step, 0))
    return pl.pallas_call(
        norm_back_kernel,
        grid=(length // block,),
        in_specs=[row, row, row, row, whole_spec((1, width))],
        out_specs=[
            row,
            row,
            pl.BlockSpec((width, block), lambda step: (0, step)),
            whole_spec((8, width)),
        ],
        out_shape=[
            jax.ShapeDtypeStruct((length, width), F32),
            jax.ShapeDtypeStruct((length, width), BF16),
            jax.ShapeDtypeStruct((width, length), BF16),
            jax.ShapeDtypeStruct((8, width), F32),
        ],
        compiler_params=pltpu.CompilerParams(vmem_limit_bytes=VMEM_BYTES),
        cost_estimate=pl.CostEstimate(
            flops=30 * length * width, bytes_accessed=16 * length * width, transcendentals=length
        ),
        name="norm_two_back",
    )(hidden, grad, *partials, gain.reshape(1, width))


def mlp_kernel(order, n_ref, g_ref, nt_ref, gt_ref, b_ref, w_ref, *refs, block, with_previous, cube):
    if with_previous:
        (before_out, before_gn), refs = refs[:2], refs[2:]
    (out_ref, gn_ref), refs = refs[:2], refs[2:]
    grad_refs, (gb_ref, out_acc, gn_acc, act, gpre, grad_w) = refs[:-6], refs[-6:]
    step = pl.program_id(0)
    length = n_ref.shape[0]
    tile = w_ref.shape[1] // 2
    ups, downs = slice(0, tile), slice(tile, 2 * tile)

    @pl.when(step == 0)
    def _():
        if with_previous:
            out_acc[...] = before_out[...].astype(F32)
            gn_acc[...] = before_gn[...].astype(F32)
        else:
            out_acc[...] = jnp.zeros_like(out_acc)
            gn_acc[...] = jnp.zeros_like(gn_acc)

    bias_sum = jnp.zeros(gb_ref.shape, F32)
    for first in range(0, length, block):
        rows = slice(first, first + block)
        unit = dot_nn(n_ref[rows, :], w_ref[:, ups]) + b_ref[...]
        grad = dot_nn(g_ref[rows, :], w_ref[:, downs])
        square = unit * unit
        curve = jnp.tanh(0.7978845608028654 * (unit + 0.044715 * (square * unit)))
        half = 0.5 + 0.5 * curve
        slope = half + (0.5 * unit) * (1.0 - curve * curve) * (
            0.7978845608028654 + (3 * 0.044715 * 0.7978845608028654) * square
        )
        active = (unit * half).astype(BF16)
        grad_pre = (grad * slope).astype(BF16)
        act[rows, :] = active
        gpre[rows, :] = grad_pre
        bias_sum = bias_sum + jnp.sum(grad_pre.astype(F32), axis=0, keepdims=True)
        out_acc[rows, :] += dot_nt(active, w_ref[:, downs])
        gn_acc[rows, :] += dot_nt(grad_pre, w_ref[:, ups])
    gb_ref[...] = bias_sum
    for columns, left, right in ((ups, nt_ref, gpre), (downs, gt_ref, act)):
        if cube:
            grad_w[...] = dot_nn(left[...], right[...]).astype(BF16)
            store_pieces(order, grad_w, grad_refs, columns)
        else:
            grad_refs[0][:, columns] = dot_nn(left[...], right[...]).astype(BF16)

    @pl.when(step == pl.num_programs(0) - 1)
    def _():
        out_ref[...] = out_acc[...].astype(BF16)
        gn_ref[...] = gn_acc[...].astype(BF16)


def mlp(order, normed, grad, normed_t, grad_t, weights, bias, previous, cube):
    length, width = normed.shape
    units = weights.shape[1] // 2
    tile = min(TILE, units)
    at_tile = lambda rows, columns: pl.BlockSpec((rows, columns), lambda u, o: (0, u))
    fixed = lambda shape: pl.BlockSpec(shape, lambda u, o: (0, 0))
    once = lambda shape: pl.BlockSpec(shape, lambda u, o: (0, 0), pipeline_mode=pl.Buffered(1))
    if cube:
        count = order.shape[0]
        grad_shapes = piece_shapes(count, width // count, 2 * units)
    else:
        grad_shapes = [jax.ShapeDtypeStruct((width, 2 * units), BF16)]
    results = pl.pallas_call(
        functools.partial(
            mlp_kernel, block=min(ROWS, length), with_previous=bool(previous), cube=cube
        ),
        grid_spec=pltpu.PrefetchScalarGridSpec(
            num_scalar_prefetch=1,
            grid=(units // tile,),
            in_specs=[
                once((length, width)),
                once((length, width)),
                once((width, length)),
                once((width, length)),
                at_tile(1, tile),
                at_tile(width, 2 * tile),
            ]
            + [once((length, width)) for _ in previous],
            out_specs=[fixed((length, width)), fixed((length, width))]
            + [at_tile(shape.shape[0], 2 * tile) for shape in grad_shapes]
            + [at_tile(1, tile)],
            scratch_shapes=[
                pltpu.VMEM((length, width), F32),
                pltpu.VMEM((length, width), F32),
                pltpu.VMEM((length, tile), BF16),
                pltpu.VMEM((length, tile), BF16),
                pltpu.VMEM((width, tile), BF16),
            ],
        ),
        out_shape=[jax.ShapeDtypeStruct((length, width), BF16)] * 2
        + grad_shapes
        + [jax.ShapeDtypeStruct((1, units), F32)],
        compiler_params=pltpu.CompilerParams(vmem_limit_bytes=VMEM_BYTES),
        cost_estimate=pl.CostEstimate(
            flops=12 * length * width * units,
            bytes_accessed=12 * length * width + 8 * width * units,
            transcendentals=length * units,
        ),
        name="mlp_second" if previous else "mlp_first",
    )(order, normed, grad, normed_t, grad_t, bias.reshape(1, units), weights, *previous)
    return results[0], results[1], results[2:-1], results[-1]


def qkv_kernel(n_ref, b_ref, w_ref, out_ref):
    scale = jnp.where(pl.program_id(0) == 0, HEAD_DIM ** (-0.5), 1.0)
    length = n_ref.shape[0]
    step = min(ROWS, length)
    for first in range(0, length, step):
        span = slice(first, first + step)
        out_ref[span, :] = ((dot_nn(n_ref[span, :], w_ref[...]) + b_ref[...]) * scale).astype(BF16)


def qkv_project(normed, weights, bias):
    length, width = normed.shape
    columns = weights.shape[1] // 4
    at_tile = lambda rows: pl.BlockSpec((rows, columns), lambda k: (0, k))
    return pl.pallas_call(
        qkv_kernel,
        grid=(3,),
        in_specs=[
            whole_spec((length, width), pipeline_mode=pl.Buffered(1)), at_tile(1), at_tile(width)
        ],
        out_specs=at_tile(length),
        out_shape=jax.ShapeDtypeStruct((length, 3 * columns), BF16),
        compiler_params=pltpu.CompilerParams(vmem_limit_bytes=VMEM_BYTES),
        cost_estimate=pl.CostEstimate(
            flops=6 * length * width * columns,
            bytes_accessed=2 * length * width + 6 * width * columns + 6 * length * columns,
            transcendentals=0,
        ),
        name="qkv_project",
    )(normed, bias.reshape(1, 3 * columns), weights)


def weight_kernel(order, nt_ref, grads_ref, gt_ref, mixed_ref, order_only, *refs):
    piece_refs, grad = refs[:5], refs[5]
    part = pl.program_id(0)

    @pl.when(part < 3)
    def _():
        grad[...] = dot_nn(nt_ref[...], grads_ref[0]).astype(BF16)

    @pl.when(part == 3)
    def _():
        grad[...] = dot_nn(gt_ref[...], mixed_ref[...]).astype(BF16)

    store_pieces(order, grad, piece_refs, slice(None))


def without(kernel, place):
    return lambda *refs: kernel(*refs[:place], *refs[place + 1 :])


ORDER_ONLY = pl.BlockSpec(memory_space=pl.ANY)


def weight_grads(order, normed_t, grads, grad_t, mixed, after):
    width, length = normed_t.shape
    columns = grads.shape[2]
    shapes = piece_shapes(order.shape[0], width // order.shape[0], 4 * columns)
    fixed = lambda shape: pl.BlockSpec(shape, lambda k, o: (0, 0), pipeline_mode=pl.Buffered(1))
    return pl.pallas_call(
        weight_kernel,
        grid_spec=pltpu.PrefetchScalarGridSpec(
            num_scalar_prefetch=1,
            grid=(4,),
            in_specs=[
                fixed((width, length)),
                pl.BlockSpec((1, length, columns), lambda k, o: (jnp.minimum(k, 2), 0, 0)),
                fixed((width, length)),
                fixed((length, columns)),
                ORDER_ONLY,
            ],
            out_specs=[
                pl.BlockSpec((shape.shape[0], columns), lambda k, o: (0, k)) for shape in shapes
            ],
            scratch_shapes=[pltpu.VMEM((width, columns), BF16)],
        ),
        out_shape=shapes,
        compiler_params=pltpu.CompilerParams(vmem_limit_bytes=VMEM_BYTES),
        cost_estimate=pl.CostEstimate(
            flops=8 * length * width * columns,
            bytes_accessed=4 * length * width + 16 * width * columns,
            transcendentals=0,
        ),
        name="weight_grads",
    )(order, normed_t, grads, grad_t, mixed, after)


def qkv_back_kernel(grads_ref, w_ref, out_ref):
    columns = grads_ref.shape[2]
    total = None
    for k in range(3):
        part = dot_nt(grads_ref[k], w_ref[:, k * columns : (k + 1) * columns])
        total = part if total is None else total + part
    out_ref[...] = total.astype(BF16)


def qkv_back(grads, weights, after):
    _, length, columns = grads.shape
    width = weights.shape[0]
    block = min(ROWS, length)
    return pl.pallas_call(
        without(qkv_back_kernel, 2),
        grid=(length // block,),
        in_specs=[
            pl.BlockSpec((3, block, columns), lambda i: (0, i, 0)),
            pl.BlockSpec((width, 4 * columns), lambda i: (0, 0), pipeline_mode=pl.Buffered(1)),
            ORDER_ONLY,
        ],
        out_specs=pl.BlockSpec((block, width), lambda i: (i, 0)),
        out_shape=jax.ShapeDtypeStruct((length, width), BF16),
        compiler_params=pltpu.CompilerParams(vmem_limit_bytes=VMEM_BYTES),
        cost_estimate=pl.CostEstimate(
            flops=6 * length * width * columns,
            bytes_accessed=2 * length * width + 6 * width * columns + 6 * length * columns,
            transcendentals=0,
        ),
        name="qkv_back",
    )(grads, weights, after)


def added(*terms):
    total = terms[0].astype(F32)
    for term in terms[1:]:
        total = total + term.astype(F32)
    return total.astype(BF16)


def first_sums_kernel(from_x, from_y, keep_y, keep_x, y_ref, x_ref):
    half = y_ref.shape[0]
    y_ref[...] = added(keep_y[...], from_x[:half, :])
    x_ref[...] = added(keep_x[...], from_y[:half, :])


def second_sums_kernel(from_x, from_y, near, from_y2, from_x2, *outs, with_small):
    if with_small:
        small, outs = outs[0], outs[1:]
    far = len(outs)
    half = from_y2.shape[0]
    rows = half * 2 // far
    if with_small:
        values = small[...]
        high = values.astype(BF16).astype(F32)
        extra = jnp.concatenate([high, values - high], axis=0).astype(BF16)
    for i, out in enumerate(outs):
        first, second, place = (from_x, from_y2, i) if i < far // 2 else (from_y, from_x2, i - far // 2)
        out[:rows, :] = added(
            near[i * rows : (i + 1) * rows, :],
            first[half + place * rows : half + (place + 1) * rows, :],
            second[place * rows : (place + 1) * rows, :],
        )
        if with_small:
            out[rows:, :] = extra


def z_sums_kernel(z_ref, from_x, from_y, near, from_y2, from_x2, out, *, far):
    half = from_y2.shape[0]
    rows = half * 2 // far
    for i in range(far):
        first, second, place = (from_x, from_y2, i) if i < far // 2 else (from_y, from_x2, i - far // 2)
        target = pl.multiple_of((z_ref[0] ^ i) * rows, rows)
        out[pl.ds(target, rows), :] = added(
            near[i * rows : (i + 1) * rows, :],
            first[half + place * rows : half + (place + 1) * rows, :],
            second[place * rows : (place + 1) * rows, :],
        )


def weights_last_kernel(*refs):
    parts, outs, small = refs[:-5], refs[-5:-1], refs[-1]
    total = parts[0][...].astype(F32)
    for part in parts[1:]:
        total = total + part[...].astype(F32)
    rows, columns = outs[0].shape
    for k, out in enumerate(outs):
        out[...] = total[:rows, k * columns : (k + 1) * columns]
    extra = small.shape[0]
    small[...] = total[rows : rows + extra, :] + total[rows + extra :, :]


def units_last_kernel(first_ref, second_ref, up_ref, down_ref, *, tile):
    units = up_ref.shape[1] // 2
    for index, ref in enumerate((first_ref, second_ref)):
        for first in range(0, units, tile):
            columns = slice(index * units + first, index * units + first + tile)
            up_ref[:, columns] = ref[:, 2 * first : 2 * first + tile].astype(F32)
            down_ref[:, columns] = ref[:, 2 * first + tile : 2 * first + 2 * tile].astype(F32)


def shards_kernel(w_up, w_down, first_ref, second_ref, *, tile):
    units = first_ref.shape[1] // 2
    for index, ref in enumerate((first_ref, second_ref)):
        for first in range(0, units, tile):
            columns = slice(index * units + first, index * units + first + tile)
            ref[:, 2 * first : 2 * first + tile] = w_up[:, columns]
            ref[:, 2 * first + tile : 2 * first + 2 * tile] = w_down[:, columns]


def sums_call(kernel, operands, shapes, after, name):
    body = kernel if after is None else without(kernel, 0)
    vmem = pl.BlockSpec(memory_space=pltpu.VMEM)
    return pl.pallas_call(
        body,
        in_specs=([pl.BlockSpec(memory_space=pl.ANY)] if after is not None else [])
        + [vmem] * len(operands),
        out_specs=[vmem] * len(shapes),
        out_shape=shapes,
        compiler_params=pltpu.CompilerParams(vmem_limit_bytes=VMEM_BYTES),
        cost_estimate=pl.CostEstimate(flops=0, bytes_accessed=1024 * 1024, transcendentals=0),
        name=name,
    )(*([after] if after is not None else []), *operands)


def flipped(sizes):
    return 1 if sizes["h"] * sizes["l"] == 2 else 0


def moves(sizes):
    groups, ranks, inner = sizes["a"], sizes["h"] * sizes["l"], sizes["l"]
    far = groups // 2
    flip = flipped(sizes)
    swap_to = {}
    for group in range(2):
        for part in range(ranks):
            place = (part % 2 ^ flip) * ranks + group * (ranks // 2) + part // 2
            swap_to[group * ranks + part] = place

    def swap(values, inverse=False):
        pairs = [(to, frm) if inverse else (frm, to) for frm, to in swap_to.items()]
        return lax.ppermute(values, SWAP, pairs)

    def swap_hop(values, a_mask, inverse=False):
        pairs = []
        for a in range(groups):
            for frm, to in swap_to.items():
                one, two = a * 2 * ranks + frm, (a ^ a_mask) * 2 * ranks + to
                pairs.append((two, one) if inverse else (one, two))
        return lax.ppermute(values, ALL, pairs)

    def hop(values, a_mask, h_mask):
        pairs = []
        for a in range(groups):
            for c in range(2):
                for h in range(2):
                    pairs.append(((a * 2 + c) * 2 + h, ((a ^ a_mask) * 2 + c) * 2 + (h ^ h_mask)))
        return lax.ppermute(values, ("z", "y", "c", "h"), pairs)

    def scatter_near(pieces, after):
        from_x, from_y = hop(pieces[0], 0, 1), hop(pieces[1], 1, 0)
        half, columns = pieces[2].shape
        y_sum, x_sum = sums_call(
            first_sums_kernel,
            [from_x, from_y, pieces[2], pieces[3]],
            [jax.ShapeDtypeStruct((half, columns), BF16)] * 2,
            after,
            "sums_one",
        )
        return from_x, from_y, pieces[4], y_sum, x_sum

    def far_sums(state, small, after):
        from_x, from_y, near, y_sum, x_sum = state
        columns = near.shape[1]
        from_y2, from_x2 = hop(y_sum, 1, 0), hop(x_sum, 0, 1)
        rows = near.shape[0] // far + sum(2 * values.shape[0] for values in small)
        return sums_call(
            functools.partial(second_sums_kernel, with_small=bool(small)),
            [from_x, from_y, near, from_y2, from_x2] + small,
            [jax.ShapeDtypeStruct((rows, columns), BF16)] * far,
            after,
            "sums_two",
        )

    def z_sums(state, after):
        from_x, from_y, near, y_sum, x_sum = state
        from_y2, from_x2 = hop(y_sum, 1, 0), hop(x_sum, 0, 1)
        vmem = pl.BlockSpec(memory_space=pltpu.VMEM)
        return pl.pallas_call(
            without(functools.partial(z_sums_kernel, far=far), 6),
            in_specs=[pl.BlockSpec(memory_space=pltpu.SMEM)] + [vmem] * 5 + [ORDER_ONLY],
            out_specs=vmem,
            out_shape=jax.ShapeDtypeStruct(near.shape, BF16),
            compiler_params=pltpu.CompilerParams(vmem_limit_bytes=VMEM_BYTES),
            name="sums_two_z",
        )(lax.axis_index("z").reshape(1), from_x, from_y, near, from_y2, from_x2, after)

    def far_parts(sums):
        return [swap_hop(sums[i], 2 * i, inverse=True) for i in range(far)]

    def near_sum(values):
        values = values + lax.ppermute(values, "c", [(0, 1), (1, 0)])
        values = values + hop(values, 1, 0)
        values = values + hop(values, 0, 1)
        return lax.psum(values, "l") if inner > 1 else values

    a, h = lax.axis_index(("z", "y")), lax.axis_index("h")
    order = []
    for a_low, h_mask in ((0, 0), (1, 0), (0, 1), (1, 1)):
        for i in range(far):
            order.append((a ^ (2 * i + a_low)) * 2 + (h ^ h_mask))
    return swap, hop, scatter_near, far_sums, z_sums, far_parts, near_sum, jnp.stack(order).astype(jnp.int32)


def per_device(sizes, *arguments):
    (
        block_input, segment_ids, ln1_gain, ln1_bias, w_query, w_key, w_value, b_query, b_value,
        w_out, b_out, ln2_gain, ln2_bias, w_up, b_up, w_down, b_down, out_grad,
    ) = arguments
    ranks = sizes["h"] * sizes["l"]
    rank = lax.axis_index("l") * 2 + (lax.axis_index("c") ^ flipped(sizes))
    own_rows, width = block_input.shape
    head_width = w_query.shape[1]
    unit_width = w_up.shape[1]
    half_units = unit_width // 2
    tile = min(TILE, half_units)
    swap, hop, scatter_near, far_sums, z_sums, far_parts, near_sum, order = moves(sizes)

    def partner(values):
        return lax.ppermute(values, "c", [(0, 1), (1, 0)])

    def tp_gather(values):
        if ranks != 2:
            return lax.all_gather(values, TP, axis=0, tiled=True)
        theirs = partner(values)
        return jnp.where(
            rank == 0,
            jnp.concatenate([values, theirs], axis=0),
            jnp.concatenate([theirs, values], axis=0),
        )

    def tp_terms(values):
        if ranks != 2:
            others = lax.psum(values.astype(F32), TP) - values.astype(F32)
            return values, others.astype(BF16)
        return values, partner(values)

    def own(values):
        return lax.dynamic_slice_in_dim(values, rank * own_rows, own_rows)

    def tp_scatter_terms(values):
        if ranks != 2:
            total = lax.psum_scatter(values, TP, scatter_dimension=0, tiled=True)
            return total, jnp.zeros_like(total)
        theirs = lax.dynamic_slice_in_dim(values, (1 - rank) * own_rows, own_rows)
        return own(values), partner(theirs)

    def tp_scatter(values):
        own_part, other_part = tp_scatter_terms(values)
        return own_part.astype(F32) + other_part.astype(F32)

    own_input = swap(block_input)
    segments = swap(segment_ids)
    own_grad = swap(out_grad)
    shard_first, shard_second = sums_call(
        functools.partial(shards_kernel, tile=tile),
        [w_up, w_down],
        [jax.ShapeDtypeStruct(w_up.shape, BF16)] * 2,
        None,
        "mlp_shards",
    )
    early_attn = lax.all_gather(
        jnp.concatenate([w_query, w_key, w_value, w_out], axis=1), ("z", "y", "c"), axis=0, tiled=True
    )
    early_first = lax.all_gather(shard_first, ("z", "y", "c"), axis=0, tiled=True)
    shard_second = swap(shard_second)
    other_second = hop(shard_second, 0, 1)
    shard_second = jnp.where(
        lax.axis_index("h") == 0,
        jnp.concatenate([shard_second, other_second], axis=0),
        jnp.concatenate([other_second, shard_second], axis=0),
    )
    bias_query = lax.dynamic_slice_in_dim(b_query, rank * head_width, head_width)
    bias_value = lax.dynamic_slice_in_dim(b_value, rank * head_width, head_width)
    bias_up = lax.dynamic_slice_in_dim(b_up, rank * unit_width, unit_width)

    rows_in = tp_gather(own_input)
    grad_rows = tp_gather(own_grad)
    grad_rows_t = grad_rows.T
    normed, normed_t = norm_rows(rows_in, ln1_gain, ln1_bias)
    early_attn, normed, segments, grad_rows, grad_rows_t, shard_second = lax.optimization_barrier(
        (early_attn, normed, segments, grad_rows, grad_rows_t, shard_second)
    )
    full_second = lax.all_gather(shard_second, ("z", "y"), axis=0, tiled=True)
    full_attn = swap(early_attn)
    biases = jnp.concatenate([bias_query, jnp.zeros((head_width,), F32), bias_value])
    qkv = qkv_project(normed, full_attn, biases)
    full_out = full_attn[:, 3 * head_width :]
    early_first, qkv = lax.optimization_barrier((early_first, qkv))
    full_first = swap(early_first)
    mixed, lse = attn_forward(segments, qkv, head_width)
    attended = tp_terms(dot_nt(mixed, full_out).astype(BF16))
    normed_two, normed_two_t, hidden = norm_rows(rows_in, ln2_gain, ln2_bias, attended, b_out)

    out_part, gn_part, first_grads, bias_first = mlp(
        order, normed_two, grad_rows, normed_two_t, grad_rows_t, full_first,
        bias_up[:half_units], (), True,
    )
    full_second, gn_part = lax.optimization_barrier((full_second, gn_part))
    out_part, gn_part, second_grads, bias_second = mlp(
        order, normed_two, grad_rows, normed_two_t, grad_rows_t, full_second,
        bias_up[half_units:], (out_part, gn_part), False,
    )
    first_state = scatter_near(first_grads, gn_part)
    gn_part, second_grads, first_state = lax.optimization_barrier(
        (gn_part, second_grads[0], first_state)
    )
    own_output = (own(hidden) + tp_scatter(out_part) + b_down).astype(BF16)

    grad_hidden, grad_attended, grad_attended_t, sums_two = norm_back_rows(
        hidden, grad_rows, tp_terms(gn_part), ln2_gain
    )
    first_sums = z_sums(first_state, grad_attended)
    second_grads, first_sums = lax.optimization_barrier((second_grads, first_sums))
    second_grads = swap(second_grads, inverse=True)
    grad_mixed = dot_nn(grad_attended, full_out).astype(BF16)
    first_mlp = lax.psum_scatter(first_sums, "z", scatter_dimension=0, tiled=True)
    grads = attn_backward(segments, qkv, mixed, lse, grad_mixed, head_width, first_sums)
    block_rows = w_query.shape[0]
    pieces = weight_grads(order, normed_t, grads, grad_attended_t, mixed, grads)
    grad_normed_part = qkv_back(grads, full_attn, pieces[0])
    second_grads, first_mlp, grad_normed_part = lax.optimization_barrier(
        (second_grads, first_mlp, grad_normed_part)
    )
    second_mlp = lax.psum_scatter(second_grads, ("z", "y", "c"), scatter_dimension=0, tiled=True)
    state = scatter_near(pieces, grad_normed_part)
    grad_normed_own, grad_normed_other = tp_scatter_terms(grad_normed_part)
    first_mlp, grad_normed_other, state = lax.optimization_barrier(
        (first_mlp, grad_normed_other, state)
    )
    first_mlp = swap(first_mlp, inverse=True)
    grad_normed = grad_normed_own.astype(F32) + grad_normed_other.astype(F32)
    own_scaled, own_inverse = normalize(own_input.astype(F32))
    grad_own = own(grad_hidden) + norm_back(grad_normed, own_scaled, own_inverse, ln1_gain)
    grad_own = grad_own.astype(BF16)

    def place_part(values, full):
        return lax.dynamic_update_slice_in_dim(
            jnp.zeros((full,), F32), values, rank * values.shape[0], 0
        )

    sums = jnp.concatenate(
        [
            jnp.sum(grad_normed * own_scaled, axis=0),
            jnp.sum(grad_normed, axis=0),
            place_part(jnp.sum(grads[0].astype(F32), axis=0), width),
            place_part(jnp.sum(grads[2].astype(F32), axis=0), width),
            (sums_two[:3] * (1.0 / ranks)).reshape(-1),
            jnp.sum(own_grad.astype(F32), axis=0),
            place_part(jnp.concatenate([bias_first[0], bias_second[0]]), b_up.shape[0]),
        ]
    )
    columns = pieces[0].shape[1]
    filled = sums.shape[0]
    sums = jnp.pad(sums, (0, -filled % (8 * columns))).reshape(-1, columns)
    sums = near_sum(sums)
    last_sums = far_sums(state, [sums], first_mlp)
    own_output, grad_own, *last_sums = lax.optimization_barrier((own_output, grad_own, *last_sums))
    leaving = swap(jnp.concatenate([own_output, grad_own], axis=0), inverse=True)
    output, grad_input = leaving[:own_rows], leaving[own_rows:]
    shard = jax.ShapeDtypeStruct((block_rows, unit_width), F32)
    grad_w_up, grad_w_down = sums_call(
        functools.partial(units_last_kernel, tile=tile),
        [first_mlp, second_mlp],
        [shard, shard],
        None,
        "units_last",
    )
    *late, sums = sums_call(
        weights_last_kernel,
        far_parts(last_sums),
        [jax.ShapeDtypeStruct((block_rows, head_width), F32)] * 4
        + [jax.ShapeDtypeStruct(sums.shape, F32)],
        grad_w_up,
        "sums_last",
    )
    sums = sums.reshape(-1)
    small = [sums[i * width : (i + 1) * width] for i in range(8)]
    return (
        output, grad_input, small[0], small[1],
        late[0], late[1], late[2], small[2], small[3], late[3], small[4], small[5], small[6],
        grad_w_up, sums[8 * width : filled], grad_w_down, small[7],
    )


def solution(mesh):
    groups, ranks = mesh.shape["dp"], mesh.shape["tensor"]
    sizes = {"a": groups // 2, "h": 2, "l": ranks // 2}
    fine = Mesh(mesh.devices.reshape(groups // 4, 2, 2, 2, ranks // 2), ALL)
    rows = P(ALL, None)
    block = P(("z", "y", "c"), ("h", "l"))
    return jax.shard_map(
        functools.partial(per_device, sizes),
        mesh=fine,
        in_specs=(
            rows, P(("z", "y", "c")), P(), P(), block, block, block, P(), P(), block, P(), P(), P(),
            block, P(), block, P(), rows,
        ),
        out_specs=(
            rows, rows, P(), P(), block, block, block, P(), P(), block, P(), P(), P(), block, P(),
            block, P(),
        ),
        check_vma=False,
    )
```

```python
import functools

import jax
import jax.numpy as jnp
from jax import lax
from jax.experimental import pallas as pl
from jax.experimental.pallas import tpu as pltpu
from jax.sharding import Mesh
from jax.sharding import PartitionSpec as P

HEAD_DIM = 64
LANES = 128
TILE = 512
ROWS = 512
MASKED = -1e30
VMEM_BYTES = 60 * 1024 * 1024
F32 = jnp.float32
BF16 = jnp.bfloat16
TP = ("l", "c")
SWAP = ("c", "h", "l")
ALL = ("z", "y", "c", "h", "l")


def normalize(values):
    center = values - jnp.mean(values, axis=-1, keepdims=True)
    spread = jnp.mean(center * center, axis=-1, keepdims=True)
    inverse = lax.rsqrt(spread + 1e-05)
    return center * inverse, inverse


def norm_back(grad_in, scaled, inverse, gain_vec):
    local_grad = grad_in * gain_vec
    return inverse * (
        local_grad
        - jnp.mean(local_grad, axis=-1, keepdims=True)
        - scaled * jnp.mean(local_grad * scaled, axis=-1, keepdims=True)
    )


def dot_nn(left, right):
    return lax.dot_general(left, right, (((1,), (0,)), ((), ())), preferred_element_type=F32)


def dot_nt(left, right):
    return lax.dot_general(left, right, (((1,), (1,)), ((), ())), preferred_element_type=F32)


def dot_tn(left, right):
    return lax.dot_general(left, right, (((0,), (0,)), ((), ())), preferred_element_type=F32)


def fill_bias(bias, seg_col, seg_row):
    length = bias.shape[0]
    block = min(256, length)
    for first in range(0, length, block):
        keys = lax.broadcasted_iota(jnp.int32, (block, length), 0) + first
        places = lax.broadcasted_iota(jnp.int32, (block, length), 1)
        same = seg_col[first : first + block, :] == seg_row[...]
        bias[first : first + block, :] = jnp.where(same & (keys <= places), 0.0, MASKED)


def head_lanes(values, head):
    lane = lax.broadcasted_iota(jnp.int32, values.shape, 1)
    inside = (lane >= head * HEAD_DIM) & (lane < (head + 1) * HEAD_DIM)
    return jnp.where(inside, values, jnp.zeros_like(values))


def attn_forward_kernel(seg_col, seg_row, q_ref, k_ref, v_ref, mixed_ref, lse_ref, bias, v_t, block):
    length = q_ref.shape[0]
    heads = LANES // HEAD_DIM

    @pl.when(pl.program_id(0) == 0)
    def _():
        fill_bias(bias, seg_col, seg_row)

    v_t[...] = v_ref[...].T
    for place in range(length // block):
        rows = slice(place * block, (place + 1) * block)
        outs = []
        for head in range(heads):
            query = head_lanes(q_ref[rows, :], head)
            scores = []
            peak = None
            for other in range(place + 1):
                keys = slice(other * block, (other + 1) * block)
                part = dot_nt(k_ref[keys, :], query) + bias[keys, rows]
                top = jnp.max(part, axis=0, keepdims=True)
                peak = top if peak is None else jnp.maximum(peak, top)
                scores.append(part)
            total = None
            acc = None
            for other in range(place + 1):
                keys = slice(other * block, (other + 1) * block)
                weight = jnp.exp(scores[other] - peak)
                part_sum = jnp.sum(weight, axis=0, keepdims=True)
                total = part_sum if total is None else total + part_sum
                part_out = dot_nn(
                    v_t[head * HEAD_DIM : (head + 1) * HEAD_DIM, keys], weight.astype(BF16)
                )
                acc = part_out if acc is None else acc + part_out
            outs.append(acc / total)
            lse_ref[0, head : head + 1, rows] = peak + jnp.log(total)
        mixed_ref[rows, :] = jnp.concatenate(outs, axis=0).T.astype(BF16)


def attn_backward_kernel(
    seg_col, seg_row, q_ref, k_ref, v_ref, mixed_ref, lse_ref, g_ref, grads_ref, bias, k_t, delta, dq_t, block
):
    length = q_ref.shape[0]
    heads = LANES // HEAD_DIM
    count = length // block

    @pl.when(pl.program_id(0) == 0)
    def _():
        fill_bias(bias, seg_col, seg_row)

    k_t[...] = k_ref[...].T
    product = (g_ref[...].astype(F32) * mixed_ref[...].astype(F32)).T
    for head in range(heads):
        delta[head : head + 1, :] = jnp.sum(
            product[head * HEAD_DIM : (head + 1) * HEAD_DIM, :], axis=0, keepdims=True
        )
    for other in range(count):
        keys = slice(other * block, (other + 1) * block)
        key_sum = None
        value_sum = None
        for head in range(heads):
            lanes = slice(head * HEAD_DIM, (head + 1) * HEAD_DIM)
            for place in range(other, count):
                rows = slice(place * block, (place + 1) * block)
                query = head_lanes(q_ref[rows, :], head)
                grad = head_lanes(g_ref[rows, :], head)
                scores = dot_nt(k_ref[keys, :], query) + bias[keys, rows]
                probs = jnp.exp(scores - lse_ref[0, head : head + 1, rows])
                grad_probs = dot_nt(v_ref[keys, :], grad)
                grad_scores = (probs * (grad_probs - delta[head : head + 1, rows])).astype(BF16)
                value_part = dot_nn(probs.astype(BF16), grad)
                key_part = dot_nn(grad_scores, query)
                query_part = dot_nn(k_t[lanes, keys], grad_scores)
                value_sum = value_part if value_sum is None else value_sum + value_part
                key_sum = key_part if key_sum is None else key_sum + key_part
                if other == 0:
                    dq_t[lanes, rows] = query_part
                else:
                    dq_t[lanes, rows] += query_part
        grads_ref[1, keys, :] = key_sum.astype(BF16)
        grads_ref[2, keys, :] = value_sum.astype(BF16)
    grads_ref[0] = (dq_t[...].T * HEAD_DIM ** (-0.5)).astype(BF16)


def attn_forward(segments, qkv, width):
    length = qkv.shape[0]
    pairs = width // LANES
    block = min(256, length)
    column = lambda first: pl.BlockSpec((length, LANES), lambda p: (0, first * pairs + p))
    whole = lambda shape: pl.BlockSpec(shape, lambda p: (0, 0))
    return pl.pallas_call(
        functools.partial(attn_forward_kernel, block=block),
        grid=(pairs,),
        in_specs=[whole((length, 1)), whole((1, length)), column(0), column(1), column(2)],
        out_specs=[
            pl.BlockSpec((length, LANES), lambda p: (0, p)),
            pl.BlockSpec((1, 8, length), lambda p: (p, 0, 0)),
        ],
        out_shape=[
            jax.ShapeDtypeStruct((length, width), BF16),
            jax.ShapeDtypeStruct((pairs, 8, length), F32),
        ],
        scratch_shapes=[pltpu.VMEM((length, length), F32), pltpu.VMEM((LANES, length), BF16)],
        compiler_params=pltpu.CompilerParams(vmem_limit_bytes=VMEM_BYTES),
        cost_estimate=pl.CostEstimate(
            flops=4 * length * length * width,
            bytes_accessed=8 * length * width,
            transcendentals=length * length * width // (2 * HEAD_DIM),
        ),
        name="attn_forward",
    )(segments.reshape(length, 1), segments.reshape(1, length), qkv, qkv, qkv)


def attn_backward(segments, qkv, mixed, lse, grad_mixed, width, after):
    length = qkv.shape[0]
    pairs = width // LANES
    block = min(256, length)
    column = lambda first: pl.BlockSpec((length, LANES), lambda p: (0, first * pairs + p))
    whole = lambda shape: pl.BlockSpec(shape, lambda p: (0, 0))
    return pl.pallas_call(
        without(functools.partial(attn_backward_kernel, block=block), 8),
        grid=(pairs,),
        in_specs=[
            whole((length, 1)),
            whole((1, length)),
            column(0),
            column(1),
            column(2),
            pl.BlockSpec((length, LANES), lambda p: (0, p)),
            pl.BlockSpec((1, 8, length), lambda p: (p, 0, 0)),
            pl.BlockSpec((length, LANES), lambda p: (0, p)),
            pl.BlockSpec(memory_space=pl.ANY),
        ],
        out_specs=pl.BlockSpec((3, length, LANES), lambda p: (0, 0, p)),
        out_shape=jax.ShapeDtypeStruct((3, length, width), BF16),
        scratch_shapes=[
            pltpu.VMEM((length, length), F32),
            pltpu.VMEM((LANES, length), BF16),
            pltpu.VMEM((8, length), F32),
            pltpu.VMEM((LANES, length), F32),
        ],
        compiler_params=pltpu.CompilerParams(vmem_limit_bytes=VMEM_BYTES),
        cost_estimate=pl.CostEstimate(
            flops=10 * length * length * width,
            bytes_accessed=16 * length * width,
            transcendentals=length * length * width // (2 * HEAD_DIM),
        ),
        name="attn_backward",
    )(segments.reshape(length, 1), segments.reshape(1, length), qkv, qkv, qkv, mixed, lse, grad_mixed, after)


def piece_blocks(count):
    far = count // 4
    half = far // 2
    near, by_y, by_x, both = (list(range(i * far, (i + 1) * far)) for i in range(4))
    return [
        both[:half] + by_x[:half],
        both[half:] + by_y[half:],
        by_y[:half],
        by_x[half:],
        near,
    ]


def store_pieces(order, grad, piece_refs, columns):
    count = order.shape[0]
    rows = grad.shape[0] // count
    for blocks, ref in zip(piece_blocks(count), piece_refs):
        for place, block in enumerate(blocks):
            first = pl.multiple_of(order[block] * rows, rows)
            ref[place * rows : (place + 1) * rows, columns] = grad[pl.ds(first, rows), :]


def piece_shapes(count, rows, columns):
    return [
        jax.ShapeDtypeStruct((len(blocks) * rows, columns), BF16) for blocks in piece_blocks(count)
    ]


def whole_spec(shape, **options):
    return pl.BlockSpec(shape, lambda step: (0,) * len(shape), **options)


def norm_kernel(*refs, residual):
    if residual:
        x_ref, own_ref, other_ref, shift_ref, gain_ref, bias_ref, n_ref, nt_ref, hidden_ref = refs
        values = (
            x_ref[...].astype(F32)
            + (own_ref[...].astype(F32) + other_ref[...].astype(F32))
            + shift_ref[...]
        )
        hidden_ref[...] = values
    else:
        x_ref, gain_ref, bias_ref, n_ref, nt_ref = refs
        values = x_ref[...].astype(F32)
    scaled, _ = normalize(values)
    normed = (scaled * gain_ref[...] + bias_ref[...]).astype(BF16)
    n_ref[...] = normed
    nt_ref[...] = normed.T


def norm_rows(x, gain, bias, partials=None, shift=None):
    length, width = x.shape
    block = min(256, length)
    row = pl.BlockSpec((block, width), lambda step: (step, 0))
    vector = whole_spec((1, width))
    residual = partials is not None
    operands = [x] + (list(partials) + [shift.reshape(1, width)] if residual else [])
    operands += [gain.reshape(1, width), bias.reshape(1, width)]
    return pl.pallas_call(
        functools.partial(norm_kernel, residual=residual),
        grid=(length // block,),
        in_specs=[row] + ([row, row, vector] if residual else []) + [vector, vector],
        out_specs=[row, pl.BlockSpec((width, block), lambda step: (0, step))]
        + ([row] if residual else []),
        out_shape=[
            jax.ShapeDtypeStruct((length, width), BF16),
            jax.ShapeDtypeStruct((width, length), BF16),
        ]
        + ([jax.ShapeDtypeStruct((length, width), F32)] if residual else []),
        compiler_params=pltpu.CompilerParams(vmem_limit_bytes=VMEM_BYTES),
        cost_estimate=pl.CostEstimate(
            flops=20 * length * width, bytes_accessed=14 * length * width, transcendentals=length
        ),
        name="norm_two" if residual else "norm_one",
    )(*operands)


def norm_back_kernel(hidden_ref, g_ref, own_ref, other_ref, gain_ref, grad_ref, low_ref, low_t_ref, sums_ref):
    scaled, inverse = normalize(hidden_ref[...])
    incoming = own_ref[...].astype(F32) + other_ref[...].astype(F32)
    grad = g_ref[...].astype(F32) + norm_back(incoming, scaled, inverse, gain_ref[...])
    grad_ref[...] = grad
    low_ref[...] = grad.astype(BF16)
    low_t_ref[...] = grad.astype(BF16).T

    @pl.when(pl.program_id(0) == 0)
    def _():
        sums_ref[...] = jnp.zeros_like(sums_ref)

    sums_ref[0:1, :] += jnp.sum(grad, axis=0, keepdims=True)
    sums_ref[1:2, :] += jnp.sum(incoming * scaled, axis=0, keepdims=True)
    sums_ref[2:3, :] += jnp.sum(incoming, axis=0, keepdims=True)


def norm_back_rows(hidden, grad, partials, gain):
    length, width = hidden.shape
    block = min(256, length)
    row = pl.BlockSpec((block, width), lambda step: (step, 0))
    return pl.pallas_call(
        norm_back_kernel,
        grid=(length // block,),
        in_specs=[row, row, row, row, whole_spec((1, width))],
        out_specs=[
            row,
            row,
            pl.BlockSpec((width, block), lambda step: (0, step)),
            whole_spec((8, width)),
        ],
        out_shape=[
            jax.ShapeDtypeStruct((length, width), F32),
            jax.ShapeDtypeStruct((length, width), BF16),
            jax.ShapeDtypeStruct((width, length), BF16),
            jax.ShapeDtypeStruct((8, width), F32),
        ],
        compiler_params=pltpu.CompilerParams(vmem_limit_bytes=VMEM_BYTES),
        cost_estimate=pl.CostEstimate(
            flops=30 * length * width, bytes_accessed=16 * length * width, transcendentals=length
        ),
        name="norm_two_back",
    )(hidden, grad, *partials, gain.reshape(1, width))


def mlp_kernel(order, n_ref, g_ref, nt_ref, gt_ref, b_ref, w_ref, *refs, block, with_previous, cube):
    if with_previous:
        (before_out, before_gn), refs = refs[:2], refs[2:]
    (out_ref, gn_ref), refs = refs[:2], refs[2:]
    grad_refs, (gb_ref, out_acc, gn_acc, act, gpre, grad_w) = refs[:-6], refs[-6:]
    step = pl.program_id(0)
    length = n_ref.shape[0]
    tile = w_ref.shape[1] // 2
    ups, downs = slice(0, tile), slice(tile, 2 * tile)

    @pl.when(step == 0)
    def _():
        if with_previous:
            out_acc[...] = before_out[...].astype(F32)
            gn_acc[...] = before_gn[...].astype(F32)
        else:
            out_acc[...] = jnp.zeros_like(out_acc)
            gn_acc[...] = jnp.zeros_like(gn_acc)

    bias_sum = jnp.zeros(gb_ref.shape, F32)
    for first in range(0, length, block):
        rows = slice(first, first + block)
        unit = dot_nn(n_ref[rows, :], w_ref[:, ups]) + b_ref[...]
        grad = dot_nn(g_ref[rows, :], w_ref[:, downs])
        square = unit * unit
        curve = jnp.tanh(0.7978845608028654 * (unit + 0.044715 * (square * unit)))
        half = 0.5 + 0.5 * curve
        slope = half + (0.5 * unit) * (1.0 - curve * curve) * (
            0.7978845608028654 + (3 * 0.044715 * 0.7978845608028654) * square
        )
        active = (unit * half).astype(BF16)
        grad_pre = (grad * slope).astype(BF16)
        act[rows, :] = active
        gpre[rows, :] = grad_pre
        bias_sum = bias_sum + jnp.sum(grad_pre.astype(F32), axis=0, keepdims=True)
        out_acc[rows, :] += dot_nt(active, w_ref[:, downs])
        gn_acc[rows, :] += dot_nt(grad_pre, w_ref[:, ups])
    gb_ref[...] = bias_sum
    for columns, left, right in ((ups, nt_ref, gpre), (downs, gt_ref, act)):
        if cube:
            grad_w[...] = dot_nn(left[...], right[...]).astype(BF16)
            store_pieces(order, grad_w, grad_refs, columns)
        else:
            grad_refs[0][:, columns] = dot_nn(left[...], right[...]).astype(BF16)

    @pl.when(step == pl.num_programs(0) - 1)
    def _():
        out_ref[...] = out_acc[...].astype(BF16)
        gn_ref[...] = gn_acc[...].astype(BF16)


def mlp(order, normed, grad, normed_t, grad_t, weights, bias, previous, cube):
    length, width = normed.shape
    units = weights.shape[1] // 2
    tile = min(TILE, units)
    at_tile = lambda rows, columns: pl.BlockSpec((rows, columns), lambda u, o: (0, u))
    fixed = lambda shape: pl.BlockSpec(shape, lambda u, o: (0, 0))
    once = lambda shape: pl.BlockSpec(shape, lambda u, o: (0, 0), pipeline_mode=pl.Buffered(1))
    if cube:
        count = order.shape[0]
        grad_shapes = piece_shapes(count, width // count, 2 * units)
    else:
        grad_shapes = [jax.ShapeDtypeStruct((width, 2 * units), BF16)]
    results = pl.pallas_call(
        functools.partial(
            mlp_kernel, block=min(ROWS, length), with_previous=bool(previous), cube=cube
        ),
        grid_spec=pltpu.PrefetchScalarGridSpec(
            num_scalar_prefetch=1,
            grid=(units // tile,),
            in_specs=[
                once((length, width)),
                once((length, width)),
                once((width, length)),
                once((width, length)),
                at_tile(1, tile),
                at_tile(width, 2 * tile),
            ]
            + [once((length, width)) for _ in previous],
            out_specs=[fixed((length, width)), fixed((length, width))]
            + [at_tile(shape.shape[0], 2 * tile) for shape in grad_shapes]
            + [at_tile(1, tile)],
            scratch_shapes=[
                pltpu.VMEM((length, width), F32),
                pltpu.VMEM((length, width), F32),
                pltpu.VMEM((length, tile), BF16),
                pltpu.VMEM((length, tile), BF16),
                pltpu.VMEM((width, tile), BF16),
            ],
        ),
        out_shape=[jax.ShapeDtypeStruct((length, width), BF16)] * 2
        + grad_shapes
        + [jax.ShapeDtypeStruct((1, units), F32)],
        compiler_params=pltpu.CompilerParams(vmem_limit_bytes=VMEM_BYTES),
        cost_estimate=pl.CostEstimate(
            flops=12 * length * width * units,
            bytes_accessed=12 * length * width + 8 * width * units,
            transcendentals=length * units,
        ),
        name="mlp_second" if previous else "mlp_first",
    )(order, normed, grad, normed_t, grad_t, bias.reshape(1, units), weights, *previous)
    return results[0], results[1], results[2:-1], results[-1]


def qkv_kernel(n_ref, b_ref, w_ref, out_ref):
    scale = jnp.where(pl.program_id(0) == 0, HEAD_DIM ** (-0.5), 1.0)
    length = n_ref.shape[0]
    step = min(ROWS, length)
    for first in range(0, length, step):
        span = slice(first, first + step)
        out_ref[span, :] = ((dot_nn(n_ref[span, :], w_ref[...]) + b_ref[...]) * scale).astype(BF16)


def qkv_project(normed, weights, bias):
    length, width = normed.shape
    columns = weights.shape[1] // 4
    at_tile = lambda rows: pl.BlockSpec((rows, columns), lambda k: (0, k))
    return pl.pallas_call(
        qkv_kernel,
        grid=(3,),
        in_specs=[
            whole_spec((length, width), pipeline_mode=pl.Buffered(1)), at_tile(1), at_tile(width)
        ],
        out_specs=at_tile(length),
        out_shape=jax.ShapeDtypeStruct((length, 3 * columns), BF16),
        compiler_params=pltpu.CompilerParams(vmem_limit_bytes=VMEM_BYTES),
        cost_estimate=pl.CostEstimate(
            flops=6 * length * width * columns,
            bytes_accessed=2 * length * width + 6 * width * columns + 6 * length * columns,
            transcendentals=0,
        ),
        name="qkv_project",
    )(normed, bias.reshape(1, 3 * columns), weights)


def weight_kernel(order, nt_ref, grads_ref, gt_ref, mixed_ref, order_only, *refs):
    piece_refs, grad = refs[:5], refs[5]
    part = pl.program_id(0)

    @pl.when(part < 3)
    def _():
        grad[...] = dot_nn(nt_ref[...], grads_ref[0]).astype(BF16)

    @pl.when(part == 3)
    def _():
        grad[...] = dot_nn(gt_ref[...], mixed_ref[...]).astype(BF16)

    store_pieces(order, grad, piece_refs, slice(None))


def without(kernel, place):
    return lambda *refs: kernel(*refs[:place], *refs[place + 1 :])


ORDER_ONLY = pl.BlockSpec(memory_space=pl.ANY)


def weight_grads(order, normed_t, grads, grad_t, mixed, after):
    width, length = normed_t.shape
    columns = grads.shape[2]
    shapes = piece_shapes(order.shape[0], width // order.shape[0], 4 * columns)
    fixed = lambda shape: pl.BlockSpec(shape, lambda k, o: (0, 0), pipeline_mode=pl.Buffered(1))
    return pl.pallas_call(
        weight_kernel,
        grid_spec=pltpu.PrefetchScalarGridSpec(
            num_scalar_prefetch=1,
            grid=(4,),
            in_specs=[
                fixed((width, length)),
                pl.BlockSpec((1, length, columns), lambda k, o: (jnp.minimum(k, 2), 0, 0)),
                fixed((width, length)),
                fixed((length, columns)),
                ORDER_ONLY,
            ],
            out_specs=[
                pl.BlockSpec((shape.shape[0], columns), lambda k, o: (0, k)) for shape in shapes
            ],
            scratch_shapes=[pltpu.VMEM((width, columns), BF16)],
        ),
        out_shape=shapes,
        compiler_params=pltpu.CompilerParams(vmem_limit_bytes=VMEM_BYTES),
        cost_estimate=pl.CostEstimate(
            flops=8 * length * width * columns,
            bytes_accessed=4 * length * width + 16 * width * columns,
            transcendentals=0,
        ),
        name="weight_grads",
    )(order, normed_t, grads, grad_t, mixed, after)


def qkv_back_kernel(grads_ref, w_ref, out_ref):
    columns = grads_ref.shape[2]
    total = None
    for k in range(3):
        part = dot_nt(grads_ref[k], w_ref[:, k * columns : (k + 1) * columns])
        total = part if total is None else total + part
    out_ref[...] = total.astype(BF16)


def qkv_back(grads, weights, after):
    _, length, columns = grads.shape
    width = weights.shape[0]
    block = min(ROWS, length)
    return pl.pallas_call(
        without(qkv_back_kernel, 2),
        grid=(length // block,),
        in_specs=[
            pl.BlockSpec((3, block, columns), lambda i: (0, i, 0)),
            pl.BlockSpec((width, 4 * columns), lambda i: (0, 0), pipeline_mode=pl.Buffered(1)),
            ORDER_ONLY,
        ],
        out_specs=pl.BlockSpec((block, width), lambda i: (i, 0)),
        out_shape=jax.ShapeDtypeStruct((length, width), BF16),
        compiler_params=pltpu.CompilerParams(vmem_limit_bytes=VMEM_BYTES),
        cost_estimate=pl.CostEstimate(
            flops=6 * length * width * columns,
            bytes_accessed=2 * length * width + 6 * width * columns + 6 * length * columns,
            transcendentals=0,
        ),
        name="qkv_back",
    )(grads, weights, after)


def added(*terms):
    total = terms[0].astype(F32)
    for term in terms[1:]:
        total = total + term.astype(F32)
    return total.astype(BF16)


def first_sums_kernel(from_x, from_y, keep_y, keep_x, y_ref, x_ref):
    half = y_ref.shape[0]
    y_ref[...] = added(keep_y[...], from_x[:half, :])
    x_ref[...] = added(keep_x[...], from_y[:half, :])


def second_sums_kernel(from_x, from_y, near, from_y2, from_x2, *outs, with_small):
    if with_small:
        small, outs = outs[0], outs[1:]
    far = len(outs)
    half = from_y2.shape[0]
    rows = half * 2 // far
    if with_small:
        values = small[...]
        high = values.astype(BF16).astype(F32)
        extra = jnp.concatenate([high, values - high], axis=0).astype(BF16)
    for i, out in enumerate(outs):
        first, second, place = (from_x, from_y2, i) if i < far // 2 else (from_y, from_x2, i - far // 2)
        out[:rows, :] = added(
            near[i * rows : (i + 1) * rows, :],
            first[half + place * rows : half + (place + 1) * rows, :],
            second[place * rows : (place + 1) * rows, :],
        )
        if with_small:
            out[rows:, :] = extra


def z_sums_kernel(z_ref, from_x, from_y, near, from_y2, from_x2, out, *, far):
    half = from_y2.shape[0]
    rows = half * 2 // far
    for i in range(far):
        first, second, place = (from_x, from_y2, i) if i < far // 2 else (from_y, from_x2, i - far // 2)
        target = pl.multiple_of((z_ref[0] ^ i) * rows, rows)
        out[pl.ds(target, rows), :] = added(
            near[i * rows : (i + 1) * rows, :],
            first[half + place * rows : half + (place + 1) * rows, :],
            second[place * rows : (place + 1) * rows, :],
        )


def weights_last_kernel(*refs):
    parts, outs, small = refs[:-5], refs[-5:-1], refs[-1]
    total = parts[0][...].astype(F32)
    for part in parts[1:]:
        total = total + part[...].astype(F32)
    rows, columns = outs[0].shape
    for k, out in enumerate(outs):
        out[...] = total[:rows, k * columns : (k + 1) * columns]
    extra = small.shape[0]
    small[...] = total[rows : rows + extra, :] + total[rows + extra :, :]


def units_last_kernel(first_ref, second_ref, up_ref, down_ref, *, tile):
    units = up_ref.shape[1] // 2
    for index, ref in enumerate((first_ref, second_ref)):
        for first in range(0, units, tile):
            columns = slice(index * units + first, index * units + first + tile)
            up_ref[:, columns] = ref[:, 2 * first : 2 * first + tile].astype(F32)
            down_ref[:, columns] = ref[:, 2 * first + tile : 2 * first + 2 * tile].astype(F32)


def shards_kernel(w_up, w_down, first_ref, second_ref, *, tile):
    units = first_ref.shape[1] // 2
    for index, ref in enumerate((first_ref, second_ref)):
        for first in range(0, units, tile):
            columns = slice(index * units + first, index * units + first + tile)
            ref[:, 2 * first : 2 * first + tile] = w_up[:, columns]
            ref[:, 2 * first + tile : 2 * first + 2 * tile] = w_down[:, columns]


def sums_call(kernel, operands, shapes, after, name):
    body = kernel if after is None else without(kernel, 0)
    vmem = pl.BlockSpec(memory_space=pltpu.VMEM)
    return pl.pallas_call(
        body,
        in_specs=([pl.BlockSpec(memory_space=pl.ANY)] if after is not None else [])
        + [vmem] * len(operands),
        out_specs=[vmem] * len(shapes),
        out_shape=shapes,
        compiler_params=pltpu.CompilerParams(vmem_limit_bytes=VMEM_BYTES),
        cost_estimate=pl.CostEstimate(flops=0, bytes_accessed=1024 * 1024, transcendentals=0),
        name=name,
    )(*([after] if after is not None else []), *operands)


def flipped(sizes):
    return 1 if sizes["h"] * sizes["l"] == 2 else 0


def moves(sizes):
    groups, ranks, inner = sizes["a"], sizes["h"] * sizes["l"], sizes["l"]
    far = groups // 2
    flip = flipped(sizes)
    swap_to = {}
    for group in range(2):
        for part in range(ranks):
            place = (part % 2 ^ flip) * ranks + group * (ranks // 2) + part // 2
            swap_to[group * ranks + part] = place

    def swap(values, inverse=False):
        pairs = [(to, frm) if inverse else (frm, to) for frm, to in swap_to.items()]
        return lax.ppermute(values, SWAP, pairs)

    def swap_hop(values, a_mask, inverse=False):
        pairs = []
        for a in range(groups):
            for frm, to in swap_to.items():
                one, two = a * 2 * ranks + frm, (a ^ a_mask) * 2 * ranks + to
                pairs.append((two, one) if inverse else (one, two))
        return lax.ppermute(values, ALL, pairs)

    def hop(values, a_mask, h_mask):
        pairs = []
        for a in range(groups):
            for c in range(2):
                for h in range(2):
                    pairs.append(((a * 2 + c) * 2 + h, ((a ^ a_mask) * 2 + c) * 2 + (h ^ h_mask)))
        return lax.ppermute(values, ("z", "y", "c", "h"), pairs)

    def scatter_near(pieces, after):
        from_x, from_y = hop(pieces[0], 0, 1), hop(pieces[1], 1, 0)
        half, columns = pieces[2].shape
        y_sum, x_sum = sums_call(
            first_sums_kernel,
            [from_x, from_y, pieces[2], pieces[3]],
            [jax.ShapeDtypeStruct((half, columns), BF16)] * 2,
            after,
            "sums_one",
        )
        return from_x, from_y, pieces[4], y_sum, x_sum

    def far_sums(state, small, after):
        from_x, from_y, near, y_sum, x_sum = state
        columns = near.shape[1]
        from_y2, from_x2 = hop(y_sum, 1, 0), hop(x_sum, 0, 1)
        rows = near.shape[0] // far + sum(2 * values.shape[0] for values in small)
        return sums_call(
            functools.partial(second_sums_kernel, with_small=bool(small)),
            [from_x, from_y, near, from_y2, from_x2] + small,
            [jax.ShapeDtypeStruct((rows, columns), BF16)] * far,
            after,
            "sums_two",
        )

    def z_sums(state, after):
        from_x, from_y, near, y_sum, x_sum = state
        from_y2, from_x2 = hop(y_sum, 1, 0), hop(x_sum, 0, 1)
        vmem = pl.BlockSpec(memory_space=pltpu.VMEM)
        return pl.pallas_call(
            without(functools.partial(z_sums_kernel, far=far), 6),
            in_specs=[pl.BlockSpec(memory_space=pltpu.SMEM)] + [vmem] * 5 + [ORDER_ONLY],
            out_specs=vmem,
            out_shape=jax.ShapeDtypeStruct(near.shape, BF16),
            compiler_params=pltpu.CompilerParams(vmem_limit_bytes=VMEM_BYTES),
            name="sums_two_z",
        )(lax.axis_index("z").reshape(1), from_x, from_y, near, from_y2, from_x2, after)

    def far_parts(sums):
        return [swap_hop(sums[i], 2 * i, inverse=True) for i in range(far)]

    def near_sum(values):
        values = values + lax.ppermute(values, "c", [(0, 1), (1, 0)])
        values = values + hop(values, 1, 0)
        values = values + hop(values, 0, 1)
        return lax.psum(values, "l") if inner > 1 else values

    a, h = lax.axis_index(("z", "y")), lax.axis_index("h")
    order = []
    for a_low, h_mask in ((0, 0), (1, 0), (0, 1), (1, 1)):
        for i in range(far):
            order.append((a ^ (2 * i + a_low)) * 2 + (h ^ h_mask))
    return swap, hop, scatter_near, far_sums, z_sums, far_parts, near_sum, jnp.stack(order).astype(jnp.int32)


def per_device(sizes, *arguments):
    (
        block_input, segment_ids, ln1_gain, ln1_bias, w_query, w_key, w_value, b_query, b_value,
        w_out, b_out, ln2_gain, ln2_bias, w_up, b_up, w_down, b_down, out_grad,
    ) = arguments
    ranks = sizes["h"] * sizes["l"]
    rank = lax.axis_index("l") * 2 + (lax.axis_index("c") ^ flipped(sizes))
    own_rows, width = block_input.shape
    head_width = w_query.shape[1]
    unit_width = w_up.shape[1]
    half_units = unit_width // 2
    tile = min(TILE, half_units)
    swap, hop, scatter_near, far_sums, z_sums, far_parts, near_sum, order = moves(sizes)

    def partner(values):
        return lax.ppermute(values, "c", [(0, 1), (1, 0)])

    def tp_gather(values):
        if ranks != 2:
            return lax.all_gather(values, TP, axis=0, tiled=True)
        theirs = partner(values)
        return jnp.where(
            rank == 0,
            jnp.concatenate([values, theirs], axis=0),
            jnp.concatenate([theirs, values], axis=0),
        )

    def tp_terms(values):
        if ranks != 2:
            others = lax.psum(values.astype(F32), TP) - values.astype(F32)
            return values, others.astype(BF16)
        return values, partner(values)

    def own(values):
        return lax.dynamic_slice_in_dim(values, rank * own_rows, own_rows)

    def tp_scatter_terms(values):
        if ranks != 2:
            total = lax.psum_scatter(values, TP, scatter_dimension=0, tiled=True)
            return total, jnp.zeros_like(total)
        theirs = lax.dynamic_slice_in_dim(values, (1 - rank) * own_rows, own_rows)
        return own(values), partner(theirs)

    def tp_scatter(values):
        own_part, other_part = tp_scatter_terms(values)
        return own_part.astype(F32) + other_part.astype(F32)

    own_input = swap(block_input)
    segments = swap(segment_ids)
    own_grad = swap(out_grad)
    shard_first, shard_second = sums_call(
        functools.partial(shards_kernel, tile=tile),
        [w_up, w_down],
        [jax.ShapeDtypeStruct(w_up.shape, BF16)] * 2,
        None,
        "mlp_shards",
    )
    early_attn = lax.all_gather(
        jnp.concatenate([w_query, w_key, w_value, w_out], axis=1), ("z", "y", "c"), axis=0, tiled=True
    )
    early_first = lax.all_gather(shard_first, ("z", "y", "c"), axis=0, tiled=True)
    shard_second = swap(shard_second)
    other_second = hop(shard_second, 0, 1)
    shard_second = jnp.where(
        lax.axis_index("h") == 0,
        jnp.concatenate([shard_second, other_second], axis=0),
        jnp.concatenate([other_second, shard_second], axis=0),
    )
    bias_query = lax.dynamic_slice_in_dim(b_query, rank * head_width, head_width)
    bias_value = lax.dynamic_slice_in_dim(b_value, rank * head_width, head_width)
    bias_up = lax.dynamic_slice_in_dim(b_up, rank * unit_width, unit_width)

    rows_in = tp_gather(own_input)
    grad_rows = tp_gather(own_grad)
    grad_rows_t = grad_rows.T
    normed, normed_t = norm_rows(rows_in, ln1_gain, ln1_bias)
    early_attn, normed, segments, grad_rows, grad_rows_t, shard_second = lax.optimization_barrier(
        (early_attn, normed, segments, grad_rows, grad_rows_t, shard_second)
    )
    full_second = lax.all_gather(shard_second, ("z", "y"), axis=0, tiled=True)
    full_attn = swap(early_attn)
    biases = jnp.concatenate([bias_query, jnp.zeros((head_width,), F32), bias_value])
    qkv = qkv_project(normed, full_attn, biases)
    full_out = full_attn[:, 3 * head_width :]
    early_first, qkv = lax.optimization_barrier((early_first, qkv))
    full_first = swap(early_first)
    mixed, lse = attn_forward(segments, qkv, head_width)
    attended = tp_terms(dot_nt(mixed, full_out).astype(BF16))
    normed_two, normed_two_t, hidden = norm_rows(rows_in, ln2_gain, ln2_bias, attended, b_out)

    out_part, gn_part, first_grads, bias_first = mlp(
        order, normed_two, grad_rows, normed_two_t, grad_rows_t, full_first,
        bias_up[:half_units], (), False,
    )
    first_grads = swap(first_grads[0], inverse=True)
    full_second, gn_part = lax.optimization_barrier((full_second, gn_part))
    out_part, gn_part, second_grads, bias_second = mlp(
        order, normed_two, grad_rows, normed_two_t, grad_rows_t, full_second,
        bias_up[half_units:], (out_part, gn_part), True,
    )
    own_output = (own(hidden) + tp_scatter(out_part) + b_down).astype(BF16)

    grad_hidden, grad_attended, grad_attended_t, sums_two = norm_back_rows(
        hidden, grad_rows, tp_terms(gn_part), ln2_gain
    )
    first_grads, grad_attended = lax.optimization_barrier((first_grads, grad_attended))
    first_mlp = lax.psum_scatter(first_grads, ("z", "y", "c"), scatter_dimension=0, tiled=True)
    grad_mixed = dot_nn(grad_attended, full_out).astype(BF16)
    grads = attn_backward(segments, qkv, mixed, lse, grad_mixed, head_width, grad_mixed)
    block_rows = w_query.shape[0]
    second_state = scatter_near(second_grads, grads)
    grad_normed_part = qkv_back(grads, full_attn, second_state[3])
    pieces = weight_grads(order, normed_t, grads, grad_attended_t, mixed, grad_normed_part)
    second_sums = z_sums(second_state, pieces[0])
    second_mlp = lax.psum_scatter(second_sums, "z", scatter_dimension=0, tiled=True)
    grad_normed = tp_scatter(grad_normed_part)
    own_scaled, own_inverse = normalize(own_input.astype(F32))
    grad_own = own(grad_hidden) + norm_back(grad_normed, own_scaled, own_inverse, ln1_gain)
    grad_own = grad_own.astype(BF16)

    def place_part(values, full):
        return lax.dynamic_update_slice_in_dim(
            jnp.zeros((full,), F32), values, rank * values.shape[0], 0
        )

    sums = jnp.concatenate(
        [
            jnp.sum(grad_normed * own_scaled, axis=0),
            jnp.sum(grad_normed, axis=0),
            place_part(jnp.sum(grads[0].astype(F32), axis=0), width),
            place_part(jnp.sum(grads[2].astype(F32), axis=0), width),
            (sums_two[:3] * (1.0 / ranks)).reshape(-1),
            jnp.sum(own_grad.astype(F32), axis=0),
            place_part(jnp.concatenate([bias_first[0], bias_second[0]]), b_up.shape[0]),
        ]
    )
    columns = pieces[0].shape[1]
    filled = sums.shape[0]
    sums = jnp.pad(sums, (0, -filled % (8 * columns))).reshape(-1, columns)
    sums = near_sum(sums)
    state = scatter_near(pieces, sums)
    last_sums = far_sums(state, [sums], None)
    own_output, grad_own, second_mlp, *last_sums = lax.optimization_barrier(
        (own_output, grad_own, second_mlp, *last_sums)
    )
    second_mlp = swap(second_mlp, inverse=True)
    leaving = swap(jnp.concatenate([own_output, grad_own], axis=0), inverse=True)
    output, grad_input = leaving[:own_rows], leaving[own_rows:]
    shard = jax.ShapeDtypeStruct((block_rows, unit_width), F32)
    grad_w_up, grad_w_down = sums_call(
        functools.partial(units_last_kernel, tile=tile),
        [first_mlp, second_mlp],
        [shard, shard],
        None,
        "units_last",
    )
    *late, sums = sums_call(
        weights_last_kernel,
        far_parts(last_sums),
        [jax.ShapeDtypeStruct((block_rows, head_width), F32)] * 4
        + [jax.ShapeDtypeStruct(sums.shape, F32)],
        grad_w_up,
        "sums_last",
    )
    sums = sums.reshape(-1)
    small = [sums[i * width : (i + 1) * width] for i in range(8)]
    return (
        output, grad_input, small[0], small[1],
        late[0], late[1], late[2], small[2], small[3], late[3], small[4], small[5], small[6],
        grad_w_up, sums[8 * width : filled], grad_w_down, small[7],
    )


def solution(mesh):
    groups, ranks = mesh.shape["dp"], mesh.shape["tensor"]
    sizes = {"a": groups // 2, "h": 2, "l": ranks // 2}
    fine = Mesh(mesh.devices.reshape(groups // 4, 2, 2, 2, ranks // 2), ALL)
    rows = P(ALL, None)
    block = P(("z", "y", "c"), ("h", "l"))
    return jax.shard_map(
        functools.partial(per_device, sizes),
        mesh=fine,
        in_specs=(
            rows, P(("z", "y", "c")), P(), P(), block, block, block, P(), P(), block, P(), P(), P(),
            block, P(), block, P(), rows,
        ),
        out_specs=(
            rows, rows, P(), P(), block, block, block, P(), P(), block, P(), P(), P(), block, P(),
            block, P(),
        ),
        check_vma=False,
    )
```

```python
import functools

import jax
import jax.numpy as jnp
from jax import lax
from jax.experimental import pallas as pl
from jax.experimental.pallas import tpu as pltpu
from jax.sharding import Mesh
from jax.sharding import PartitionSpec as P

HEAD_DIM = 64
LANES = 128
TILE = 512
ROWS = 512
MASKED = -1e30
VMEM_BYTES = 60 * 1024 * 1024
F32 = jnp.float32
BF16 = jnp.bfloat16
TP = ("l", "c")
SWAP = ("c", "h", "l")
ALL = ("z", "y", "c", "h", "l")


def normalize(values):
    center = values - jnp.mean(values, axis=-1, keepdims=True)
    spread = jnp.mean(center * center, axis=-1, keepdims=True)
    inverse = lax.rsqrt(spread + 1e-05)
    return center * inverse, inverse


def norm_back(grad_in, scaled, inverse, gain_vec):
    local_grad = grad_in * gain_vec
    return inverse * (
        local_grad
        - jnp.mean(local_grad, axis=-1, keepdims=True)
        - scaled * jnp.mean(local_grad * scaled, axis=-1, keepdims=True)
    )


def dot_nn(left, right):
    return lax.dot_general(left, right, (((1,), (0,)), ((), ())), preferred_element_type=F32)


def dot_nt(left, right):
    return lax.dot_general(left, right, (((1,), (1,)), ((), ())), preferred_element_type=F32)


def dot_tn(left, right):
    return lax.dot_general(left, right, (((0,), (0,)), ((), ())), preferred_element_type=F32)


def fill_bias(bias, seg_col, seg_row):
    length = bias.shape[0]
    block = min(256, length)
    for first in range(0, length, block):
        keys = lax.broadcasted_iota(jnp.int32, (block, length), 0) + first
        places = lax.broadcasted_iota(jnp.int32, (block, length), 1)
        same = seg_col[first : first + block, :] == seg_row[...]
        bias[first : first + block, :] = jnp.where(same & (keys <= places), 0.0, MASKED)


def head_lanes(values, head):
    lane = lax.broadcasted_iota(jnp.int32, values.shape, 1)
    inside = (lane >= head * HEAD_DIM) & (lane < (head + 1) * HEAD_DIM)
    return jnp.where(inside, values, jnp.zeros_like(values))


def attn_forward_kernel(seg_col, seg_row, q_ref, k_ref, v_ref, mixed_ref, lse_ref, bias, v_t, block):
    length = q_ref.shape[0]
    heads = LANES // HEAD_DIM

    @pl.when(pl.program_id(0) == 0)
    def _():
        fill_bias(bias, seg_col, seg_row)

    v_t[...] = v_ref[...].T
    for place in range(length // block):
        rows = slice(place * block, (place + 1) * block)
        outs = []
        for head in range(heads):
            query = head_lanes(q_ref[rows, :], head)
            scores = []
            peak = None
            for other in range(place + 1):
                keys = slice(other * block, (other + 1) * block)
                part = dot_nt(k_ref[keys, :], query) + bias[keys, rows]
                top = jnp.max(part, axis=0, keepdims=True)
                peak = top if peak is None else jnp.maximum(peak, top)
                scores.append(part)
            total = None
            acc = None
            for other in range(place + 1):
                keys = slice(other * block, (other + 1) * block)
                weight = jnp.exp(scores[other] - peak)
                part_sum = jnp.sum(weight, axis=0, keepdims=True)
                total = part_sum if total is None else total + part_sum
                part_out = dot_nn(
                    v_t[head * HEAD_DIM : (head + 1) * HEAD_DIM, keys], weight.astype(BF16)
                )
                acc = part_out if acc is None else acc + part_out
            outs.append(acc / total)
            lse_ref[0, head : head + 1, rows] = peak + jnp.log(total)
        mixed_ref[rows, :] = jnp.concatenate(outs, axis=0).T.astype(BF16)


def attn_backward_kernel(
    seg_col, seg_row, q_ref, k_ref, v_ref, mixed_ref, lse_ref, g_ref, grads_ref, bias, k_t, delta, dq_t, block
):
    length = q_ref.shape[0]
    heads = LANES // HEAD_DIM
    count = length // block

    @pl.when(pl.program_id(0) == 0)
    def _():
        fill_bias(bias, seg_col, seg_row)

    k_t[...] = k_ref[...].T
    product = (g_ref[...].astype(F32) * mixed_ref[...].astype(F32)).T
    for head in range(heads):
        delta[head : head + 1, :] = jnp.sum(
            product[head * HEAD_DIM : (head + 1) * HEAD_DIM, :], axis=0, keepdims=True
        )
    for other in range(count):
        keys = slice(other * block, (other + 1) * block)
        key_sum = None
        value_sum = None
        for head in range(heads):
            lanes = slice(head * HEAD_DIM, (head + 1) * HEAD_DIM)
            for place in range(other, count):
                rows = slice(place * block, (place + 1) * block)
                query = head_lanes(q_ref[rows, :], head)
                grad = head_lanes(g_ref[rows, :], head)
                scores = dot_nt(k_ref[keys, :], query) + bias[keys, rows]
                probs = jnp.exp(scores - lse_ref[0, head : head + 1, rows])
                grad_probs = dot_nt(v_ref[keys, :], grad)
                grad_scores = (probs * (grad_probs - delta[head : head + 1, rows])).astype(BF16)
                value_part = dot_nn(probs.astype(BF16), grad)
                key_part = dot_nn(grad_scores, query)
                query_part = dot_nn(k_t[lanes, keys], grad_scores)
                value_sum = value_part if value_sum is None else value_sum + value_part
                key_sum = key_part if key_sum is None else key_sum + key_part
                if other == 0:
                    dq_t[lanes, rows] = query_part
                else:
                    dq_t[lanes, rows] += query_part
        grads_ref[1, keys, :] = key_sum.astype(BF16)
        grads_ref[2, keys, :] = value_sum.astype(BF16)
    grads_ref[0] = (dq_t[...].T * HEAD_DIM ** (-0.5)).astype(BF16)


def attn_forward(segments, qkv, width):
    length = qkv.shape[0]
    pairs = width // LANES
    block = min(256, length)
    column = lambda first: pl.BlockSpec((length, LANES), lambda p: (0, first * pairs + p))
    whole = lambda shape: pl.BlockSpec(shape, lambda p: (0, 0))
    return pl.pallas_call(
        functools.partial(attn_forward_kernel, block=block),
        grid=(pairs,),
        in_specs=[whole((length, 1)), whole((1, length)), column(0), column(1), column(2)],
        out_specs=[
            pl.BlockSpec((length, LANES), lambda p: (0, p)),
            pl.BlockSpec((1, 8, length), lambda p: (p, 0, 0)),
        ],
        out_shape=[
            jax.ShapeDtypeStruct((length, width), BF16),
            jax.ShapeDtypeStruct((pairs, 8, length), F32),
        ],
        scratch_shapes=[pltpu.VMEM((length, length), F32), pltpu.VMEM((LANES, length), BF16)],
        compiler_params=pltpu.CompilerParams(vmem_limit_bytes=VMEM_BYTES),
        cost_estimate=pl.CostEstimate(
            flops=4 * length * length * width,
            bytes_accessed=8 * length * width,
            transcendentals=length * length * width // (2 * HEAD_DIM),
        ),
        name="attn_forward",
    )(segments.reshape(length, 1), segments.reshape(1, length), qkv, qkv, qkv)


def attn_backward(segments, qkv, mixed, lse, grad_mixed, width, after):
    length = qkv.shape[0]
    pairs = width // LANES
    block = min(256, length)
    column = lambda first: pl.BlockSpec((length, LANES), lambda p: (0, first * pairs + p))
    whole = lambda shape: pl.BlockSpec(shape, lambda p: (0, 0))
    return pl.pallas_call(
        without(functools.partial(attn_backward_kernel, block=block), 8),
        grid=(pairs,),
        in_specs=[
            whole((length, 1)),
            whole((1, length)),
            column(0),
            column(1),
            column(2),
            pl.BlockSpec((length, LANES), lambda p: (0, p)),
            pl.BlockSpec((1, 8, length), lambda p: (p, 0, 0)),
            pl.BlockSpec((length, LANES), lambda p: (0, p)),
            pl.BlockSpec(memory_space=pl.ANY),
        ],
        out_specs=pl.BlockSpec((3, length, LANES), lambda p: (0, 0, p)),
        out_shape=jax.ShapeDtypeStruct((3, length, width), BF16),
        scratch_shapes=[
            pltpu.VMEM((length, length), F32),
            pltpu.VMEM((LANES, length), BF16),
            pltpu.VMEM((8, length), F32),
            pltpu.VMEM((LANES, length), F32),
        ],
        compiler_params=pltpu.CompilerParams(vmem_limit_bytes=VMEM_BYTES),
        cost_estimate=pl.CostEstimate(
            flops=10 * length * length * width,
            bytes_accessed=16 * length * width,
            transcendentals=length * length * width // (2 * HEAD_DIM),
        ),
        name="attn_backward",
    )(segments.reshape(length, 1), segments.reshape(1, length), qkv, qkv, qkv, mixed, lse, grad_mixed, after)


def piece_blocks(count):
    far = count // 4
    half = far // 2
    near, by_y, by_x, both = (list(range(i * far, (i + 1) * far)) for i in range(4))
    return [
        both[:half] + by_x[:half],
        both[half:] + by_y[half:],
        by_y[:half],
        by_x[half:],
        near,
    ]


def store_pieces(order, grad, piece_refs, columns):
    count = order.shape[0]
    rows = grad.shape[0] // count
    for blocks, ref in zip(piece_blocks(count), piece_refs):
        for place, block in enumerate(blocks):
            first = pl.multiple_of(order[block] * rows, rows)
            ref[place * rows : (place + 1) * rows, columns] = grad[pl.ds(first, rows), :]


def piece_shapes(count, rows, columns):
    return [
        jax.ShapeDtypeStruct((len(blocks) * rows, columns), BF16) for blocks in piece_blocks(count)
    ]


def whole_spec(shape, **options):
    return pl.BlockSpec(shape, lambda step: (0,) * len(shape), **options)


def norm_kernel(*refs, residual):
    if residual:
        x_ref, own_ref, other_ref, shift_ref, gain_ref, bias_ref, n_ref, nt_ref, hidden_ref = refs
        values = (
            x_ref[...].astype(F32)
            + (own_ref[...].astype(F32) + other_ref[...].astype(F32))
            + shift_ref[...]
        )
        hidden_ref[...] = values
    else:
        x_ref, gain_ref, bias_ref, n_ref, nt_ref = refs
        values = x_ref[...].astype(F32)
    scaled, _ = normalize(values)
    normed = (scaled * gain_ref[...] + bias_ref[...]).astype(BF16)
    n_ref[...] = normed
    nt_ref[...] = normed.T


def norm_rows(x, gain, bias, partials=None, shift=None):
    length, width = x.shape
    block = min(256, length)
    row = pl.BlockSpec((block, width), lambda step: (step, 0))
    vector = whole_spec((1, width))
    residual = partials is not None
    operands = [x] + (list(partials) + [shift.reshape(1, width)] if residual else [])
    operands += [gain.reshape(1, width), bias.reshape(1, width)]
    return pl.pallas_call(
        functools.partial(norm_kernel, residual=residual),
        grid=(length // block,),
        in_specs=[row] + ([row, row, vector] if residual else []) + [vector, vector],
        out_specs=[row, pl.BlockSpec((width, block), lambda step: (0, step))]
        + ([row] if residual else []),
        out_shape=[
            jax.ShapeDtypeStruct((length, width), BF16),
            jax.ShapeDtypeStruct((width, length), BF16),
        ]
        + ([jax.ShapeDtypeStruct((length, width), F32)] if residual else []),
        compiler_params=pltpu.CompilerParams(vmem_limit_bytes=VMEM_BYTES),
        cost_estimate=pl.CostEstimate(
            flops=20 * length * width, bytes_accessed=14 * length * width, transcendentals=length
        ),
        name="norm_two" if residual else "norm_one",
    )(*operands)


def norm_back_kernel(hidden_ref, g_ref, own_ref, other_ref, gain_ref, grad_ref, low_ref, low_t_ref, sums_ref):
    scaled, inverse = normalize(hidden_ref[...])
    incoming = own_ref[...].astype(F32) + other_ref[...].astype(F32)
    grad = g_ref[...].astype(F32) + norm_back(incoming, scaled, inverse, gain_ref[...])
    grad_ref[...] = grad
    low_ref[...] = grad.astype(BF16)
    low_t_ref[...] = grad.astype(BF16).T

    @pl.when(pl.program_id(0) == 0)
    def _():
        sums_ref[...] = jnp.zeros_like(sums_ref)

    sums_ref[0:1, :] += jnp.sum(grad, axis=0, keepdims=True)
    sums_ref[1:2, :] += jnp.sum(incoming * scaled, axis=0, keepdims=True)
    sums_ref[2:3, :] += jnp.sum(incoming, axis=0, keepdims=True)


def norm_back_rows(hidden, grad, partials, gain):
    length, width = hidden.shape
    block = min(256, length)
    row = pl.BlockSpec((block, width), lambda step: (step, 0))
    return pl.pallas_call(
        norm_back_kernel,
        grid=(length // block,),
        in_specs=[row, row, row, row, whole_spec((1, width))],
        out_specs=[
            row,
            row,
            pl.BlockSpec((width, block), lambda step: (0, step)),
            whole_spec((8, width)),
        ],
        out_shape=[
            jax.ShapeDtypeStruct((length, width), F32),
            jax.ShapeDtypeStruct((length, width), BF16),
            jax.ShapeDtypeStruct((width, length), BF16),
            jax.ShapeDtypeStruct((8, width), F32),
        ],
        compiler_params=pltpu.CompilerParams(vmem_limit_bytes=VMEM_BYTES),
        cost_estimate=pl.CostEstimate(
            flops=30 * length * width, bytes_accessed=16 * length * width, transcendentals=length
        ),
        name="norm_two_back",
    )(hidden, grad, *partials, gain.reshape(1, width))


def mlp_kernel(order, n_ref, g_ref, nt_ref, gt_ref, b_ref, w_ref, *refs, block, with_previous, cube):
    if with_previous:
        (before_out, before_gn), refs = refs[:2], refs[2:]
    (out_ref, gn_ref), refs = refs[:2], refs[2:]
    grad_refs, (gb_ref, out_acc, gn_acc, act, gpre, grad_w) = refs[:-6], refs[-6:]
    step = pl.program_id(0)
    length = n_ref.shape[0]
    tile = w_ref.shape[1] // 2
    ups, downs = slice(0, tile), slice(tile, 2 * tile)

    @pl.when(step == 0)
    def _():
        if with_previous:
            out_acc[...] = before_out[...].astype(F32)
            gn_acc[...] = before_gn[...].astype(F32)
        else:
            out_acc[...] = jnp.zeros_like(out_acc)
            gn_acc[...] = jnp.zeros_like(gn_acc)

    bias_sum = jnp.zeros(gb_ref.shape, F32)
    for first in range(0, length, block):
        rows = slice(first, first + block)
        unit = dot_nn(n_ref[rows, :], w_ref[:, ups]) + b_ref[...]
        grad = dot_nn(g_ref[rows, :], w_ref[:, downs])
        square = unit * unit
        curve = jnp.tanh(0.7978845608028654 * (unit + 0.044715 * (square * unit)))
        half = 0.5 + 0.5 * curve
        slope = half + (0.5 * unit) * (1.0 - curve * curve) * (
            0.7978845608028654 + (3 * 0.044715 * 0.7978845608028654) * square
        )
        active = (unit * half).astype(BF16)
        grad_pre = (grad * slope).astype(BF16)
        act[rows, :] = active
        gpre[rows, :] = grad_pre
        bias_sum = bias_sum + jnp.sum(grad_pre.astype(F32), axis=0, keepdims=True)
        out_acc[rows, :] += dot_nt(active, w_ref[:, downs])
        gn_acc[rows, :] += dot_nt(grad_pre, w_ref[:, ups])
    gb_ref[...] = bias_sum
    for columns, left, right in ((ups, nt_ref, gpre), (downs, gt_ref, act)):
        if cube:
            grad_w[...] = dot_nn(left[...], right[...]).astype(BF16)
            store_pieces(order, grad_w, grad_refs, columns)
        else:
            grad_refs[0][:, columns] = dot_nn(left[...], right[...]).astype(BF16)

    @pl.when(step == pl.num_programs(0) - 1)
    def _():
        out_ref[...] = out_acc[...].astype(BF16)
        gn_ref[...] = gn_acc[...].astype(BF16)


def mlp(order, normed, grad, normed_t, grad_t, weights, bias, previous, cube):
    length, width = normed.shape
    units = weights.shape[1] // 2
    tile = min(TILE, units)
    at_tile = lambda rows, columns: pl.BlockSpec((rows, columns), lambda u, o: (0, u))
    fixed = lambda shape: pl.BlockSpec(shape, lambda u, o: (0, 0))
    once = lambda shape: pl.BlockSpec(shape, lambda u, o: (0, 0), pipeline_mode=pl.Buffered(1))
    if cube:
        count = order.shape[0]
        grad_shapes = piece_shapes(count, width // count, 2 * units)
    else:
        grad_shapes = [jax.ShapeDtypeStruct((width, 2 * units), BF16)]
    results = pl.pallas_call(
        functools.partial(
            mlp_kernel, block=min(ROWS, length), with_previous=bool(previous), cube=cube
        ),
        grid_spec=pltpu.PrefetchScalarGridSpec(
            num_scalar_prefetch=1,
            grid=(units // tile,),
            in_specs=[
                once((length, width)),
                once((length, width)),
                once((width, length)),
                once((width, length)),
                at_tile(1, tile),
                at_tile(width, 2 * tile),
            ]
            + [once((length, width)) for _ in previous],
            out_specs=[fixed((length, width)), fixed((length, width))]
            + [at_tile(shape.shape[0], 2 * tile) for shape in grad_shapes]
            + [at_tile(1, tile)],
            scratch_shapes=[
                pltpu.VMEM((length, width), F32),
                pltpu.VMEM((length, width), F32),
                pltpu.VMEM((length, tile), BF16),
                pltpu.VMEM((length, tile), BF16),
                pltpu.VMEM((width, tile), BF16),
            ],
        ),
        out_shape=[jax.ShapeDtypeStruct((length, width), BF16)] * 2
        + grad_shapes
        + [jax.ShapeDtypeStruct((1, units), F32)],
        compiler_params=pltpu.CompilerParams(vmem_limit_bytes=VMEM_BYTES),
        cost_estimate=pl.CostEstimate(
            flops=12 * length * width * units,
            bytes_accessed=12 * length * width + 8 * width * units,
            transcendentals=length * units,
        ),
        name="mlp_second" if previous else "mlp_first",
    )(order, normed, grad, normed_t, grad_t, bias.reshape(1, units), weights, *previous)
    return results[0], results[1], results[2:-1], results[-1]


def qkv_kernel(n_ref, b_ref, w_ref, out_ref):
    scale = jnp.where(pl.program_id(0) == 0, HEAD_DIM ** (-0.5), 1.0)
    length = n_ref.shape[0]
    step = min(ROWS, length)
    for first in range(0, length, step):
        span = slice(first, first + step)
        out_ref[span, :] = ((dot_nn(n_ref[span, :], w_ref[...]) + b_ref[...]) * scale).astype(BF16)


def qkv_project(normed, weights, bias):
    length, width = normed.shape
    columns = weights.shape[1] // 4
    at_tile = lambda rows: pl.BlockSpec((rows, columns), lambda k: (0, k))
    return pl.pallas_call(
        qkv_kernel,
        grid=(3,),
        in_specs=[
            whole_spec((length, width), pipeline_mode=pl.Buffered(1)), at_tile(1), at_tile(width)
        ],
        out_specs=at_tile(length),
        out_shape=jax.ShapeDtypeStruct((length, 3 * columns), BF16),
        compiler_params=pltpu.CompilerParams(vmem_limit_bytes=VMEM_BYTES),
        cost_estimate=pl.CostEstimate(
            flops=6 * length * width * columns,
            bytes_accessed=2 * length * width + 6 * width * columns + 6 * length * columns,
            transcendentals=0,
        ),
        name="qkv_project",
    )(normed, bias.reshape(1, 3 * columns), weights)


def weight_kernel(order, nt_ref, grads_ref, gt_ref, mixed_ref, order_only, *refs):
    piece_refs, grad = refs[:5], refs[5]
    part = pl.program_id(0)

    @pl.when(part < 3)
    def _():
        grad[...] = dot_nn(nt_ref[...], grads_ref[0]).astype(BF16)

    @pl.when(part == 3)
    def _():
        grad[...] = dot_nn(gt_ref[...], mixed_ref[...]).astype(BF16)

    store_pieces(order, grad, piece_refs, slice(None))


def without(kernel, place):
    return lambda *refs: kernel(*refs[:place], *refs[place + 1 :])


ORDER_ONLY = pl.BlockSpec(memory_space=pl.ANY)


def weight_grads(order, normed_t, grads, grad_t, mixed, after):
    width, length = normed_t.shape
    columns = grads.shape[2]
    shapes = piece_shapes(order.shape[0], width // order.shape[0], 4 * columns)
    fixed = lambda shape: pl.BlockSpec(shape, lambda k, o: (0, 0), pipeline_mode=pl.Buffered(1))
    return pl.pallas_call(
        weight_kernel,
        grid_spec=pltpu.PrefetchScalarGridSpec(
            num_scalar_prefetch=1,
            grid=(4,),
            in_specs=[
                fixed((width, length)),
                pl.BlockSpec((1, length, columns), lambda k, o: (jnp.minimum(k, 2), 0, 0)),
                fixed((width, length)),
                fixed((length, columns)),
                ORDER_ONLY,
            ],
            out_specs=[
                pl.BlockSpec((shape.shape[0], columns), lambda k, o: (0, k)) for shape in shapes
            ],
            scratch_shapes=[pltpu.VMEM((width, columns), BF16)],
        ),
        out_shape=shapes,
        compiler_params=pltpu.CompilerParams(vmem_limit_bytes=VMEM_BYTES),
        cost_estimate=pl.CostEstimate(
            flops=8 * length * width * columns,
            bytes_accessed=4 * length * width + 16 * width * columns,
            transcendentals=0,
        ),
        name="weight_grads",
    )(order, normed_t, grads, grad_t, mixed, after)


def qkv_back_kernel(grads_ref, w_ref, out_ref):
    columns = grads_ref.shape[2]
    total = None
    for k in range(3):
        part = dot_nt(grads_ref[k], w_ref[:, k * columns : (k + 1) * columns])
        total = part if total is None else total + part
    out_ref[...] = total.astype(BF16)


def qkv_back(grads, weights, after):
    _, length, columns = grads.shape
    width = weights.shape[0]
    block = min(ROWS, length)
    return pl.pallas_call(
        without(qkv_back_kernel, 2),
        grid=(length // block,),
        in_specs=[
            pl.BlockSpec((3, block, columns), lambda i: (0, i, 0)),
            pl.BlockSpec((width, 4 * columns), lambda i: (0, 0), pipeline_mode=pl.Buffered(1)),
            ORDER_ONLY,
        ],
        out_specs=pl.BlockSpec((block, width), lambda i: (i, 0)),
        out_shape=jax.ShapeDtypeStruct((length, width), BF16),
        compiler_params=pltpu.CompilerParams(vmem_limit_bytes=VMEM_BYTES),
        cost_estimate=pl.CostEstimate(
            flops=6 * length * width * columns,
            bytes_accessed=2 * length * width + 6 * width * columns + 6 * length * columns,
            transcendentals=0,
        ),
        name="qkv_back",
    )(grads, weights, after)


def added(*terms):
    total = terms[0].astype(F32)
    for term in terms[1:]:
        total = total + term.astype(F32)
    return total.astype(BF16)


def high_low(values):
    high = values.astype(BF16).astype(F32)
    return jnp.concatenate([high, values - high], axis=0).astype(BF16)


def from_high_low(rows):
    rows = rows.astype(F32)
    half = rows.shape[0] // 2
    return rows[:half, :] + rows[half:, :]


def first_sums_kernel(from_x, from_y, keep_y, keep_x, *refs):
    small, (y_ref, x_ref) = refs[:-2], refs[-2:]
    half = y_ref.shape[0]
    y_ref[...] = added(keep_y[...], from_x[:half, :])
    x_ref[:half, :] = added(keep_x[...], from_y[:half, :])
    for values in small:
        x_ref[half:, :] = high_low(values[...])


def second_sums_kernel(from_x, from_y, near, from_y2, from_x2, *outs, with_small):
    if with_small:
        small, outs = outs[0], outs[1:]
    far = len(outs)
    half = from_y2.shape[0]
    rows = half * 2 // far
    if with_small:
        extra = high_low(small[...] + from_high_low(from_x2[half:, :]))
    for i, out in enumerate(outs):
        first, second, place = (from_x, from_y2, i) if i < far // 2 else (from_y, from_x2, i - far // 2)
        out[:rows, :] = added(
            near[i * rows : (i + 1) * rows, :],
            first[half + place * rows : half + (place + 1) * rows, :],
            second[place * rows : (place + 1) * rows, :],
        )
        if with_small:
            out[rows:, :] = extra


def z_sums_kernel(z_ref, from_x, from_y, near, from_y2, from_x2, out, *, far):
    half = from_y2.shape[0]
    rows = half * 2 // far
    for i in range(far):
        first, second, place = (from_x, from_y2, i) if i < far // 2 else (from_y, from_x2, i - far // 2)
        target = pl.multiple_of((z_ref[0] ^ i) * rows, rows)
        out[pl.ds(target, rows), :] = added(
            near[i * rows : (i + 1) * rows, :],
            first[half + place * rows : half + (place + 1) * rows, :],
            second[place * rows : (place + 1) * rows, :],
        )


def weights_last_kernel(*refs):
    parts, outs, small = refs[:-5], refs[-5:-1], refs[-1]
    total = parts[0][...].astype(F32)
    for part in parts[1:]:
        total = total + part[...].astype(F32)
    rows, columns = outs[0].shape
    for k, out in enumerate(outs):
        out[...] = total[:rows, k * columns : (k + 1) * columns]
    small[...] = from_high_low(total[rows:, :])


def units_last_kernel(first_ref, second_ref, up_ref, down_ref, *, tile):
    units = up_ref.shape[1] // 2
    for index, ref in enumerate((first_ref, second_ref)):
        for first in range(0, units, tile):
            columns = slice(index * units + first, index * units + first + tile)
            up_ref[:, columns] = ref[:, 2 * first : 2 * first + tile].astype(F32)
            down_ref[:, columns] = ref[:, 2 * first + tile : 2 * first + 2 * tile].astype(F32)


def shards_kernel(w_up, w_down, first_ref, second_ref, *, tile):
    units = first_ref.shape[1] // 2
    for index, ref in enumerate((first_ref, second_ref)):
        for first in range(0, units, tile):
            columns = slice(index * units + first, index * units + first + tile)
            ref[:, 2 * first : 2 * first + tile] = w_up[:, columns]
            ref[:, 2 * first + tile : 2 * first + 2 * tile] = w_down[:, columns]


def sums_call(kernel, operands, shapes, after, name):
    body = kernel if after is None else without(kernel, 0)
    vmem = pl.BlockSpec(memory_space=pltpu.VMEM)
    return pl.pallas_call(
        body,
        in_specs=([pl.BlockSpec(memory_space=pl.ANY)] if after is not None else [])
        + [vmem] * len(operands),
        out_specs=[vmem] * len(shapes),
        out_shape=shapes,
        compiler_params=pltpu.CompilerParams(vmem_limit_bytes=VMEM_BYTES),
        cost_estimate=pl.CostEstimate(flops=0, bytes_accessed=1024 * 1024, transcendentals=0),
        name=name,
    )(*([after] if after is not None else []), *operands)


def flipped(sizes):
    return 1 if sizes["h"] * sizes["l"] == 2 else 0


def moves(sizes):
    groups, ranks, inner = sizes["a"], sizes["h"] * sizes["l"], sizes["l"]
    far = groups // 2
    flip = flipped(sizes)
    swap_to = {}
    for group in range(2):
        for part in range(ranks):
            place = (part % 2 ^ flip) * ranks + group * (ranks // 2) + part // 2
            swap_to[group * ranks + part] = place

    def swap(values, inverse=False):
        pairs = [(to, frm) if inverse else (frm, to) for frm, to in swap_to.items()]
        return lax.ppermute(values, SWAP, pairs)

    def swap_hop(values, a_mask, inverse=False):
        pairs = []
        for a in range(groups):
            for frm, to in swap_to.items():
                one, two = a * 2 * ranks + frm, (a ^ a_mask) * 2 * ranks + to
                pairs.append((two, one) if inverse else (one, two))
        return lax.ppermute(values, ALL, pairs)

    def hop(values, a_mask, h_mask):
        pairs = []
        for a in range(groups):
            for c in range(2):
                for h in range(2):
                    pairs.append(((a * 2 + c) * 2 + h, ((a ^ a_mask) * 2 + c) * 2 + (h ^ h_mask)))
        return lax.ppermute(values, ("z", "y", "c", "h"), pairs)

    def scatter_near(pieces, after, small=()):
        from_x, from_y = hop(pieces[0], 0, 1), hop(pieces[1], 1, 0)
        half, columns = pieces[2].shape
        y_sum, x_sum = sums_call(
            first_sums_kernel,
            [from_x, from_y, pieces[2], pieces[3], *small],
            [
                jax.ShapeDtypeStruct((half, columns), BF16),
                jax.ShapeDtypeStruct(
                    (half + sum(2 * values.shape[0] for values in small), columns), BF16
                ),
            ],
            after,
            "sums_one",
        )
        return from_x, from_y, pieces[4], y_sum, x_sum

    def far_sums(state, small, after):
        from_x, from_y, near, y_sum, x_sum = state
        columns = near.shape[1]
        from_y2, from_x2 = hop(y_sum, 1, 0), hop(x_sum, 0, 1)
        rows = near.shape[0] // far + sum(2 * values.shape[0] for values in small)
        return sums_call(
            functools.partial(second_sums_kernel, with_small=bool(small)),
            [from_x, from_y, near, from_y2, from_x2] + small,
            [jax.ShapeDtypeStruct((rows, columns), BF16)] * far,
            after,
            "sums_two",
        )

    def z_sums(state, after):
        from_x, from_y, near, y_sum, x_sum = state
        from_y2, from_x2 = hop(y_sum, 1, 0), hop(x_sum, 0, 1)
        vmem = pl.BlockSpec(memory_space=pltpu.VMEM)
        return pl.pallas_call(
            without(functools.partial(z_sums_kernel, far=far), 6),
            in_specs=[pl.BlockSpec(memory_space=pltpu.SMEM)] + [vmem] * 5 + [ORDER_ONLY],
            out_specs=vmem,
            out_shape=jax.ShapeDtypeStruct(near.shape, BF16),
            compiler_params=pltpu.CompilerParams(vmem_limit_bytes=VMEM_BYTES),
            name="sums_two_z",
        )(lax.axis_index("z").reshape(1), from_x, from_y, near, from_y2, from_x2, after)

    def far_parts(sums):
        return [swap_hop(sums[i], 2 * i, inverse=True) for i in range(far)]

    def core_sum(values):
        values = values + lax.ppermute(values, "c", [(0, 1), (1, 0)])
        return lax.psum(values, "l") if inner > 1 else values

    a, h = lax.axis_index(("z", "y")), lax.axis_index("h")
    order = []
    for a_low, h_mask in ((0, 0), (1, 0), (0, 1), (1, 1)):
        for i in range(far):
            order.append((a ^ (2 * i + a_low)) * 2 + (h ^ h_mask))
    return swap, hop, scatter_near, far_sums, z_sums, far_parts, core_sum, jnp.stack(order).astype(jnp.int32)


def per_device(sizes, *arguments):
    (
        block_input, segment_ids, ln1_gain, ln1_bias, w_query, w_key, w_value, b_query, b_value,
        w_out, b_out, ln2_gain, ln2_bias, w_up, b_up, w_down, b_down, out_grad,
    ) = arguments
    ranks = sizes["h"] * sizes["l"]
    rank = lax.axis_index("l") * 2 + (lax.axis_index("c") ^ flipped(sizes))
    own_rows, width = block_input.shape
    head_width = w_query.shape[1]
    unit_width = w_up.shape[1]
    half_units = unit_width // 2
    tile = min(TILE, half_units)
    swap, hop, scatter_near, far_sums, z_sums, far_parts, core_sum, order = moves(sizes)

    def partner(values):
        return lax.ppermute(values, "c", [(0, 1), (1, 0)])

    def tp_gather(values):
        if ranks != 2:
            return lax.all_gather(values, TP, axis=0, tiled=True)
        theirs = partner(values)
        return jnp.where(
            rank == 0,
            jnp.concatenate([values, theirs], axis=0),
            jnp.concatenate([theirs, values], axis=0),
        )

    def tp_terms(values):
        if ranks != 2:
            others = lax.psum(values.astype(F32), TP) - values.astype(F32)
            return values, others.astype(BF16)
        return values, partner(values)

    def own(values):
        return lax.dynamic_slice_in_dim(values, rank * own_rows, own_rows)

    def tp_scatter_terms(values):
        if ranks != 2:
            total = lax.psum_scatter(values, TP, scatter_dimension=0, tiled=True)
            return total, jnp.zeros_like(total)
        theirs = lax.dynamic_slice_in_dim(values, (1 - rank) * own_rows, own_rows)
        return own(values), partner(theirs)

    def tp_scatter(values):
        own_part, other_part = tp_scatter_terms(values)
        return own_part.astype(F32) + other_part.astype(F32)

    own_input = swap(block_input)
    segments = swap(segment_ids)
    own_grad = swap(out_grad)
    shard_first, shard_second = sums_call(
        functools.partial(shards_kernel, tile=tile),
        [w_up, w_down],
        [jax.ShapeDtypeStruct(w_up.shape, BF16)] * 2,
        None,
        "mlp_shards",
    )
    early_attn = lax.all_gather(
        jnp.concatenate([w_query, w_key, w_value, w_out], axis=1), ("z", "y", "c"), axis=0, tiled=True
    )
    early_first = lax.all_gather(shard_first, ("z", "y", "c"), axis=0, tiled=True)
    shard_second = swap(shard_second)
    other_second = hop(shard_second, 0, 1)
    shard_second = jnp.where(
        lax.axis_index("h") == 0,
        jnp.concatenate([shard_second, other_second], axis=0),
        jnp.concatenate([other_second, shard_second], axis=0),
    )
    bias_query = lax.dynamic_slice_in_dim(b_query, rank * head_width, head_width)
    bias_value = lax.dynamic_slice_in_dim(b_value, rank * head_width, head_width)
    bias_up = lax.dynamic_slice_in_dim(b_up, rank * unit_width, unit_width)

    rows_in = tp_gather(own_input)
    grad_rows = tp_gather(own_grad)
    grad_rows_t = grad_rows.T
    normed, normed_t = norm_rows(rows_in, ln1_gain, ln1_bias)
    early_attn, normed, segments, grad_rows, grad_rows_t, shard_second = lax.optimization_barrier(
        (early_attn, normed, segments, grad_rows, grad_rows_t, shard_second)
    )
    full_second = lax.all_gather(shard_second, ("z", "y"), axis=0, tiled=True)
    full_attn = swap(early_attn)
    biases = jnp.concatenate([bias_query, jnp.zeros((head_width,), F32), bias_value])
    qkv = qkv_project(normed, full_attn, biases)
    full_out = full_attn[:, 3 * head_width :]
    early_first, qkv = lax.optimization_barrier((early_first, qkv))
    full_first = swap(early_first)
    mixed, lse = attn_forward(segments, qkv, head_width)
    attended = tp_terms(dot_nt(mixed, full_out).astype(BF16))
    normed_two, normed_two_t, hidden = norm_rows(rows_in, ln2_gain, ln2_bias, attended, b_out)

    out_part, gn_part, first_grads, bias_first = mlp(
        order, normed_two, grad_rows, normed_two_t, grad_rows_t, full_first,
        bias_up[:half_units], (), True,
    )
    full_second, gn_part = lax.optimization_barrier((full_second, gn_part))
    out_part, gn_part, second_grads, bias_second = mlp(
        order, normed_two, grad_rows, normed_two_t, grad_rows_t, full_second,
        bias_up[half_units:], (out_part, gn_part), False,
    )
    first_state = scatter_near(first_grads, gn_part)
    gn_part, second_grads, first_state = lax.optimization_barrier(
        (gn_part, second_grads[0], first_state)
    )
    own_output = (own(hidden) + tp_scatter(out_part) + b_down).astype(BF16)

    grad_hidden, grad_attended, grad_attended_t, sums_two = norm_back_rows(
        hidden, grad_rows, tp_terms(gn_part), ln2_gain
    )
    first_sums = z_sums(first_state, grad_attended)
    second_grads, first_sums = lax.optimization_barrier((second_grads, first_sums))
    second_grads = swap(second_grads, inverse=True)
    grad_mixed = dot_nn(grad_attended, full_out).astype(BF16)
    first_mlp = lax.psum_scatter(first_sums, "z", scatter_dimension=0, tiled=True)
    grads = attn_backward(segments, qkv, mixed, lse, grad_mixed, head_width, first_sums)
    block_rows = w_query.shape[0]
    pieces = weight_grads(order, normed_t, grads, grad_attended_t, mixed, grads)
    grad_normed_part = qkv_back(grads, full_attn, pieces[0])
    second_grads, first_mlp, grad_normed_part = lax.optimization_barrier(
        (second_grads, first_mlp, grad_normed_part)
    )
    second_mlp = lax.psum_scatter(second_grads, ("z", "y", "c"), scatter_dimension=0, tiled=True)
    grad_normed = tp_scatter(grad_normed_part)
    own_scaled, own_inverse = normalize(own_input.astype(F32))
    grad_own = own(grad_hidden) + norm_back(grad_normed, own_scaled, own_inverse, ln1_gain)
    grad_own = grad_own.astype(BF16)

    def place_part(values, full):
        return lax.dynamic_update_slice_in_dim(
            jnp.zeros((full,), F32), values, rank * values.shape[0], 0
        )

    sums = jnp.concatenate(
        [
            jnp.sum(grad_normed * own_scaled, axis=0),
            jnp.sum(grad_normed, axis=0),
            place_part(jnp.sum(grads[0].astype(F32), axis=0), width),
            place_part(jnp.sum(grads[2].astype(F32), axis=0), width),
            (sums_two[:3] * (1.0 / ranks)).reshape(-1),
            jnp.sum(own_grad.astype(F32), axis=0),
            place_part(jnp.concatenate([bias_first[0], bias_second[0]]), b_up.shape[0]),
        ]
    )
    columns = pieces[0].shape[1]
    filled = sums.shape[0]
    sums = jnp.pad(sums, (0, -filled % (8 * columns))).reshape(-1, columns)
    sums = core_sum(sums)
    state = scatter_near(pieces, None, [sums])
    first_mlp, state = lax.optimization_barrier((first_mlp, state))
    first_mlp = swap(first_mlp, inverse=True)
    last_sums = far_sums(state, [sums], first_mlp)
    own_output, grad_own, *last_sums = lax.optimization_barrier((own_output, grad_own, *last_sums))
    leaving = swap(jnp.concatenate([own_output, grad_own], axis=0), inverse=True)
    output, grad_input = leaving[:own_rows], leaving[own_rows:]
    shard = jax.ShapeDtypeStruct((block_rows, unit_width), F32)
    grad_w_up, grad_w_down = sums_call(
        functools.partial(units_last_kernel, tile=tile),
        [first_mlp, second_mlp],
        [shard, shard],
        None,
        "units_last",
    )
    *late, sums = sums_call(
        weights_last_kernel,
        far_parts(last_sums),
        [jax.ShapeDtypeStruct((block_rows, head_width), F32)] * 4
        + [jax.ShapeDtypeStruct(sums.shape, F32)],
        grad_w_up,
        "sums_last",
    )
    sums = (sums + hop(sums, 1, 0)).reshape(-1)
    small = [sums[i * width : (i + 1) * width] for i in range(8)]
    return (
        output, grad_input, small[0], small[1],
        late[0], late[1], late[2], small[2], small[3], late[3], small[4], small[5], small[6],
        grad_w_up, sums[8 * width : filled], grad_w_down, small[7],
    )


def solution(mesh):
    groups, ranks = mesh.shape["dp"], mesh.shape["tensor"]
    sizes = {"a": groups // 2, "h": 2, "l": ranks // 2}
    fine = Mesh(mesh.devices.reshape(groups // 4, 2, 2, 2, ranks // 2), ALL)
    rows = P(ALL, None)
    block = P(("z", "y", "c"), ("h", "l"))
    return jax.shard_map(
        functools.partial(per_device, sizes),
        mesh=fine,
        in_specs=(
            rows, P(("z", "y", "c")), P(), P(), block, block, block, P(), P(), block, P(), P(), P(),
            block, P(), block, P(), rows,
        ),
        out_specs=(
            rows, rows, P(), P(), block, block, block, P(), P(), block, P(), P(), P(), block, P(),
            block, P(),
        ),
        check_vma=False,
    )
```

```python
import functools

import jax
import jax.numpy as jnp
from jax import lax
from jax.experimental import pallas as pl
from jax.experimental.pallas import tpu as pltpu
from jax.sharding import Mesh
from jax.sharding import PartitionSpec as P

HEAD_DIM = 64
LANES = 128
TILE = 512
ROWS = 512
MASKED = -1e30
VMEM_BYTES = 60 * 1024 * 1024
F32 = jnp.float32
BF16 = jnp.bfloat16
TP = ("l", "c")
SWAP = ("c", "h", "l")
ALL = ("z", "y", "c", "h", "l")


def normalize(values):
    center = values - jnp.mean(values, axis=-1, keepdims=True)
    spread = jnp.mean(center * center, axis=-1, keepdims=True)
    inverse = lax.rsqrt(spread + 1e-05)
    return center * inverse, inverse


def norm_back(grad_in, scaled, inverse, gain_vec):
    local_grad = grad_in * gain_vec
    return inverse * (
        local_grad
        - jnp.mean(local_grad, axis=-1, keepdims=True)
        - scaled * jnp.mean(local_grad * scaled, axis=-1, keepdims=True)
    )


def dot_nn(left, right):
    return lax.dot_general(left, right, (((1,), (0,)), ((), ())), preferred_element_type=F32)


def dot_nt(left, right):
    return lax.dot_general(left, right, (((1,), (1,)), ((), ())), preferred_element_type=F32)


def dot_tn(left, right):
    return lax.dot_general(left, right, (((0,), (0,)), ((), ())), preferred_element_type=F32)


def fill_bias(bias, seg_col, seg_row):
    length = bias.shape[0]
    block = min(256, length)
    for first in range(0, length, block):
        keys = lax.broadcasted_iota(jnp.int32, (block, length), 0) + first
        places = lax.broadcasted_iota(jnp.int32, (block, length), 1)
        same = seg_col[first : first + block, :] == seg_row[...]
        bias[first : first + block, :] = jnp.where(same & (keys <= places), 0.0, MASKED)


def head_lanes(values, head):
    lane = lax.broadcasted_iota(jnp.int32, values.shape, 1)
    inside = (lane >= head * HEAD_DIM) & (lane < (head + 1) * HEAD_DIM)
    return jnp.where(inside, values, jnp.zeros_like(values))


def attn_forward_kernel(seg_col, seg_row, q_ref, k_ref, v_ref, mixed_ref, lse_ref, bias, v_t, block):
    length = q_ref.shape[0]
    heads = LANES // HEAD_DIM

    @pl.when(pl.program_id(0) == 0)
    def _():
        fill_bias(bias, seg_col, seg_row)

    v_t[...] = v_ref[...].T
    for place in range(length // block):
        rows = slice(place * block, (place + 1) * block)
        outs = []
        for head in range(heads):
            query = head_lanes(q_ref[rows, :], head)
            scores = []
            peak = None
            for other in range(place + 1):
                keys = slice(other * block, (other + 1) * block)
                part = dot_nt(k_ref[keys, :], query) + bias[keys, rows]
                top = jnp.max(part, axis=0, keepdims=True)
                peak = top if peak is None else jnp.maximum(peak, top)
                scores.append(part)
            total = None
            acc = None
            for other in range(place + 1):
                keys = slice(other * block, (other + 1) * block)
                weight = jnp.exp(scores[other] - peak)
                part_sum = jnp.sum(weight, axis=0, keepdims=True)
                total = part_sum if total is None else total + part_sum
                part_out = dot_nn(
                    v_t[head * HEAD_DIM : (head + 1) * HEAD_DIM, keys], weight.astype(BF16)
                )
                acc = part_out if acc is None else acc + part_out
            outs.append(acc / total)
            lse_ref[0, head : head + 1, rows] = peak + jnp.log(total)
        mixed_ref[rows, :] = jnp.concatenate(outs, axis=0).T.astype(BF16)


def attn_backward_kernel(
    seg_col, seg_row, q_ref, k_ref, v_ref, mixed_ref, lse_ref, g_ref, grads_ref, bias, k_t, delta, dq_t, block
):
    length = q_ref.shape[0]
    heads = LANES // HEAD_DIM
    count = length // block

    @pl.when(pl.program_id(0) == 0)
    def _():
        fill_bias(bias, seg_col, seg_row)

    k_t[...] = k_ref[...].T
    product = (g_ref[...].astype(F32) * mixed_ref[...].astype(F32)).T
    for head in range(heads):
        delta[head : head + 1, :] = jnp.sum(
            product[head * HEAD_DIM : (head + 1) * HEAD_DIM, :], axis=0, keepdims=True
        )
    for other in range(count):
        keys = slice(other * block, (other + 1) * block)
        key_sum = None
        value_sum = None
        for head in range(heads):
            lanes = slice(head * HEAD_DIM, (head + 1) * HEAD_DIM)
            for place in range(other, count):
                rows = slice(place * block, (place + 1) * block)
                query = head_lanes(q_ref[rows, :], head)
                grad = head_lanes(g_ref[rows, :], head)
                scores = dot_nt(k_ref[keys, :], query) + bias[keys, rows]
                probs = jnp.exp(scores - lse_ref[0, head : head + 1, rows])
                grad_probs = dot_nt(v_ref[keys, :], grad)
                grad_scores = (probs * (grad_probs - delta[head : head + 1, rows])).astype(BF16)
                value_part = dot_nn(probs.astype(BF16), grad)
                key_part = dot_nn(grad_scores, query)
                query_part = dot_nn(k_t[lanes, keys], grad_scores)
                value_sum = value_part if value_sum is None else value_sum + value_part
                key_sum = key_part if key_sum is None else key_sum + key_part
                if other == 0:
                    dq_t[lanes, rows] = query_part
                else:
                    dq_t[lanes, rows] += query_part
        grads_ref[1, keys, :] = key_sum.astype(BF16)
        grads_ref[2, keys, :] = value_sum.astype(BF16)
    grads_ref[0] = (dq_t[...].T * HEAD_DIM ** (-0.5)).astype(BF16)


def attn_forward(segments, qkv, width):
    length = qkv.shape[0]
    pairs = width // LANES
    block = min(256, length)
    column = lambda first: pl.BlockSpec((length, LANES), lambda p: (0, first * pairs + p))
    whole = lambda shape: pl.BlockSpec(shape, lambda p: (0, 0))
    return pl.pallas_call(
        functools.partial(attn_forward_kernel, block=block),
        grid=(pairs,),
        in_specs=[whole((length, 1)), whole((1, length)), column(0), column(1), column(2)],
        out_specs=[
            pl.BlockSpec((length, LANES), lambda p: (0, p)),
            pl.BlockSpec((1, 8, length), lambda p: (p, 0, 0)),
        ],
        out_shape=[
            jax.ShapeDtypeStruct((length, width), BF16),
            jax.ShapeDtypeStruct((pairs, 8, length), F32),
        ],
        scratch_shapes=[pltpu.VMEM((length, length), F32), pltpu.VMEM((LANES, length), BF16)],
        compiler_params=pltpu.CompilerParams(vmem_limit_bytes=VMEM_BYTES),
        cost_estimate=pl.CostEstimate(
            flops=4 * length * length * width,
            bytes_accessed=8 * length * width,
            transcendentals=length * length * width // (2 * HEAD_DIM),
        ),
        name="attn_forward",
    )(segments.reshape(length, 1), segments.reshape(1, length), qkv, qkv, qkv)


def attn_backward(segments, qkv, mixed, lse, grad_mixed, width, after):
    length = qkv.shape[0]
    pairs = width // LANES
    block = min(256, length)
    column = lambda first: pl.BlockSpec((length, LANES), lambda p: (0, first * pairs + p))
    whole = lambda shape: pl.BlockSpec(shape, lambda p: (0, 0))
    return pl.pallas_call(
        without(functools.partial(attn_backward_kernel, block=block), 8),
        grid=(pairs,),
        in_specs=[
            whole((length, 1)),
            whole((1, length)),
            column(0),
            column(1),
            column(2),
            pl.BlockSpec((length, LANES), lambda p: (0, p)),
            pl.BlockSpec((1, 8, length), lambda p: (p, 0, 0)),
            pl.BlockSpec((length, LANES), lambda p: (0, p)),
            pl.BlockSpec(memory_space=pl.ANY),
        ],
        out_specs=pl.BlockSpec((3, length, LANES), lambda p: (0, 0, p)),
        out_shape=jax.ShapeDtypeStruct((3, length, width), BF16),
        scratch_shapes=[
            pltpu.VMEM((length, length), F32),
            pltpu.VMEM((LANES, length), BF16),
            pltpu.VMEM((8, length), F32),
            pltpu.VMEM((LANES, length), F32),
        ],
        compiler_params=pltpu.CompilerParams(vmem_limit_bytes=VMEM_BYTES),
        cost_estimate=pl.CostEstimate(
            flops=10 * length * length * width,
            bytes_accessed=16 * length * width,
            transcendentals=length * length * width // (2 * HEAD_DIM),
        ),
        name="attn_backward",
    )(segments.reshape(length, 1), segments.reshape(1, length), qkv, qkv, qkv, mixed, lse, grad_mixed, after)


def piece_blocks(count):
    far = count // 4
    half = far // 2
    near, by_y, by_x, both = (list(range(i * far, (i + 1) * far)) for i in range(4))
    return [
        both[:half] + by_x[:half],
        both[half:] + by_y[half:],
        by_y[:half],
        by_x[half:],
        near,
    ]


def store_pieces(order, grad, piece_refs, columns):
    count = order.shape[0]
    rows = grad.shape[0] // count
    for blocks, ref in zip(piece_blocks(count), piece_refs):
        for place, block in enumerate(blocks):
            first = pl.multiple_of(order[block] * rows, rows)
            ref[place * rows : (place + 1) * rows, columns] = grad[pl.ds(first, rows), :]


def piece_shapes(count, rows, columns):
    return [
        jax.ShapeDtypeStruct((len(blocks) * rows, columns), BF16) for blocks in piece_blocks(count)
    ]


def whole_spec(shape, **options):
    return pl.BlockSpec(shape, lambda step: (0,) * len(shape), **options)


def norm_kernel(*refs, residual):
    if residual:
        x_ref, own_ref, other_ref, shift_ref, gain_ref, bias_ref, n_ref, nt_ref, hidden_ref = refs
        values = (
            x_ref[...].astype(F32)
            + (own_ref[...].astype(F32) + other_ref[...].astype(F32))
            + shift_ref[...]
        )
        hidden_ref[...] = values
    else:
        x_ref, gain_ref, bias_ref, n_ref, nt_ref = refs
        values = x_ref[...].astype(F32)
    scaled, _ = normalize(values)
    normed = (scaled * gain_ref[...] + bias_ref[...]).astype(BF16)
    n_ref[...] = normed
    nt_ref[...] = normed.T


def norm_rows(x, gain, bias, partials=None, shift=None):
    length, width = x.shape
    block = min(256, length)
    row = pl.BlockSpec((block, width), lambda step: (step, 0))
    vector = whole_spec((1, width))
    residual = partials is not None
    operands = [x] + (list(partials) + [shift.reshape(1, width)] if residual else [])
    operands += [gain.reshape(1, width), bias.reshape(1, width)]
    return pl.pallas_call(
        functools.partial(norm_kernel, residual=residual),
        grid=(length // block,),
        in_specs=[row] + ([row, row, vector] if residual else []) + [vector, vector],
        out_specs=[row, pl.BlockSpec((width, block), lambda step: (0, step))]
        + ([row] if residual else []),
        out_shape=[
            jax.ShapeDtypeStruct((length, width), BF16),
            jax.ShapeDtypeStruct((width, length), BF16),
        ]
        + ([jax.ShapeDtypeStruct((length, width), F32)] if residual else []),
        compiler_params=pltpu.CompilerParams(vmem_limit_bytes=VMEM_BYTES),
        cost_estimate=pl.CostEstimate(
            flops=20 * length * width, bytes_accessed=14 * length * width, transcendentals=length
        ),
        name="norm_two" if residual else "norm_one",
    )(*operands)


def norm_back_kernel(hidden_ref, g_ref, own_ref, other_ref, gain_ref, grad_ref, low_ref, low_t_ref, sums_ref):
    scaled, inverse = normalize(hidden_ref[...])
    incoming = own_ref[...].astype(F32) + other_ref[...].astype(F32)
    grad = g_ref[...].astype(F32) + norm_back(incoming, scaled, inverse, gain_ref[...])
    grad_ref[...] = grad
    low_ref[...] = grad.astype(BF16)
    low_t_ref[...] = grad.astype(BF16).T

    @pl.when(pl.program_id(0) == 0)
    def _():
        sums_ref[...] = jnp.zeros_like(sums_ref)

    sums_ref[0:1, :] += jnp.sum(grad, axis=0, keepdims=True)
    sums_ref[1:2, :] += jnp.sum(incoming * scaled, axis=0, keepdims=True)
    sums_ref[2:3, :] += jnp.sum(incoming, axis=0, keepdims=True)


def norm_back_rows(hidden, grad, partials, gain):
    length, width = hidden.shape
    block = min(256, length)
    row = pl.BlockSpec((block, width), lambda step: (step, 0))
    return pl.pallas_call(
        norm_back_kernel,
        grid=(length // block,),
        in_specs=[row, row, row, row, whole_spec((1, width))],
        out_specs=[
            row,
            row,
            pl.BlockSpec((width, block), lambda step: (0, step)),
            whole_spec((8, width)),
        ],
        out_shape=[
            jax.ShapeDtypeStruct((length, width), F32),
            jax.ShapeDtypeStruct((length, width), BF16),
            jax.ShapeDtypeStruct((width, length), BF16),
            jax.ShapeDtypeStruct((8, width), F32),
        ],
        compiler_params=pltpu.CompilerParams(vmem_limit_bytes=VMEM_BYTES),
        cost_estimate=pl.CostEstimate(
            flops=30 * length * width, bytes_accessed=16 * length * width, transcendentals=length
        ),
        name="norm_two_back",
    )(hidden, grad, *partials, gain.reshape(1, width))


def mlp_kernel(order, n_ref, g_ref, nt_ref, gt_ref, b_ref, w_ref, *refs, block, with_previous, cube):
    if with_previous:
        (before_out, before_gn), refs = refs[:2], refs[2:]
    (out_ref, gn_ref), refs = refs[:2], refs[2:]
    grad_refs, (gb_ref, out_acc, gn_acc, act, gpre, grad_w) = refs[:-6], refs[-6:]
    step = pl.program_id(0)
    length = n_ref.shape[0]
    tile = w_ref.shape[1] // 2
    ups, downs = slice(0, tile), slice(tile, 2 * tile)

    @pl.when(step == 0)
    def _():
        if with_previous:
            out_acc[...] = before_out[...].astype(F32)
            gn_acc[...] = before_gn[...].astype(F32)
        else:
            out_acc[...] = jnp.zeros_like(out_acc)
            gn_acc[...] = jnp.zeros_like(gn_acc)

    bias_sum = jnp.zeros(gb_ref.shape, F32)
    for first in range(0, length, block):
        rows = slice(first, first + block)
        unit = dot_nn(n_ref[rows, :], w_ref[:, ups]) + b_ref[...]
        grad = dot_nn(g_ref[rows, :], w_ref[:, downs])
        square = unit * unit
        curve = jnp.tanh(0.7978845608028654 * (unit + 0.044715 * (square * unit)))
        half = 0.5 + 0.5 * curve
        slope = half + (0.5 * unit) * (1.0 - curve * curve) * (
            0.7978845608028654 + (3 * 0.044715 * 0.7978845608028654) * square
        )
        active = (unit * half).astype(BF16)
        grad_pre = (grad * slope).astype(BF16)
        act[rows, :] = active
        gpre[rows, :] = grad_pre
        bias_sum = bias_sum + jnp.sum(grad_pre.astype(F32), axis=0, keepdims=True)
        out_acc[rows, :] += dot_nt(active, w_ref[:, downs])
        gn_acc[rows, :] += dot_nt(grad_pre, w_ref[:, ups])
    gb_ref[...] = bias_sum
    for columns, left, right in ((ups, nt_ref, gpre), (downs, gt_ref, act)):
        if cube:
            grad_w[...] = dot_nn(left[...], right[...]).astype(BF16)
            store_pieces(order, grad_w, grad_refs, columns)
        else:
            grad_refs[0][:, columns] = dot_nn(left[...], right[...]).astype(BF16)

    @pl.when(step == pl.num_programs(0) - 1)
    def _():
        out_ref[...] = out_acc[...].astype(BF16)
        gn_ref[...] = gn_acc[...].astype(BF16)


def mlp(order, normed, grad, normed_t, grad_t, weights, bias, previous, cube):
    length, width = normed.shape
    units = weights.shape[1] // 2
    tile = min(TILE, units)
    at_tile = lambda rows, columns: pl.BlockSpec((rows, columns), lambda u, o: (0, u))
    fixed = lambda shape: pl.BlockSpec(shape, lambda u, o: (0, 0))
    once = lambda shape: pl.BlockSpec(shape, lambda u, o: (0, 0), pipeline_mode=pl.Buffered(1))
    if cube:
        count = order.shape[0]
        grad_shapes = piece_shapes(count, width // count, 2 * units)
    else:
        grad_shapes = [jax.ShapeDtypeStruct((width, 2 * units), BF16)]
    results = pl.pallas_call(
        functools.partial(
            mlp_kernel, block=min(ROWS, length), with_previous=bool(previous), cube=cube
        ),
        grid_spec=pltpu.PrefetchScalarGridSpec(
            num_scalar_prefetch=1,
            grid=(units // tile,),
            in_specs=[
                once((length, width)),
                once((length, width)),
                once((width, length)),
                once((width, length)),
                at_tile(1, tile),
                at_tile(width, 2 * tile),
            ]
            + [once((length, width)) for _ in previous],
            out_specs=[fixed((length, width)), fixed((length, width))]
            + [at_tile(shape.shape[0], 2 * tile) for shape in grad_shapes]
            + [at_tile(1, tile)],
            scratch_shapes=[
                pltpu.VMEM((length, width), F32),
                pltpu.VMEM((length, width), F32),
                pltpu.VMEM((length, tile), BF16),
                pltpu.VMEM((length, tile), BF16),
                pltpu.VMEM((width, tile), BF16),
            ],
        ),
        out_shape=[jax.ShapeDtypeStruct((length, width), BF16)] * 2
        + grad_shapes
        + [jax.ShapeDtypeStruct((1, units), F32)],
        compiler_params=pltpu.CompilerParams(vmem_limit_bytes=VMEM_BYTES),
        cost_estimate=pl.CostEstimate(
            flops=12 * length * width * units,
            bytes_accessed=12 * length * width + 8 * width * units,
            transcendentals=length * units,
        ),
        name="mlp_second" if previous else "mlp_first",
    )(order, normed, grad, normed_t, grad_t, bias.reshape(1, units), weights, *previous)
    return results[0], results[1], results[2:-1], results[-1]


def qkv_kernel(n_ref, b_ref, w_ref, out_ref):
    scale = jnp.where(pl.program_id(0) == 0, HEAD_DIM ** (-0.5), 1.0)
    length = n_ref.shape[0]
    step = min(ROWS, length)
    for first in range(0, length, step):
        span = slice(first, first + step)
        out_ref[span, :] = ((dot_nn(n_ref[span, :], w_ref[...]) + b_ref[...]) * scale).astype(BF16)


def qkv_project(normed, weights, bias):
    length, width = normed.shape
    columns = weights.shape[1] // 4
    at_tile = lambda rows: pl.BlockSpec((rows, columns), lambda k: (0, k))
    return pl.pallas_call(
        qkv_kernel,
        grid=(3,),
        in_specs=[
            whole_spec((length, width), pipeline_mode=pl.Buffered(1)), at_tile(1), at_tile(width)
        ],
        out_specs=at_tile(length),
        out_shape=jax.ShapeDtypeStruct((length, 3 * columns), BF16),
        compiler_params=pltpu.CompilerParams(vmem_limit_bytes=VMEM_BYTES),
        cost_estimate=pl.CostEstimate(
            flops=6 * length * width * columns,
            bytes_accessed=2 * length * width + 6 * width * columns + 6 * length * columns,
            transcendentals=0,
        ),
        name="qkv_project",
    )(normed, bias.reshape(1, 3 * columns), weights)


def weight_kernel(order, nt_ref, grads_ref, gt_ref, mixed_ref, order_only, *refs):
    piece_refs, grad = refs[:5], refs[5]
    part = pl.program_id(0)

    @pl.when(part < 3)
    def _():
        grad[...] = dot_nn(nt_ref[...], grads_ref[0]).astype(BF16)

    @pl.when(part == 3)
    def _():
        grad[...] = dot_nn(gt_ref[...], mixed_ref[...]).astype(BF16)

    store_pieces(order, grad, piece_refs, slice(None))


def without(kernel, place):
    return lambda *refs: kernel(*refs[:place], *refs[place + 1 :])


ORDER_ONLY = pl.BlockSpec(memory_space=pl.ANY)


def weight_grads(order, normed_t, grads, grad_t, mixed, after):
    width, length = normed_t.shape
    columns = grads.shape[2]
    shapes = piece_shapes(order.shape[0], width // order.shape[0], 4 * columns)
    fixed = lambda shape: pl.BlockSpec(shape, lambda k, o: (0, 0), pipeline_mode=pl.Buffered(1))
    return pl.pallas_call(
        weight_kernel,
        grid_spec=pltpu.PrefetchScalarGridSpec(
            num_scalar_prefetch=1,
            grid=(4,),
            in_specs=[
                fixed((width, length)),
                pl.BlockSpec((1, length, columns), lambda k, o: (jnp.minimum(k, 2), 0, 0)),
                fixed((width, length)),
                fixed((length, columns)),
                ORDER_ONLY,
            ],
            out_specs=[
                pl.BlockSpec((shape.shape[0], columns), lambda k, o: (0, k)) for shape in shapes
            ],
            scratch_shapes=[pltpu.VMEM((width, columns), BF16)],
        ),
        out_shape=shapes,
        compiler_params=pltpu.CompilerParams(vmem_limit_bytes=VMEM_BYTES),
        cost_estimate=pl.CostEstimate(
            flops=8 * length * width * columns,
            bytes_accessed=4 * length * width + 16 * width * columns,
            transcendentals=0,
        ),
        name="weight_grads",
    )(order, normed_t, grads, grad_t, mixed, after)


def qkv_back_kernel(grads_ref, w_ref, out_ref):
    columns = grads_ref.shape[2]
    total = None
    for k in range(3):
        part = dot_nt(grads_ref[k], w_ref[:, k * columns : (k + 1) * columns])
        total = part if total is None else total + part
    out_ref[...] = total.astype(BF16)


def qkv_back(grads, weights, after):
    _, length, columns = grads.shape
    width = weights.shape[0]
    block = min(ROWS, length)
    return pl.pallas_call(
        without(qkv_back_kernel, 2),
        grid=(length // block,),
        in_specs=[
            pl.BlockSpec((3, block, columns), lambda i: (0, i, 0)),
            pl.BlockSpec((width, 4 * columns), lambda i: (0, 0), pipeline_mode=pl.Buffered(1)),
            ORDER_ONLY,
        ],
        out_specs=pl.BlockSpec((block, width), lambda i: (i, 0)),
        out_shape=jax.ShapeDtypeStruct((length, width), BF16),
        compiler_params=pltpu.CompilerParams(vmem_limit_bytes=VMEM_BYTES),
        cost_estimate=pl.CostEstimate(
            flops=6 * length * width * columns,
            bytes_accessed=2 * length * width + 6 * width * columns + 6 * length * columns,
            transcendentals=0,
        ),
        name="qkv_back",
    )(grads, weights, after)


def added(*terms):
    total = terms[0].astype(F32)
    for term in terms[1:]:
        total = total + term.astype(F32)
    return total.astype(BF16)


def high_low(values):
    high = values.astype(BF16).astype(F32)
    return jnp.concatenate([high, values - high], axis=0).astype(BF16)


def from_high_low(rows):
    rows = rows.astype(F32)
    half = rows.shape[0] // 2
    return rows[:half, :] + rows[half:, :]


def first_sums_kernel(from_x, from_y, keep_y, keep_x, *refs):
    small, (y_ref, x_ref) = refs[:-2], refs[-2:]
    half = y_ref.shape[0]
    y_ref[...] = added(keep_y[...], from_x[:half, :])
    x_ref[:half, :] = added(keep_x[...], from_y[:half, :])
    for values in small:
        x_ref[half:, :] = high_low(values[...])


def second_sums_kernel(from_x, from_y, near, from_y2, from_x2, *outs, with_small):
    if with_small:
        small, outs = outs[0], outs[1:]
    far = len(outs)
    half = from_y2.shape[0]
    rows = half * 2 // far
    if with_small:
        extra = high_low(small[...] + from_high_low(from_x2[half:, :]))
    for i, out in enumerate(outs):
        first, second, place = (from_x, from_y2, i) if i < far // 2 else (from_y, from_x2, i - far // 2)
        out[:rows, :] = added(
            near[i * rows : (i + 1) * rows, :],
            first[half + place * rows : half + (place + 1) * rows, :],
            second[place * rows : (place + 1) * rows, :],
        )
        if with_small:
            out[rows:, :] = extra


def z_sums_kernel(z_ref, from_x, from_y, near, from_y2, from_x2, out, *, far):
    half = from_y2.shape[0]
    rows = half * 2 // far
    for i in range(far):
        first, second, place = (from_x, from_y2, i) if i < far // 2 else (from_y, from_x2, i - far // 2)
        target = pl.multiple_of((z_ref[0] ^ i) * rows, rows)
        out[pl.ds(target, rows), :] = added(
            near[i * rows : (i + 1) * rows, :],
            first[half + place * rows : half + (place + 1) * rows, :],
            second[place * rows : (place + 1) * rows, :],
        )


def weights_last_kernel(*refs):
    parts, outs, small = refs[:-5], refs[-5:-1], refs[-1]
    total = parts[0][...].astype(F32)
    for part in parts[1:]:
        total = total + part[...].astype(F32)
    rows, columns = outs[0].shape
    for k, out in enumerate(outs):
        out[...] = total[:rows, k * columns : (k + 1) * columns]
    small[...] = from_high_low(total[rows:, :])


def units_last_kernel(first_ref, second_ref, up_ref, down_ref, *, tile):
    units = up_ref.shape[1] // 2
    for index, ref in enumerate((first_ref, second_ref)):
        for first in range(0, units, tile):
            columns = slice(index * units + first, index * units + first + tile)
            up_ref[:, columns] = ref[:, 2 * first : 2 * first + tile].astype(F32)
            down_ref[:, columns] = ref[:, 2 * first + tile : 2 * first + 2 * tile].astype(F32)


def shards_kernel(w_up, w_down, first_ref, second_ref, *, tile):
    units = first_ref.shape[1] // 2
    for index, ref in enumerate((first_ref, second_ref)):
        for first in range(0, units, tile):
            columns = slice(index * units + first, index * units + first + tile)
            ref[:, 2 * first : 2 * first + tile] = w_up[:, columns]
            ref[:, 2 * first + tile : 2 * first + 2 * tile] = w_down[:, columns]


def sums_call(kernel, operands, shapes, after, name):
    body = kernel if after is None else without(kernel, 0)
    vmem = pl.BlockSpec(memory_space=pltpu.VMEM)
    return pl.pallas_call(
        body,
        in_specs=([pl.BlockSpec(memory_space=pl.ANY)] if after is not None else [])
        + [vmem] * len(operands),
        out_specs=[vmem] * len(shapes),
        out_shape=shapes,
        compiler_params=pltpu.CompilerParams(vmem_limit_bytes=VMEM_BYTES),
        cost_estimate=pl.CostEstimate(flops=0, bytes_accessed=1024 * 1024, transcendentals=0),
        name=name,
    )(*([after] if after is not None else []), *operands)


def flipped(sizes):
    return 1 if sizes["h"] * sizes["l"] == 2 else 0


def moves(sizes):
    groups, ranks, inner = sizes["a"], sizes["h"] * sizes["l"], sizes["l"]
    far = groups // 2
    flip = flipped(sizes)
    swap_to = {}
    for group in range(2):
        for part in range(ranks):
            place = (part % 2 ^ flip) * ranks + group * (ranks // 2) + part // 2
            swap_to[group * ranks + part] = place

    def swap(values, inverse=False):
        pairs = [(to, frm) if inverse else (frm, to) for frm, to in swap_to.items()]
        return lax.ppermute(values, SWAP, pairs)

    def swap_hop(values, a_mask, inverse=False):
        pairs = []
        for a in range(groups):
            for frm, to in swap_to.items():
                one, two = a * 2 * ranks + frm, (a ^ a_mask) * 2 * ranks + to
                pairs.append((two, one) if inverse else (one, two))
        return lax.ppermute(values, ALL, pairs)

    def hop(values, a_mask, h_mask):
        pairs = []
        for a in range(groups):
            for c in range(2):
                for h in range(2):
                    pairs.append(((a * 2 + c) * 2 + h, ((a ^ a_mask) * 2 + c) * 2 + (h ^ h_mask)))
        return lax.ppermute(values, ("z", "y", "c", "h"), pairs)

    def scatter_near(pieces, after, small=()):
        from_x, from_y = hop(pieces[0], 0, 1), hop(pieces[1], 1, 0)
        half, columns = pieces[2].shape
        y_sum, x_sum = sums_call(
            first_sums_kernel,
            [from_x, from_y, pieces[2], pieces[3], *small],
            [
                jax.ShapeDtypeStruct((half, columns), BF16),
                jax.ShapeDtypeStruct(
                    (half + sum(2 * values.shape[0] for values in small), columns), BF16
                ),
            ],
            after,
            "sums_one",
        )
        return from_x, from_y, pieces[4], y_sum, x_sum

    def far_sums(state, small, after):
        from_x, from_y, near, y_sum, x_sum = state
        columns = near.shape[1]
        from_y2, from_x2 = hop(y_sum, 1, 0), hop(x_sum, 0, 1)
        rows = near.shape[0] // far + sum(2 * values.shape[0] for values in small)
        return sums_call(
            functools.partial(second_sums_kernel, with_small=bool(small)),
            [from_x, from_y, near, from_y2, from_x2] + small,
            [jax.ShapeDtypeStruct((rows, columns), BF16)] * far,
            after,
            "sums_two",
        )

    def z_sums(state, after):
        from_x, from_y, near, y_sum, x_sum = state
        from_y2, from_x2 = hop(y_sum, 1, 0), hop(x_sum, 0, 1)
        vmem = pl.BlockSpec(memory_space=pltpu.VMEM)
        return pl.pallas_call(
            without(functools.partial(z_sums_kernel, far=far), 6),
            in_specs=[pl.BlockSpec(memory_space=pltpu.SMEM)] + [vmem] * 5 + [ORDER_ONLY],
            out_specs=vmem,
            out_shape=jax.ShapeDtypeStruct(near.shape, BF16),
            compiler_params=pltpu.CompilerParams(vmem_limit_bytes=VMEM_BYTES),
            name="sums_two_z",
        )(lax.axis_index("z").reshape(1), from_x, from_y, near, from_y2, from_x2, after)

    def far_parts(sums):
        return [swap_hop(sums[i], 2 * i, inverse=True) for i in range(far)]

    def core_sum(values):
        values = values + lax.ppermute(values, "c", [(0, 1), (1, 0)])
        return lax.psum(values, "l") if inner > 1 else values

    a, h = lax.axis_index(("z", "y")), lax.axis_index("h")
    order = []
    for a_low, h_mask in ((0, 0), (1, 0), (0, 1), (1, 1)):
        for i in range(far):
            order.append((a ^ (2 * i + a_low)) * 2 + (h ^ h_mask))
    return swap, hop, scatter_near, far_sums, z_sums, far_parts, core_sum, jnp.stack(order).astype(jnp.int32)


def per_device(sizes, *arguments):
    (
        block_input, segment_ids, ln1_gain, ln1_bias, w_query, w_key, w_value, b_query, b_value,
        w_out, b_out, ln2_gain, ln2_bias, w_up, b_up, w_down, b_down, out_grad,
    ) = arguments
    ranks = sizes["h"] * sizes["l"]
    rank = lax.axis_index("l") * 2 + (lax.axis_index("c") ^ flipped(sizes))
    own_rows, width = block_input.shape
    head_width = w_query.shape[1]
    unit_width = w_up.shape[1]
    half_units = unit_width // 2
    tile = min(TILE, half_units)
    swap, hop, scatter_near, far_sums, z_sums, far_parts, core_sum, order = moves(sizes)

    def partner(values):
        return lax.ppermute(values, "c", [(0, 1), (1, 0)])

    def tp_gather(values):
        if ranks != 2:
            return lax.all_gather(values, TP, axis=0, tiled=True)
        theirs = partner(values)
        return jnp.where(
            rank == 0,
            jnp.concatenate([values, theirs], axis=0),
            jnp.concatenate([theirs, values], axis=0),
        )

    def tp_terms(values):
        if ranks != 2:
            others = lax.psum(values.astype(F32), TP) - values.astype(F32)
            return values, others.astype(BF16)
        return values, partner(values)

    def own(values):
        return lax.dynamic_slice_in_dim(values, rank * own_rows, own_rows)

    def tp_scatter_terms(values):
        if ranks != 2:
            total = lax.psum_scatter(values, TP, scatter_dimension=0, tiled=True)
            return total, jnp.zeros_like(total)
        theirs = lax.dynamic_slice_in_dim(values, (1 - rank) * own_rows, own_rows)
        return own(values), partner(theirs)

    def tp_scatter(values):
        own_part, other_part = tp_scatter_terms(values)
        return own_part.astype(F32) + other_part.astype(F32)

    own_input = swap(block_input)
    segments = swap(segment_ids)
    own_grad = swap(out_grad)
    shard_first, shard_second = sums_call(
        functools.partial(shards_kernel, tile=tile),
        [w_up, w_down],
        [jax.ShapeDtypeStruct(w_up.shape, BF16)] * 2,
        None,
        "mlp_shards",
    )
    early_attn = lax.all_gather(
        jnp.concatenate([w_query, w_key, w_value, w_out], axis=1), ("z", "y", "c"), axis=0, tiled=True
    )
    early_first = lax.all_gather(shard_first, ("z", "y", "c"), axis=0, tiled=True)
    shard_second = swap(shard_second)
    other_second = hop(shard_second, 0, 1)
    shard_second = jnp.where(
        lax.axis_index("h") == 0,
        jnp.concatenate([shard_second, other_second], axis=0),
        jnp.concatenate([other_second, shard_second], axis=0),
    )
    bias_query = lax.dynamic_slice_in_dim(b_query, rank * head_width, head_width)
    bias_value = lax.dynamic_slice_in_dim(b_value, rank * head_width, head_width)
    bias_up = lax.dynamic_slice_in_dim(b_up, rank * unit_width, unit_width)

    rows_in = tp_gather(own_input)
    grad_rows = tp_gather(own_grad)
    grad_rows_t = grad_rows.T
    normed, normed_t = norm_rows(rows_in, ln1_gain, ln1_bias)
    early_attn, normed, segments, grad_rows, grad_rows_t, shard_second = lax.optimization_barrier(
        (early_attn, normed, segments, grad_rows, grad_rows_t, shard_second)
    )
    full_second = lax.all_gather(shard_second, ("z", "y"), axis=0, tiled=True)
    full_attn = swap(early_attn)
    biases = jnp.concatenate([bias_query, jnp.zeros((head_width,), F32), bias_value])
    qkv = qkv_project(normed, full_attn, biases)
    full_out = full_attn[:, 3 * head_width :]
    early_first, qkv = lax.optimization_barrier((early_first, qkv))
    full_first = swap(early_first)
    mixed, lse = attn_forward(segments, qkv, head_width)
    attended = tp_terms(dot_nt(mixed, full_out).astype(BF16))
    normed_two, normed_two_t, hidden = norm_rows(rows_in, ln2_gain, ln2_bias, attended, b_out)

    out_part, gn_part, first_grads, bias_first = mlp(
        order, normed_two, grad_rows, normed_two_t, grad_rows_t, full_first,
        bias_up[:half_units], (), True,
    )
    full_second, gn_part = lax.optimization_barrier((full_second, gn_part))
    out_part, gn_part, second_grads, bias_second = mlp(
        order, normed_two, grad_rows, normed_two_t, grad_rows_t, full_second,
        bias_up[half_units:], (out_part, gn_part), False,
    )
    first_state = scatter_near(first_grads, gn_part)
    gn_part, second_grads, first_state = lax.optimization_barrier(
        (gn_part, second_grads[0], first_state)
    )
    own_output = (own(hidden) + tp_scatter(out_part) + b_down).astype(BF16)

    grad_hidden, grad_attended, grad_attended_t, sums_two = norm_back_rows(
        hidden, grad_rows, tp_terms(gn_part), ln2_gain
    )
    first_sums = z_sums(first_state, grad_attended)
    second_grads, first_sums = lax.optimization_barrier((second_grads, first_sums))
    second_grads = swap(second_grads, inverse=True)
    grad_mixed = dot_nn(grad_attended, full_out).astype(BF16)
    first_mlp = lax.psum_scatter(first_sums, "z", scatter_dimension=0, tiled=True)
    grads = attn_backward(segments, qkv, mixed, lse, grad_mixed, head_width, first_sums)
    block_rows = w_query.shape[0]
    pieces = weight_grads(order, normed_t, grads, grad_attended_t, mixed, grads)
    grad_normed_part = qkv_back(grads, full_attn, pieces[0])
    second_grads, first_mlp, grad_normed_part = lax.optimization_barrier(
        (second_grads, first_mlp, grad_normed_part)
    )
    second_mlp = lax.psum_scatter(second_grads, ("z", "y", "c"), scatter_dimension=0, tiled=True)
    grad_normed = tp_scatter(grad_normed_part)
    own_scaled, own_inverse = normalize(own_input.astype(F32))
    grad_own = own(grad_hidden) + norm_back(grad_normed, own_scaled, own_inverse, ln1_gain)
    grad_own = grad_own.astype(BF16)

    def place_part(values, full):
        return lax.dynamic_update_slice_in_dim(
            jnp.zeros((full,), F32), values, rank * values.shape[0], 0
        )

    sums = jnp.concatenate(
        [
            jnp.sum(grad_normed * own_scaled, axis=0),
            jnp.sum(grad_normed, axis=0),
            place_part(jnp.sum(grads[0].astype(F32), axis=0), width),
            place_part(jnp.sum(grads[2].astype(F32), axis=0), width),
            (sums_two[:3] * (1.0 / ranks)).reshape(-1),
            jnp.sum(own_grad.astype(F32), axis=0),
            place_part(jnp.concatenate([bias_first[0], bias_second[0]]), b_up.shape[0]),
        ]
    )
    columns = pieces[0].shape[1]
    filled = sums.shape[0]
    sums = jnp.pad(sums, (0, -filled % (8 * columns))).reshape(-1, columns)
    sums = core_sum(sums)
    state = scatter_near(pieces, own_output, [sums])
    first_mlp, state = lax.optimization_barrier((first_mlp, state))
    first_mlp = swap(first_mlp, inverse=True)
    last_sums = far_sums(state, [sums], first_mlp)
    own_output, grad_own, *last_sums = lax.optimization_barrier((own_output, grad_own, *last_sums))
    leaving = swap(jnp.concatenate([own_output, grad_own], axis=0), inverse=True)
    output, grad_input = leaving[:own_rows], leaving[own_rows:]
    shard = jax.ShapeDtypeStruct((block_rows, unit_width), F32)
    grad_w_up, grad_w_down = sums_call(
        functools.partial(units_last_kernel, tile=tile),
        [first_mlp, second_mlp],
        [shard, shard],
        None,
        "units_last",
    )
    *late, sums = sums_call(
        weights_last_kernel,
        far_parts(last_sums),
        [jax.ShapeDtypeStruct((block_rows, head_width), F32)] * 4
        + [jax.ShapeDtypeStruct(sums.shape, F32)],
        grad_w_up,
        "sums_last",
    )
    sums = (sums + hop(sums, 1, 0)).reshape(-1)
    small = [sums[i * width : (i + 1) * width] for i in range(8)]
    return (
        output, grad_input, small[0], small[1],
        late[0], late[1], late[2], small[2], small[3], late[3], small[4], small[5], small[6],
        grad_w_up, sums[8 * width : filled], grad_w_down, small[7],
    )


def solution(mesh):
    groups, ranks = mesh.shape["dp"], mesh.shape["tensor"]
    sizes = {"a": groups // 2, "h": 2, "l": ranks // 2}
    fine = Mesh(mesh.devices.reshape(groups // 4, 2, 2, 2, ranks // 2), ALL)
    rows = P(ALL, None)
    block = P(("z", "y", "c"), ("h", "l"))
    return jax.shard_map(
        functools.partial(per_device, sizes),
        mesh=fine,
        in_specs=(
            rows, P(("z", "y", "c")), P(), P(), block, block, block, P(), P(), block, P(), P(), P(),
            block, P(), block, P(), rows,
        ),
        out_specs=(
            rows, rows, P(), P(), block, block, block, P(), P(), block, P(), P(), P(), block, P(),
            block, P(),
        ),
        check_vma=False,
    )
```
